32 devices in a mesh: fsdp: 8 (over z, y), seq: 4 (over x, core).
Axes of the slice: x: 2, y: 2, z: 4, core: 2. Of those that a mesh axis runs over, the one named last changes fastest.
Arguments:
- tokens: bfloat16 [16, 2048, 768], P('fsdp', 'seq'), may hold values from -6 to 6
- counts: int32 [16, 4], P('fsdp'), may hold values from 256 to 512, as said below
- norm1_gain: bfloat16 [768], P('fsdp'), may hold values from 0.5 to 1.5
- norm1_bias: bfloat16 [768], P('fsdp'), may hold values from -4 to 4
- qkv_weight: bfloat16 [768, 2304], P('fsdp'), may hold values from -0.21875 to 0.21875
- query_bias: bfloat16 [768], P('fsdp'), may hold values from -4 to 4
- value_bias: bfloat16 [768], P('fsdp'), may hold values from -4 to 4
- proj_weight: bfloat16 [768, 768], P('fsdp'), may hold values from -0.875 to 0.875
- proj_bias: bfloat16 [768], P('fsdp'), may hold values from -4 to 4
- norm2_gain: bfloat16 [768], P('fsdp'), may hold values from 0.5 to 1.5
- norm2_bias: bfloat16 [768], P('fsdp'), may hold values from -4 to 4
- fc1_weight: bfloat16 [768, 3072], P('fsdp'), may hold values from -0.21875 to 0.21875
- fc1_bias: bfloat16 [3072], P('fsdp'), may hold values from -4 to 4
- fc2_weight: bfloat16 [3072, 768], P('fsdp'), may hold values from -0.109375 to 0.109375
- fc2_bias: bfloat16 [768], P('fsdp'), may hold values from -4 to 4
- cotangent: bfloat16 [16, 2048, 768], P('fsdp', 'seq'), may hold values from -6 to 6
Outputs:
- output: bfloat16 [16, 2048, 768], P('fsdp', 'seq')
- input_grad: float32 [16, 2048, 768], P('fsdp', 'seq')
- grad_norm1_gain: float32 [768], P('fsdp')
- grad_norm1_bias: float32 [768], P('fsdp')
- grad_qkv_weight: float32 [768, 2304], P('fsdp')
- grad_query_bias: float32 [768], P('fsdp')
- grad_value_bias: float32 [768], P('fsdp')
- grad_proj_weight: float32 [768, 768], P('fsdp')
- grad_proj_bias: float32 [768], P('fsdp')
- grad_norm2_gain: float32 [768], P('fsdp')
- grad_norm2_bias: float32 [768], P('fsdp')
- grad_fc1_weight: float32 [768, 3072], P('fsdp')
- grad_fc1_bias: float32 [3072], P('fsdp')
- grad_fc2_weight: float32 [3072, 768], P('fsdp')
- grad_fc2_bias: float32 [768], P('fsdp')
The draws below stay inside these ranges and needn't reach their ends.
Inputs may be any that keep to these rules, and one draw needn't show every extreme that they name: `counts`: in every image the first device along seq keeps all 512 of its slots; every other keeps at least half of them and fewer than all.
All inputs are finite; a program needn't handle non-finite values.
Results may differ from the reference program's by a relative error of at most 0.018.
Values may be sent and summed in bfloat16 or wider, within the bound.
No kernel may reach another device: no remote copies, remote signals or barrier semaphores. Data moves between devices by JAX's collectives and lax.ppermute only.
A program may use at most 320 MiB of HBM per device.

```python
import jax
import jax.numpy as jnp
from jax import lax

D = 768
HEADS = 12
HEAD_DIM = 64
FF = 3072
SLOT = 512
IMAGES = 16
N_SEQ = 4


def draw_counts(key, part):
    key = jax.random.fold_in(key, 5)
    others = jax.random.randint(key, (IMAGES, N_SEQ), SLOT // 2, SLOT)
    first_column = jnp.arange(N_SEQ, dtype=jnp.int32)[None, :] == 0
    return jnp.where(first_column, SLOT, others).astype(jnp.int32)


def shard_levels(own_key, shape, shards, low, top_value):
    factor_of, own = 1.0, jax.random.fold_in(own_key, 6)
    for axis_at, parts in shards:
        heights = jnp.exp(jax.random.uniform(jax.random.fold_in(own, axis_at), (parts,), jnp.float32, low / len(shards), top_value / len(shards)))
        factor_of = factor_of * jnp.repeat(heights, shape[axis_at] // parts).reshape([-1 if axis == axis_at else 1 for axis in range(len(shape))])
    return factor_of


def scatter_about(key, shape, spread, bound, cuts=(), held_as=jnp.bfloat16):
    entries = jax.random.normal(key, shape, jnp.float32) * spread
    if len(cuts) > 0:
        entries = shard_levels(key, shape, cuts, -0.22, 0.18) * entries
    return jnp.clip(entries, min=-bound, max=bound).astype(held_as)


def setup_inputs(seed: int = 0) -> dict:
    arg_keys = jax.random.split(jax.random.key(seed), 17)
    tokens = scatter_about(arg_keys[0], (IMAGES, N_SEQ * SLOT, D), 1.0, 6.0, ((0, 8), (1, 4)))
    counts = draw_counts(jax.random.fold_in(arg_keys[16], 71), 0)
    norm1_gain = jnp.clip(1.0 + 0.1 * jax.random.normal(arg_keys[2], (D,), jnp.float32), 0.5, 1.5).astype(jnp.bfloat16)
    norm1_bias = scatter_about(arg_keys[3], (D,), 0.3, 4.0, ((0, 8),))
    qkv_weight = scatter_about(arg_keys[4], (D, 3 * D), D ** -0.5, 0.21875, ((0, 8),))
    query_bias = scatter_about(arg_keys[5], (D,), 0.3, 4.0, ((0, 8),))
    value_bias = scatter_about(arg_keys[6], (D,), 0.3, 4.0, ((0, 8),))
    proj_weight = scatter_about(arg_keys[7], (D, D), (D // 16) ** -0.5, 0.875, ((0, 8),))
    proj_bias = scatter_about(arg_keys[8], (D,), 0.3, 4.0, ((0, 8),))
    norm2_gain = jnp.clip(1.0 + 0.1 * jax.random.normal(arg_keys[9], (D,), jnp.float32), 0.5, 1.5).astype(jnp.bfloat16)
    norm2_bias = scatter_about(arg_keys[10], (D,), 0.3, 4.0, ((0, 8),))
    fc1_weight = scatter_about(arg_keys[11], (D, FF), D ** -0.5, 0.21875, ((0, 8),))
    fc1_bias = scatter_about(arg_keys[12], (FF,), 0.3, 4.0, ((0, 8),))
    fc2_weight = scatter_about(arg_keys[13], (FF, D), FF ** -0.5, 0.109375, ((0, 8),))
    fc2_bias = scatter_about(arg_keys[14], (D,), 0.3, 4.0, ((0, 8),))
    cotangent = scatter_about(arg_keys[15], (IMAGES, N_SEQ * SLOT, D), 1.0, 6.0, ((0, 8), (1, 4)))
    return dict(tokens=tokens, counts=counts, norm1_gain=norm1_gain, norm1_bias=norm1_bias, qkv_weight=qkv_weight, query_bias=query_bias, value_bias=value_bias, proj_weight=proj_weight, proj_bias=proj_bias, norm2_gain=norm2_gain, norm2_bias=norm2_bias, fc1_weight=fc1_weight, fc1_bias=fc1_bias, fc2_weight=fc2_weight, fc2_bias=fc2_bias, cotangent=cotangent)


EPSILON = 1e-06
PRECISE = lax.Precision.HIGHEST

@jax.custom_vjp
def low(v):
    return lax.optimization_barrier(v.astype(jnp.bfloat16)).astype(jnp.float32)

@jax.custom_vjp
def low_back(v):
    return v

def low_keep(v):
    return (low(v), None)

def low_pass(kept, grad):
    return (grad,)

def back_keep(v):
    return (v, None)

def back_low(kept, grad):
    return (low(grad),)
low.defvjp(low_keep, low_pass)
low_back.defvjp(back_keep, back_low)

def layer_norm(values, gain, offset):
    center_mean = lax.optimization_barrier(jnp.mean(values, axis=-1, keepdims=True))
    centred = values - center_mean
    variance = lax.optimization_barrier(jnp.mean(centred * centred, axis=-1, keepdims=True))
    return centred * lax.rsqrt(variance + EPSILON) * gain + offset

def one_image(inputs, valid, params):
    norm1_gain, norm1_bias, qkv_weight, query_bias, value_bias, proj_weight, proj_bias, norm2_gain, norm2_bias, fc1_weight, fc1_bias, fc2_weight, fc2_bias = params
    length = inputs.shape[0]
    width = inputs.shape[1]
    normed = low(layer_norm(inputs, norm1_gain, norm1_bias))
    packed = jnp.dot(normed, qkv_weight, precision=PRECISE)
    queries = low(low_back(packed[:, :width] + query_bias)).reshape(length, HEADS, HEAD_DIM)
    keys_all = low(low_back(packed[:, width:2 * width])).reshape(length, HEADS, HEAD_DIM)
    values_all = low(low_back(packed[:, 2 * width:] + value_bias)).reshape(length, HEADS, HEAD_DIM)
    scores = low_back(jnp.einsum('qhe,khe->hqk', queries, keys_all, precision=PRECISE) * HEAD_DIM ** (-0.5))
    scores = jnp.where(valid[None, None, :], scores, -1e+30)
    probs = low(jax.nn.softmax(scores, axis=-1))
    mixed = jnp.einsum('hqk,khe->qhe', probs, values_all, precision=PRECISE).reshape(length, width)
    mixed = low(low_back(mixed))
    middle = inputs + low_back(jnp.dot(mixed, proj_weight, precision=PRECISE) + proj_bias)
    normed_two = low(layer_norm(middle, norm2_gain, norm2_bias))
    hidden = low_back(jnp.dot(normed_two, fc1_weight, precision=PRECISE) + fc1_bias)
    active = low(jax.nn.gelu(hidden, approximate=False))
    return middle + low_back(jnp.dot(active, fc2_weight, precision=PRECISE) + fc2_bias)

def reference(tokens, counts, norm1_gain, norm1_bias, qkv_weight, query_bias, value_bias, proj_weight, proj_bias, norm2_gain, norm2_bias, fc1_weight, fc1_bias, fc2_weight, fc2_bias, cotangent):
    params = tuple((element.astype(jnp.float32) for element in (norm1_gain, norm1_bias, qkv_weight, query_bias, value_bias, proj_weight, proj_bias, norm2_gain, norm2_bias, fc1_weight, fc1_bias, fc2_weight, fc2_bias)))
    inputs = tokens.astype(jnp.float32)
    places = jnp.arange(SLOT, dtype=jnp.int32)
    valid = (counts[:, :, None] > places[None, None, :]).reshape(IMAGES, N_SEQ * SLOT)
    blocked = jax.checkpoint(one_image)

    def forward(images_in, weights):
        return lax.map(lambda element: blocked(element[0], element[1], weights), (images_in, valid))
    result, pullback = jax.vjp(forward, inputs, params)
    input_grad, grads = pullback(cotangent.astype(jnp.float32))
    return (result.astype(jnp.bfloat16), input_grad, grads[0], grads[1], grads[2], grads[3], grads[4], grads[5], grads[6], grads[7], grads[8], grads[9], grads[10], grads[11], grads[12])
```

```python
import functools

import jax
import jax.numpy as jnp
from jax import lax
from jax.experimental import pallas as pl
from jax.experimental.pallas import tpu as pltpu
from jax.sharding import PartitionSpec as P

HEADS = 12
HEAD_DIM = 64
EPSILON = 1e-06
MASKED = -1e30
BF = jnp.bfloat16
F32 = jnp.float32
VMEM_BYTES = 60 * 1024 * 1024
PAIR = 2 * HEAD_DIM
VEC_ROWS = 16


def params(*semantics):
    return pltpu.CompilerParams(
        dimension_semantics=semantics, vmem_limit_bytes=VMEM_BYTES
    )


def dot(left, right, left_dim=1, right_dim=0):
    return lax.dot_general(
        left, right, (((left_dim,), (right_dim,)), ((), ())), preferred_element_type=F32
    )


def cost(flops, bytes_accessed, transcendentals=0):
    return pl.CostEstimate(
        flops=int(flops), bytes_accessed=int(bytes_accessed), transcendentals=int(transcendentals)
    )


def whole(shape):
    return pl.BlockSpec(shape, lambda *_: tuple(0 for _ in shape))


def key_bias(counts_ref, keys, slots):
    row = lax.broadcasted_iota(jnp.int32, (slots, PAIR), 0)
    parts = [
        jnp.where(row < counts_ref[at], 0.0, MASKED).astype(F32) for at in range(keys // slots)
    ]
    return jnp.concatenate(parts, axis=0)


def augment_keys(pair, bias, which, ones):
    lane = lax.broadcasted_iota(jnp.int32, pair.shape, 1)
    mine = (lane < HEAD_DIM) if which == 0 else (lane >= HEAD_DIM)
    start = HEAD_DIM if which == 0 else 0
    extra = jnp.where(
        lane == start, bias, jnp.where((lane > start) & (lane <= start + ones), 1.0, 0.0)
    )
    return jnp.where(mine, pair.astype(F32), extra).astype(BF)


def augment_values(pair, which, ones):
    lane = lax.broadcasted_iota(jnp.int32, pair.shape, 1)
    mine = (lane < HEAD_DIM) if which == 0 else (lane >= HEAD_DIM)
    start = HEAD_DIM if which == 0 else 0
    extra = jnp.where((lane >= start) & (lane < start + ones), 1.0, 0.0)
    return jnp.where(mine, pair.astype(F32), extra).astype(BF)


def pieces(value):
    first = value.astype(BF).astype(F32)
    rest = value - first
    second = rest.astype(BF).astype(F32)
    return first, second, rest - second


def extra_rows(rows, width):
    place = lax.broadcasted_iota(jnp.int32, (HEAD_DIM, width), 0)
    out = jnp.zeros((HEAD_DIM, width), F32)
    for at, row in enumerate(rows):
        out = jnp.where(place == at, row, out)
    return out.astype(BF)


def place_rows(head, extra, which):
    return jnp.concatenate([head, extra] if which == 0 else [extra, head], axis=0)


def attend_forward_kernel(
    slots, bq, chunk, counts_ref, k_ref, qt_ref, vt_ref, mixed_ref, ot_ref, lse_ref,
    kaug, vaug, s_a, s_b, m_a, m_b
):
    keys = k_ref.shape[0]
    step = pl.program_id(1)
    steps = pl.num_programs(1)
    scores = (s_a, s_b)
    peaks = (m_a, m_b)
    ones_row = extra_rows([jnp.ones((1, bq), F32)], bq)

    @pl.when(step == 0)
    def _():
        bias = key_bias(counts_ref, keys, slots)
        ones = jnp.ones((16, keys), BF)
        for which in range(2):
            kaug[which] = augment_keys(k_ref[...], bias, which, 0)
            vaug[which] = jnp.concatenate(
                [vt_ref[which * HEAD_DIM : (which + 1) * HEAD_DIM, :], ones], axis=0
            )

    def query_block(at, which):
        head = qt_ref[which * HEAD_DIM : (which + 1) * HEAD_DIM, pl.ds(at * bq, bq)]
        head = (head.astype(F32) * HEAD_DIM ** (-0.5)).astype(BF)
        return place_rows(head, ones_row, which)

    def score_chunk(query, which, at, peak):
        rows = slice(at * chunk, (at + 1) * chunk)
        s = dot(kaug[which, rows, :], query)
        scores[which][rows, :] = s
        top = jnp.max(s.reshape(chunk // 8, 8, bq), axis=0)
        return top if peak is None else jnp.maximum(peak, top)

    def weigh_chunk(which, at, peak, total):
        rows = slice(at * chunk, (at + 1) * chunk)
        p = jnp.exp(scores[which][rows, :] - peak).astype(BF)
        o = dot(vaug[which, :, rows], p)
        return o if total is None else total + o

    @pl.when(step == 0)
    def _():
        query = query_block(0, 0)
        peak = None
        for at in range(keys // chunk):
            peak = score_chunk(query, 0, at, peak)
        m_a[...] = peak

    later = jnp.minimum(step + 1, steps - 1)
    outs = []
    for which in range(2):
        other = 1 - which
        query = query_block(step if which == 0 else later, other)
        peak = jnp.max(peaks[which][...], axis=0, keepdims=True)
        next_peak, total = None, None
        for at in range(keys // chunk):
            next_peak = score_chunk(query, other, at, next_peak)
            total = weigh_chunk(which, at, peak, total)
        peaks[other][...] = next_peak
        norm = total[HEAD_DIM : HEAD_DIM + 1, :]
        outs.append(total[:HEAD_DIM, :] * (1.0 / norm))
        lse_ref[0, which : which + 1, :] = peak + jnp.log(norm)
    both = jnp.concatenate(outs, axis=0)
    ot_ref[...] = both
    mixed_ref[...] = both.T.astype(BF)


def attend_forward(counts, packed, packed_t, slots):
    keys, width = packed.shape
    width //= 3
    pairs = width // PAIR
    bq, chunk = 256, 256
    kernel = functools.partial(attend_forward_kernel, slots, bq, chunk)
    return pl.pallas_call(
        kernel,
        grid=(pairs, keys // bq),
        in_specs=[
            pl.BlockSpec(memory_space=pltpu.SMEM),
            pl.BlockSpec((keys, PAIR), lambda p, i: (0, pairs + p)),
            pl.BlockSpec((PAIR, keys), lambda p, i: (p, 0)),
            pl.BlockSpec((PAIR, keys), lambda p, i: (2 * pairs + p, 0)),
        ],
        out_specs=[
            pl.BlockSpec((bq, PAIR), lambda p, i: (i, p)),
            pl.BlockSpec((PAIR, bq), lambda p, i: (p, i)),
            pl.BlockSpec((1, 8, bq), lambda p, i: (p, 0, i)),
        ],
        out_shape=[
            jax.ShapeDtypeStruct((keys, width), BF),
            jax.ShapeDtypeStruct((width, keys), F32),
            jax.ShapeDtypeStruct((pairs, 8, keys), F32),
        ],
        scratch_shapes=[
            pltpu.VMEM((2, keys, PAIR), BF),
            pltpu.VMEM((2, HEAD_DIM + 16, keys), BF),
            pltpu.VMEM((keys, bq), F32),
            pltpu.VMEM((keys, bq), F32),
            pltpu.VMEM((8, bq), F32),
            pltpu.VMEM((8, bq), F32),
        ],
        compiler_params=params("arbitrary", "arbitrary"),
        cost_estimate=cost(
            2 * pairs * 2 * 2 * keys * keys * 256, 12 * keys * width, 2 * pairs * keys * keys
        ),
        name="attend_forward",
    )(counts, packed, packed_t, packed_t)


def attend_backward_kernel(
    slots, bq, chunk, counts_ref, q_ref, k_ref, v_ref, qt_ref, kt_ref, do_ref, dot_ref, ot_ref,
    lse_ref, gq_ref, gk_ref, gv_ref, kaug, vaug, acc_k, acc_v
):
    keys = k_ref.shape[0]
    step = pl.program_id(1)
    steps = pl.num_programs(1)
    scale = HEAD_DIM ** (-0.5)

    @pl.when(step == 0)
    def _():
        bias = key_bias(counts_ref, keys, slots)
        for which in range(2):
            kaug[which] = augment_keys(k_ref[...], bias, which, 3)
            vaug[which] = augment_values(v_ref[...], which, 3)
        acc_k[...] = jnp.zeros_like(acc_k)
        acc_v[...] = jnp.zeros_like(acc_v)

    ones_row = jnp.ones((1, bq), F32)
    queries, grads = [], []
    for which in range(2):
        rows = slice(which * HEAD_DIM, (which + 1) * HEAD_DIM)
        head = (qt_ref[rows, :].astype(F32) * scale).astype(BF)
        log_total = lse_ref[0, which : which + 1, :]
        queries.append(
            place_rows(head, extra_rows([ones_row, *pieces(-log_total)], bq), which)
        )
        grad = dot_ref[rows, :]
        delta = jnp.sum(grad.astype(F32) * ot_ref[rows, :], axis=0, keepdims=True)
        grads.append(place_rows(grad, extra_rows(list(pieces(-delta)), bq), which))

    do_pair = do_ref[...]
    q_pair = q_ref[...]
    totals = [None, None]
    for at in range(keys // chunk):
        rows = slice(at * chunk, (at + 1) * chunk)
        for which in range(2):
            p = jnp.exp(dot(kaug[which, rows, :], queries[which]))
            dp = dot(vaug[which, rows, :], grads[which])
            p_low = p.astype(BF)
            ds = (p * dp).astype(BF)
            acc_v[which, rows, :] += dot(p_low, do_pair)
            acc_k[which, rows, :] += dot(ds, q_pair)
            part = dot(kt_ref[which * HEAD_DIM : (which + 1) * HEAD_DIM, rows], ds)
            totals[which] = part if totals[which] is None else totals[which] + part
    both = jnp.concatenate(totals, axis=0) * scale
    gq_ref[...] = both.T.astype(BF)

    @pl.when(step == steps - 1)
    def _():
        lane = lax.broadcasted_iota(jnp.int32, (keys, PAIR), 1)
        gk_ref[...] = (jnp.where(lane < HEAD_DIM, acc_k[0], acc_k[1]) * scale).astype(BF)
        gv_ref[...] = jnp.where(lane < HEAD_DIM, acc_v[0], acc_v[1]).astype(BF)


def attend_backward(counts, packed, packed_t, grad, grad_t, result_t, log_total, slots):
    keys, width = packed.shape
    width //= 3
    pairs = width // PAIR
    bq, chunk = 512, 256
    kernel = functools.partial(attend_backward_kernel, slots, bq, chunk)
    return pl.pallas_call(
        kernel,
        grid=(pairs, keys // bq),
        in_specs=[
            pl.BlockSpec(memory_space=pltpu.SMEM),
            pl.BlockSpec((bq, PAIR), lambda p, i: (i, p)),
            pl.BlockSpec((keys, PAIR), lambda p, i: (0, pairs + p)),
            pl.BlockSpec((keys, PAIR), lambda p, i: (0, 2 * pairs + p)),
            pl.BlockSpec((PAIR, bq), lambda p, i: (p, i)),
            pl.BlockSpec((PAIR, keys), lambda p, i: (pairs + p, 0)),
            pl.BlockSpec((bq, PAIR), lambda p, i: (i, p)),
            pl.BlockSpec((PAIR, bq), lambda p, i: (p, i)),
            pl.BlockSpec((PAIR, bq), lambda p, i: (p, i)),
            pl.BlockSpec((1, 8, bq), lambda p, i: (p, 0, i)),
        ],
        out_specs=[
            pl.BlockSpec((bq, PAIR), lambda p, i: (i, p)),
            pl.BlockSpec((keys, PAIR), lambda p, i: (0, p)),
            pl.BlockSpec((keys, PAIR), lambda p, i: (0, p)),
        ],
        out_shape=[jax.ShapeDtypeStruct((keys, width), BF)] * 3,
        scratch_shapes=[
            pltpu.VMEM((2, keys, PAIR), BF),
            pltpu.VMEM((2, keys, PAIR), BF),
            pltpu.VMEM((2, keys, PAIR), F32),
            pltpu.VMEM((2, keys, PAIR), F32),
        ],
        compiler_params=params("arbitrary", "arbitrary"),
        cost_estimate=cost(
            2 * pairs * 5 * 2 * keys * keys * 256, 24 * keys * width, 2 * pairs * keys * keys
        ),
        name="attend_backward",
    )(counts, packed, packed, packed, packed_t, packed_t, grad, grad_t, result_t, log_total)


def normalised(values):
    centred = values - jnp.mean(values, axis=-1, keepdims=True)
    variance = jnp.mean(centred * centred, axis=-1, keepdims=True)
    inverse = lax.rsqrt(variance + EPSILON)
    return centred * inverse, inverse


def norm_pull(grad, gain, unit, inverse):
    scaled = grad * gain
    mean = jnp.mean(scaled, axis=-1, keepdims=True)
    along = jnp.mean(scaled * unit, axis=-1, keepdims=True)
    return inverse * (scaled - mean - unit * along)


def fold(values):
    return jnp.sum(values.reshape(values.shape[0] // 8, 8, values.shape[1]), axis=0)


def feed_forward_kernel(
    chunk, tok_ref, mo_ref, ms_ref, cot_ref, wpo_ref, wps_ref, g2_ref, vec_ref, f1b_ref,
    mid_ref, out_ref, gn_ref, dw1_ref, dw2_ref, gf1_ref, gf2_ref, acc1, acc2, accb, accc
):
    step = pl.program_id(0)
    steps = pl.num_programs(0)
    width = tok_ref.shape[1]
    half = f1b_ref.shape[1]

    @pl.when(step == 0)
    def _():
        acc1[...] = jnp.zeros_like(acc1)
        acc2[...] = jnp.zeros_like(acc2)
        accb[...] = jnp.zeros_like(accb)
        accc[...] = jnp.zeros_like(accc)

    middle = (
        tok_ref[...].astype(F32)
        + dot(mo_ref[...], wpo_ref[...])
        + dot(ms_ref[...], wps_ref[...])
        + vec_ref[0:1, :]
    )
    mid_ref[...] = middle
    unit, _ = normalised(middle)
    normed = (unit * vec_ref[1:2, :] + vec_ref[2:3, :]).astype(BF)
    cot = cot_ref[...]
    out = None
    grad = None
    for at in range(half // chunk):
        cols = slice(at * chunk, (at + 1) * chunk)
        w1 = g2_ref[:, width + at * chunk : width + (at + 1) * chunk]
        piece, row = divmod(at * chunk, width)
        start = width + half + piece * width
        w2 = g2_ref[row : row + chunk, start : start + width]
        hidden = dot(normed, w1) + f1b_ref[0:1, cols]
        below = 0.5 + 0.5 * lax.erf(hidden * (0.5**0.5))
        slope = below + hidden * (jnp.exp(hidden * hidden * -0.5) * 0.3989422804014327)
        active = (hidden * below).astype(BF)
        grad_hidden = (dot(cot, w2, 1, 1) * slope).astype(BF)
        more = dot(active, w2)
        out = more if out is None else out + more
        more = dot(grad_hidden, w1, 1, 1)
        grad = more if grad is None else grad + more
        acc1[:, cols] += dot(normed, grad_hidden, 0, 0)
        acc2[cols, :] += dot(active, cot, 0, 0)
        accb[:, cols] += fold(grad_hidden.astype(F32))
    accc[...] += fold(cot.astype(F32))
    out_ref[...] = out.astype(BF)
    gn_ref[...] = grad.astype(BF)

    @pl.when(step == steps - 1)
    def _():
        dw1_ref[...] = acc1[...].astype(BF)
        dw2_ref[...] = acc2[...].astype(BF)
        gf1_ref[...] = accb[...]
        gf2_ref[...] = accc[...]


def feed_forward(tokens, mixed_own, mixed_sib, cot, wp_own, wp_sib, weights, vec, f1b):
    rows, width = tokens.shape
    half = f1b.shape[1]
    heads = mixed_own.shape[1]
    bt, chunk = 256, 384
    blocks = rows // bt
    kernel = functools.partial(feed_forward_kernel, chunk)
    return pl.pallas_call(
        kernel,
        grid=(blocks,),
        in_specs=[
            pl.BlockSpec((bt, width), lambda i: (i, 0)),
            pl.BlockSpec((bt, heads), lambda i: (i, 0)),
            pl.BlockSpec((bt, heads), lambda i: (lax.rem(i + blocks // 2, blocks), 0)),
            pl.BlockSpec((bt, width), lambda i: (i, 0)),
            whole(wp_own.shape),
            whole(wp_sib.shape),
            whole(weights.shape),
            whole(vec.shape),
            whole(f1b.shape),
        ],
        out_specs=[
            pl.BlockSpec((bt, width), lambda i: (i, 0)),
            pl.BlockSpec((bt, width), lambda i: (i, 0)),
            pl.BlockSpec((bt, width), lambda i: (i, 0)),
            whole((width, half)),
            whole((half, width)),
            whole((8, half)),
            whole((8, width)),
        ],
        out_shape=[
            jax.ShapeDtypeStruct((rows, width), F32),
            jax.ShapeDtypeStruct((rows, width), BF),
            jax.ShapeDtypeStruct((rows, width), BF),
            jax.ShapeDtypeStruct((width, half), BF),
            jax.ShapeDtypeStruct((half, width), BF),
            jax.ShapeDtypeStruct((8, half), F32),
            jax.ShapeDtypeStruct((8, width), F32),
        ],
        scratch_shapes=[
            pltpu.VMEM((width, half), F32),
            pltpu.VMEM((half, width), F32),
            pltpu.VMEM((8, half), F32),
            pltpu.VMEM((8, width), F32),
        ],
        compiler_params=params("arbitrary"),
        cost_estimate=cost(
            2 * rows * width * (6 * half + width), 20 * rows * width + 8 * width * half,
            2 * rows * half,
        ),
        name="feed_forward",
    )(tokens, mixed_own, mixed_sib, cot, wp_own, wp_sib, weights, vec, f1b)


def branch_kernel(
    core_ref, mid_ref, ga_ref, gb_ref, cot_ref, mo_ref, ms_ref, wpo_ref, vec_ref,
    gm_ref, do_ref, dot_ref, dwo_ref, dws_ref, vecs_ref, acco, accs, accv, low_ref
):
    step = pl.program_id(0)
    steps = pl.num_programs(0)
    half = do_ref.shape[1]

    @pl.when(step == 0)
    def _():
        acco[...] = jnp.zeros_like(acco)
        accs[...] = jnp.zeros_like(accs)
        accv[...] = jnp.zeros_like(accv)

    unit, inverse = normalised(mid_ref[...])
    grad = ga_ref[...].astype(F32) + gb_ref[...].astype(F32)
    accv[0:8, :] += fold(grad * unit)
    accv[8:16, :] += fold(grad)
    grad_middle = cot_ref[...].astype(F32) + norm_pull(grad, vec_ref[1:2, :], unit, inverse)

    @pl.when(step < steps // 2)
    def _():
        gm_ref[...] = grad_middle

    low = grad_middle.astype(BF)
    low_ref[...] = low
    accv[16:24, :] += fold(low.astype(F32))
    do_ref[...] = dot(low, wpo_ref[...], 1, 1).astype(BF)
    dot_ref[...] = dot(wpo_ref[...], low, 1, 1).astype(BF)
    mine = low_ref[:, pl.ds(pl.multiple_of(core_ref[0] * half, half), half)]
    acco[...] += dot(mo_ref[...], mine, 0, 0)
    accs[...] += dot(ms_ref[...], mine, 0, 0)

    @pl.when(step == steps - 1)
    def _():
        dwo_ref[...] = acco[...].astype(BF)
        dws_ref[...] = accs[...].astype(BF)
        vecs_ref[...] = accv[...]


def branch(core, middle, grad_own, grad_sib, cot, mixed_own, mixed_sib, wp_own, vec):
    rows, width = middle.shape
    half = mixed_own.shape[1]
    bt = 256
    blocks = rows // bt
    swap = lambda i: (lax.rem(i + blocks // 2, blocks), 0)
    straight = lambda i: (i, 0)
    return pl.pallas_call(
        branch_kernel,
        grid=(blocks,),
        in_specs=[
            pl.BlockSpec(memory_space=pltpu.SMEM),
            pl.BlockSpec((bt, width), straight),
            pl.BlockSpec((bt, width), straight),
            pl.BlockSpec((bt, width), swap),
            pl.BlockSpec((bt, width), straight),
            pl.BlockSpec((bt, half), straight),
            pl.BlockSpec((bt, half), swap),
            whole(wp_own.shape),
            whole(vec.shape),
        ],
        out_specs=[
            pl.BlockSpec((bt, width), lambda i: (jnp.minimum(i, blocks // 2 - 1), 0)),
            pl.BlockSpec((bt, half), straight),
            pl.BlockSpec((half, bt), lambda i: (0, i)),
            whole((half, half)),
            whole((half, half)),
            whole((24, width)),
        ],
        out_shape=[
            jax.ShapeDtypeStruct((rows // 2, width), F32),
            jax.ShapeDtypeStruct((rows, half), BF),
            jax.ShapeDtypeStruct((half, rows), BF),
            jax.ShapeDtypeStruct((half, half), BF),
            jax.ShapeDtypeStruct((half, half), BF),
            jax.ShapeDtypeStruct((24, width), F32),
        ],
        scratch_shapes=[
            pltpu.VMEM((half, half), F32),
            pltpu.VMEM((half, half), F32),
            pltpu.VMEM((24, width), F32),
            pltpu.VMEM((bt, width), BF),
        ],
        compiler_params=params("arbitrary"),
        cost_estimate=cost(2 * rows * width * 3 * half, 18 * rows * width),
        name="branch",
    )(core, middle, grad_own, grad_sib, cot, mixed_own, mixed_sib, wp_own, vec)


def project_back_kernel(
    tok_ref, gq_ref, gk_ref, gv_ref, w_ref, vec_ref,
    own_ref, sib_ref, dw_ref, vecs_ref, qv_ref, accw, accv, accqv
):
    step = pl.program_id(0)
    steps = pl.num_programs(0)
    part = gq_ref.shape[1]

    @pl.when(step == 0)
    def _():
        accw[...] = jnp.zeros_like(accw)
        accv[...] = jnp.zeros_like(accv)
        accqv[...] = jnp.zeros_like(accqv)

    unit, _ = normalised(tok_ref[...].astype(F32))
    normed = (unit * vec_ref[0:1, :] + vec_ref[1:2, :]).astype(BF)
    grad = None
    for at, ref in enumerate((gq_ref, gk_ref, gv_ref)):
        cols = slice(at * part, (at + 1) * part)
        value = ref[...]
        more = dot(value, w_ref[:, cols], 1, 1)
        grad = more if grad is None else grad + more
        accw[:, cols] += dot(normed, value, 0, 0)
        if at != 1:
            here = 0 if at == 0 else 8
            accqv[here : here + 8, :] += fold(value.astype(F32))
    accv[0:8, :] += fold(grad * unit)
    accv[8:16, :] += fold(grad)

    @pl.when(step < steps // 2)
    def _():
        own_ref[...] = grad

    @pl.when(step >= steps // 2)
    def _():
        sib_ref[...] = grad.astype(BF)

    @pl.when(step == steps - 1)
    def _():
        dw_ref[...] = accw[...].astype(BF)
        vecs_ref[...] = accv[...]
        qv_ref[...] = accqv[...]


def project_back(tokens, gq, gk, gv, weight, vec):
    rows, width = tokens.shape
    part = gq.shape[1]
    bt = 256
    blocks = rows // bt
    straight = lambda i: (i, 0)
    return pl.pallas_call(
        project_back_kernel,
        grid=(blocks,),
        in_specs=[
            pl.BlockSpec((bt, width), straight),
            pl.BlockSpec((bt, part), straight),
            pl.BlockSpec((bt, part), straight),
            pl.BlockSpec((bt, part), straight),
            whole(weight.shape),
            whole(vec.shape),
        ],
        out_specs=[
            pl.BlockSpec((bt, width), lambda i: (jnp.minimum(i, blocks // 2 - 1), 0)),
            pl.BlockSpec((bt, width), lambda i: (jnp.maximum(i - blocks // 2, 0), 0)),
            whole((width, 3 * part)),
            whole((16, width)),
            whole((16, part)),
        ],
        out_shape=[
            jax.ShapeDtypeStruct((rows // 2, width), F32),
            jax.ShapeDtypeStruct((rows // 2, width), BF),
            jax.ShapeDtypeStruct((width, 3 * part), BF),
            jax.ShapeDtypeStruct((16, width), F32),
            jax.ShapeDtypeStruct((16, part), F32),
        ],
        scratch_shapes=[
            pltpu.VMEM((width, 3 * part), F32),
            pltpu.VMEM((16, width), F32),
            pltpu.VMEM((16, part), F32),
        ],
        compiler_params=params("arbitrary"),
        cost_estimate=cost(2 * rows * width * 6 * part, 14 * rows * width),
        name="project_back",
    )(tokens, gq, gk, gv, weight, vec)


def per_device(
    tokens,
    counts,
    norm1_gain,
    norm1_bias,
    qkv_weight,
    query_bias,
    value_bias,
    proj_weight,
    proj_bias,
    norm2_gain,
    norm2_bias,
    fc1_weight,
    fc1_bias,
    fc2_weight,
    fc2_bias,
    cotangent,
):
    images, slots, width = tokens.shape
    owners = lax.axis_size("fsdp")
    seq = lax.axis_size("seq")
    place = lax.axis_index("seq")
    core = lax.rem(place, 2)
    image = place // 2
    part = width // 2
    shard = width // owners
    ff = fc1_weight.shape[1]
    ff_shard = ff // owners
    quarter = ff_shard // 4
    half = ff // 2
    to_sibling = [(at, at ^ 1) for at in range(seq)]
    to_partner = [(at, at ^ 2) for at in range(seq)]

    def sibling(value):
        return lax.ppermute(value, "seq", to_sibling)

    def partner(value):
        return lax.ppermute(value, "seq", to_partner)

    def pick(value, at, axis):
        return lax.dynamic_index_in_dim(value, at, axis, keepdims=False)

    qkv_half = pick(qkv_weight.reshape(shard, 3, 2, part), core, 2).reshape(shard, 3 * part)
    small = jnp.concatenate(
        [
            norm1_gain, norm1_bias, query_bias, value_bias, proj_bias, norm2_gain, norm2_bias,
            fc2_bias, fc1_bias,
        ]
    )
    small_row = jnp.zeros((VEC_ROWS, 3 * part), BF).at[0, : small.shape[0]].set(small)
    first = lax.all_gather(
        jnp.concatenate([qkv_half, small_row], axis=0), "fsdp", axis=0, tiled=False
    )
    fc1_half = pick(fc1_weight.reshape(shard, owners, 2, 2, quarter), core, 2)
    fc1_half = fc1_half.transpose(0, 2, 1, 3).reshape(shard, half)
    fc2_half = lax.dynamic_slice_in_dim(fc2_weight, core * 2 * quarter, 2 * quarter, 0)
    fc2_half = fc2_half.reshape(2, quarter, width).transpose(1, 0, 2).reshape(shard, 2 * width)
    second = lax.all_gather(
        jnp.concatenate([proj_weight, fc1_half, fc2_half], axis=1), "fsdp", axis=0, tiled=True
    )

    def collect(value):
        mine = pick(value, image, 0)
        theirs = partner(pick(value, 1 - image, 0))
        return jnp.concatenate([mine, theirs, sibling(mine), sibling(theirs)], axis=0)

    tok = collect(tokens)
    kept = pick(counts, image, 0)
    kept = jnp.stack([pick(kept, place ^ at, 0) for at in (0, 2, 1, 3)])
    core_row = core.reshape(1).astype(jnp.int32)

    w_qkv = first[:, :shard].reshape(width, 3 * part)
    vecs = first[:, shard, : small.shape[0]].astype(F32)
    g1, b1, qb, vb, pb, g2, b2, f2b = (
        vecs[:, at * shard : (at + 1) * shard].reshape(width) for at in range(8)
    )
    f1b = pick(vecs[:, 8 * shard :].reshape(owners, 2, 2, quarter), core, 1)
    f1b = f1b.transpose(1, 0, 2).reshape(1, half)

    def mine_of(vector):
        return lax.dynamic_slice_in_dim(vector, core * part, part, 0)

    qkv_bias = jnp.concatenate([mine_of(qb), jnp.zeros((part,), F32), mine_of(vb)])
    unit, _ = normalised(tok.astype(F32))
    normed = (unit * g1 + b1).astype(BF)
    packed = (jnp.dot(normed, w_qkv, preferred_element_type=F32) + qkv_bias).astype(BF)
    packed_t = packed.T
    mixed, result_t, log_total = attend_forward(kept, packed, packed_t, slots)
    mixed_sib = sibling(mixed)

    cot = collect(cotangent)
    wp = second[:, :width]
    wp_own = lax.dynamic_slice_in_dim(wp, core * part, part, 0)
    wp_sib = lax.dynamic_slice_in_dim(wp, (1 - core) * part, part, 0)
    vec_two = jnp.concatenate([jnp.stack([pb, g2, b2]), jnp.zeros((5, width), F32)])
    middle, out_part, gn_part, dw1, dw2, gf1, gf2 = feed_forward(
        tok, mixed, mixed_sib, cot, wp_own, wp_sib, second, vec_two, f1b
    )
    gn_sib = sibling(gn_part)
    rows_own = 2 * slots
    out_sib = sibling(out_part[rows_own:])
    out_own = (
        middle[:rows_own] + out_part[:rows_own].astype(F32) + out_sib.astype(F32) + f2b
    ).astype(BF)

    def hand_back(own, sent):
        kept_part = own[:slots]
        came = partner(sent).astype(own.dtype)
        straight = jnp.stack([kept_part, came])
        crossed = jnp.stack([came, kept_part])
        return jnp.where(image == 0, straight, crossed)

    output = hand_back(out_own, out_own[slots:])
    grad_middle, grad_mixed, grad_mixed_t, dwp_own, dwp_sib, vec_back = branch(
        core_row, middle, gn_part, gn_sib, cot, mixed, mixed_sib, wp_own, vec_two
    )
    dwp = jnp.where(
        core == 0,
        jnp.concatenate([dwp_own, dwp_sib], axis=0),
        jnp.concatenate([dwp_sib, dwp_own], axis=0),
    )
    dw2 = dw2.reshape(2, owners, quarter, width).transpose(1, 2, 0, 3).reshape(width, 2 * width)
    scattered_one = lax.psum_scatter(
        jnp.concatenate([dwp, dw1, dw2], axis=1), "fsdp", scatter_dimension=0, tiled=True
    )
    gq, gk, gv = attend_backward(
        kept, packed, packed_t, grad_mixed, grad_mixed_t, result_t, log_total, slots
    )
    vec_one = jnp.concatenate([jnp.stack([g1, b1]), jnp.zeros((6, width), F32)])
    gn1_own, gn1_send, dw_qkv, vec_first, vec_qv = project_back(tok, gq, gk, gv, w_qkv, vec_one)

    def spread(vector):
        both = jnp.zeros((2, part), F32)
        return lax.dynamic_update_index_in_dim(both, vector, core, 0).reshape(width)

    def rows_of(block):
        return jnp.sum(block.reshape(block.shape[0] // 8, 8, block.shape[1]), axis=1)

    once = (core == 0).astype(F32)
    gg1, gb1 = rows_of(vec_first)
    gqb, gvb = rows_of(vec_qv)
    gg2, gb2, gpb = rows_of(vec_back) * once
    gf2b = jnp.sum(gf2, axis=0) * once
    gf1b = jnp.sum(gf1, axis=0).reshape(2, owners, quarter).transpose(1, 0, 2)
    gf1b = lax.dynamic_update_index_in_dim(
        jnp.zeros((owners, 2, 2, quarter), F32), gf1b, core, 1
    ).reshape(owners, ff_shard)
    small_grads = jnp.concatenate(
        [
            vector.reshape(owners, shard)
            for vector in (gg1, gb1, spread(gqb), spread(gvb), gpb, gg2, gb2, gf2b)
        ]
        + [gf1b],
        axis=1,
    ).astype(BF)
    small_block = (
        jnp.zeros((owners, VEC_ROWS, 3 * part), BF).at[:, 0, : small.shape[0]].set(small_grads)
    )
    scattered_two = lax.psum_scatter(
        jnp.concatenate([dw_qkv.reshape(owners, shard, 3 * part), small_block], axis=1),
        "fsdp",
        scatter_dimension=0,
        tiled=False,
    )

    gn1 = gn1_own + sibling(gn1_send).astype(F32)
    unit_own, inverse_own = normalised(tok[:rows_own].astype(F32))
    input_own = grad_middle + norm_pull(gn1, g1, unit_own, inverse_own)
    input_grad = hand_back(input_own, input_own[slots:].astype(BF))

    def finish(value):
        total = value.astype(F32) + partner(value).astype(F32)
        other = sibling(total.astype(BF)).astype(F32)
        return total, other

    def in_order(mine, other):
        return jnp.where(core == 0, mine, other), jnp.where(core == 0, other, mine)

    one_mine, one_other = finish(scattered_one)
    lower, upper = in_order(one_mine, one_other)
    grad_proj = jnp.concatenate([lower[:, :part], upper[:, :part]], axis=1)

    def fc1_of(value):
        return value[:, part : part + half].reshape(shard, 2, owners, quarter).transpose(0, 2, 1, 3)

    grad_fc1 = jnp.stack([fc1_of(lower), fc1_of(upper)], axis=2).reshape(shard, ff)

    def fc2_of(value):
        return value[:, part + half :].reshape(quarter, 2, width).transpose(1, 0, 2)

    grad_fc2 = jnp.stack([fc2_of(lower), fc2_of(upper)]).reshape(ff_shard, width)
    two_mine, two_other = finish(scattered_two)
    lower, upper = in_order(two_mine[:shard], two_other[:shard])
    grad_qkv = jnp.stack(
        [lower.reshape(shard, 3, part), upper.reshape(shard, 3, part)], axis=2
    ).reshape(shard, 6 * part)
    small_sum = two_mine[shard] + two_other[shard]
    s = [small_sum[at * shard : (at + 1) * shard] for at in range(8)]
    grad_f1b = small_sum[8 * shard : 8 * shard + ff_shard]
    return (
        output,
        input_grad,
        s[0],
        s[1],
        grad_qkv,
        s[2],
        s[3],
        grad_proj,
        s[4],
        s[5],
        s[6],
        grad_fc1,
        grad_f1b,
        grad_fc2,
        s[7],
    )


def solution(mesh):
    placed = (
        P("fsdp", "seq", None),
        P("fsdp", None),
        P("fsdp"),
        P("fsdp"),
        P("fsdp", None),
        P("fsdp"),
        P("fsdp"),
        P("fsdp", None),
        P("fsdp"),
        P("fsdp"),
        P("fsdp"),
        P("fsdp", None),
        P("fsdp"),
        P("fsdp", None),
        P("fsdp"),
        P("fsdp", "seq", None),
    )
    return jax.shard_map(
        per_device,
        mesh=mesh,
        in_specs=placed,
        out_specs=(
            P("fsdp", "seq", None),
            P("fsdp", "seq", None),
            P("fsdp"),
            P("fsdp"),
            P("fsdp", None),
            P("fsdp"),
            P("fsdp"),
            P("fsdp", None),
            P("fsdp"),
            P("fsdp"),
            P("fsdp"),
            P("fsdp", None),
            P("fsdp"),
            P("fsdp", None),
            P("fsdp"),
        ),
        check_vma=False,
    )
```

```python
import functools

import jax
import jax.numpy as jnp
from jax import lax
from jax.experimental import pallas as pl
from jax.experimental.pallas import tpu as pltpu
from jax.sharding import PartitionSpec as P

HEADS = 12
HEAD_DIM = 64
EPSILON = 1e-06
MASKED = -1e30
BF = jnp.bfloat16
F32 = jnp.float32
VMEM_BYTES = 60 * 1024 * 1024
PAIR = 2 * HEAD_DIM
VEC_ROWS = 16
SLOT_ORDER = (0, 2, 1, 3)


def params(*semantics):
    return pltpu.CompilerParams(
        dimension_semantics=semantics, vmem_limit_bytes=VMEM_BYTES
    )


def dot(left, right, left_dim=1, right_dim=0):
    return lax.dot_general(
        left, right, (((left_dim,), (right_dim,)), ((), ())), preferred_element_type=F32
    )


def cost(flops, bytes_accessed, transcendentals=0):
    return pl.CostEstimate(
        flops=int(flops), bytes_accessed=int(bytes_accessed), transcendentals=int(transcendentals)
    )


def whole(shape):
    return pl.BlockSpec(shape, lambda *_: tuple(0 for _ in shape))


def key_bias(counts_ref, place_ref, keys, slots):
    row = lax.broadcasted_iota(jnp.int32, (slots, PAIR), 0)
    place = place_ref[0]
    parts = []
    for flip in SLOT_ORDER:
        kept = counts_ref[place // 2, jnp.bitwise_xor(place, flip)]
        parts.append(jnp.where(row < kept, 0.0, MASKED).astype(F32))
    return jnp.concatenate(parts, axis=0)


def augment_keys(pair, bias, which, ones):
    lane = lax.broadcasted_iota(jnp.int32, pair.shape, 1)
    mine = (lane < HEAD_DIM) if which == 0 else (lane >= HEAD_DIM)
    start = HEAD_DIM if which == 0 else 0
    extra = jnp.where(
        lane == start, bias, jnp.where((lane > start) & (lane <= start + ones), 1.0, 0.0)
    )
    return jnp.where(mine, pair.astype(F32), extra).astype(BF)


def augment_values(pair, which, ones):
    lane = lax.broadcasted_iota(jnp.int32, pair.shape, 1)
    mine = (lane < HEAD_DIM) if which == 0 else (lane >= HEAD_DIM)
    start = HEAD_DIM if which == 0 else 0
    extra = jnp.where((lane >= start) & (lane < start + ones), 1.0, 0.0)
    return jnp.where(mine, pair.astype(F32), extra).astype(BF)


def pieces(value):
    first = value.astype(BF).astype(F32)
    rest = value - first
    second = rest.astype(BF).astype(F32)
    return first, second, rest - second


def extra_rows(rows, width):
    place = lax.broadcasted_iota(jnp.int32, (HEAD_DIM, width), 0)
    out = jnp.zeros((HEAD_DIM, width), F32)
    for at, row in enumerate(rows):
        out = jnp.where(place == at, row, out)
    return out.astype(BF)


def place_rows(head, extra, which):
    return jnp.concatenate([head, extra] if which == 0 else [extra, head], axis=0)


def attend_forward_kernel(
    slots, bq, chunk, counts_ref, place_ref, k_ref, qt_ref, vt_ref, mixed_ref, ot_ref, lse_ref,
    kaug, vaug, s_a, s_b, m_a, m_b
):
    keys = k_ref.shape[0]
    step = pl.program_id(1)
    steps = pl.num_programs(1)
    scores = (s_a, s_b)
    peaks = (m_a, m_b)
    ones_row = extra_rows([jnp.ones((1, bq), F32)], bq)

    @pl.when(step == 0)
    def _():
        bias = key_bias(counts_ref, place_ref, keys, slots)
        ones = jnp.ones((16, keys), BF)
        for which in range(2):
            kaug[which] = augment_keys(k_ref[...], bias, which, 0)
            vaug[which] = jnp.concatenate(
                [vt_ref[which * HEAD_DIM : (which + 1) * HEAD_DIM, :], ones], axis=0
            )

    def query_block(at, which):
        head = qt_ref[which * HEAD_DIM : (which + 1) * HEAD_DIM, pl.ds(at * bq, bq)]
        head = (head.astype(F32) * HEAD_DIM ** (-0.5)).astype(BF)
        return place_rows(head, ones_row, which)

    def score_chunk(query, which, at, peak):
        rows = slice(at * chunk, (at + 1) * chunk)
        s = dot(kaug[which, rows, :], query)
        scores[which][rows, :] = s
        top = jnp.max(s.reshape(chunk // 8, 8, bq), axis=0)
        return top if peak is None else jnp.maximum(peak, top)

    def weigh_chunk(which, at, peak, total):
        rows = slice(at * chunk, (at + 1) * chunk)
        p = jnp.exp(scores[which][rows, :] - peak).astype(BF)
        o = dot(vaug[which, :, rows], p)
        return o if total is None else total + o

    @pl.when(step == 0)
    def _():
        query = query_block(0, 0)
        peak = None
        for at in range(keys // chunk):
            peak = score_chunk(query, 0, at, peak)
        m_a[...] = peak

    later = jnp.minimum(step + 1, steps - 1)
    outs = []
    for which in range(2):
        other = 1 - which
        query = query_block(step if which == 0 else later, other)
        peak = jnp.max(peaks[which][...], axis=0, keepdims=True)
        next_peak, total = None, None
        for at in range(keys // chunk):
            next_peak = score_chunk(query, other, at, next_peak)
            total = weigh_chunk(which, at, peak, total)
        peaks[other][...] = next_peak
        norm = total[HEAD_DIM : HEAD_DIM + 1, :]
        outs.append(total[:HEAD_DIM, :] * (1.0 / norm))
        lse_ref[0, which : which + 1, :] = peak + jnp.log(norm)
    both = jnp.concatenate(outs, axis=0)
    ot_ref[...] = both
    mixed_ref[...] = both.T.astype(BF)


def attend_forward(counts, place, packed, packed_t, slots):
    keys, width = packed.shape
    width //= 3
    pairs = width // PAIR
    bq, chunk = 256, 256
    kernel = functools.partial(attend_forward_kernel, slots, bq, chunk)
    return pl.pallas_call(
        kernel,
        grid=(pairs, keys // bq),
        in_specs=[
            pl.BlockSpec(memory_space=pltpu.SMEM),
            pl.BlockSpec(memory_space=pltpu.SMEM),
            pl.BlockSpec((keys, PAIR), lambda p, i: (0, pairs + p)),
            pl.BlockSpec((PAIR, keys), lambda p, i: (p, 0)),
            pl.BlockSpec((PAIR, keys), lambda p, i: (2 * pairs + p, 0)),
        ],
        out_specs=[
            pl.BlockSpec((bq, PAIR), lambda p, i: (i, p)),
            pl.BlockSpec((PAIR, bq), lambda p, i: (p, i)),
            pl.BlockSpec((1, 8, bq), lambda p, i: (p, 0, i)),
        ],
        out_shape=[
            jax.ShapeDtypeStruct((keys, width), BF),
            jax.ShapeDtypeStruct((width, keys), F32),
            jax.ShapeDtypeStruct((pairs, 8, keys), F32),
        ],
        scratch_shapes=[
            pltpu.VMEM((2, keys, PAIR), BF),
            pltpu.VMEM((2, HEAD_DIM + 16, keys), BF),
            pltpu.VMEM((keys, bq), F32),
            pltpu.VMEM((keys, bq), F32),
            pltpu.VMEM((8, bq), F32),
            pltpu.VMEM((8, bq), F32),
        ],
        compiler_params=params("arbitrary", "arbitrary"),
        cost_estimate=cost(
            2 * pairs * 2 * 2 * keys * keys * 256, 12 * keys * width, 2 * pairs * keys * keys
        ),
        name="attend_forward",
    )(counts, place, packed, packed_t, packed_t)


def attend_backward_kernel(
    slots, bq, chunk, counts_ref, place_ref, q_ref, k_ref, v_ref, qt_ref, kt_ref, do_ref, dot_ref, ot_ref,
    lse_ref, gq_ref, gk_ref, gv_ref, kaug, vaug, acc_k, acc_v
):
    keys = k_ref.shape[0]
    step = pl.program_id(1)
    steps = pl.num_programs(1)
    scale = HEAD_DIM ** (-0.5)

    @pl.when(step == 0)
    def _():
        bias = key_bias(counts_ref, place_ref, keys, slots)
        for which in range(2):
            kaug[which] = augment_keys(k_ref[...], bias, which, 3)
            vaug[which] = augment_values(v_ref[...], which, 3)
        acc_k[...] = jnp.zeros_like(acc_k)
        acc_v[...] = jnp.zeros_like(acc_v)

    ones_row = jnp.ones((1, bq), F32)
    queries, grads = [], []
    for which in range(2):
        rows = slice(which * HEAD_DIM, (which + 1) * HEAD_DIM)
        head = (qt_ref[rows, :].astype(F32) * scale).astype(BF)
        log_total = lse_ref[0, which : which + 1, :]
        queries.append(
            place_rows(head, extra_rows([ones_row, *pieces(-log_total)], bq), which)
        )
        grad = dot_ref[rows, :]
        delta = jnp.sum(grad.astype(F32) * ot_ref[rows, :], axis=0, keepdims=True)
        grads.append(place_rows(grad, extra_rows(list(pieces(-delta)), bq), which))

    do_pair = do_ref[...]
    q_pair = q_ref[...]
    totals = [None, None]
    for at in range(keys // chunk):
        rows = slice(at * chunk, (at + 1) * chunk)
        for which in range(2):
            p = jnp.exp(dot(kaug[which, rows, :], queries[which]))
            dp = dot(vaug[which, rows, :], grads[which])
            p_low = p.astype(BF)
            ds = (p * dp).astype(BF)
            acc_v[which, rows, :] += dot(p_low, do_pair)
            acc_k[which, rows, :] += dot(ds, q_pair)
            part = dot(kt_ref[which * HEAD_DIM : (which + 1) * HEAD_DIM, rows], ds)
            totals[which] = part if totals[which] is None else totals[which] + part
    both = jnp.concatenate(totals, axis=0) * scale
    gq_ref[...] = both.T.astype(BF)

    @pl.when(step == steps - 1)
    def _():
        lane = lax.broadcasted_iota(jnp.int32, (keys, PAIR), 1)
        gk_ref[...] = (jnp.where(lane < HEAD_DIM, acc_k[0], acc_k[1]) * scale).astype(BF)
        gv_ref[...] = jnp.where(lane < HEAD_DIM, acc_v[0], acc_v[1]).astype(BF)


def attend_backward(counts, place, packed, packed_t, grad, grad_t, result_t, log_total, slots):
    keys, width = packed.shape
    width //= 3
    pairs = width // PAIR
    bq, chunk = 512, 256
    kernel = functools.partial(attend_backward_kernel, slots, bq, chunk)
    return pl.pallas_call(
        kernel,
        grid=(pairs, keys // bq),
        in_specs=[
            pl.BlockSpec(memory_space=pltpu.SMEM),
            pl.BlockSpec(memory_space=pltpu.SMEM),
            pl.BlockSpec((bq, PAIR), lambda p, i: (i, p)),
            pl.BlockSpec((keys, PAIR), lambda p, i: (0, pairs + p)),
            pl.BlockSpec((keys, PAIR), lambda p, i: (0, 2 * pairs + p)),
            pl.BlockSpec((PAIR, bq), lambda p, i: (p, i)),
            pl.BlockSpec((PAIR, keys), lambda p, i: (pairs + p, 0)),
            pl.BlockSpec((bq, PAIR), lambda p, i: (i, p)),
            pl.BlockSpec((PAIR, bq), lambda p, i: (p, i)),
            pl.BlockSpec((PAIR, bq), lambda p, i: (p, i)),
            pl.BlockSpec((1, 8, bq), lambda p, i: (p, 0, i)),
        ],
        out_specs=[
            pl.BlockSpec((bq, PAIR), lambda p, i: (i, p)),
            pl.BlockSpec((keys, PAIR), lambda p, i: (0, p)),
            pl.BlockSpec((keys, PAIR), lambda p, i: (0, p)),
        ],
        out_shape=[jax.ShapeDtypeStruct((keys, width), BF)] * 3,
        scratch_shapes=[
            pltpu.VMEM((2, keys, PAIR), BF),
            pltpu.VMEM((2, keys, PAIR), BF),
            pltpu.VMEM((2, keys, PAIR), F32),
            pltpu.VMEM((2, keys, PAIR), F32),
        ],
        compiler_params=params("arbitrary", "arbitrary"),
        cost_estimate=cost(
            2 * pairs * 5 * 2 * keys * keys * 256, 24 * keys * width, 2 * pairs * keys * keys
        ),
        name="attend_backward",
    )(counts, place, packed, packed, packed, packed_t, packed_t, grad, grad_t, result_t, log_total)


def normalised(values):
    centred = values - jnp.mean(values, axis=-1, keepdims=True)
    variance = jnp.mean(centred * centred, axis=-1, keepdims=True)
    inverse = lax.rsqrt(variance + EPSILON)
    return centred * inverse, inverse


def norm_pull(grad, gain, unit, inverse):
    scaled = grad * gain
    mean = jnp.mean(scaled, axis=-1, keepdims=True)
    along = jnp.mean(scaled * unit, axis=-1, keepdims=True)
    return inverse * (scaled - mean - unit * along)


def fold(values):
    return jnp.sum(values.reshape(values.shape[0] // 8, 8, values.shape[1]), axis=0)


def feed_forward_kernel(
    chunk, tok_ref, mo_ref, ms_ref, cot_ref, wpo_ref, wps_ref, g2_ref, vec_ref, f1b_ref,
    mid_ref, out_ref, gn_ref, dw_ref, gf1_ref, gf2_ref, acc1, acc2, accb, accc
):
    step = pl.program_id(0)
    steps = pl.num_programs(0)
    width = tok_ref.shape[1]
    half = f1b_ref.shape[1]

    @pl.when(step == 0)
    def _():
        acc1[...] = jnp.zeros_like(acc1)
        acc2[...] = jnp.zeros_like(acc2)
        accb[...] = jnp.zeros_like(accb)
        accc[...] = jnp.zeros_like(accc)

    middle = (
        tok_ref[...].astype(F32)
        + dot(mo_ref[...], wpo_ref[...])
        + dot(ms_ref[...], wps_ref[...])
        + vec_ref[0:1, :]
    )
    mid_ref[...] = middle
    unit, _ = normalised(middle)
    normed = (unit * vec_ref[1:2, :] + vec_ref[2:3, :]).astype(BF)
    normed_t = normed.T
    cot = cot_ref[...]
    out = None
    grad = None
    for at in range(half // chunk):
        cols = slice(at * chunk, (at + 1) * chunk)
        w1 = g2_ref[:, width + at * chunk : width + (at + 1) * chunk]
        piece, row = divmod(at * chunk, width)
        start = width + half + piece * width
        w2 = g2_ref[row : row + chunk, start : start + width]
        hidden = dot(normed, w1) + f1b_ref[0:1, cols]
        below = 0.5 + 0.5 * lax.erf(hidden * (0.5**0.5))
        slope = below + hidden * (jnp.exp(hidden * hidden * -0.5) * 0.3989422804014327)
        active = (hidden * below).astype(BF)
        grad_hidden = (dot(cot, w2, 1, 1) * slope).astype(BF)
        more = dot(active, w2)
        out = more if out is None else out + more
        more = dot(grad_hidden, w1, 1, 1)
        grad = more if grad is None else grad + more
        acc1[:, cols] += dot(normed_t, grad_hidden)
        acc2[cols, :] += dot(active, cot, 0, 0)
        accb[:, cols] += fold(grad_hidden.astype(F32))
    accc[...] += fold(cot.astype(F32))
    out_ref[...] = out.astype(BF)
    gn_ref[...] = grad.astype(BF)

    @pl.when(step == steps - 1)
    def _():
        dw_ref[:, :half] = acc1[...].astype(BF)
        for piece in range(half // width):
            dw_ref[:, half + piece * width : half + (piece + 1) * width] = acc2[
                piece * width : (piece + 1) * width, :
            ].astype(BF)
        gf1_ref[...] = accb[...]
        gf2_ref[...] = accc[...]


def feed_forward(tokens, mixed_own, mixed_sib, cot, wp_own, wp_sib, weights, vec, f1b):
    rows, width = tokens.shape
    half = f1b.shape[1]
    heads = mixed_own.shape[1]
    bt, chunk = 256, 384
    blocks = rows // bt
    kernel = functools.partial(feed_forward_kernel, chunk)
    return pl.pallas_call(
        kernel,
        grid=(blocks,),
        in_specs=[
            pl.BlockSpec((bt, width), lambda i: (i, 0)),
            pl.BlockSpec((bt, heads), lambda i: (i, 0)),
            pl.BlockSpec((bt, heads), lambda i: (lax.rem(i + blocks // 2, blocks), 0)),
            pl.BlockSpec((bt, width), lambda i: (i, 0)),
            whole(wp_own.shape),
            whole(wp_sib.shape),
            whole(weights.shape),
            whole(vec.shape),
            whole(f1b.shape),
        ],
        out_specs=[
            pl.BlockSpec((bt, width), lambda i: (i, 0)),
            pl.BlockSpec((bt, width), lambda i: (i, 0)),
            pl.BlockSpec((bt, width), lambda i: (i, 0)),
            whole((width, 2 * half)),
            whole((8, half)),
            whole((8, width)),
        ],
        out_shape=[
            jax.ShapeDtypeStruct((rows, width), F32),
            jax.ShapeDtypeStruct((rows, width), BF),
            jax.ShapeDtypeStruct((rows, width), BF),
            jax.ShapeDtypeStruct((width, 2 * half), BF),
            jax.ShapeDtypeStruct((8, half), F32),
            jax.ShapeDtypeStruct((8, width), F32),
        ],
        scratch_shapes=[
            pltpu.VMEM((width, half), F32),
            pltpu.VMEM((half, width), F32),
            pltpu.VMEM((8, half), F32),
            pltpu.VMEM((8, width), F32),
        ],
        compiler_params=params("arbitrary"),
        cost_estimate=cost(
            2 * rows * width * (6 * half + width), 20 * rows * width + 8 * width * half,
            2 * rows * half,
        ),
        name="feed_forward",
    )(tokens, mixed_own, mixed_sib, cot, wp_own, wp_sib, weights, vec, f1b)


def branch_kernel(
    core_ref, mid_ref, ga_ref, gb_ref, cot_ref, mo_ref, ms_ref, wpo_ref, vec_ref,
    gm_ref, do_ref, dot_ref, dwo_ref, dws_ref, vecs_ref, acco, accs, accv, low_ref
):
    step = pl.program_id(0)
    steps = pl.num_programs(0)
    half = do_ref.shape[1]

    @pl.when(step == 0)
    def _():
        acco[...] = jnp.zeros_like(acco)
        accs[...] = jnp.zeros_like(accs)
        accv[...] = jnp.zeros_like(accv)

    unit, inverse = normalised(mid_ref[...])
    grad = ga_ref[...].astype(F32) + gb_ref[...].astype(F32)
    accv[0:8, :] += fold(grad * unit)
    accv[8:16, :] += fold(grad)
    grad_middle = cot_ref[...].astype(F32) + norm_pull(grad, vec_ref[1:2, :], unit, inverse)

    @pl.when(step < steps // 2)
    def _():
        gm_ref[...] = grad_middle

    low = grad_middle.astype(BF)
    low_ref[...] = low
    accv[16:24, :] += fold(low.astype(F32))
    do_ref[...] = dot(low, wpo_ref[...], 1, 1).astype(BF)
    dot_ref[...] = dot(wpo_ref[...], low, 1, 1).astype(BF)
    mine = low_ref[:, pl.ds(pl.multiple_of(core_ref[0] * half, half), half)]
    acco[...] += dot(mo_ref[...], mine, 0, 0)
    accs[...] += dot(ms_ref[...], mine, 0, 0)

    @pl.when(step == steps - 1)
    def _():
        dwo_ref[...] = acco[...].astype(BF)
        dws_ref[...] = accs[...].astype(BF)
        vecs_ref[...] = accv[...]


def branch(core, middle, grad_own, grad_sib, cot, mixed_own, mixed_sib, wp_own, vec):
    rows, width = middle.shape
    half = mixed_own.shape[1]
    bt = 256
    blocks = rows // bt
    swap = lambda i: (lax.rem(i + blocks // 2, blocks), 0)
    straight = lambda i: (i, 0)
    return pl.pallas_call(
        branch_kernel,
        grid=(blocks,),
        in_specs=[
            pl.BlockSpec(memory_space=pltpu.SMEM),
            pl.BlockSpec((bt, width), straight),
            pl.BlockSpec((bt, width), straight),
            pl.BlockSpec((bt, width), swap),
            pl.BlockSpec((bt, width), straight),
            pl.BlockSpec((bt, half), straight),
            pl.BlockSpec((bt, half), swap),
            whole(wp_own.shape),
            whole(vec.shape),
        ],
        out_specs=[
            pl.BlockSpec((bt, width), lambda i: (jnp.minimum(i, blocks // 2 - 1), 0)),
            pl.BlockSpec((bt, half), straight),
            pl.BlockSpec((half, bt), lambda i: (0, i)),
            whole((half, half)),
            whole((half, half)),
            whole((24, width)),
        ],
        out_shape=[
            jax.ShapeDtypeStruct((rows // 2, width), F32),
            jax.ShapeDtypeStruct((rows, half), BF),
            jax.ShapeDtypeStruct((half, rows), BF),
            jax.ShapeDtypeStruct((half, half), BF),
            jax.ShapeDtypeStruct((half, half), BF),
            jax.ShapeDtypeStruct((24, width), F32),
        ],
        scratch_shapes=[
            pltpu.VMEM((half, half), F32),
            pltpu.VMEM((half, half), F32),
            pltpu.VMEM((24, width), F32),
            pltpu.VMEM((bt, width), BF),
        ],
        compiler_params=params("arbitrary"),
        cost_estimate=cost(2 * rows * width * 3 * half, 18 * rows * width),
        name="branch",
    )(core, middle, grad_own, grad_sib, cot, mixed_own, mixed_sib, wp_own, vec)


def project_back_kernel(
    tok_ref, gq_ref, gk_ref, gv_ref, w_ref, vec_ref,
    own_ref, sib_ref, dw_ref, vecs_ref, qv_ref, accw, accv, accqv
):
    step = pl.program_id(0)
    steps = pl.num_programs(0)
    part = gq_ref.shape[1]

    @pl.when(step == 0)
    def _():
        accw[...] = jnp.zeros_like(accw)
        accv[...] = jnp.zeros_like(accv)
        accqv[...] = jnp.zeros_like(accqv)

    unit, _ = normalised(tok_ref[...].astype(F32))
    normed_t = (unit * vec_ref[0:1, :] + vec_ref[1:2, :]).astype(BF).T
    grad = None
    for at, ref in enumerate((gq_ref, gk_ref, gv_ref)):
        cols = slice(at * part, (at + 1) * part)
        value = ref[...]
        more = dot(value, w_ref[:, cols], 1, 1)
        grad = more if grad is None else grad + more
        accw[:, cols] += dot(normed_t, value)
        if at != 1:
            here = 0 if at == 0 else 8
            accqv[here : here + 8, :] += fold(value.astype(F32))
    accv[0:8, :] += fold(grad * unit)
    accv[8:16, :] += fold(grad)

    @pl.when(step < steps // 2)
    def _():
        own_ref[...] = grad

    @pl.when(step >= steps // 2)
    def _():
        sib_ref[...] = grad.astype(BF)

    @pl.when(step == steps - 1)
    def _():
        dw_ref[...] = accw[...].astype(BF)
        vecs_ref[...] = accv[...]
        qv_ref[...] = accqv[...]


def project_back(tokens, gq, gk, gv, weight, vec):
    rows, width = tokens.shape
    part = gq.shape[1]
    bt = 256
    blocks = rows // bt
    straight = lambda i: (i, 0)
    return pl.pallas_call(
        project_back_kernel,
        grid=(blocks,),
        in_specs=[
            pl.BlockSpec((bt, width), straight),
            pl.BlockSpec((bt, part), straight),
            pl.BlockSpec((bt, part), straight),
            pl.BlockSpec((bt, part), straight),
            whole(weight.shape),
            whole(vec.shape),
        ],
        out_specs=[
            pl.BlockSpec((bt, width), lambda i: (jnp.minimum(i, blocks // 2 - 1), 0)),
            pl.BlockSpec((bt, width), lambda i: (jnp.maximum(i - blocks // 2, 0), 0)),
            whole((width, 3 * part)),
            whole((16, width)),
            whole((16, part)),
        ],
        out_shape=[
            jax.ShapeDtypeStruct((rows // 2, width), F32),
            jax.ShapeDtypeStruct((rows // 2, width), BF),
            jax.ShapeDtypeStruct((width, 3 * part), BF),
            jax.ShapeDtypeStruct((16, width), F32),
            jax.ShapeDtypeStruct((16, part), F32),
        ],
        scratch_shapes=[
            pltpu.VMEM((width, 3 * part), F32),
            pltpu.VMEM((16, width), F32),
            pltpu.VMEM((16, part), F32),
        ],
        compiler_params=params("arbitrary"),
        cost_estimate=cost(2 * rows * width * 6 * part, 14 * rows * width),
        name="project_back",
    )(tokens, gq, gk, gv, weight, vec)


def pack_kernel(core_ref, qkv_ref, small_ref, proj_ref, fc1_ref, fc2_ref, one_ref, two_ref):
    first_core = core_ref[0] == 0
    shard, width = proj_ref.shape
    part = width // 2
    ff = fc1_ref.shape[1]
    owners = width // shard
    quarter = ff // owners // 4
    half = ff // 2
    one_ref[:VEC_ROWS, :] = small_ref[...]

    for at in range(3):
        low = qkv_ref[:, at * width : at * width + part]
        high = qkv_ref[:, at * width + part : (at + 1) * width]
        one_ref[VEC_ROWS:, at * part : (at + 1) * part] = jnp.where(first_core, low, high)
    two_ref[:, :width] = proj_ref[...]
    pieces_low, pieces_high = [], []
    for piece in range(2):
        for owner in range(owners):
            base = owner * 4 * quarter + piece * quarter
            pieces_low.append(fc1_ref[:, base : base + quarter])
            pieces_high.append(fc1_ref[:, base + 2 * quarter : base + 3 * quarter])
    two_ref[:, width : width + half] = jnp.where(
        first_core, jnp.concatenate(pieces_low, axis=1), jnp.concatenate(pieces_high, axis=1)
    )
    for piece in range(2):
        low = fc2_ref[piece * quarter : (piece + 1) * quarter, :]
        high = fc2_ref[(2 + piece) * quarter : (3 + piece) * quarter, :]
        start = width + half + piece * width
        two_ref[:, start : start + width] = jnp.where(first_core, low, high)


def pack_weights(core, qkv, small, proj, fc1, fc2):
    shard, width = proj.shape
    half = fc1.shape[1] // 2
    return pl.pallas_call(
        pack_kernel,
        grid=(1,),
        in_specs=[pl.BlockSpec(memory_space=pltpu.SMEM)]
        + [whole(value.shape) for value in (qkv, small, proj, fc1, fc2)],
        out_specs=[whole((VEC_ROWS + shard, 3 * width // 2)), whole((shard, 3 * width + half))],
        out_shape=[
            jax.ShapeDtypeStruct((VEC_ROWS + shard, 3 * width // 2), BF),
            jax.ShapeDtypeStruct((shard, 3 * width + half), BF),
        ],
        compiler_params=params("arbitrary"),
        cost_estimate=cost(0, 5 * shard * width * 8),
        name="pack_weights",
    )(core, qkv, small, proj, fc1, fc2)


def project_kernel(tok_ref, w_ref, bias_ref, vec_ref, out_ref, out_t_ref):
    unit, _ = normalised(tok_ref[...].astype(F32))
    normed = (unit * vec_ref[0:1, :] + vec_ref[1:2, :]).astype(BF)
    packed = dot(normed, w_ref[...]) + bias_ref[0:1, :]
    out_ref[...] = packed.astype(BF)
    out_t_ref[...] = packed.T.astype(BF)


def project(tokens, weight, bias, vec):
    rows, width = tokens.shape
    wide = weight.shape[1]
    bt = 256
    return pl.pallas_call(
        project_kernel,
        grid=(rows // bt,),
        in_specs=[
            pl.BlockSpec((bt, width), lambda i: (i, 0)),
            whole(weight.shape),
            whole(bias.shape),
            whole(vec.shape),
        ],
        out_specs=[
            pl.BlockSpec((bt, wide), lambda i: (i, 0)),
            pl.BlockSpec((wide, bt), lambda i: (0, i)),
        ],
        out_shape=[
            jax.ShapeDtypeStruct((rows, wide), BF),
            jax.ShapeDtypeStruct((wide, rows), BF),
        ],
        compiler_params=params("arbitrary"),
        cost_estimate=cost(2 * rows * width * wide, 12 * rows * width),
        name="project",
    )(tokens, weight, bias, vec)


def gather_line(value):
    owners = lax.axis_size("fsdp")
    lines = owners // 2
    at = lax.axis_index("fsdp")
    line, odd = at // 2, lax.rem(at, 2)
    other = lax.ppermute(value, "fsdp", [(f, f ^ 1) for f in range(owners)])
    pair = jnp.stack([jnp.where(odd == 0, value, other), jnp.where(odd == 0, other, value)])
    ups, downs = [pair], [pair]
    for hop in range(1, lines):
        up = [(f, f + 2) for f in range(owners - 2) if f // 2 >= hop - 1]
        down = [(f, f - 2) for f in range(2, owners) if f // 2 <= lines - hop]
        ups.append(lax.ppermute(ups[-1], "fsdp", up))
        downs.append(lax.ppermute(downs[-1], "fsdp", down))
    gathered = []
    for target in range(lines):
        options = [
            downs[target - here] if here < target else ups[here - target] for here in range(lines)
        ]
        gathered.append(choose_at(line, options))
    return jnp.stack(gathered).reshape(owners, *value.shape)


def choose_at(index, options):
    out = options[-1]
    for at in range(len(options) - 2, -1, -1):
        out = jnp.where(index == at, options[at], out)
    return out


def per_device(
    tokens,
    counts,
    norm1_gain,
    norm1_bias,
    qkv_weight,
    query_bias,
    value_bias,
    proj_weight,
    proj_bias,
    norm2_gain,
    norm2_bias,
    fc1_weight,
    fc1_bias,
    fc2_weight,
    fc2_bias,
    cotangent,
):
    images, slots, width = tokens.shape
    owners = lax.axis_size("fsdp")
    seq = lax.axis_size("seq")
    place = lax.axis_index("seq")
    core = lax.rem(place, 2)
    image = place // 2
    part = width // 2
    shard = width // owners
    ff = fc1_weight.shape[1]
    ff_shard = ff // owners
    quarter = ff_shard // 4
    half = ff // 2
    to_sibling = [(at, at ^ 1) for at in range(seq)]
    to_partner = [(at, at ^ 2) for at in range(seq)]

    def sibling(value):
        return lax.ppermute(value, "seq", to_sibling)

    def partner(value):
        return lax.ppermute(value, "seq", to_partner)

    def pick(value, at, axis):
        return lax.dynamic_index_in_dim(value, at, axis, keepdims=False)

    place_row = place.reshape(1).astype(jnp.int32)
    core_row = core.reshape(1).astype(jnp.int32)
    small = [
        norm1_gain, norm1_bias, query_bias, value_bias, proj_bias, norm2_gain, norm2_bias,
        fc2_bias, fc1_bias,
    ]
    small_rows = jnp.stack([jnp.pad(vector, (0, 3 * part - vector.shape[0])) for vector in small])
    small_rows = jnp.pad(small_rows, ((0, VEC_ROWS - len(small)), (0, 0)))
    one, two = pack_weights(core_row, qkv_weight, small_rows, proj_weight, fc1_weight, fc2_weight)
    second = lax.all_gather(two, "fsdp", axis=0, tiled=True)
    first = gather_line(one)

    def collect(value, theirs):
        mine = pick(value, image, 0)
        return jnp.concatenate([mine, theirs, sibling(mine), sibling(theirs)], axis=0)

    tok = collect(tokens, partner(pick(tokens, 1 - image, 0)))
    w_qkv = first[:, VEC_ROWS:].reshape(width, 3 * part)
    vecs = first[:, :8, :shard].astype(F32).transpose(1, 0, 2).reshape(8, width)
    g1, b1, qb, vb, pb, g2, b2, f2b = vecs
    f1b = first[:, 8, :ff_shard].astype(F32)
    f1b = pick(f1b.reshape(owners, 2, 2, quarter), core, 1)
    f1b = f1b.transpose(1, 0, 2).reshape(1, half)

    def mine_of(vector):
        return lax.dynamic_slice_in_dim(vector, core * part, part, 0)

    qkv_bias = jnp.concatenate([mine_of(qb), jnp.zeros((part,), F32), mine_of(vb)])
    vec_one = jnp.concatenate([jnp.stack([g1, b1]), jnp.zeros((6, width), F32)])
    packed, packed_t = project(tok, w_qkv, qkv_bias.reshape(1, 3 * part), vec_one)
    cot_theirs = partner(pick(cotangent, 1 - image, 0))
    packed, cot_theirs = lax.optimization_barrier((packed, cot_theirs))
    mixed, result_t, log_total = attend_forward(counts, place_row, packed, packed_t, slots)
    mixed_sib = sibling(mixed)

    cot = collect(cotangent, cot_theirs)
    wp = second[:, :width]
    wp_own = lax.dynamic_slice_in_dim(wp, core * part, part, 0)
    wp_sib = lax.dynamic_slice_in_dim(wp, (1 - core) * part, part, 0)
    vec_two = jnp.concatenate([jnp.stack([pb, g2, b2]), jnp.zeros((5, width), F32)])
    middle, out_part, gn_part, dw_ff, gf1, gf2 = feed_forward(
        tok, mixed, mixed_sib, cot, wp_own, wp_sib, second, vec_two, f1b
    )
    scattered_one = lax.psum_scatter(dw_ff, "fsdp", scatter_dimension=0, tiled=True)
    gn_sib = sibling(gn_part)
    rows_own = 2 * slots
    out_sib = sibling(out_part[rows_own:])
    out_own = (
        middle[:rows_own] + out_part[:rows_own].astype(F32) + out_sib.astype(F32) + f2b
    ).astype(BF)

    def hand_back(own, sent):
        kept_part = own[:slots]
        came = partner(sent).astype(own.dtype)
        straight = jnp.stack([kept_part, came])
        crossed = jnp.stack([came, kept_part])
        return jnp.where(image == 0, straight, crossed)

    output = hand_back(out_own, out_own[slots:])
    grad_middle, grad_mixed, grad_mixed_t, dwp_own, dwp_sib, vec_back = branch(
        core_row, middle, gn_part, gn_sib, cot, mixed, mixed_sib, wp_own, vec_two
    )
    dwp = jnp.where(
        core == 0,
        jnp.concatenate([dwp_own, dwp_sib], axis=0),
        jnp.concatenate([dwp_sib, dwp_own], axis=0),
    )
    grad_mixed, output = lax.optimization_barrier((grad_mixed, output))
    gq, gk, gv = attend_backward(
        counts, place_row, packed, packed_t, grad_mixed, grad_mixed_t, result_t, log_total, slots
    )
    gn1_own, gn1_send, dw_qkv, vec_first, vec_qv = project_back(tok, gq, gk, gv, w_qkv, vec_one)

    def spread(vector):
        both = jnp.zeros((2, part), F32)
        return lax.dynamic_update_index_in_dim(both, vector, core, 0).reshape(width)

    def rows_of(block):
        return jnp.sum(block.reshape(block.shape[0] // 8, 8, block.shape[1]), axis=1)

    once = (core == 0).astype(F32)
    gg1, gb1 = rows_of(vec_first)
    gqb, gvb = rows_of(vec_qv)
    gg2, gb2, gpb = rows_of(vec_back) * once
    gf2b = jnp.sum(gf2, axis=0) * once
    gf1b = jnp.sum(gf1, axis=0).reshape(2, owners, quarter).transpose(1, 0, 2)
    gf1b = lax.dynamic_update_index_in_dim(
        jnp.zeros((owners, 2, 2, quarter), F32), gf1b, core, 1
    ).reshape(owners, ff_shard)
    wide = 4 * part
    small_grads = jnp.stack(
        [gg1, gb1, spread(gqb), spread(gvb), gpb, gg2, gb2, gf2b]
    ).reshape(8, owners, shard).transpose(1, 0, 2)
    small_block = jnp.concatenate(
        [
            jnp.pad(small_grads, ((0, 0), (0, 0), (0, wide - shard))),
            jnp.pad(gf1b[:, None], ((0, 0), (0, VEC_ROWS - 9), (0, wide - ff_shard))),
        ],
        axis=1,
    ).astype(BF)
    dw_attend = jnp.concatenate([dw_qkv, dwp], axis=1).reshape(owners, shard, wide)
    block_two = jnp.concatenate([small_block, dw_attend], axis=1)
    block_two, scattered_one = lax.optimization_barrier((block_two, scattered_one))
    scattered_two = lax.psum_scatter(block_two, "fsdp", scatter_dimension=0, tiled=False)

    gn1 = gn1_own + sibling(gn1_send).astype(F32)
    unit_own, inverse_own = normalised(tok[:rows_own].astype(F32))
    input_own = grad_middle + norm_pull(gn1, g1, unit_own, inverse_own)
    input_grad = hand_back(input_own, input_own[slots:].astype(BF))

    def finish(value):
        total = value.astype(F32) + partner(value).astype(F32)
        other = sibling(total.astype(BF)).astype(F32)
        return total, other

    def in_order(mine, other):
        return jnp.where(core == 0, mine, other), jnp.where(core == 0, other, mine)

    one_mine, one_other = finish(scattered_one)
    lower, upper = in_order(one_mine, one_other)

    def fc1_of(value):
        return value[:, :half].reshape(shard, 2, owners, quarter).transpose(0, 2, 1, 3)

    grad_fc1 = jnp.stack([fc1_of(lower), fc1_of(upper)], axis=2).reshape(shard, ff)

    def fc2_of(value):
        return value[:, half:].reshape(quarter, 2, width).transpose(1, 0, 2)

    grad_fc2 = jnp.stack([fc2_of(lower), fc2_of(upper)]).reshape(ff_shard, width)
    two_mine, two_other = finish(scattered_two)
    lower, upper = in_order(two_mine[VEC_ROWS:], two_other[VEC_ROWS:])
    grad_qkv = jnp.concatenate(
        [
            value[:, at * part : (at + 1) * part]
            for at in range(3)
            for value in (lower, upper)
        ],
        axis=1,
    )
    grad_proj = jnp.concatenate([lower[:, 3 * part :], upper[:, 3 * part :]], axis=1)
    small_sum = two_mine[:VEC_ROWS] + two_other[:VEC_ROWS]
    s = [small_sum[at, :shard] for at in range(8)]
    grad_f1b = small_sum[8, :ff_shard]
    return (
        output,
        input_grad,
        s[0],
        s[1],
        grad_qkv,
        s[2],
        s[3],
        grad_proj,
        s[4],
        s[5],
        s[6],
        grad_fc1,
        grad_f1b,
        grad_fc2,
        s[7],
    )


def solution(mesh):
    placed = (
        P("fsdp", "seq", None),
        P("fsdp", None),
        P("fsdp"),
        P("fsdp"),
        P("fsdp", None),
        P("fsdp"),
        P("fsdp"),
        P("fsdp", None),
        P("fsdp"),
        P("fsdp"),
        P("fsdp"),
        P("fsdp", None),
        P("fsdp"),
        P("fsdp", None),
        P("fsdp"),
        P("fsdp", "seq", None),
    )
    return jax.shard_map(
        per_device,
        mesh=mesh,
        in_specs=placed,
        out_specs=(
            P("fsdp", "seq", None),
            P("fsdp", "seq", None),
            P("fsdp"),
            P("fsdp"),
            P("fsdp", None),
            P("fsdp"),
            P("fsdp"),
            P("fsdp", None),
            P("fsdp"),
            P("fsdp"),
            P("fsdp"),
            P("fsdp", None),
            P("fsdp"),
            P("fsdp", None),
            P("fsdp"),
        ),
        check_vma=False,
    )
```

```python
import functools

import jax
import jax.numpy as jnp
from jax import lax
from jax.experimental import pallas as pl
from jax.experimental.pallas import tpu as pltpu
from jax.sharding import PartitionSpec as P

HEADS = 12
HEAD_DIM = 64
EPSILON = 1e-06
MASKED = -1e30
BF = jnp.bfloat16
F32 = jnp.float32
VMEM_BYTES = 60 * 1024 * 1024
PAIR = 2 * HEAD_DIM
VEC_ROWS = 16
SLOT_ORDER = (0, 2, 1, 3)


def params(*semantics):
    return pltpu.CompilerParams(
        dimension_semantics=semantics, vmem_limit_bytes=VMEM_BYTES
    )


def dot(left, right, left_dim=1, right_dim=0):
    return lax.dot_general(
        left, right, (((left_dim,), (right_dim,)), ((), ())), preferred_element_type=F32
    )


def cost(flops, bytes_accessed, transcendentals=0):
    return pl.CostEstimate(
        flops=int(flops), bytes_accessed=int(bytes_accessed), transcendentals=int(transcendentals)
    )


def whole(shape):
    return pl.BlockSpec(shape, lambda *_: tuple(0 for _ in shape))


def key_bias(counts_ref, place_ref, keys, slots):
    row = lax.broadcasted_iota(jnp.int32, (slots, PAIR), 0)
    place = place_ref[0]
    parts = []
    for flip in SLOT_ORDER:
        kept = counts_ref[place // 2, jnp.bitwise_xor(place, flip)]
        parts.append(jnp.where(row < kept, 0.0, MASKED).astype(F32))
    return jnp.concatenate(parts, axis=0)


def augment_keys(pair, bias, which, ones):
    lane = lax.broadcasted_iota(jnp.int32, pair.shape, 1)
    mine = (lane < HEAD_DIM) if which == 0 else (lane >= HEAD_DIM)
    start = HEAD_DIM if which == 0 else 0
    extra = jnp.where(
        lane == start, bias, jnp.where((lane > start) & (lane <= start + ones), 1.0, 0.0)
    )
    return jnp.where(mine, pair.astype(F32), extra).astype(BF)


def augment_values(pair, which, ones):
    lane = lax.broadcasted_iota(jnp.int32, pair.shape, 1)
    mine = (lane < HEAD_DIM) if which == 0 else (lane >= HEAD_DIM)
    start = HEAD_DIM if which == 0 else 0
    extra = jnp.where((lane >= start) & (lane < start + ones), 1.0, 0.0)
    return jnp.where(mine, pair.astype(F32), extra).astype(BF)


def pieces(value):
    first = value.astype(BF).astype(F32)
    rest = value - first
    second = rest.astype(BF).astype(F32)
    return first, second, rest - second


def extra_rows(rows, width):
    place = lax.broadcasted_iota(jnp.int32, (HEAD_DIM, width), 0)
    out = jnp.zeros((HEAD_DIM, width), F32)
    for at, row in enumerate(rows):
        out = jnp.where(place == at, row, out)
    return out.astype(BF)


def place_rows(head, extra, which):
    return jnp.concatenate([head, extra] if which == 0 else [extra, head], axis=0)


def attend_forward_kernel(
    slots, bq, chunk, counts_ref, place_ref, k_ref, qt_ref, vt_ref, mixed_ref, ot_ref, lse_ref,
    kaug, vaug, s_a, s_b, m_a, m_b
):
    keys = k_ref.shape[0]
    step = pl.program_id(1)
    steps = pl.num_programs(1)
    scores = (s_a, s_b)
    peaks = (m_a, m_b)
    ones_row = extra_rows([jnp.ones((1, bq), F32)], bq)

    @pl.when(step == 0)
    def _():
        bias = key_bias(counts_ref, place_ref, keys, slots)
        ones = jnp.ones((16, keys), BF)
        for which in range(2):
            kaug[which] = augment_keys(k_ref[...], bias, which, 0)
            vaug[which] = jnp.concatenate(
                [vt_ref[which * HEAD_DIM : (which + 1) * HEAD_DIM, :], ones], axis=0
            )

    def query_block(at, which):
        head = qt_ref[which * HEAD_DIM : (which + 1) * HEAD_DIM, pl.ds(at * bq, bq)]
        head = (head.astype(F32) * HEAD_DIM ** (-0.5)).astype(BF)
        return place_rows(head, ones_row, which)

    def score_chunk(query, which, at, peak):
        rows = slice(at * chunk, (at + 1) * chunk)
        s = dot(kaug[which, rows, :], query)
        scores[which][rows, :] = s
        top = jnp.max(s.reshape(chunk // 8, 8, bq), axis=0)
        return top if peak is None else jnp.maximum(peak, top)

    def weigh_chunk(which, at, peak, total):
        rows = slice(at * chunk, (at + 1) * chunk)
        p = jnp.exp(scores[which][rows, :] - peak).astype(BF)
        o = dot(vaug[which, :, rows], p)
        return o if total is None else total + o

    @pl.when(step == 0)
    def _():
        query = query_block(0, 0)
        peak = None
        for at in range(keys // chunk):
            peak = score_chunk(query, 0, at, peak)
        m_a[...] = peak

    later = jnp.minimum(step + 1, steps - 1)
    outs = []
    for which in range(2):
        other = 1 - which
        query = query_block(step if which == 0 else later, other)
        peak = jnp.max(peaks[which][...], axis=0, keepdims=True)
        next_peak, total = None, None
        for at in range(keys // chunk):
            next_peak = score_chunk(query, other, at, next_peak)
            total = weigh_chunk(which, at, peak, total)
        peaks[other][...] = next_peak
        norm = total[HEAD_DIM : HEAD_DIM + 1, :]
        outs.append(total[:HEAD_DIM, :] * (1.0 / norm))
        lse_ref[0, which : which + 1, :] = peak + jnp.log(norm)
    both = jnp.concatenate(outs, axis=0)
    ot_ref[...] = both
    mixed_ref[...] = both.T.astype(BF)


def attend_forward(counts, place, packed, packed_t, slots):
    keys, width = packed.shape
    width //= 3
    pairs = width // PAIR
    bq, chunk = 256, 256
    kernel = functools.partial(attend_forward_kernel, slots, bq, chunk)
    return pl.pallas_call(
        kernel,
        grid=(pairs, keys // bq),
        in_specs=[
            pl.BlockSpec(memory_space=pltpu.SMEM),
            pl.BlockSpec(memory_space=pltpu.SMEM),
            pl.BlockSpec((keys, PAIR), lambda p, i: (0, pairs + p)),
            pl.BlockSpec((PAIR, keys), lambda p, i: (p, 0)),
            pl.BlockSpec((PAIR, keys), lambda p, i: (2 * pairs + p, 0)),
        ],
        out_specs=[
            pl.BlockSpec((bq, PAIR), lambda p, i: (i, p)),
            pl.BlockSpec((PAIR, bq), lambda p, i: (p, i)),
            pl.BlockSpec((1, 8, bq), lambda p, i: (p, 0, i)),
        ],
        out_shape=[
            jax.ShapeDtypeStruct((keys, width), BF),
            jax.ShapeDtypeStruct((width, keys), F32),
            jax.ShapeDtypeStruct((pairs, 8, keys), F32),
        ],
        scratch_shapes=[
            pltpu.VMEM((2, keys, PAIR), BF),
            pltpu.VMEM((2, HEAD_DIM + 16, keys), BF),
            pltpu.VMEM((keys, bq), F32),
            pltpu.VMEM((keys, bq), F32),
            pltpu.VMEM((8, bq), F32),
            pltpu.VMEM((8, bq), F32),
        ],
        compiler_params=params("arbitrary", "arbitrary"),
        cost_estimate=cost(
            2 * pairs * 2 * 2 * keys * keys * 256, 12 * keys * width, 2 * pairs * keys * keys
        ),
        name="attend_forward",
    )(counts, place, packed, packed_t, packed_t)


def attend_backward_kernel(
    slots, bq, chunk, counts_ref, place_ref, q_ref, k_ref, v_ref, qt_ref, kt_ref, do_ref, dot_ref, ot_ref,
    lse_ref, gq_ref, gk_ref, gv_ref, kaug, vaug, acc_k, acc_v
):
    keys = k_ref.shape[0]
    step = pl.program_id(1)
    steps = pl.num_programs(1)
    scale = HEAD_DIM ** (-0.5)

    @pl.when(step == 0)
    def _():
        bias = key_bias(counts_ref, place_ref, keys, slots)
        for which in range(2):
            kaug[which] = augment_keys(k_ref[...], bias, which, 3)
            vaug[which] = augment_values(v_ref[...], which, 3)
        acc_k[...] = jnp.zeros_like(acc_k)
        acc_v[...] = jnp.zeros_like(acc_v)

    ones_row = jnp.ones((1, bq), F32)
    queries, grads = [], []
    for which in range(2):
        rows = slice(which * HEAD_DIM, (which + 1) * HEAD_DIM)
        head = (qt_ref[rows, :].astype(F32) * scale).astype(BF)
        log_total = lse_ref[0, which : which + 1, :]
        queries.append(
            place_rows(head, extra_rows([ones_row, *pieces(-log_total)], bq), which)
        )
        grad = dot_ref[rows, :]
        delta = jnp.sum(grad.astype(F32) * ot_ref[rows, :], axis=0, keepdims=True)
        grads.append(place_rows(grad, extra_rows(list(pieces(-delta)), bq), which))

    do_pair = do_ref[...]
    q_pair = q_ref[...]
    totals = [None, None]
    for at in range(keys // chunk):
        rows = slice(at * chunk, (at + 1) * chunk)
        for which in range(2):
            p = jnp.exp(dot(kaug[which, rows, :], queries[which]))
            dp = dot(vaug[which, rows, :], grads[which])
            p_low = p.astype(BF)
            ds = (p * dp).astype(BF)
            acc_v[which, rows, :] += dot(p_low, do_pair)
            acc_k[which, rows, :] += dot(ds, q_pair)
            part = dot(kt_ref[which * HEAD_DIM : (which + 1) * HEAD_DIM, rows], ds)
            totals[which] = part if totals[which] is None else totals[which] + part
    both = jnp.concatenate(totals, axis=0) * scale
    gq_ref[...] = both.T.astype(BF)

    @pl.when(step == steps - 1)
    def _():
        lane = lax.broadcasted_iota(jnp.int32, (keys, PAIR), 1)
        gk_ref[...] = (jnp.where(lane < HEAD_DIM, acc_k[0], acc_k[1]) * scale).astype(BF)
        gv_ref[...] = jnp.where(lane < HEAD_DIM, acc_v[0], acc_v[1]).astype(BF)


def attend_backward(
    counts, place, packed, packed_t, grad, grad_t, result_t, log_total, slots, start, count
):
    keys, width = packed.shape
    width //= 3
    pairs = width // PAIR
    bq, chunk = 512, 256
    kernel = functools.partial(attend_backward_kernel, slots, bq, chunk)
    at = lambda p: p + start
    return pl.pallas_call(
        kernel,
        grid=(count, keys // bq),
        in_specs=[
            pl.BlockSpec(memory_space=pltpu.SMEM),
            pl.BlockSpec(memory_space=pltpu.SMEM),
            pl.BlockSpec((bq, PAIR), lambda p, i: (i, at(p))),
            pl.BlockSpec((keys, PAIR), lambda p, i: (0, pairs + at(p))),
            pl.BlockSpec((keys, PAIR), lambda p, i: (0, 2 * pairs + at(p))),
            pl.BlockSpec((PAIR, bq), lambda p, i: (at(p), i)),
            pl.BlockSpec((PAIR, keys), lambda p, i: (pairs + at(p), 0)),
            pl.BlockSpec((bq, PAIR), lambda p, i: (i, at(p))),
            pl.BlockSpec((PAIR, bq), lambda p, i: (at(p), i)),
            pl.BlockSpec((PAIR, bq), lambda p, i: (at(p), i)),
            pl.BlockSpec((1, 8, bq), lambda p, i: (at(p), 0, i)),
        ],
        out_specs=[
            pl.BlockSpec((bq, PAIR), lambda p, i: (i, p)),
            pl.BlockSpec((keys, PAIR), lambda p, i: (0, p)),
            pl.BlockSpec((keys, PAIR), lambda p, i: (0, p)),
        ],
        out_shape=[jax.ShapeDtypeStruct((keys, count * PAIR), BF)] * 3,
        scratch_shapes=[
            pltpu.VMEM((2, keys, PAIR), BF),
            pltpu.VMEM((2, keys, PAIR), BF),
            pltpu.VMEM((2, keys, PAIR), F32),
            pltpu.VMEM((2, keys, PAIR), F32),
        ],
        compiler_params=params("arbitrary", "arbitrary"),
        cost_estimate=cost(
            2 * count * 5 * 2 * keys * keys * 256, 24 * keys * count * PAIR,
            2 * count * keys * keys,
        ),
        name="attend_backward",
    )(counts, place, packed, packed, packed, packed_t, packed_t, grad, grad_t, result_t, log_total)


def normalised(values):
    centred = values - jnp.mean(values, axis=-1, keepdims=True)
    variance = jnp.mean(centred * centred, axis=-1, keepdims=True)
    inverse = lax.rsqrt(variance + EPSILON)
    return centred * inverse, inverse


def norm_pull(grad, gain, unit, inverse):
    scaled = grad * gain
    mean = jnp.mean(scaled, axis=-1, keepdims=True)
    along = jnp.mean(scaled * unit, axis=-1, keepdims=True)
    return inverse * (scaled - mean - unit * along)


def fold(values):
    return jnp.sum(values.reshape(values.shape[0] // 8, 8, values.shape[1]), axis=0)


def feed_forward_kernel(
    chunk, core_ref, tok_ref, mo_ref, ms_ref, cot_ref, wpx_ref, g2_ref, vec_ref, f1b_ref,
    mid_ref, out_ref, gn_ref, dw_ref, gf1_ref, gf2_ref, wpo_ref, acc1, acc2, accb, accc, wps_ref
):
    step = pl.program_id(0)
    steps = pl.num_programs(0)
    width = tok_ref.shape[1]
    half = f1b_ref.shape[1]
    part = width // 2

    @pl.when(step == 0)
    def _():
        acc1[...] = jnp.zeros_like(acc1)
        acc2[...] = jnp.zeros_like(acc2)
        accb[...] = jnp.zeros_like(accb)
        accc[...] = jnp.zeros_like(accc)
        here = pl.ds(pl.multiple_of(core_ref[0] * part, part), part)
        there = pl.ds(pl.multiple_of((1 - core_ref[0]) * part, part), part)
        wpo_ref[:, here] = g2_ref[here, :part]
        wpo_ref[:, there] = wpx_ref[here, :]
        wps_ref[:, here] = g2_ref[there, :part]
        wps_ref[:, there] = wpx_ref[there, :]

    middle = (
        tok_ref[...].astype(F32)
        + dot(mo_ref[...], wpo_ref[...])
        + dot(ms_ref[...], wps_ref[...])
        + vec_ref[0:1, :]
    )
    mid_ref[...] = middle
    unit, _ = normalised(middle)
    normed = (unit * vec_ref[1:2, :] + vec_ref[2:3, :]).astype(BF)
    normed_t = normed.T
    cot = cot_ref[...]
    out = None
    grad = None
    for at in range(half // chunk):
        cols = slice(at * chunk, (at + 1) * chunk)
        w1 = g2_ref[:, part + at * chunk : part + (at + 1) * chunk]
        piece, row = divmod(at * chunk, width)
        start = part + half + piece * width
        w2 = g2_ref[row : row + chunk, start : start + width]
        hidden = dot(normed, w1) + f1b_ref[0:1, cols]
        below = 0.5 + 0.5 * lax.erf(hidden * (0.5**0.5))
        slope = below + hidden * (jnp.exp(hidden * hidden * -0.5) * 0.3989422804014327)
        active = (hidden * below).astype(BF)
        grad_hidden = (dot(cot, w2, 1, 1) * slope).astype(BF)
        more = dot(active, w2)
        out = more if out is None else out + more
        more = dot(grad_hidden, w1, 1, 1)
        grad = more if grad is None else grad + more
        acc1[:, cols] += dot(normed_t, grad_hidden)
        acc2[cols, :] += dot(active, cot, 0, 0)
        accb[:, cols] += fold(grad_hidden.astype(F32))
    accc[...] += fold(cot.astype(F32))
    out_ref[...] = out.astype(BF)
    gn_ref[...] = grad.astype(BF)

    @pl.when(step == steps - 1)
    def _():
        dw_ref[:, :half] = acc1[...].astype(BF)
        for piece in range(half // width):
            dw_ref[:, half + piece * width : half + (piece + 1) * width] = acc2[
                piece * width : (piece + 1) * width, :
            ].astype(BF)
        gf1_ref[...] = accb[...]
        gf2_ref[...] = accc[...]


def feed_forward(core, tokens, mixed_own, mixed_sib, cot, wp_other, weights, vec, f1b):
    rows, width = tokens.shape
    half = f1b.shape[1]
    heads = mixed_own.shape[1]
    bt, chunk = 256, 384
    blocks = rows // bt
    kernel = functools.partial(feed_forward_kernel, chunk)
    return pl.pallas_call(
        kernel,
        grid=(blocks,),
        in_specs=[
            pl.BlockSpec(memory_space=pltpu.SMEM),
            pl.BlockSpec((bt, width), lambda i: (i, 0)),
            pl.BlockSpec((bt, heads), lambda i: (i, 0)),
            pl.BlockSpec((bt, heads), lambda i: (lax.rem(i + blocks // 2, blocks), 0)),
            pl.BlockSpec((bt, width), lambda i: (i, 0)),
            whole(wp_other.shape),
            whole(weights.shape),
            whole(vec.shape),
            whole(f1b.shape),
        ],
        out_specs=[
            pl.BlockSpec((bt, width), lambda i: (i, 0)),
            pl.BlockSpec((bt, width), lambda i: (i, 0)),
            pl.BlockSpec((bt, width), lambda i: (i, 0)),
            whole((width, 2 * half)),
            whole((8, half)),
            whole((8, width)),
            whole((width // 2, width)),
        ],
        out_shape=[
            jax.ShapeDtypeStruct((rows, width), F32),
            jax.ShapeDtypeStruct((rows, width), BF),
            jax.ShapeDtypeStruct((rows, width), BF),
            jax.ShapeDtypeStruct((width, 2 * half), BF),
            jax.ShapeDtypeStruct((8, half), F32),
            jax.ShapeDtypeStruct((8, width), F32),
            jax.ShapeDtypeStruct((width // 2, width), BF),
        ],
        scratch_shapes=[
            pltpu.VMEM((width, half), F32),
            pltpu.VMEM((half, width), F32),
            pltpu.VMEM((8, half), F32),
            pltpu.VMEM((8, width), F32),
            pltpu.VMEM((width // 2, width), BF),
        ],
        compiler_params=params("arbitrary"),
        cost_estimate=cost(
            2 * rows * width * (6 * half + width), 20 * rows * width + 8 * width * half,
            2 * rows * half,
        ),
        name="feed_forward",
    )(core, tokens, mixed_own, mixed_sib, cot, wp_other, weights, vec, f1b)


def branch_kernel(
    core_ref, mid_ref, ga_ref, gb_ref, cot_ref, mo_ref, ms_ref, wpo_ref, vec_ref,
    gm_ref, do_ref, dot_ref, dwo_ref, dws_ref, vecs_ref, acco, accs, accv, low_ref
):
    step = pl.program_id(0)
    steps = pl.num_programs(0)
    half = do_ref.shape[1]

    @pl.when(step == 0)
    def _():
        acco[...] = jnp.zeros_like(acco)
        accs[...] = jnp.zeros_like(accs)
        accv[...] = jnp.zeros_like(accv)

    unit, inverse = normalised(mid_ref[...])
    grad = ga_ref[...].astype(F32) + gb_ref[...].astype(F32)
    accv[0:8, :] += fold(grad * unit)
    accv[8:16, :] += fold(grad)
    grad_middle = cot_ref[...].astype(F32) + norm_pull(grad, vec_ref[1:2, :], unit, inverse)

    @pl.when(step < steps // 2)
    def _():
        gm_ref[...] = grad_middle

    low = grad_middle.astype(BF)
    low_ref[...] = low
    accv[16:24, :] += fold(low.astype(F32))
    do_ref[...] = dot(low, wpo_ref[...], 1, 1).astype(BF)
    dot_ref[...] = dot(wpo_ref[...], low, 1, 1).astype(BF)
    mine = low_ref[:, pl.ds(pl.multiple_of(core_ref[0] * half, half), half)]
    acco[...] += dot(mo_ref[...], mine, 0, 0)
    accs[...] += dot(ms_ref[...], mine, 0, 0)

    @pl.when(step == steps - 1)
    def _():
        dwo_ref[...] = acco[...].astype(BF)
        dws_ref[...] = accs[...].astype(BF)
        vecs_ref[...] = accv[...]


def branch(core, middle, grad_own, grad_sib, cot, mixed_own, mixed_sib, wp_own, vec):
    rows, width = middle.shape
    half = mixed_own.shape[1]
    bt = 256
    blocks = rows // bt
    swap = lambda i: (lax.rem(i + blocks // 2, blocks), 0)
    straight = lambda i: (i, 0)
    return pl.pallas_call(
        branch_kernel,
        grid=(blocks,),
        in_specs=[
            pl.BlockSpec(memory_space=pltpu.SMEM),
            pl.BlockSpec((bt, width), straight),
            pl.BlockSpec((bt, width), straight),
            pl.BlockSpec((bt, width), swap),
            pl.BlockSpec((bt, width), straight),
            pl.BlockSpec((bt, half), straight),
            pl.BlockSpec((bt, half), swap),
            whole(wp_own.shape),
            whole(vec.shape),
        ],
        out_specs=[
            pl.BlockSpec((bt, width), lambda i: (jnp.minimum(i, blocks // 2 - 1), 0)),
            pl.BlockSpec((bt, half), straight),
            pl.BlockSpec((half, bt), lambda i: (0, i)),
            whole((half, half)),
            whole((half, half)),
            whole((24, width)),
        ],
        out_shape=[
            jax.ShapeDtypeStruct((rows // 2, width), F32),
            jax.ShapeDtypeStruct((rows, half), BF),
            jax.ShapeDtypeStruct((half, rows), BF),
            jax.ShapeDtypeStruct((half, half), BF),
            jax.ShapeDtypeStruct((half, half), BF),
            jax.ShapeDtypeStruct((24, width), F32),
        ],
        scratch_shapes=[
            pltpu.VMEM((half, half), F32),
            pltpu.VMEM((half, half), F32),
            pltpu.VMEM((24, width), F32),
            pltpu.VMEM((bt, width), BF),
        ],
        compiler_params=params("arbitrary"),
        cost_estimate=cost(2 * rows * width * 3 * half, 18 * rows * width),
        name="branch",
    )(core, middle, grad_own, grad_sib, cot, mixed_own, mixed_sib, wp_own, vec)


def weight_grad_kernel(tok_ref, gq_ref, gk_ref, gv_ref, vec_ref, dw_ref, qv_ref, accw, accqv):
    step = pl.program_id(0)
    steps = pl.num_programs(0)
    part = gq_ref.shape[1]

    @pl.when(step == 0)
    def _():
        accw[...] = jnp.zeros_like(accw)
        accqv[...] = jnp.zeros_like(accqv)

    unit, _ = normalised(tok_ref[...].astype(F32))
    normed_t = (unit * vec_ref[0:1, :] + vec_ref[1:2, :]).astype(BF).T
    for at, ref in enumerate((gq_ref, gk_ref, gv_ref)):
        cols = slice(at * part, (at + 1) * part)
        value = ref[...]
        accw[:, cols] += dot(normed_t, value)
        if at != 1:
            here = 0 if at == 0 else 8
            accqv[here : here + 8, :] += fold(value.astype(F32))

    @pl.when(step == steps - 1)
    def _():
        dw_ref[...] = accw[...].astype(BF)
        qv_ref[...] = accqv[...]


def weight_grad(tokens, gq, gk, gv, vec):
    rows, width = tokens.shape
    part = gq.shape[1]
    bt = 256
    straight = lambda i: (i, 0)
    return pl.pallas_call(
        weight_grad_kernel,
        grid=(rows // bt,),
        in_specs=[
            pl.BlockSpec((bt, width), straight),
            pl.BlockSpec((bt, part), straight),
            pl.BlockSpec((bt, part), straight),
            pl.BlockSpec((bt, part), straight),
            whole(vec.shape),
        ],
        out_specs=[whole((width, 3 * part)), whole((16, part))],
        out_shape=[
            jax.ShapeDtypeStruct((width, 3 * part), BF),
            jax.ShapeDtypeStruct((16, part), F32),
        ],
        scratch_shapes=[pltpu.VMEM((width, 3 * part), F32), pltpu.VMEM((16, part), F32)],
        compiler_params=params("arbitrary"),
        cost_estimate=cost(2 * rows * width * 3 * part, 2 * rows * (width + 3 * part)),
        name="weight_grad",
    )(tokens, gq, gk, gv, vec)


def project_back_kernel(
    tok_ref, gqa_ref, gka_ref, gva_ref, gq_ref, gk_ref, gv_ref, w_ref, vec_ref,
    own_ref, sib_ref, dw_ref, vecs_ref, qv_ref, accw, accv, accqv
):
    step = pl.program_id(0)
    steps = pl.num_programs(0)
    early = gqa_ref.shape[1]
    part = gq_ref.shape[1]
    wide = early + part

    @pl.when(step == 0)
    def _():
        accw[...] = jnp.zeros_like(accw)
        accv[...] = jnp.zeros_like(accv)
        accqv[...] = jnp.zeros_like(accqv)

    unit, _ = normalised(tok_ref[...].astype(F32))
    normed_t = (unit * vec_ref[0:1, :] + vec_ref[1:2, :]).astype(BF).T
    grad = None
    before = (gqa_ref, gka_ref, gva_ref)
    for at, ref in enumerate((gq_ref, gk_ref, gv_ref)):
        cols = slice(at * part, (at + 1) * part)
        value = ref[...]
        more = dot(
            jnp.concatenate([before[at][...], value], axis=1),
            w_ref[:, at * wide : (at + 1) * wide], 1, 1,
        )
        grad = more if grad is None else grad + more
        accw[:, cols] += dot(normed_t, value)
        if at != 1:
            here = 0 if at == 0 else 8
            accqv[here : here + 8, :] += fold(value.astype(F32))
    accv[0:8, :] += fold(grad * unit)
    accv[8:16, :] += fold(grad)

    @pl.when(step < steps // 2)
    def _():
        own_ref[...] = grad

    @pl.when(step >= steps // 2)
    def _():
        sib_ref[...] = grad.astype(BF)

    @pl.when(step == steps - 1)
    def _():
        dw_ref[...] = accw[...].astype(BF)
        vecs_ref[...] = accv[...]
        qv_ref[...] = accqv[...]


def project_back(tokens, before, grads, weight, vec):
    rows, width = tokens.shape
    early, part = before[0].shape[1], grads[0].shape[1]
    bt = 256
    blocks = rows // bt
    straight = lambda i: (i, 0)
    return pl.pallas_call(
        project_back_kernel,
        grid=(blocks,),
        in_specs=[pl.BlockSpec((bt, width), straight)]
        + [pl.BlockSpec((bt, early), straight)] * 3
        + [pl.BlockSpec((bt, part), straight)] * 3
        + [whole(weight.shape), whole(vec.shape)],
        out_specs=[
            pl.BlockSpec((bt, width), lambda i: (jnp.minimum(i, blocks // 2 - 1), 0)),
            pl.BlockSpec((bt, width), lambda i: (jnp.maximum(i - blocks // 2, 0), 0)),
            whole((width, 3 * part)),
            whole((16, width)),
            whole((16, part)),
        ],
        out_shape=[
            jax.ShapeDtypeStruct((rows // 2, width), F32),
            jax.ShapeDtypeStruct((rows // 2, width), BF),
            jax.ShapeDtypeStruct((width, 3 * part), BF),
            jax.ShapeDtypeStruct((16, width), F32),
            jax.ShapeDtypeStruct((16, part), F32),
        ],
        scratch_shapes=[
            pltpu.VMEM((width, 3 * part), F32),
            pltpu.VMEM((16, width), F32),
            pltpu.VMEM((16, part), F32),
        ],
        compiler_params=params("arbitrary"),
        cost_estimate=cost(2 * rows * width * (6 * part + 3 * early), 14 * rows * width),
        name="project_back",
    )(tokens, *before, *grads, weight, vec)


def pack_kernel(place_ref, *refs):
    vectors, (qkv_ref, proj_ref, fc1_ref, fc2_ref, one_ref, two_ref) = refs[:-6], refs[-6:]
    first_core = lax.rem(place_ref[0], 2) == 0
    first_chip = place_ref[0] // 2 == 0
    shard, width = proj_ref.shape
    part = width // 2
    ff = fc1_ref.shape[1]
    owners = one_ref.shape[0]
    quarter = ff // owners // 4
    half = ff // 2
    one_ref[0, :VEC_ROWS, :] = jnp.zeros((VEC_ROWS, 3 * part), BF)
    for at, ref in enumerate(vectors):
        one_ref[0, at : at + 1, : ref.shape[1]] = ref[...]
    for at in range(3):
        low = qkv_ref[:, at * width : at * width + part]
        high = qkv_ref[:, at * width + part : (at + 1) * width]
        mine = jnp.where(first_core, low, high)
        mine = jnp.where(first_chip, mine[: shard // 2], mine[shard // 2 :])
        one_ref[0, VEC_ROWS:, at * part : (at + 1) * part] = mine
    for owner in range(1, owners):
        one_ref[owner] = one_ref[0]
    two_ref[:, :part] = jnp.where(first_core, proj_ref[:, :part], proj_ref[:, part:])
    pieces_low, pieces_high = [], []
    for piece in range(2):
        for owner in range(owners):
            base = owner * 4 * quarter + piece * quarter
            pieces_low.append(fc1_ref[:, base : base + quarter])
            pieces_high.append(fc1_ref[:, base + 2 * quarter : base + 3 * quarter])
    two_ref[:, part : part + half] = jnp.where(
        first_core, jnp.concatenate(pieces_low, axis=1), jnp.concatenate(pieces_high, axis=1)
    )
    for piece in range(2):
        low = fc2_ref[piece * quarter : (piece + 1) * quarter, :]
        high = fc2_ref[(2 + piece) * quarter : (3 + piece) * quarter, :]
        start = part + half + piece * width
        two_ref[:, start : start + width] = jnp.where(first_core, low, high)


def pack_weights(place, owners, vectors, qkv, proj, fc1, fc2):
    shard, width = proj.shape
    half = fc1.shape[1] // 2
    part = width // 2
    vectors = [vector.reshape(1, -1) for vector in vectors]
    values = (*vectors, qkv, proj, fc1, fc2)
    rows = VEC_ROWS + shard // 2
    return pl.pallas_call(
        pack_kernel,
        grid=(1,),
        in_specs=[pl.BlockSpec(memory_space=pltpu.SMEM)] + [whole(value.shape) for value in values],
        out_specs=[whole((owners, rows, 3 * part)), whole((shard, 5 * part + half))],
        out_shape=[
            jax.ShapeDtypeStruct((owners, rows, 3 * part), BF),
            jax.ShapeDtypeStruct((shard, 5 * part + half), BF),
        ],
        compiler_params=params("arbitrary"),
        cost_estimate=cost(0, 5 * shard * width * 8),
        name="pack_weights",
    )(place, *values)


def project_kernel(tok_ref, w_ref, bias_ref, vec_ref, out_ref, out_t_ref):
    unit, _ = normalised(tok_ref[...].astype(F32))
    normed = (unit * vec_ref[0:1, :] + vec_ref[1:2, :]).astype(BF)
    packed = dot(normed, w_ref[...]) + bias_ref[0:1, :]
    out_ref[...] = packed.astype(BF)
    out_t_ref[...] = packed.T.astype(BF)


def project(tokens, weight, bias, vec):
    rows, width = tokens.shape
    wide = weight.shape[1]
    bt = 256
    return pl.pallas_call(
        project_kernel,
        grid=(rows // bt,),
        in_specs=[
            pl.BlockSpec((bt, width), lambda i: (i, 0)),
            whole(weight.shape),
            whole(bias.shape),
            whole(vec.shape),
        ],
        out_specs=[
            pl.BlockSpec((bt, wide), lambda i: (i, 0)),
            pl.BlockSpec((wide, bt), lambda i: (0, i)),
        ],
        out_shape=[
            jax.ShapeDtypeStruct((rows, wide), BF),
            jax.ShapeDtypeStruct((wide, rows), BF),
        ],
        compiler_params=params("arbitrary"),
        cost_estimate=cost(2 * rows * width * wide, 12 * rows * width),
        name="project",
    )(tokens, weight, bias, vec)


def exchange(value):
    return lax.all_to_all(value, "fsdp", split_axis=0, concat_axis=0, tiled=True)


def per_device(
    tokens,
    counts,
    norm1_gain,
    norm1_bias,
    qkv_weight,
    query_bias,
    value_bias,
    proj_weight,
    proj_bias,
    norm2_gain,
    norm2_bias,
    fc1_weight,
    fc1_bias,
    fc2_weight,
    fc2_bias,
    cotangent,
):
    images, slots, width = tokens.shape
    owners = lax.axis_size("fsdp")
    seq = lax.axis_size("seq")
    place = lax.axis_index("seq")
    core = lax.rem(place, 2)
    image = place // 2
    part = width // 2
    shard = width // owners
    ff = fc1_weight.shape[1]
    ff_shard = ff // owners
    quarter = ff_shard // 4
    half = ff // 2
    to_sibling = [(at, at ^ 1) for at in range(seq)]
    to_partner = [(at, at ^ 2) for at in range(seq)]

    def sibling(value):
        return lax.ppermute(value, "seq", to_sibling)

    def partner(value):
        return lax.ppermute(value, "seq", to_partner)

    def pick(value, at, axis):
        return lax.dynamic_index_in_dim(value, at, axis, keepdims=False)

    place_row = place.reshape(1).astype(jnp.int32)
    core_row = core.reshape(1).astype(jnp.int32)
    small = [
        norm1_gain, norm1_bias, query_bias, value_bias, proj_bias, norm2_gain, norm2_bias,
        fc2_bias, fc1_bias,
    ]
    one, two = pack_weights(
        place_row, owners, small, qkv_weight, proj_weight, fc1_weight, fc2_weight
    )
    mine_one = exchange(one)
    mine_one, two = lax.optimization_barrier((mine_one, two))
    second = lax.all_gather(two, "fsdp", axis=0, tiled=True)
    own_rows = mine_one[:, VEC_ROWS:]
    other_rows = partner(own_rows)
    w_qkv = jnp.where(
        image == 0,
        jnp.stack([own_rows, other_rows], axis=1),
        jnp.stack([other_rows, own_rows], axis=1),
    ).reshape(width, 3 * part)

    def collect(value, theirs):
        mine = pick(value, image, 0)
        return jnp.concatenate([mine, theirs, sibling(mine), sibling(theirs)], axis=0)

    tok = collect(tokens, partner(pick(tokens, 1 - image, 0)))
    vecs = mine_one[:, :8, :shard].astype(F32).transpose(1, 0, 2).reshape(8, width)
    g1, b1, qb, vb, pb, g2, b2, f2b = vecs
    f1b = mine_one[:, 8, :ff_shard].astype(F32)
    f1b = pick(f1b.reshape(owners, 2, 2, quarter), core, 1)
    f1b = f1b.transpose(1, 0, 2).reshape(1, half)

    def mine_of(vector):
        return lax.dynamic_slice_in_dim(vector, core * part, part, 0)

    qkv_bias = jnp.concatenate([mine_of(qb), jnp.zeros((part,), F32), mine_of(vb)])
    vec_one = jnp.concatenate([jnp.stack([g1, b1]), jnp.zeros((6, width), F32)])
    packed, packed_t = project(tok, w_qkv, qkv_bias.reshape(1, 3 * part), vec_one)
    cot = collect(cotangent, partner(pick(cotangent, 1 - image, 0)))
    packed, cot = lax.optimization_barrier((packed, cot))
    mixed, result_t, log_total = attend_forward(counts, place_row, packed, packed_t, slots)
    mixed_sib = sibling(mixed)

    wp_other = sibling(second[:, :part])
    vec_two = jnp.concatenate([jnp.stack([pb, g2, b2]), jnp.zeros((5, width), F32)])
    middle, out_part, gn_part, dw_ff, gf1, gf2, wp_own = feed_forward(
        core_row, tok, mixed, mixed_sib, cot, wp_other, second, vec_two, f1b
    )
    scattered_one = lax.psum_scatter(dw_ff, "fsdp", scatter_dimension=0, tiled=True)
    gn_sib = sibling(gn_part)
    rows_own = 2 * slots
    out_sib = sibling(out_part[rows_own:])
    out_own = (
        middle[:rows_own] + out_part[:rows_own].astype(F32) + out_sib.astype(F32) + f2b
    ).astype(BF)

    def hand_back(own, sent):
        kept_part = own[:slots]
        came = partner(sent).astype(own.dtype)
        straight = jnp.stack([kept_part, came])
        crossed = jnp.stack([came, kept_part])
        return jnp.where(image == 0, straight, crossed)

    output = hand_back(out_own, out_own[slots:])
    grad_middle, grad_mixed, grad_mixed_t, dwp_own, dwp_sib, vec_back = branch(
        core_row, middle, gn_part, gn_sib, cot, mixed, mixed_sib, wp_own, vec_two
    )
    dwp = jnp.where(
        core == 0,
        jnp.concatenate([dwp_own, dwp_sib], axis=0),
        jnp.concatenate([dwp_sib, dwp_own], axis=0),
    )
    early, late = 2, 1
    attend = functools.partial(attend_backward, counts, place_row, packed, packed_t)
    before = attend(grad_mixed, grad_mixed_t, result_t, log_total, slots, 0, early)
    dw_early, qv_early = weight_grad(tok, *before, vec_one)
    block_one = jnp.concatenate([dw_early, dwp], axis=1).reshape(owners, shard, -1)
    came_one = exchange(block_one)
    grad_mixed, output, block_one = lax.optimization_barrier((grad_mixed, output, block_one))
    grads = attend(grad_mixed, grad_mixed_t, result_t, log_total, slots, early, late)
    gn1_own, gn1_send, dw_late, vec_first, qv_late = project_back(
        tok, before, grads, w_qkv, vec_one
    )

    def spread(vector):
        both = jnp.zeros((2, part), F32)
        return lax.dynamic_update_index_in_dim(both, vector, core, 0).reshape(width)

    def rows_of(block):
        return jnp.sum(block.reshape(block.shape[0] // 8, 8, block.shape[1]), axis=1)

    once = (core == 0).astype(F32)
    gg1, gb1 = rows_of(vec_first)
    gqb, gvb = rows_of(jnp.concatenate([qv_early, qv_late], axis=1))
    gg2, gb2, gpb = rows_of(vec_back) * once
    gf2b = jnp.sum(gf2, axis=0) * once
    gf1b = jnp.sum(gf1, axis=0).reshape(2, owners, quarter).transpose(1, 0, 2)
    gf1b = lax.dynamic_update_index_in_dim(
        jnp.zeros((owners, 2, 2, quarter), F32), gf1b, core, 1
    ).reshape(owners, ff_shard)
    late_wide = 3 * late * PAIR
    small_grads = jnp.stack(
        [gg1, gb1, spread(gqb), spread(gvb), gpb, gg2, gb2, gf2b]
    ).reshape(8, owners, shard).transpose(1, 0, 2)
    small_block = jnp.concatenate(
        [
            jnp.pad(small_grads, ((0, 0), (0, 0), (0, late_wide - shard))),
            jnp.pad(gf1b[:, None], ((0, 0), (0, VEC_ROWS - 9), (0, late_wide - ff_shard))),
        ],
        axis=1,
    ).astype(BF)
    block_two = jnp.concatenate(
        [small_block, dw_late.reshape(owners, shard, late_wide)], axis=1
    )
    came_two = exchange(block_two)

    def total(came):
        return jnp.sum(came.astype(F32), axis=0).astype(BF)

    gn1 = gn1_own + sibling(gn1_send).astype(F32)
    unit_own, inverse_own = normalised(tok[:rows_own].astype(F32))
    input_own = grad_middle + norm_pull(gn1, g1, unit_own, inverse_own)
    input_grad = hand_back(input_own, input_own[slots:].astype(BF))

    def finish(value):
        summed = value.astype(F32) + partner(value).astype(F32)
        other = sibling(summed.astype(BF)).astype(F32)
        return summed, other

    def in_order(mine, other):
        return jnp.where(core == 0, mine, other), jnp.where(core == 0, other, mine)

    one_mine, one_other = finish(scattered_one)
    lower, upper = in_order(one_mine, one_other)

    def fc1_of(value):
        return value[:, :half].reshape(shard, 2, owners, quarter).transpose(0, 2, 1, 3)

    grad_fc1 = jnp.stack([fc1_of(lower), fc1_of(upper)], axis=2).reshape(shard, ff)

    def fc2_of(value):
        return value[:, half:].reshape(quarter, 2, width).transpose(1, 0, 2)

    grad_fc2 = jnp.stack([fc2_of(lower), fc2_of(upper)]).reshape(ff_shard, width)
    early_mine, early_other = finish(total(came_one))
    early_sum = in_order(early_mine, early_other)
    late_mine, late_other = finish(total(came_two))
    late_sum = in_order(late_mine[VEC_ROWS:], late_other[VEC_ROWS:])
    cut, tail = early * PAIR, late * PAIR
    grad_qkv = jnp.concatenate(
        [
            piece
            for at in range(3)
            for of in range(2)
            for piece in (
                early_sum[of][:, at * cut : (at + 1) * cut],
                late_sum[of][:, at * tail : (at + 1) * tail],
            )
        ],
        axis=1,
    )
    grad_proj = jnp.concatenate([early_sum[0][:, 3 * cut :], early_sum[1][:, 3 * cut :]], axis=1)
    small_sum = late_mine[:VEC_ROWS] + late_other[:VEC_ROWS]
    s = [small_sum[at, :shard] for at in range(8)]
    grad_f1b = small_sum[8, :ff_shard]
    return (
        output,
        input_grad,
        s[0],
        s[1],
        grad_qkv,
        s[2],
        s[3],
        grad_proj,
        s[4],
        s[5],
        s[6],
        grad_fc1,
        grad_f1b,
        grad_fc2,
        s[7],
    )


def solution(mesh):
    placed = (
        P("fsdp", "seq", None),
        P("fsdp", None),
        P("fsdp"),
        P("fsdp"),
        P("fsdp", None),
        P("fsdp"),
        P("fsdp"),
        P("fsdp", None),
        P("fsdp"),
        P("fsdp"),
        P("fsdp"),
        P("fsdp", None),
        P("fsdp"),
        P("fsdp", None),
        P("fsdp"),
        P("fsdp", "seq", None),
    )
    return jax.shard_map(
        per_device,
        mesh=mesh,
        in_specs=placed,
        out_specs=(
            P("fsdp", "seq", None),
            P("fsdp", "seq", None),
            P("fsdp"),
            P("fsdp"),
            P("fsdp", None),
            P("fsdp"),
            P("fsdp"),
            P("fsdp", None),
            P("fsdp"),
            P("fsdp"),
            P("fsdp"),
            P("fsdp", None),
            P("fsdp"),
            P("fsdp", None),
            P("fsdp"),
        ),
        check_vma=False,
    )
```

```python
import functools

import jax
import jax.numpy as jnp
from jax import lax
from jax.experimental import pallas as pl
from jax.experimental.pallas import tpu as pltpu
from jax.sharding import PartitionSpec as P

HEADS = 12
HEAD_DIM = 64
EPSILON = 1e-06
MASKED = -1e30
BF = jnp.bfloat16
F32 = jnp.float32
VMEM_BYTES = 60 * 1024 * 1024
PAIR = 2 * HEAD_DIM
VEC_ROWS = 16
SLOT_ORDER = (0, 2, 1, 3)


def params(*semantics):
    return pltpu.CompilerParams(
        dimension_semantics=semantics, vmem_limit_bytes=VMEM_BYTES
    )


def dot(left, right, left_dim=1, right_dim=0):
    return lax.dot_general(
        left, right, (((left_dim,), (right_dim,)), ((), ())), preferred_element_type=F32
    )


def cost(flops, bytes_accessed, transcendentals=0):
    return pl.CostEstimate(
        flops=int(flops), bytes_accessed=int(bytes_accessed), transcendentals=int(transcendentals)
    )


def whole(shape):
    return pl.BlockSpec(shape, lambda *_: tuple(0 for _ in shape))


def key_bias(counts_ref, place_ref, keys, slots):
    row = lax.broadcasted_iota(jnp.int32, (slots, PAIR), 0)
    place = place_ref[0]
    parts = []
    for flip in SLOT_ORDER:
        kept = counts_ref[place // 2, jnp.bitwise_xor(place, flip)]
        parts.append(jnp.where(row < kept, 0.0, MASKED).astype(F32))
    return jnp.concatenate(parts, axis=0)


def augment_keys(pair, bias, which, ones):
    lane = lax.broadcasted_iota(jnp.int32, pair.shape, 1)
    mine = (lane < HEAD_DIM) if which == 0 else (lane >= HEAD_DIM)
    start = HEAD_DIM if which == 0 else 0
    extra = jnp.where(
        lane == start, bias, jnp.where((lane > start) & (lane <= start + ones), 1.0, 0.0)
    )
    return jnp.where(mine, pair.astype(F32), extra).astype(BF)


def augment_values(pair, which, ones):
    lane = lax.broadcasted_iota(jnp.int32, pair.shape, 1)
    mine = (lane < HEAD_DIM) if which == 0 else (lane >= HEAD_DIM)
    start = HEAD_DIM if which == 0 else 0
    extra = jnp.where((lane >= start) & (lane < start + ones), 1.0, 0.0)
    return jnp.where(mine, pair.astype(F32), extra).astype(BF)


def pieces(value):
    first = value.astype(BF).astype(F32)
    rest = value - first
    second = rest.astype(BF).astype(F32)
    return first, second, rest - second


def extra_rows(rows, width):
    place = lax.broadcasted_iota(jnp.int32, (HEAD_DIM, width), 0)
    out = jnp.zeros((HEAD_DIM, width), F32)
    for at, row in enumerate(rows):
        out = jnp.where(place == at, row, out)
    return out.astype(BF)


def place_rows(head, extra, which):
    return jnp.concatenate([head, extra] if which == 0 else [extra, head], axis=0)


def attend_forward_kernel(
    slots, bq, chunk, counts_ref, place_ref, k_ref, qt_ref, vt_ref, mixed_ref, ot_ref, lse_ref,
    kaug, vaug, s_a, s_b, m_a, m_b
):
    keys = k_ref.shape[0]
    step = pl.program_id(1)
    steps = pl.num_programs(1)
    scores = (s_a, s_b)
    peaks = (m_a, m_b)
    ones_row = extra_rows([jnp.ones((1, bq), F32)], bq)

    @pl.when(step == 0)
    def _():
        bias = key_bias(counts_ref, place_ref, keys, slots)
        ones = jnp.ones((16, keys), BF)
        for which in range(2):
            kaug[which] = augment_keys(k_ref[...], bias, which, 0)
            vaug[which] = jnp.concatenate(
                [vt_ref[which * HEAD_DIM : (which + 1) * HEAD_DIM, :], ones], axis=0
            )

    def query_block(at, which):
        head = qt_ref[which * HEAD_DIM : (which + 1) * HEAD_DIM, pl.ds(at * bq, bq)]
        head = (head.astype(F32) * HEAD_DIM ** (-0.5)).astype(BF)
        return place_rows(head, ones_row, which)

    def score_chunk(query, which, at, peak):
        rows = slice(at * chunk, (at + 1) * chunk)
        s = dot(kaug[which, rows, :], query)
        scores[which][rows, :] = s
        top = jnp.max(s.reshape(chunk // 8, 8, bq), axis=0)
        return top if peak is None else jnp.maximum(peak, top)

    def weigh_chunk(which, at, peak, total):
        rows = slice(at * chunk, (at + 1) * chunk)
        p = jnp.exp(scores[which][rows, :] - peak).astype(BF)
        o = dot(vaug[which, :, rows], p)
        return o if total is None else total + o

    @pl.when(step == 0)
    def _():
        query = query_block(0, 0)
        peak = None
        for at in range(keys // chunk):
            peak = score_chunk(query, 0, at, peak)
        m_a[...] = peak

    later = jnp.minimum(step + 1, steps - 1)
    outs = []
    for which in range(2):
        other = 1 - which
        query = query_block(step if which == 0 else later, other)
        peak = jnp.max(peaks[which][...], axis=0, keepdims=True)
        next_peak, total = None, None
        for at in range(keys // chunk):
            next_peak = score_chunk(query, other, at, next_peak)
            total = weigh_chunk(which, at, peak, total)
        peaks[other][...] = next_peak
        norm = total[HEAD_DIM : HEAD_DIM + 1, :]
        outs.append(total[:HEAD_DIM, :] * (1.0 / norm))
        lse_ref[0, which : which + 1, :] = peak + jnp.log(norm)
    both = jnp.concatenate(outs, axis=0)
    ot_ref[...] = both
    mixed_ref[...] = both.T.astype(BF)


def attend_forward(counts, place, packed, packed_t, slots):
    keys, width = packed.shape
    width //= 3
    pairs = width // PAIR
    bq, chunk = 256, 256
    kernel = functools.partial(attend_forward_kernel, slots, bq, chunk)
    return pl.pallas_call(
        kernel,
        grid=(pairs, keys // bq),
        in_specs=[
            pl.BlockSpec(memory_space=pltpu.SMEM),
            pl.BlockSpec(memory_space=pltpu.SMEM),
            pl.BlockSpec((keys, PAIR), lambda p, i: (0, pairs + p)),
            pl.BlockSpec((PAIR, keys), lambda p, i: (p, 0)),
            pl.BlockSpec((PAIR, keys), lambda p, i: (2 * pairs + p, 0)),
        ],
        out_specs=[
            pl.BlockSpec((bq, PAIR), lambda p, i: (i, p)),
            pl.BlockSpec((PAIR, bq), lambda p, i: (p, i)),
            pl.BlockSpec((1, 8, bq), lambda p, i: (p, 0, i)),
        ],
        out_shape=[
            jax.ShapeDtypeStruct((keys, width), BF),
            jax.ShapeDtypeStruct((width, keys), F32),
            jax.ShapeDtypeStruct((pairs, 8, keys), F32),
        ],
        scratch_shapes=[
            pltpu.VMEM((2, keys, PAIR), BF),
            pltpu.VMEM((2, HEAD_DIM + 16, keys), BF),
            pltpu.VMEM((keys, bq), F32),
            pltpu.VMEM((keys, bq), F32),
            pltpu.VMEM((8, bq), F32),
            pltpu.VMEM((8, bq), F32),
        ],
        compiler_params=params("arbitrary", "arbitrary"),
        cost_estimate=cost(
            2 * pairs * 2 * 2 * keys * keys * 256, 12 * keys * width, 2 * pairs * keys * keys
        ),
        name="attend_forward",
    )(counts, place, packed, packed_t, packed_t)


def attend_backward_kernel(
    slots, bq, chunk, counts_ref, place_ref, q_ref, k_ref, v_ref, qt_ref, kt_ref, do_ref, dot_ref, ot_ref,
    lse_ref, gq_ref, gk_ref, gv_ref, kaug, vaug, acc_k, acc_v
):
    keys = k_ref.shape[0]
    step = pl.program_id(1)
    steps = pl.num_programs(1)
    scale = HEAD_DIM ** (-0.5)

    @pl.when(step == 0)
    def _():
        bias = key_bias(counts_ref, place_ref, keys, slots)
        for which in range(2):
            kaug[which] = augment_keys(k_ref[...], bias, which, 3)
            vaug[which] = augment_values(v_ref[...], which, 3)
        acc_k[...] = jnp.zeros_like(acc_k)
        acc_v[...] = jnp.zeros_like(acc_v)

    ones_row = jnp.ones((1, bq), F32)
    queries, grads = [], []
    for which in range(2):
        rows = slice(which * HEAD_DIM, (which + 1) * HEAD_DIM)
        head = (qt_ref[rows, :].astype(F32) * scale).astype(BF)
        log_total = lse_ref[0, which : which + 1, :]
        queries.append(
            place_rows(head, extra_rows([ones_row, *pieces(-log_total)], bq), which)
        )
        grad = dot_ref[rows, :]
        delta = jnp.sum(grad.astype(F32) * ot_ref[rows, :], axis=0, keepdims=True)
        grads.append(place_rows(grad, extra_rows(list(pieces(-delta)), bq), which))

    do_pair = do_ref[...]
    q_pair = q_ref[...]
    totals = [None, None]
    for at in range(keys // chunk):
        rows = slice(at * chunk, (at + 1) * chunk)
        for which in range(2):
            p = jnp.exp(dot(kaug[which, rows, :], queries[which]))
            dp = dot(vaug[which, rows, :], grads[which])
            p_low = p.astype(BF)
            ds = (p * dp).astype(BF)
            acc_v[which, rows, :] += dot(p_low, do_pair)
            acc_k[which, rows, :] += dot(ds, q_pair)
            part = dot(kt_ref[which * HEAD_DIM : (which + 1) * HEAD_DIM, rows], ds)
            totals[which] = part if totals[which] is None else totals[which] + part
    both = jnp.concatenate(totals, axis=0) * scale
    gq_ref[...] = both.T.astype(BF)

    @pl.when(step == steps - 1)
    def _():
        lane = lax.broadcasted_iota(jnp.int32, (keys, PAIR), 1)
        gk_ref[...] = (jnp.where(lane < HEAD_DIM, acc_k[0], acc_k[1]) * scale).astype(BF)
        gv_ref[...] = jnp.where(lane < HEAD_DIM, acc_v[0], acc_v[1]).astype(BF)


def attend_backward(
    counts, place, packed, packed_t, grad, grad_t, result_t, log_total, slots, start, count
):
    keys, width = packed.shape
    width //= 3
    pairs = width // PAIR
    bq, chunk = 512, 256
    kernel = functools.partial(attend_backward_kernel, slots, bq, chunk)
    at = lambda p: p + start
    return pl.pallas_call(
        kernel,
        grid=(count, keys // bq),
        in_specs=[
            pl.BlockSpec(memory_space=pltpu.SMEM),
            pl.BlockSpec(memory_space=pltpu.SMEM),
            pl.BlockSpec((bq, PAIR), lambda p, i: (i, at(p))),
            pl.BlockSpec((keys, PAIR), lambda p, i: (0, pairs + at(p))),
            pl.BlockSpec((keys, PAIR), lambda p, i: (0, 2 * pairs + at(p))),
            pl.BlockSpec((PAIR, bq), lambda p, i: (at(p), i)),
            pl.BlockSpec((PAIR, keys), lambda p, i: (pairs + at(p), 0)),
            pl.BlockSpec((bq, PAIR), lambda p, i: (i, at(p))),
            pl.BlockSpec((PAIR, bq), lambda p, i: (at(p), i)),
            pl.BlockSpec((PAIR, bq), lambda p, i: (at(p), i)),
            pl.BlockSpec((1, 8, bq), lambda p, i: (at(p), 0, i)),
        ],
        out_specs=[
            pl.BlockSpec((bq, PAIR), lambda p, i: (i, p)),
            pl.BlockSpec((keys, PAIR), lambda p, i: (0, p)),
            pl.BlockSpec((keys, PAIR), lambda p, i: (0, p)),
        ],
        out_shape=[jax.ShapeDtypeStruct((keys, count * PAIR), BF)] * 3,
        scratch_shapes=[
            pltpu.VMEM((2, keys, PAIR), BF),
            pltpu.VMEM((2, keys, PAIR), BF),
            pltpu.VMEM((2, keys, PAIR), F32),
            pltpu.VMEM((2, keys, PAIR), F32),
        ],
        compiler_params=params("arbitrary", "arbitrary"),
        cost_estimate=cost(
            2 * count * 5 * 2 * keys * keys * 256, 24 * keys * count * PAIR,
            2 * count * keys * keys,
        ),
        name="attend_backward",
    )(counts, place, packed, packed, packed, packed_t, packed_t, grad, grad_t, result_t, log_total)


def normalised(values):
    centred = values - jnp.mean(values, axis=-1, keepdims=True)
    variance = jnp.mean(centred * centred, axis=-1, keepdims=True)
    inverse = lax.rsqrt(variance + EPSILON)
    return centred * inverse, inverse


def norm_pull(grad, gain, unit, inverse):
    scaled = grad * gain
    mean = jnp.mean(scaled, axis=-1, keepdims=True)
    along = jnp.mean(scaled * unit, axis=-1, keepdims=True)
    return inverse * (scaled - mean - unit * along)


def fold(values):
    return jnp.sum(values.reshape(values.shape[0] // 8, 8, values.shape[1]), axis=0)


def feed_forward_kernel(
    chunk, core_ref, tok_ref, mo_ref, ms_ref, cot_ref, wpx_ref, g2_ref, vec_ref, f1b_ref,
    mid_ref, out_ref, gn_ref, dw_ref, gf1_ref, gf2_ref, wpo_ref, acc1, acc2, accb, accc, wps_ref
):
    step = pl.program_id(0)
    steps = pl.num_programs(0)
    width = tok_ref.shape[1]
    half = f1b_ref.shape[1]
    part = width // 2

    @pl.when(step == 0)
    def _():
        acc1[...] = jnp.zeros_like(acc1)
        acc2[...] = jnp.zeros_like(acc2)
        accb[...] = jnp.zeros_like(accb)
        accc[...] = jnp.zeros_like(accc)
        here = pl.ds(pl.multiple_of(core_ref[0] * part, part), part)
        there = pl.ds(pl.multiple_of((1 - core_ref[0]) * part, part), part)
        wpo_ref[:, here] = g2_ref[here, :part]
        wpo_ref[:, there] = wpx_ref[here, :]
        wps_ref[:, here] = g2_ref[there, :part]
        wps_ref[:, there] = wpx_ref[there, :]

    middle = (
        tok_ref[...].astype(F32)
        + dot(mo_ref[...], wpo_ref[...])
        + dot(ms_ref[...], wps_ref[...])
        + vec_ref[0:1, :]
    )
    mid_ref[...] = middle
    unit, _ = normalised(middle)
    normed = (unit * vec_ref[1:2, :] + vec_ref[2:3, :]).astype(BF)
    normed_t = normed.T
    cot = cot_ref[...]
    out = None
    grad = None
    for at in range(half // chunk):
        cols = slice(at * chunk, (at + 1) * chunk)
        w1 = g2_ref[:, part + at * chunk : part + (at + 1) * chunk]
        piece, row = divmod(at * chunk, width)
        start = part + half + piece * width
        w2 = g2_ref[row : row + chunk, start : start + width]
        hidden = dot(normed, w1) + f1b_ref[0:1, cols]
        below = 0.5 + 0.5 * lax.erf(hidden * (0.5**0.5))
        slope = below + hidden * (jnp.exp(hidden * hidden * -0.5) * 0.3989422804014327)
        active = (hidden * below).astype(BF)
        grad_hidden = (dot(cot, w2, 1, 1) * slope).astype(BF)
        more = dot(active, w2)
        out = more if out is None else out + more
        more = dot(grad_hidden, w1, 1, 1)
        grad = more if grad is None else grad + more
        acc1[:, cols] += dot(normed_t, grad_hidden)
        acc2[cols, :] += dot(active, cot, 0, 0)
        accb[:, cols] += fold(grad_hidden.astype(F32))
    accc[...] += fold(cot.astype(F32))
    out_ref[...] = out.astype(BF)
    gn_ref[...] = grad.astype(BF)

    @pl.when(step == steps - 1)
    def _():
        dw_ref[:, :half] = acc1[...].astype(BF)
        for piece in range(half // width):
            dw_ref[:, half + piece * width : half + (piece + 1) * width] = acc2[
                piece * width : (piece + 1) * width, :
            ].astype(BF)
        gf1_ref[...] = accb[...]
        gf2_ref[...] = accc[...]


def feed_forward(core, tokens, mixed_own, mixed_sib, cot, wp_other, weights, vec, f1b):
    rows, width = tokens.shape
    half = f1b.shape[1]
    heads = mixed_own.shape[1]
    bt, chunk = 256, 384
    blocks = rows // bt
    kernel = functools.partial(feed_forward_kernel, chunk)
    return pl.pallas_call(
        kernel,
        grid=(blocks,),
        in_specs=[
            pl.BlockSpec(memory_space=pltpu.SMEM),
            pl.BlockSpec((bt, width), lambda i: (i, 0)),
            pl.BlockSpec((bt, heads), lambda i: (i, 0)),
            pl.BlockSpec((bt, heads), lambda i: (lax.rem(i + blocks // 2, blocks), 0)),
            pl.BlockSpec((bt, width), lambda i: (i, 0)),
            whole(wp_other.shape),
            whole(weights.shape),
            whole(vec.shape),
            whole(f1b.shape),
        ],
        out_specs=[
            pl.BlockSpec((bt, width), lambda i: (i, 0)),
            pl.BlockSpec((bt, width), lambda i: (i, 0)),
            pl.BlockSpec((bt, width), lambda i: (i, 0)),
            whole((width, 2 * half)),
            whole((8, half)),
            whole((8, width)),
            whole((width // 2, width)),
        ],
        out_shape=[
            jax.ShapeDtypeStruct((rows, width), F32),
            jax.ShapeDtypeStruct((rows, width), BF),
            jax.ShapeDtypeStruct((rows, width), BF),
            jax.ShapeDtypeStruct((width, 2 * half), BF),
            jax.ShapeDtypeStruct((8, half), F32),
            jax.ShapeDtypeStruct((8, width), F32),
            jax.ShapeDtypeStruct((width // 2, width), BF),
        ],
        scratch_shapes=[
            pltpu.VMEM((width, half), F32),
            pltpu.VMEM((half, width), F32),
            pltpu.VMEM((8, half), F32),
            pltpu.VMEM((8, width), F32),
            pltpu.VMEM((width // 2, width), BF),
        ],
        compiler_params=params("arbitrary"),
        cost_estimate=cost(
            2 * rows * width * (6 * half + width), 20 * rows * width + 8 * width * half,
            2 * rows * half,
        ),
        name="feed_forward",
    )(core, tokens, mixed_own, mixed_sib, cot, wp_other, weights, vec, f1b)


def branch_kernel(
    core_ref, mid_ref, ga_ref, gb_ref, cot_ref, mo_ref, ms_ref, wpo_ref, vec_ref,
    gm_ref, do_ref, dot_ref, dwo_ref, dws_ref, vecs_ref, acco, accs, accv, low_ref
):
    step = pl.program_id(0)
    steps = pl.num_programs(0)
    half = do_ref.shape[1]

    @pl.when(step == 0)
    def _():
        acco[...] = jnp.zeros_like(acco)
        accs[...] = jnp.zeros_like(accs)
        accv[...] = jnp.zeros_like(accv)

    unit, inverse = normalised(mid_ref[...])
    grad = ga_ref[...].astype(F32) + gb_ref[...].astype(F32)
    accv[0:8, :] += fold(grad * unit)
    accv[8:16, :] += fold(grad)
    grad_middle = cot_ref[...].astype(F32) + norm_pull(grad, vec_ref[1:2, :], unit, inverse)

    @pl.when(step < steps // 2)
    def _():
        gm_ref[...] = grad_middle

    low = grad_middle.astype(BF)
    low_ref[...] = low
    accv[16:24, :] += fold(low.astype(F32))
    do_ref[...] = dot(low, wpo_ref[...], 1, 1).astype(BF)
    dot_ref[...] = dot(wpo_ref[...], low, 1, 1).astype(BF)
    mine = low_ref[:, pl.ds(pl.multiple_of(core_ref[0] * half, half), half)]
    acco[...] += dot(mo_ref[...], mine, 0, 0)
    accs[...] += dot(ms_ref[...], mine, 0, 0)

    @pl.when(step == steps - 1)
    def _():
        dwo_ref[...] = acco[...].astype(BF)
        dws_ref[...] = accs[...].astype(BF)
        vecs_ref[...] = accv[...]


def branch(core, middle, grad_own, grad_sib, cot, mixed_own, mixed_sib, wp_own, vec):
    rows, width = middle.shape
    half = mixed_own.shape[1]
    bt = 256
    blocks = rows // bt
    swap = lambda i: (lax.rem(i + blocks // 2, blocks), 0)
    straight = lambda i: (i, 0)
    return pl.pallas_call(
        branch_kernel,
        grid=(blocks,),
        in_specs=[
            pl.BlockSpec(memory_space=pltpu.SMEM),
            pl.BlockSpec((bt, width), straight),
            pl.BlockSpec((bt, width), straight),
            pl.BlockSpec((bt, width), swap),
            pl.BlockSpec((bt, width), straight),
            pl.BlockSpec((bt, half), straight),
            pl.BlockSpec((bt, half), swap),
            whole(wp_own.shape),
            whole(vec.shape),
        ],
        out_specs=[
            pl.BlockSpec((bt, width), lambda i: (jnp.minimum(i, blocks // 2 - 1), 0)),
            pl.BlockSpec((bt, half), straight),
            pl.BlockSpec((half, bt), lambda i: (0, i)),
            whole((half, half)),
            whole((half, half)),
            whole((24, width)),
        ],
        out_shape=[
            jax.ShapeDtypeStruct((rows // 2, width), F32),
            jax.ShapeDtypeStruct((rows, half), BF),
            jax.ShapeDtypeStruct((half, rows), BF),
            jax.ShapeDtypeStruct((half, half), BF),
            jax.ShapeDtypeStruct((half, half), BF),
            jax.ShapeDtypeStruct((24, width), F32),
        ],
        scratch_shapes=[
            pltpu.VMEM((half, half), F32),
            pltpu.VMEM((half, half), F32),
            pltpu.VMEM((24, width), F32),
            pltpu.VMEM((bt, width), BF),
        ],
        compiler_params=params("arbitrary"),
        cost_estimate=cost(2 * rows * width * 3 * half, 18 * rows * width),
        name="branch",
    )(core, middle, grad_own, grad_sib, cot, mixed_own, mixed_sib, wp_own, vec)


def weight_grad_kernel(tok_ref, gq_ref, gk_ref, gv_ref, vec_ref, dw_ref, qv_ref, accw, accqv):
    step = pl.program_id(0)
    steps = pl.num_programs(0)
    part = gq_ref.shape[1]

    @pl.when(step == 0)
    def _():
        accw[...] = jnp.zeros_like(accw)
        accqv[...] = jnp.zeros_like(accqv)

    unit, _ = normalised(tok_ref[...].astype(F32))
    normed_t = (unit * vec_ref[0:1, :] + vec_ref[1:2, :]).astype(BF).T
    for at, ref in enumerate((gq_ref, gk_ref, gv_ref)):
        cols = slice(at * part, (at + 1) * part)
        value = ref[...]
        accw[:, cols] += dot(normed_t, value)
        if at != 1:
            here = 0 if at == 0 else 8
            accqv[here : here + 8, :] += fold(value.astype(F32))

    @pl.when(step == steps - 1)
    def _():
        dw_ref[...] = accw[...].astype(BF)
        qv_ref[...] = accqv[...]


def weight_grad(tokens, gq, gk, gv, vec):
    rows, width = tokens.shape
    part = gq.shape[1]
    bt = 256
    straight = lambda i: (i, 0)
    return pl.pallas_call(
        weight_grad_kernel,
        grid=(rows // bt,),
        in_specs=[
            pl.BlockSpec((bt, width), straight),
            pl.BlockSpec((bt, part), straight),
            pl.BlockSpec((bt, part), straight),
            pl.BlockSpec((bt, part), straight),
            whole(vec.shape),
        ],
        out_specs=[whole((width, 3 * part)), whole((16, part))],
        out_shape=[
            jax.ShapeDtypeStruct((width, 3 * part), BF),
            jax.ShapeDtypeStruct((16, part), F32),
        ],
        scratch_shapes=[pltpu.VMEM((width, 3 * part), F32), pltpu.VMEM((16, part), F32)],
        compiler_params=params("arbitrary"),
        cost_estimate=cost(2 * rows * width * 3 * part, 2 * rows * (width + 3 * part)),
        name="weight_grad",
    )(tokens, gq, gk, gv, vec)


def project_back_kernel(
    tok_ref, gqa_ref, gka_ref, gva_ref, gq_ref, gk_ref, gv_ref, w_ref, vec_ref,
    own_ref, sib_ref, dw_ref, vecs_ref, qv_ref, accw, accv, accqv
):
    step = pl.program_id(0)
    steps = pl.num_programs(0)
    early = gqa_ref.shape[1]
    part = gq_ref.shape[1]
    wide = early + part

    @pl.when(step == 0)
    def _():
        accw[...] = jnp.zeros_like(accw)
        accv[...] = jnp.zeros_like(accv)
        accqv[...] = jnp.zeros_like(accqv)

    unit, _ = normalised(tok_ref[...].astype(F32))
    normed_t = (unit * vec_ref[0:1, :] + vec_ref[1:2, :]).astype(BF).T
    grad = None
    before = (gqa_ref, gka_ref, gva_ref)
    for at, ref in enumerate((gq_ref, gk_ref, gv_ref)):
        cols = slice(at * part, (at + 1) * part)
        value = ref[...]
        more = dot(
            jnp.concatenate([before[at][...], value], axis=1),
            w_ref[:, at * wide : (at + 1) * wide], 1, 1,
        )
        grad = more if grad is None else grad + more
        accw[:, cols] += dot(normed_t, value)
        if at != 1:
            here = 0 if at == 0 else 8
            accqv[here : here + 8, :] += fold(value.astype(F32))
    accv[0:8, :] += fold(grad * unit)
    accv[8:16, :] += fold(grad)

    @pl.when(step < steps // 2)
    def _():
        own_ref[...] = grad

    @pl.when(step >= steps // 2)
    def _():
        sib_ref[...] = grad.astype(BF)

    @pl.when(step == steps - 1)
    def _():
        dw_ref[...] = accw[...].astype(BF)
        vecs_ref[...] = accv[...]
        qv_ref[...] = accqv[...]


def project_back(tokens, before, grads, weight, vec):
    rows, width = tokens.shape
    early, part = before[0].shape[1], grads[0].shape[1]
    bt = 256
    blocks = rows // bt
    straight = lambda i: (i, 0)
    return pl.pallas_call(
        project_back_kernel,
        grid=(blocks,),
        in_specs=[pl.BlockSpec((bt, width), straight)]
        + [pl.BlockSpec((bt, early), straight)] * 3
        + [pl.BlockSpec((bt, part), straight)] * 3
        + [whole(weight.shape), whole(vec.shape)],
        out_specs=[
            pl.BlockSpec((bt, width), lambda i: (jnp.minimum(i, blocks // 2 - 1), 0)),
            pl.BlockSpec((bt, width), lambda i: (jnp.maximum(i - blocks // 2, 0), 0)),
            whole((width, 3 * part)),
            whole((16, width)),
            whole((16, part)),
        ],
        out_shape=[
            jax.ShapeDtypeStruct((rows // 2, width), F32),
            jax.ShapeDtypeStruct((rows // 2, width), BF),
            jax.ShapeDtypeStruct((width, 3 * part), BF),
            jax.ShapeDtypeStruct((16, width), F32),
            jax.ShapeDtypeStruct((16, part), F32),
        ],
        scratch_shapes=[
            pltpu.VMEM((width, 3 * part), F32),
            pltpu.VMEM((16, width), F32),
            pltpu.VMEM((16, part), F32),
        ],
        compiler_params=params("arbitrary"),
        cost_estimate=cost(2 * rows * width * (6 * part + 3 * early), 14 * rows * width),
        name="project_back",
    )(tokens, *before, *grads, weight, vec)


def pack_kernel(place_ref, *refs):
    vectors, (qkv_ref, proj_ref, fc1_ref, fc2_ref, one_ref, two_ref) = refs[:-6], refs[-6:]
    first_core = lax.rem(place_ref[0], 2) == 0
    first_chip = place_ref[0] // 2 == 0
    shard, width = proj_ref.shape
    part = width // 2
    ff = fc1_ref.shape[1]
    owners = width // shard
    quarter = ff // owners // 4
    half = ff // 2
    one_ref[:VEC_ROWS, :] = jnp.zeros((VEC_ROWS, 3 * part), BF)
    for at, ref in enumerate(vectors):
        one_ref[at : at + 1, : ref.shape[1]] = ref[...]
    for at in range(3):
        low = qkv_ref[:, at * width : at * width + part]
        high = qkv_ref[:, at * width + part : (at + 1) * width]
        mine = jnp.where(first_core, low, high)
        mine = jnp.where(first_chip, mine[: shard // 2], mine[shard // 2 :])
        one_ref[VEC_ROWS:, at * part : (at + 1) * part] = mine
    two_ref[:, :part] = jnp.where(first_core, proj_ref[:, :part], proj_ref[:, part:])
    pieces_low, pieces_high = [], []
    for piece in range(2):
        for owner in range(owners):
            base = owner * 4 * quarter + piece * quarter
            pieces_low.append(fc1_ref[:, base : base + quarter])
            pieces_high.append(fc1_ref[:, base + 2 * quarter : base + 3 * quarter])
    two_ref[:, part : part + half] = jnp.where(
        first_core, jnp.concatenate(pieces_low, axis=1), jnp.concatenate(pieces_high, axis=1)
    )
    for piece in range(2):
        low = fc2_ref[piece * quarter : (piece + 1) * quarter, :]
        high = fc2_ref[(2 + piece) * quarter : (3 + piece) * quarter, :]
        start = part + half + piece * width
        two_ref[:, start : start + width] = jnp.where(first_core, low, high)


def pack_weights(place, vectors, qkv, proj, fc1, fc2):
    shard, width = proj.shape
    half = fc1.shape[1] // 2
    part = width // 2
    vectors = [vector.reshape(1, -1) for vector in vectors]
    values = (*vectors, qkv, proj, fc1, fc2)
    rows = VEC_ROWS + shard // 2
    return pl.pallas_call(
        pack_kernel,
        grid=(1,),
        in_specs=[pl.BlockSpec(memory_space=pltpu.SMEM)] + [whole(value.shape) for value in values],
        out_specs=[whole((rows, 3 * part)), whole((shard, 5 * part + half))],
        out_shape=[
            jax.ShapeDtypeStruct((rows, 3 * part), BF),
            jax.ShapeDtypeStruct((shard, 5 * part + half), BF),
        ],
        compiler_params=params("arbitrary"),
        cost_estimate=cost(0, 5 * shard * width * 8),
        name="pack_weights",
    )(place, *values)


def project_kernel(tok_ref, w_ref, bias_ref, vec_ref, out_ref, out_t_ref):
    unit, _ = normalised(tok_ref[...].astype(F32))
    normed = (unit * vec_ref[0:1, :] + vec_ref[1:2, :]).astype(BF)
    packed = dot(normed, w_ref[...]) + bias_ref[0:1, :]
    out_ref[...] = packed.astype(BF)
    out_t_ref[...] = packed.T.astype(BF)


def project(tokens, weight, bias, vec):
    rows, width = tokens.shape
    wide = weight.shape[1]
    bt = 256
    return pl.pallas_call(
        project_kernel,
        grid=(rows // bt,),
        in_specs=[
            pl.BlockSpec((bt, width), lambda i: (i, 0)),
            whole(weight.shape),
            whole(bias.shape),
            whole(vec.shape),
        ],
        out_specs=[
            pl.BlockSpec((bt, wide), lambda i: (i, 0)),
            pl.BlockSpec((wide, bt), lambda i: (0, i)),
        ],
        out_shape=[
            jax.ShapeDtypeStruct((rows, wide), BF),
            jax.ShapeDtypeStruct((wide, rows), BF),
        ],
        compiler_params=params("arbitrary"),
        cost_estimate=cost(2 * rows * width * wide, 12 * rows * width),
        name="project",
    )(tokens, weight, bias, vec)


def exchange(value):
    return lax.all_to_all(value, "fsdp", split_axis=0, concat_axis=0, tiled=True)


def per_device(
    tokens,
    counts,
    norm1_gain,
    norm1_bias,
    qkv_weight,
    query_bias,
    value_bias,
    proj_weight,
    proj_bias,
    norm2_gain,
    norm2_bias,
    fc1_weight,
    fc1_bias,
    fc2_weight,
    fc2_bias,
    cotangent,
):
    images, slots, width = tokens.shape
    owners = lax.axis_size("fsdp")
    seq = lax.axis_size("seq")
    place = lax.axis_index("seq")
    core = lax.rem(place, 2)
    image = place // 2
    part = width // 2
    shard = width // owners
    ff = fc1_weight.shape[1]
    ff_shard = ff // owners
    quarter = ff_shard // 4
    half = ff // 2
    to_sibling = [(at, at ^ 1) for at in range(seq)]
    to_partner = [(at, at ^ 2) for at in range(seq)]

    def sibling(value):
        return lax.ppermute(value, "seq", to_sibling)

    def partner(value):
        return lax.ppermute(value, "seq", to_partner)

    def pick(value, at, axis):
        return lax.dynamic_index_in_dim(value, at, axis, keepdims=False)

    place_row = place.reshape(1).astype(jnp.int32)
    core_row = core.reshape(1).astype(jnp.int32)
    small = [
        norm1_gain, norm1_bias, query_bias, value_bias, proj_bias, norm2_gain, norm2_bias,
        fc2_bias, fc1_bias,
    ]
    one, two = pack_weights(
        place_row, small, qkv_weight, proj_weight, fc1_weight, fc2_weight
    )
    mine_one = lax.all_gather(one, "fsdp", axis=0, tiled=False)
    mine_one, two = lax.optimization_barrier((mine_one, two))
    second = lax.all_gather(two, "fsdp", axis=0, tiled=True)
    own_rows = mine_one[:, VEC_ROWS:]
    other_rows = partner(own_rows)
    w_qkv = jnp.where(
        image == 0,
        jnp.stack([own_rows, other_rows], axis=1),
        jnp.stack([other_rows, own_rows], axis=1),
    ).reshape(width, 3 * part)

    def collect(value, theirs):
        mine = pick(value, image, 0)
        return jnp.concatenate([mine, theirs, sibling(mine), sibling(theirs)], axis=0)

    tok = collect(tokens, partner(pick(tokens, 1 - image, 0)))
    vecs = mine_one[:, :8, :shard].astype(F32).transpose(1, 0, 2).reshape(8, width)
    g1, b1, qb, vb, pb, g2, b2, f2b = vecs
    f1b = mine_one[:, 8, :ff_shard].astype(F32)
    f1b = pick(f1b.reshape(owners, 2, 2, quarter), core, 1)
    f1b = f1b.transpose(1, 0, 2).reshape(1, half)

    def mine_of(vector):
        return lax.dynamic_slice_in_dim(vector, core * part, part, 0)

    qkv_bias = jnp.concatenate([mine_of(qb), jnp.zeros((part,), F32), mine_of(vb)])
    vec_one = jnp.concatenate([jnp.stack([g1, b1]), jnp.zeros((6, width), F32)])
    packed, packed_t = project(tok, w_qkv, qkv_bias.reshape(1, 3 * part), vec_one)
    cot = collect(cotangent, partner(pick(cotangent, 1 - image, 0)))
    packed, cot = lax.optimization_barrier((packed, cot))
    mixed, result_t, log_total = attend_forward(counts, place_row, packed, packed_t, slots)
    mixed_sib = sibling(mixed)

    wp_other = sibling(second[:, :part])
    vec_two = jnp.concatenate([jnp.stack([pb, g2, b2]), jnp.zeros((5, width), F32)])
    middle, out_part, gn_part, dw_ff, gf1, gf2, wp_own = feed_forward(
        core_row, tok, mixed, mixed_sib, cot, wp_other, second, vec_two, f1b
    )
    scattered_one = lax.psum_scatter(dw_ff, "fsdp", scatter_dimension=0, tiled=True)
    gn_sib = sibling(gn_part)
    rows_own = 2 * slots

    def hand_back(own, came):
        kept_part = own[:slots]
        came = came.astype(own.dtype)
        straight = jnp.stack([kept_part, came])
        crossed = jnp.stack([came, kept_part])
        return jnp.where(image == 0, straight, crossed)

    grad_middle, grad_mixed, grad_mixed_t, dwp_own, dwp_sib, vec_back = branch(
        core_row, middle, gn_part, gn_sib, cot, mixed, mixed_sib, wp_own, vec_two
    )
    dwp = jnp.where(
        core == 0,
        jnp.concatenate([dwp_own, dwp_sib], axis=0),
        jnp.concatenate([dwp_sib, dwp_own], axis=0),
    )
    grad_mixed, out_part = lax.optimization_barrier((grad_mixed, out_part))
    out_sib = sibling(out_part[rows_own:])
    early, late = 2, 1
    attend = functools.partial(attend_backward, counts, place_row, packed, packed_t)
    before = attend(grad_mixed, grad_mixed_t, result_t, log_total, slots, 0, early)
    dw_early, qv_early = weight_grad(tok, *before, vec_one)
    block_one = jnp.concatenate([dw_early, dwp], axis=1).reshape(owners, shard, -1)
    came_one = exchange(block_one)
    out_own = (
        middle[:rows_own] + out_part[:rows_own].astype(F32) + out_sib.astype(F32) + f2b
    ).astype(BF)
    grad_mixed, out_own, block_one = lax.optimization_barrier((grad_mixed, out_own, block_one))
    out_came = partner(out_own[slots:])
    grads = attend(grad_mixed, grad_mixed_t, result_t, log_total, slots, early, late)
    vec_one, out_came, scattered_one = lax.optimization_barrier((vec_one, out_came, scattered_one))
    one_came = partner(scattered_one)
    output = hand_back(out_own, out_came)
    gn1_own, gn1_send, dw_late, vec_first, qv_late = project_back(
        tok, before, grads, w_qkv, vec_one
    )

    def spread(vector):
        both = jnp.zeros((2, part), F32)
        return lax.dynamic_update_index_in_dim(both, vector, core, 0).reshape(width)

    def rows_of(block):
        return jnp.sum(block.reshape(block.shape[0] // 8, 8, block.shape[1]), axis=1)

    once = (core == 0).astype(F32)
    gg1, gb1 = rows_of(vec_first)
    gqb, gvb = rows_of(jnp.concatenate([qv_early, qv_late], axis=1))
    gg2, gb2, gpb = rows_of(vec_back) * once
    gf2b = jnp.sum(gf2, axis=0) * once
    gf1b = jnp.sum(gf1, axis=0).reshape(2, owners, quarter).transpose(1, 0, 2)
    gf1b = lax.dynamic_update_index_in_dim(
        jnp.zeros((owners, 2, 2, quarter), F32), gf1b, core, 1
    ).reshape(owners, ff_shard)
    late_wide = 3 * late * PAIR
    small_grads = jnp.stack(
        [gg1, gb1, spread(gqb), spread(gvb), gpb, gg2, gb2, gf2b]
    ).reshape(8, owners, shard).transpose(1, 0, 2)
    small_block = jnp.concatenate(
        [
            jnp.pad(small_grads, ((0, 0), (0, 0), (0, late_wide - shard))),
            jnp.pad(gf1b[:, None], ((0, 0), (0, VEC_ROWS - 9), (0, late_wide - ff_shard))),
        ],
        axis=1,
    ).astype(BF)
    block_two = jnp.concatenate(
        [small_block, dw_late.reshape(owners, shard, late_wide)], axis=1
    )
    gn1 = gn1_own + sibling(gn1_send).astype(F32)
    unit_own, inverse_own = normalised(tok[:rows_own].astype(F32))
    input_own = grad_middle + norm_pull(gn1, g1, unit_own, inverse_own)
    block_two, came_one, one_came = lax.optimization_barrier((block_two, came_one, one_came))
    came_two = exchange(block_two)
    came_two, input_own = lax.optimization_barrier((came_two, input_own))

    def total(came):
        return jnp.sum(came.astype(F32), axis=0).astype(BF)

    input_grad = hand_back(input_own, partner(input_own[slots:].astype(BF)))

    def finish(value, came=None):
        came = partner(value) if came is None else came
        summed = value.astype(F32) + came.astype(F32)
        other = sibling(summed.astype(BF)).astype(F32)
        return summed, other

    def in_order(mine, other):
        return jnp.where(core == 0, mine, other), jnp.where(core == 0, other, mine)

    one_mine, one_other = finish(scattered_one, one_came)
    lower, upper = in_order(one_mine, one_other)

    def fc1_of(value):
        return value[:, :half].reshape(shard, 2, owners, quarter).transpose(0, 2, 1, 3)

    grad_fc1 = jnp.stack([fc1_of(lower), fc1_of(upper)], axis=2).reshape(shard, ff)

    def fc2_of(value):
        return value[:, half:].reshape(quarter, 2, width).transpose(1, 0, 2)

    grad_fc2 = jnp.stack([fc2_of(lower), fc2_of(upper)]).reshape(ff_shard, width)
    early_mine, early_other = finish(total(came_one))
    early_sum = in_order(early_mine, early_other)
    late_mine, late_other = finish(total(came_two))
    late_sum = in_order(late_mine[VEC_ROWS:], late_other[VEC_ROWS:])
    cut, tail = early * PAIR, late * PAIR
    grad_qkv = jnp.concatenate(
        [
            piece
            for at in range(3)
            for of in range(2)
            for piece in (
                early_sum[of][:, at * cut : (at + 1) * cut],
                late_sum[of][:, at * tail : (at + 1) * tail],
            )
        ],
        axis=1,
    )
    grad_proj = jnp.concatenate([early_sum[0][:, 3 * cut :], early_sum[1][:, 3 * cut :]], axis=1)
    small_sum = late_mine[:VEC_ROWS] + late_other[:VEC_ROWS]
    s = [small_sum[at, :shard] for at in range(8)]
    grad_f1b = small_sum[8, :ff_shard]
    return (
        output,
        input_grad,
        s[0],
        s[1],
        grad_qkv,
        s[2],
        s[3],
        grad_proj,
        s[4],
        s[5],
        s[6],
        grad_fc1,
        grad_f1b,
        grad_fc2,
        s[7],
    )


def solution(mesh):
    placed = (
        P("fsdp", "seq", None),
        P("fsdp", None),
        P("fsdp"),
        P("fsdp"),
        P("fsdp", None),
        P("fsdp"),
        P("fsdp"),
        P("fsdp", None),
        P("fsdp"),
        P("fsdp"),
        P("fsdp"),
        P("fsdp", None),
        P("fsdp"),
        P("fsdp", None),
        P("fsdp"),
        P("fsdp", "seq", None),
    )
    return jax.shard_map(
        per_device,
        mesh=mesh,
        in_specs=placed,
        out_specs=(
            P("fsdp", "seq", None),
            P("fsdp", "seq", None),
            P("fsdp"),
            P("fsdp"),
            P("fsdp", None),
            P("fsdp"),
            P("fsdp"),
            P("fsdp", None),
            P("fsdp"),
            P("fsdp"),
            P("fsdp"),
            P("fsdp", None),
            P("fsdp"),
            P("fsdp", None),
            P("fsdp"),
        ),
        check_vma=False,
    )
```

```python
import functools

import jax
import jax.numpy as jnp
from jax import lax
from jax.experimental import pallas as pl
from jax.experimental.pallas import tpu as pltpu
from jax.sharding import PartitionSpec as P

HEADS = 12
HEAD_DIM = 64
EPSILON = 1e-06
MASKED = -1e30
BF = jnp.bfloat16
F32 = jnp.float32
VMEM_BYTES = 60 * 1024 * 1024
PAIR = 2 * HEAD_DIM
VEC_ROWS = 16
SLOT_ORDER = (0, 2, 1, 3)


def params(*semantics):
    return pltpu.CompilerParams(
        dimension_semantics=semantics, vmem_limit_bytes=VMEM_BYTES
    )


def dot(left, right, left_dim=1, right_dim=0):
    return lax.dot_general(
        left, right, (((left_dim,), (right_dim,)), ((), ())), preferred_element_type=F32
    )


def cost(flops, bytes_accessed, transcendentals=0):
    return pl.CostEstimate(
        flops=int(flops), bytes_accessed=int(bytes_accessed), transcendentals=int(transcendentals)
    )


def whole(shape):
    return pl.BlockSpec(shape, lambda *_: tuple(0 for _ in shape))


def key_bias(counts_ref, place_ref, keys, slots):
    row = lax.broadcasted_iota(jnp.int32, (slots, PAIR), 0)
    place = place_ref[0]
    parts = []
    for flip in SLOT_ORDER:
        kept = counts_ref[place // 2, jnp.bitwise_xor(place, flip)]
        parts.append(jnp.where(row < kept, 0.0, MASKED).astype(F32))
    return jnp.concatenate(parts, axis=0)


def augment_keys(pair, bias, which, ones):
    lane = lax.broadcasted_iota(jnp.int32, pair.shape, 1)
    mine = (lane < HEAD_DIM) if which == 0 else (lane >= HEAD_DIM)
    start = HEAD_DIM if which == 0 else 0
    extra = jnp.where(
        lane == start, bias, jnp.where((lane > start) & (lane <= start + ones), 1.0, 0.0)
    )
    return jnp.where(mine, pair.astype(F32), extra).astype(BF)


def augment_values(pair, which, ones):
    lane = lax.broadcasted_iota(jnp.int32, pair.shape, 1)
    mine = (lane < HEAD_DIM) if which == 0 else (lane >= HEAD_DIM)
    start = HEAD_DIM if which == 0 else 0
    extra = jnp.where((lane >= start) & (lane < start + ones), 1.0, 0.0)
    return jnp.where(mine, pair.astype(F32), extra).astype(BF)


def pieces(value):
    first = value.astype(BF).astype(F32)
    rest = value - first
    second = rest.astype(BF).astype(F32)
    return first, second, rest - second


def extra_rows(rows, width):
    place = lax.broadcasted_iota(jnp.int32, (HEAD_DIM, width), 0)
    out = jnp.zeros((HEAD_DIM, width), F32)
    for at, row in enumerate(rows):
        out = jnp.where(place == at, row, out)
    return out.astype(BF)


def place_rows(head, extra, which):
    return jnp.concatenate([head, extra] if which == 0 else [extra, head], axis=0)


def attend_forward_kernel(
    slots, bq, chunk, counts_ref, place_ref, k_ref, qt_ref, vt_ref, mixed_ref, ot_ref, lse_ref,
    kaug, vaug, s_a, s_b, m_a, m_b
):
    keys = k_ref.shape[0]
    step = pl.program_id(1)
    steps = pl.num_programs(1)
    scores = (s_a, s_b)
    peaks = (m_a, m_b)
    ones_row = extra_rows([jnp.ones((1, bq), F32)], bq)

    @pl.when(step == 0)
    def _():
        bias = key_bias(counts_ref, place_ref, keys, slots)
        ones = jnp.ones((16, keys), BF)
        for which in range(2):
            kaug[which] = augment_keys(k_ref[...], bias, which, 0)
            vaug[which] = jnp.concatenate(
                [vt_ref[which * HEAD_DIM : (which + 1) * HEAD_DIM, :], ones], axis=0
            )

    def query_block(at, which):
        head = qt_ref[which * HEAD_DIM : (which + 1) * HEAD_DIM, pl.ds(at * bq, bq)]
        head = (head.astype(F32) * HEAD_DIM ** (-0.5)).astype(BF)
        return place_rows(head, ones_row, which)

    def score_chunk(query, which, at, peak):
        rows = slice(at * chunk, (at + 1) * chunk)
        s = dot(kaug[which, rows, :], query)
        scores[which][rows, :] = s
        top = jnp.max(s.reshape(chunk // 8, 8, bq), axis=0)
        return top if peak is None else jnp.maximum(peak, top)

    def weigh_chunk(which, at, peak, total):
        rows = slice(at * chunk, (at + 1) * chunk)
        p = jnp.exp(scores[which][rows, :] - peak).astype(BF)
        o = dot(vaug[which, :, rows], p)
        return o if total is None else total + o

    @pl.when(step == 0)
    def _():
        query = query_block(0, 0)
        peak = None
        for at in range(keys // chunk):
            peak = score_chunk(query, 0, at, peak)
        m_a[...] = peak

    later = jnp.minimum(step + 1, steps - 1)
    outs = []
    for which in range(2):
        other = 1 - which
        query = query_block(step if which == 0 else later, other)
        peak = jnp.max(peaks[which][...], axis=0, keepdims=True)
        next_peak, total = None, None
        for at in range(keys // chunk):
            next_peak = score_chunk(query, other, at, next_peak)
            total = weigh_chunk(which, at, peak, total)
        peaks[other][...] = next_peak
        norm = total[HEAD_DIM : HEAD_DIM + 1, :]
        outs.append(total[:HEAD_DIM, :] * (1.0 / norm))
        lse_ref[0, which : which + 1, :] = peak + jnp.log(norm)
    both = jnp.concatenate(outs, axis=0)
    ot_ref[...] = both
    mixed_ref[...] = both.T.astype(BF)


def attend_forward(counts, place, packed, packed_t, slots):
    keys, width = packed.shape
    width //= 3
    pairs = width // PAIR
    bq, chunk = 256, 256
    kernel = functools.partial(attend_forward_kernel, slots, bq, chunk)
    return pl.pallas_call(
        kernel,
        grid=(pairs, keys // bq),
        in_specs=[
            pl.BlockSpec(memory_space=pltpu.SMEM),
            pl.BlockSpec(memory_space=pltpu.SMEM),
            pl.BlockSpec((keys, PAIR), lambda p, i: (0, pairs + p)),
            pl.BlockSpec((PAIR, keys), lambda p, i: (p, 0)),
            pl.BlockSpec((PAIR, keys), lambda p, i: (2 * pairs + p, 0)),
        ],
        out_specs=[
            pl.BlockSpec((bq, PAIR), lambda p, i: (i, p)),
            pl.BlockSpec((PAIR, bq), lambda p, i: (p, i)),
            pl.BlockSpec((1, 8, bq), lambda p, i: (p, 0, i)),
        ],
        out_shape=[
            jax.ShapeDtypeStruct((keys, width), BF),
            jax.ShapeDtypeStruct((width, keys), F32),
            jax.ShapeDtypeStruct((pairs, 8, keys), F32),
        ],
        scratch_shapes=[
            pltpu.VMEM((2, keys, PAIR), BF),
            pltpu.VMEM((2, HEAD_DIM + 16, keys), BF),
            pltpu.VMEM((keys, bq), F32),
            pltpu.VMEM((keys, bq), F32),
            pltpu.VMEM((8, bq), F32),
            pltpu.VMEM((8, bq), F32),
        ],
        compiler_params=params("arbitrary", "arbitrary"),
        cost_estimate=cost(
            2 * pairs * 2 * 2 * keys * keys * 256, 12 * keys * width, 2 * pairs * keys * keys
        ),
        name="attend_forward",
    )(counts, place, packed, packed_t, packed_t)


def attend_backward_kernel(
    slots, bq, chunk, counts_ref, place_ref, q_ref, k_ref, v_ref, qt_ref, kt_ref, do_ref, dot_ref, ot_ref,
    lse_ref, gq_ref, gk_ref, gv_ref, kaug, vaug, acc_k, acc_v
):
    keys = k_ref.shape[0]
    step = pl.program_id(1)
    steps = pl.num_programs(1)
    scale = HEAD_DIM ** (-0.5)

    @pl.when(step == 0)
    def _():
        bias = key_bias(counts_ref, place_ref, keys, slots)
        for which in range(2):
            kaug[which] = augment_keys(k_ref[...], bias, which, 3)
            vaug[which] = augment_values(v_ref[...], which, 3)
        acc_k[...] = jnp.zeros_like(acc_k)
        acc_v[...] = jnp.zeros_like(acc_v)

    ones_row = jnp.ones((1, bq), F32)
    queries, grads = [], []
    for which in range(2):
        rows = slice(which * HEAD_DIM, (which + 1) * HEAD_DIM)
        head = (qt_ref[rows, :].astype(F32) * scale).astype(BF)
        log_total = lse_ref[0, which : which + 1, :]
        queries.append(
            place_rows(head, extra_rows([ones_row, *pieces(-log_total)], bq), which)
        )
        grad = dot_ref[rows, :]
        delta = jnp.sum(grad.astype(F32) * ot_ref[rows, :], axis=0, keepdims=True)
        grads.append(place_rows(grad, extra_rows(list(pieces(-delta)), bq), which))

    do_pair = do_ref[...]
    q_pair = q_ref[...]
    totals = [None, None]
    for at in range(keys // chunk):
        rows = slice(at * chunk, (at + 1) * chunk)
        for which in range(2):
            p = jnp.exp(dot(kaug[which, rows, :], queries[which]))
            dp = dot(vaug[which, rows, :], grads[which])
            p_low = p.astype(BF)
            ds = (p * dp).astype(BF)
            acc_v[which, rows, :] += dot(p_low, do_pair)
            acc_k[which, rows, :] += dot(ds, q_pair)
            part = dot(kt_ref[which * HEAD_DIM : (which + 1) * HEAD_DIM, rows], ds)
            totals[which] = part if totals[which] is None else totals[which] + part
    both = jnp.concatenate(totals, axis=0) * scale
    gq_ref[...] = both.T.astype(BF)

    @pl.when(step == steps - 1)
    def _():
        lane = lax.broadcasted_iota(jnp.int32, (keys, PAIR), 1)
        gk_ref[...] = (jnp.where(lane < HEAD_DIM, acc_k[0], acc_k[1]) * scale).astype(BF)
        gv_ref[...] = jnp.where(lane < HEAD_DIM, acc_v[0], acc_v[1]).astype(BF)


def attend_backward(
    counts, place, packed, packed_t, grad, grad_t, result_t, log_total, slots, start, count
):
    keys, width = packed.shape
    width //= 3
    pairs = width // PAIR
    bq, chunk = 512, 256
    kernel = functools.partial(attend_backward_kernel, slots, bq, chunk)
    at = lambda p: p + start
    return pl.pallas_call(
        kernel,
        grid=(count, keys // bq),
        in_specs=[
            pl.BlockSpec(memory_space=pltpu.SMEM),
            pl.BlockSpec(memory_space=pltpu.SMEM),
            pl.BlockSpec((bq, PAIR), lambda p, i: (i, at(p))),
            pl.BlockSpec((keys, PAIR), lambda p, i: (0, pairs + at(p))),
            pl.BlockSpec((keys, PAIR), lambda p, i: (0, 2 * pairs + at(p))),
            pl.BlockSpec((PAIR, bq), lambda p, i: (at(p), i)),
            pl.BlockSpec((PAIR, keys), lambda p, i: (pairs + at(p), 0)),
            pl.BlockSpec((bq, PAIR), lambda p, i: (i, at(p))),
            pl.BlockSpec((PAIR, bq), lambda p, i: (at(p), i)),
            pl.BlockSpec((PAIR, bq), lambda p, i: (at(p), i)),
            pl.BlockSpec((1, 8, bq), lambda p, i: (at(p), 0, i)),
        ],
        out_specs=[
            pl.BlockSpec((bq, PAIR), lambda p, i: (i, p)),
            pl.BlockSpec((keys, PAIR), lambda p, i: (0, p)),
            pl.BlockSpec((keys, PAIR), lambda p, i: (0, p)),
        ],
        out_shape=[jax.ShapeDtypeStruct((keys, count * PAIR), BF)] * 3,
        scratch_shapes=[
            pltpu.VMEM((2, keys, PAIR), BF),
            pltpu.VMEM((2, keys, PAIR), BF),
            pltpu.VMEM((2, keys, PAIR), F32),
            pltpu.VMEM((2, keys, PAIR), F32),
        ],
        compiler_params=params("arbitrary", "arbitrary"),
        cost_estimate=cost(
            2 * count * 5 * 2 * keys * keys * 256, 24 * keys * count * PAIR,
            2 * count * keys * keys,
        ),
        name="attend_backward",
    )(counts, place, packed, packed, packed, packed_t, packed_t, grad, grad_t, result_t, log_total)


def normalised(values):
    centred = values - jnp.mean(values, axis=-1, keepdims=True)
    variance = jnp.mean(centred * centred, axis=-1, keepdims=True)
    inverse = lax.rsqrt(variance + EPSILON)
    return centred * inverse, inverse


def norm_pull(grad, gain, unit, inverse):
    scaled = grad * gain
    mean = jnp.mean(scaled, axis=-1, keepdims=True)
    along = jnp.mean(scaled * unit, axis=-1, keepdims=True)
    return inverse * (scaled - mean - unit * along)


def fold(values):
    return jnp.sum(values.reshape(values.shape[0] // 8, 8, values.shape[1]), axis=0)


def feed_forward_kernel(
    chunk, core_ref, tok_ref, mo_ref, ms_ref, cot_ref, wpx_ref, g2_ref, vec_ref, f1b_ref,
    mid_ref, out_ref, send_ref, gn_ref, dw_ref, gf1_ref, gf2_ref, wpo_ref, acc1, acc2, accb, accc, wps_ref
):
    step = pl.program_id(0)
    steps = pl.num_programs(0)
    width = tok_ref.shape[1]
    half = f1b_ref.shape[1]
    part = width // 2

    @pl.when(step == 0)
    def _():
        acc1[...] = jnp.zeros_like(acc1)
        acc2[...] = jnp.zeros_like(acc2)
        accb[...] = jnp.zeros_like(accb)
        accc[...] = jnp.zeros_like(accc)
        here = pl.ds(pl.multiple_of(core_ref[0] * part, part), part)
        there = pl.ds(pl.multiple_of((1 - core_ref[0]) * part, part), part)
        wpo_ref[:, here] = g2_ref[here, :part]
        wpo_ref[:, there] = wpx_ref[here, :]
        wps_ref[:, here] = g2_ref[there, :part]
        wps_ref[:, there] = wpx_ref[there, :]

    middle = (
        tok_ref[...].astype(F32)
        + dot(mo_ref[...], wpo_ref[...])
        + dot(ms_ref[...], wps_ref[...])
        + vec_ref[0:1, :]
    )
    mid_ref[...] = middle
    unit, _ = normalised(middle)
    normed = (unit * vec_ref[1:2, :] + vec_ref[2:3, :]).astype(BF)
    normed_t = normed.T
    cot = cot_ref[...]
    out = None
    grad = None
    for at in range(half // chunk):
        cols = slice(at * chunk, (at + 1) * chunk)
        w1 = g2_ref[:, part + at * chunk : part + (at + 1) * chunk]
        piece, row = divmod(at * chunk, width)
        start = part + half + piece * width
        w2 = g2_ref[row : row + chunk, start : start + width]
        hidden = dot(normed, w1) + f1b_ref[0:1, cols]
        below = 0.5 + 0.5 * lax.erf(hidden * (0.5**0.5))
        slope = below + hidden * (jnp.exp(hidden * hidden * -0.5) * 0.3989422804014327)
        active = (hidden * below).astype(BF)
        grad_hidden = (dot(cot, w2, 1, 1) * slope).astype(BF)
        more = dot(active, w2)
        out = more if out is None else out + more
        more = dot(grad_hidden, w1, 1, 1)
        grad = more if grad is None else grad + more
        acc1[:, cols] += dot(normed_t, grad_hidden)
        acc2[cols, :] += dot(active, cot, 0, 0)
        accb[:, cols] += fold(grad_hidden.astype(F32))
    accc[...] += fold(cot.astype(F32))
    gn_ref[...] = grad.astype(BF)

    @pl.when(step < steps // 2)
    def _():
        out_ref[...] = middle + out + vec_ref[3:4, :]

    @pl.when(step >= steps // 2)
    def _():
        send_ref[...] = out.astype(BF)

    @pl.when(step == steps - 1)
    def _():
        dw_ref[:, :half] = acc1[...].astype(BF)
        for piece in range(half // width):
            dw_ref[:, half + piece * width : half + (piece + 1) * width] = acc2[
                piece * width : (piece + 1) * width, :
            ].astype(BF)
        gf1_ref[...] = accb[...]
        gf2_ref[...] = accc[...]


def feed_forward(core, tokens, mixed_own, mixed_sib, cot, wp_other, weights, vec, f1b):
    rows, width = tokens.shape
    half = f1b.shape[1]
    heads = mixed_own.shape[1]
    bt, chunk = 256, 384
    blocks = rows // bt
    kernel = functools.partial(feed_forward_kernel, chunk)
    return pl.pallas_call(
        kernel,
        grid=(blocks,),
        in_specs=[
            pl.BlockSpec(memory_space=pltpu.SMEM),
            pl.BlockSpec((bt, width), lambda i: (i, 0)),
            pl.BlockSpec((bt, heads), lambda i: (i, 0)),
            pl.BlockSpec((bt, heads), lambda i: (lax.rem(i + blocks // 2, blocks), 0)),
            pl.BlockSpec((bt, width), lambda i: (i, 0)),
            whole(wp_other.shape),
            whole(weights.shape),
            whole(vec.shape),
            whole(f1b.shape),
        ],
        out_specs=[
            pl.BlockSpec((bt, width), lambda i: (i, 0)),
            pl.BlockSpec((bt, width), lambda i: (jnp.minimum(i, blocks // 2 - 1), 0)),
            pl.BlockSpec((bt, width), lambda i: (jnp.maximum(i - blocks // 2, 0), 0)),
            pl.BlockSpec((bt, width), lambda i: (i, 0)),
            whole((width, 2 * half)),
            whole((8, half)),
            whole((8, width)),
            whole((width // 2, width)),
        ],
        out_shape=[
            jax.ShapeDtypeStruct((rows, width), F32),
            jax.ShapeDtypeStruct((rows // 2, width), F32),
            jax.ShapeDtypeStruct((rows // 2, width), BF),
            jax.ShapeDtypeStruct((rows, width), BF),
            jax.ShapeDtypeStruct((width, 2 * half), BF),
            jax.ShapeDtypeStruct((8, half), F32),
            jax.ShapeDtypeStruct((8, width), F32),
            jax.ShapeDtypeStruct((width // 2, width), BF),
        ],
        scratch_shapes=[
            pltpu.VMEM((width, half), F32),
            pltpu.VMEM((half, width), F32),
            pltpu.VMEM((8, half), F32),
            pltpu.VMEM((8, width), F32),
            pltpu.VMEM((width // 2, width), BF),
        ],
        compiler_params=params("arbitrary"),
        cost_estimate=cost(
            2 * rows * width * (6 * half + width), 20 * rows * width + 8 * width * half,
            2 * rows * half,
        ),
        name="feed_forward",
    )(core, tokens, mixed_own, mixed_sib, cot, wp_other, weights, vec, f1b)


def branch_kernel(
    core_ref, mid_ref, ga_ref, gb_ref, cot_ref, mo_ref, ms_ref, wpo_ref, vec_ref,
    gm_ref, do_ref, dot_ref, dwo_ref, dws_ref, vecs_ref, acco, accs, accv, low_ref
):
    step = pl.program_id(0)
    steps = pl.num_programs(0)
    half = do_ref.shape[1]

    @pl.when(step == 0)
    def _():
        acco[...] = jnp.zeros_like(acco)
        accs[...] = jnp.zeros_like(accs)
        accv[...] = jnp.zeros_like(accv)

    unit, inverse = normalised(mid_ref[...])
    grad = ga_ref[...].astype(F32) + gb_ref[...].astype(F32)
    accv[0:8, :] += fold(grad * unit)
    accv[8:16, :] += fold(grad)
    grad_middle = cot_ref[...].astype(F32) + norm_pull(grad, vec_ref[1:2, :], unit, inverse)

    @pl.when(step < steps // 2)
    def _():
        gm_ref[...] = grad_middle

    low = grad_middle.astype(BF)
    low_ref[...] = low
    accv[16:24, :] += fold(low.astype(F32))
    do_ref[...] = dot(low, wpo_ref[...], 1, 1).astype(BF)
    dot_ref[...] = dot(wpo_ref[...], low, 1, 1).astype(BF)
    mine = low_ref[:, pl.ds(pl.multiple_of(core_ref[0] * half, half), half)]
    acco[...] += dot(mo_ref[...], mine, 0, 0)
    accs[...] += dot(ms_ref[...], mine, 0, 0)

    @pl.when(step == steps - 1)
    def _():
        dwo_ref[...] = acco[...].astype(BF)
        dws_ref[...] = accs[...].astype(BF)
        vecs_ref[...] = accv[...]


def branch(core, middle, grad_own, grad_sib, cot, mixed_own, mixed_sib, wp_own, vec):
    rows, width = middle.shape
    half = mixed_own.shape[1]
    bt = 256
    blocks = rows // bt
    swap = lambda i: (lax.rem(i + blocks // 2, blocks), 0)
    straight = lambda i: (i, 0)
    return pl.pallas_call(
        branch_kernel,
        grid=(blocks,),
        in_specs=[
            pl.BlockSpec(memory_space=pltpu.SMEM),
            pl.BlockSpec((bt, width), straight),
            pl.BlockSpec((bt, width), straight),
            pl.BlockSpec((bt, width), swap),
            pl.BlockSpec((bt, width), straight),
            pl.BlockSpec((bt, half), straight),
            pl.BlockSpec((bt, half), swap),
            whole(wp_own.shape),
            whole(vec.shape),
        ],
        out_specs=[
            pl.BlockSpec((bt, width), lambda i: (jnp.minimum(i, blocks // 2 - 1), 0)),
            pl.BlockSpec((bt, half), straight),
            pl.BlockSpec((half, bt), lambda i: (0, i)),
            whole((half, half)),
            whole((half, half)),
            whole((24, width)),
        ],
        out_shape=[
            jax.ShapeDtypeStruct((rows // 2, width), F32),
            jax.ShapeDtypeStruct((rows, half), BF),
            jax.ShapeDtypeStruct((half, rows), BF),
            jax.ShapeDtypeStruct((half, half), BF),
            jax.ShapeDtypeStruct((half, half), BF),
            jax.ShapeDtypeStruct((24, width), F32),
        ],
        scratch_shapes=[
            pltpu.VMEM((half, half), F32),
            pltpu.VMEM((half, half), F32),
            pltpu.VMEM((24, width), F32),
            pltpu.VMEM((bt, width), BF),
        ],
        compiler_params=params("arbitrary"),
        cost_estimate=cost(2 * rows * width * 3 * half, 18 * rows * width),
        name="branch",
    )(core, middle, grad_own, grad_sib, cot, mixed_own, mixed_sib, wp_own, vec)


def weight_grad_kernel(normed_ref, gq_ref, gk_ref, gv_ref, dw_ref, qv_ref, accw, accqv):
    step = pl.program_id(0)
    steps = pl.num_programs(0)
    part = gq_ref.shape[1]

    @pl.when(step == 0)
    def _():
        accw[...] = jnp.zeros_like(accw)
        accqv[...] = jnp.zeros_like(accqv)

    normed_t = normed_ref[...].T
    for at, ref in enumerate((gq_ref, gk_ref, gv_ref)):
        cols = slice(at * part, (at + 1) * part)
        value = ref[...]
        accw[:, cols] += dot(normed_t, value)
        if at != 1:
            here = 0 if at == 0 else 8
            accqv[here : here + 8, :] += fold(value.astype(F32))

    @pl.when(step == steps - 1)
    def _():
        dw_ref[...] = accw[...].astype(BF)
        qv_ref[...] = accqv[...]


def weight_grad(normed, gq, gk, gv):
    rows, width = normed.shape
    part = gq.shape[1]
    bt = 256
    straight = lambda i: (i, 0)
    return pl.pallas_call(
        weight_grad_kernel,
        grid=(rows // bt,),
        in_specs=[
            pl.BlockSpec((bt, width), straight),
            pl.BlockSpec((bt, part), straight),
            pl.BlockSpec((bt, part), straight),
            pl.BlockSpec((bt, part), straight),
        ],
        out_specs=[whole((width, 3 * part)), whole((16, part))],
        out_shape=[
            jax.ShapeDtypeStruct((width, 3 * part), BF),
            jax.ShapeDtypeStruct((16, part), F32),
        ],
        scratch_shapes=[pltpu.VMEM((width, 3 * part), F32), pltpu.VMEM((16, part), F32)],
        compiler_params=params("arbitrary"),
        cost_estimate=cost(2 * rows * width * 3 * part, 2 * rows * (width + 3 * part)),
        name="weight_grad",
    )(normed, gq, gk, gv)


def project_back_kernel(
    tok_ref, normed_ref, gqa_ref, gka_ref, gva_ref, gq_ref, gk_ref, gv_ref, w_ref,
    own_ref, sib_ref, dw_ref, vecs_ref, qv_ref, accw, accv, accqv
):
    step = pl.program_id(0)
    steps = pl.num_programs(0)
    early = gqa_ref.shape[1]
    part = gq_ref.shape[1]
    wide = early + part

    @pl.when(step == 0)
    def _():
        accw[...] = jnp.zeros_like(accw)
        accv[...] = jnp.zeros_like(accv)
        accqv[...] = jnp.zeros_like(accqv)

    unit, _ = normalised(tok_ref[...].astype(F32))
    normed_t = normed_ref[...].T
    grad = None
    before = (gqa_ref, gka_ref, gva_ref)
    for at, ref in enumerate((gq_ref, gk_ref, gv_ref)):
        cols = slice(at * part, (at + 1) * part)
        value = ref[...]
        more = dot(
            jnp.concatenate([before[at][...], value], axis=1),
            w_ref[:, at * wide : (at + 1) * wide], 1, 1,
        )
        grad = more if grad is None else grad + more
        accw[:, cols] += dot(normed_t, value)
        if at != 1:
            here = 0 if at == 0 else 8
            accqv[here : here + 8, :] += fold(value.astype(F32))
    accv[0:8, :] += fold(grad * unit)
    accv[8:16, :] += fold(grad)

    @pl.when(step < steps // 2)
    def _():
        own_ref[...] = grad

    @pl.when(step >= steps // 2)
    def _():
        sib_ref[...] = grad.astype(BF)

    @pl.when(step == steps - 1)
    def _():
        dw_ref[...] = accw[...].astype(BF)
        vecs_ref[...] = accv[...]
        qv_ref[...] = accqv[...]


def project_back(tokens, normed, before, grads, weight):
    rows, width = tokens.shape
    early, part = before[0].shape[1], grads[0].shape[1]
    bt = 256
    blocks = rows // bt
    straight = lambda i: (i, 0)
    return pl.pallas_call(
        project_back_kernel,
        grid=(blocks,),
        in_specs=[pl.BlockSpec((bt, width), straight)] * 2
        + [pl.BlockSpec((bt, early), straight)] * 3
        + [pl.BlockSpec((bt, part), straight)] * 3
        + [whole(weight.shape)],
        out_specs=[
            pl.BlockSpec((bt, width), lambda i: (jnp.minimum(i, blocks // 2 - 1), 0)),
            pl.BlockSpec((bt, width), lambda i: (jnp.maximum(i - blocks // 2, 0), 0)),
            whole((width, 3 * part)),
            whole((16, width)),
            whole((16, part)),
        ],
        out_shape=[
            jax.ShapeDtypeStruct((rows // 2, width), F32),
            jax.ShapeDtypeStruct((rows // 2, width), BF),
            jax.ShapeDtypeStruct((width, 3 * part), BF),
            jax.ShapeDtypeStruct((16, width), F32),
            jax.ShapeDtypeStruct((16, part), F32),
        ],
        scratch_shapes=[
            pltpu.VMEM((width, 3 * part), F32),
            pltpu.VMEM((16, width), F32),
            pltpu.VMEM((16, part), F32),
        ],
        compiler_params=params("arbitrary"),
        cost_estimate=cost(2 * rows * width * (6 * part + 3 * early), 14 * rows * width),
        name="project_back",
    )(tokens, normed, *before, *grads, weight)


def input_back_kernel(tok_ref, own_ref, sib_ref, gm_ref, vec_ref, keep_ref, send_ref):
    unit, inverse = normalised(tok_ref[...].astype(F32))
    grad = own_ref[...] + sib_ref[...].astype(F32)
    total = gm_ref[...] + norm_pull(grad, vec_ref[0:1, :], unit, inverse)
    step = pl.program_id(0)
    steps = pl.num_programs(0)

    @pl.when(step < steps // 2)
    def _():
        keep_ref[...] = total

    @pl.when(step >= steps // 2)
    def _():
        send_ref[...] = total.astype(BF)


def input_back(tokens, grad_own, grad_sib, grad_middle, vec):
    rows, width = grad_own.shape
    bt = 256
    blocks = rows // bt
    straight = lambda i: (i, 0)
    return pl.pallas_call(
        input_back_kernel,
        grid=(blocks,),
        in_specs=[pl.BlockSpec((bt, width), straight)] * 4 + [whole(vec.shape)],
        out_specs=[
            pl.BlockSpec((bt, width), lambda i: (jnp.minimum(i, blocks // 2 - 1), 0)),
            pl.BlockSpec((bt, width), lambda i: (jnp.maximum(i - blocks // 2, 0), 0)),
        ],
        out_shape=[
            jax.ShapeDtypeStruct((rows // 2, width), F32),
            jax.ShapeDtypeStruct((rows // 2, width), BF),
        ],
        compiler_params=params("arbitrary"),
        cost_estimate=cost(20 * rows * width, 16 * rows * width),
        name="input_back",
    )(tokens, grad_own, grad_sib, grad_middle, vec)


def finish_ff_kernel(place_ref, mine_ref, other_ref, fc1_ref, fc2_ref):
    first_core = lax.rem(place_ref[0], 2) == 0
    shard, ff = fc1_ref.shape
    half = ff // 2
    quarter = fc2_ref.shape[0] // 4
    width = fc2_ref.shape[1]
    owners = ff // (4 * quarter)
    mine = mine_ref[...].astype(F32)
    other = other_ref[...].astype(F32)
    cores = (jnp.where(first_core, mine, other), jnp.where(first_core, other, mine))
    pieces = []
    for owner in range(owners):
        for value in cores:
            for piece in range(2):
                start = (piece * owners + owner) * quarter
                pieces.append(value[:, start : start + quarter])
    fc1_ref[...] = jnp.concatenate(pieces, axis=1)
    for at, value in enumerate(cores):
        for piece in range(2):
            row = (2 * at + piece) * quarter
            start = half + piece * width
            fc2_ref[row : row + quarter, :] = value[:, start : start + width]


def finish_ff(place, mine, other, width, quarter):
    shard, wide = mine.shape
    return pl.pallas_call(
        finish_ff_kernel,
        grid=(1,),
        in_specs=[
            pl.BlockSpec(memory_space=pltpu.SMEM), whole(mine.shape), whole(other.shape)
        ],
        out_specs=[whole((shard, wide)), whole((4 * quarter, width))],
        out_shape=[
            jax.ShapeDtypeStruct((shard, wide), F32),
            jax.ShapeDtypeStruct((4 * quarter, width), F32),
        ],
        compiler_params=params("arbitrary"),
        cost_estimate=cost(0, 12 * shard * wide),
        name="finish_ff",
    )(place, mine, other)


def finish_attend_kernel(place_ref, em_ref, eo_ref, lm_ref, lo_ref, qkv_ref, proj_ref, small_ref):
    first_core = lax.rem(place_ref[0], 2) == 0
    shard, width = proj_ref.shape
    part = width // 2
    late = lm_ref.shape[1] // 3
    early = part - late
    rows = lm_ref.shape[0] - shard
    lm = lm_ref[...].astype(F32)
    lo = lo_ref[...].astype(F32)
    small_ref[...] = lm[:rows] + lo[:rows]
    em = em_ref[...].astype(F32)
    eo = eo_ref[...].astype(F32)
    firsts = (jnp.where(first_core, em, eo), jnp.where(first_core, eo, em))
    lasts = (jnp.where(first_core, lm, lo)[rows:], jnp.where(first_core, lo, lm)[rows:])
    for at in range(3):
        for of in range(2):
            start = at * width + of * part
            qkv_ref[:, start : start + early] = firsts[of][:, at * early : (at + 1) * early]
            qkv_ref[:, start + early : start + part] = lasts[of][:, at * late : (at + 1) * late]
    for of in range(2):
        proj_ref[:, of * part : (of + 1) * part] = firsts[of][:, 3 * early :]


def finish_attend(place, early_mine, early_other, late_mine, late_other, width):
    shard = early_mine.shape[0]
    rows = late_mine.shape[0] - shard
    return pl.pallas_call(
        finish_attend_kernel,
        grid=(1,),
        in_specs=[pl.BlockSpec(memory_space=pltpu.SMEM)]
        + [whole(value.shape) for value in (early_mine, early_other, late_mine, late_other)],
        out_specs=[
            whole((shard, 3 * width)), whole((shard, width)), whole((rows, late_mine.shape[1]))
        ],
        out_shape=[
            jax.ShapeDtypeStruct((shard, 3 * width), F32),
            jax.ShapeDtypeStruct((shard, width), F32),
            jax.ShapeDtypeStruct((rows, late_mine.shape[1]), F32),
        ],
        compiler_params=params("arbitrary"),
        cost_estimate=cost(0, 24 * shard * width),
        name="finish_attend",
    )(place, early_mine, early_other, late_mine, late_other)


def pack_kernel(place_ref, *refs):
    vectors, (qkv_ref, proj_ref, fc1_ref, fc2_ref, one_ref, two_ref) = refs[:-6], refs[-6:]
    first_core = lax.rem(place_ref[0], 2) == 0
    first_chip = place_ref[0] // 2 == 0
    shard, width = proj_ref.shape
    part = width // 2
    ff = fc1_ref.shape[1]
    owners = width // shard
    quarter = ff // owners // 4
    half = ff // 2
    one_ref[:VEC_ROWS, :] = jnp.zeros((VEC_ROWS, 3 * part), BF)
    for at, ref in enumerate(vectors):
        one_ref[at : at + 1, : ref.shape[1]] = ref[...]
    for at in range(3):
        low = qkv_ref[:, at * width : at * width + part]
        high = qkv_ref[:, at * width + part : (at + 1) * width]
        mine = jnp.where(first_core, low, high)
        mine = jnp.where(first_chip, mine[: shard // 2], mine[shard // 2 :])
        one_ref[VEC_ROWS:, at * part : (at + 1) * part] = mine
    two_ref[:, :part] = jnp.where(first_core, proj_ref[:, :part], proj_ref[:, part:])
    pieces_low, pieces_high = [], []
    for piece in range(2):
        for owner in range(owners):
            base = owner * 4 * quarter + piece * quarter
            pieces_low.append(fc1_ref[:, base : base + quarter])
            pieces_high.append(fc1_ref[:, base + 2 * quarter : base + 3 * quarter])
    two_ref[:, part : part + half] = jnp.where(
        first_core, jnp.concatenate(pieces_low, axis=1), jnp.concatenate(pieces_high, axis=1)
    )
    for piece in range(2):
        low = fc2_ref[piece * quarter : (piece + 1) * quarter, :]
        high = fc2_ref[(2 + piece) * quarter : (3 + piece) * quarter, :]
        start = part + half + piece * width
        two_ref[:, start : start + width] = jnp.where(first_core, low, high)


def pack_weights(place, vectors, qkv, proj, fc1, fc2):
    shard, width = proj.shape
    half = fc1.shape[1] // 2
    part = width // 2
    vectors = [vector.reshape(1, -1) for vector in vectors]
    values = (*vectors, qkv, proj, fc1, fc2)
    rows = VEC_ROWS + shard // 2
    return pl.pallas_call(
        pack_kernel,
        grid=(1,),
        in_specs=[pl.BlockSpec(memory_space=pltpu.SMEM)] + [whole(value.shape) for value in values],
        out_specs=[whole((rows, 3 * part)), whole((shard, 5 * part + half))],
        out_shape=[
            jax.ShapeDtypeStruct((rows, 3 * part), BF),
            jax.ShapeDtypeStruct((shard, 5 * part + half), BF),
        ],
        compiler_params=params("arbitrary"),
        cost_estimate=cost(0, 5 * shard * width * 8),
        name="pack_weights",
    )(place, *values)


def project_kernel(tok_ref, w_ref, bias_ref, vec_ref, out_ref, out_t_ref, normed_ref):
    unit, _ = normalised(tok_ref[...].astype(F32))
    normed = (unit * vec_ref[0:1, :] + vec_ref[1:2, :]).astype(BF)
    normed_ref[...] = normed
    packed = dot(normed, w_ref[...]) + bias_ref[0:1, :]
    out_ref[...] = packed.astype(BF)
    out_t_ref[...] = packed.T.astype(BF)


def project(tokens, weight, bias, vec):
    rows, width = tokens.shape
    wide = weight.shape[1]
    bt = 256
    return pl.pallas_call(
        project_kernel,
        grid=(rows // bt,),
        in_specs=[
            pl.BlockSpec((bt, width), lambda i: (i, 0)),
            whole(weight.shape),
            whole(bias.shape),
            whole(vec.shape),
        ],
        out_specs=[
            pl.BlockSpec((bt, wide), lambda i: (i, 0)),
            pl.BlockSpec((wide, bt), lambda i: (0, i)),
            pl.BlockSpec((bt, width), lambda i: (i, 0)),
        ],
        out_shape=[
            jax.ShapeDtypeStruct((rows, wide), BF),
            jax.ShapeDtypeStruct((wide, rows), BF),
            jax.ShapeDtypeStruct((rows, width), BF),
        ],
        compiler_params=params("arbitrary"),
        cost_estimate=cost(2 * rows * width * wide, 12 * rows * width),
        name="project",
    )(tokens, weight, bias, vec)


def exchange(value):
    return lax.all_to_all(value, "fsdp", split_axis=0, concat_axis=0, tiled=True)


def per_device(
    tokens,
    counts,
    norm1_gain,
    norm1_bias,
    qkv_weight,
    query_bias,
    value_bias,
    proj_weight,
    proj_bias,
    norm2_gain,
    norm2_bias,
    fc1_weight,
    fc1_bias,
    fc2_weight,
    fc2_bias,
    cotangent,
):
    images, slots, width = tokens.shape
    owners = lax.axis_size("fsdp")
    seq = lax.axis_size("seq")
    place = lax.axis_index("seq")
    core = lax.rem(place, 2)
    image = place // 2
    part = width // 2
    shard = width // owners
    ff = fc1_weight.shape[1]
    ff_shard = ff // owners
    quarter = ff_shard // 4
    half = ff // 2
    to_sibling = [(at, at ^ 1) for at in range(seq)]
    to_partner = [(at, at ^ 2) for at in range(seq)]

    def sibling(value):
        return lax.ppermute(value, "seq", to_sibling)

    def partner(value):
        return lax.ppermute(value, "seq", to_partner)

    def pick(value, at, axis):
        return lax.dynamic_index_in_dim(value, at, axis, keepdims=False)

    place_row = place.reshape(1).astype(jnp.int32)
    core_row = core.reshape(1).astype(jnp.int32)
    small = [
        norm1_gain, norm1_bias, query_bias, value_bias, proj_bias, norm2_gain, norm2_bias,
        fc2_bias, fc1_bias,
    ]
    one, two = pack_weights(
        place_row, small, qkv_weight, proj_weight, fc1_weight, fc2_weight
    )
    one, tokens, cotangent = lax.optimization_barrier((one, tokens, cotangent))
    mine_one = lax.all_gather(one, "fsdp", axis=0, tiled=False)
    def collect(value, theirs):
        mine = pick(value, image, 0)
        return jnp.concatenate([mine, theirs, sibling(mine), sibling(theirs)], axis=0)

    tok_came = partner(pick(tokens, 1 - image, 0))
    cot_came = partner(pick(cotangent, 1 - image, 0))
    mine_one, two, tok_came, cot_came = lax.optimization_barrier(
        (mine_one, two, tok_came, cot_came)
    )
    tok = collect(tokens, tok_came)
    cot = collect(cotangent, cot_came)
    second = lax.all_gather(two, "fsdp", axis=0, tiled=True)

    own_rows = mine_one[:, VEC_ROWS:]
    other_rows = partner(own_rows)
    w_qkv = jnp.where(
        image == 0,
        jnp.stack([own_rows, other_rows], axis=1),
        jnp.stack([other_rows, own_rows], axis=1),
    ).reshape(width, 3 * part)

    vecs = mine_one[:, :8, :shard].astype(F32).transpose(1, 0, 2).reshape(8, width)
    g1, b1, qb, vb, pb, g2, b2, f2b = vecs
    f1b = mine_one[:, 8, :ff_shard].astype(F32)
    f1b = pick(f1b.reshape(owners, 2, 2, quarter), core, 1)
    f1b = f1b.transpose(1, 0, 2).reshape(1, half)

    def mine_of(vector):
        return lax.dynamic_slice_in_dim(vector, core * part, part, 0)

    qkv_bias = jnp.concatenate([mine_of(qb), jnp.zeros((part,), F32), mine_of(vb)])
    vec_one = jnp.concatenate([jnp.stack([g1, b1]), jnp.zeros((6, width), F32)])
    packed, packed_t, normed = project(tok, w_qkv, qkv_bias.reshape(1, 3 * part), vec_one)
    packed, cot = lax.optimization_barrier((packed, cot))
    mixed, result_t, log_total = attend_forward(counts, place_row, packed, packed_t, slots)
    mixed_sib = sibling(mixed)

    wp_other = sibling(second[:, :part])
    vec_two = jnp.concatenate([jnp.stack([pb, g2, b2, f2b]), jnp.zeros((4, width), F32)])
    middle, out_own, out_send, gn_part, dw_ff, gf1, gf2, wp_own = feed_forward(
        core_row, tok, mixed, mixed_sib, cot, wp_other, second, vec_two, f1b
    )
    scattered_one = lax.psum_scatter(dw_ff, "fsdp", scatter_dimension=0, tiled=True)
    gn_sib = sibling(gn_part)
    rows_own = 2 * slots

    def hand_back(own, came):
        kept_part = own[:slots]
        came = came.astype(own.dtype)
        straight = jnp.stack([kept_part, came])
        crossed = jnp.stack([came, kept_part])
        return jnp.where(image == 0, straight, crossed)

    grad_middle, grad_mixed, grad_mixed_t, dwp_own, dwp_sib, vec_back = branch(
        core_row, middle, gn_part, gn_sib, cot, mixed, mixed_sib, wp_own, vec_two
    )
    dwp = jnp.where(
        core == 0,
        jnp.concatenate([dwp_own, dwp_sib], axis=0),
        jnp.concatenate([dwp_sib, dwp_own], axis=0),
    )
    out_own = (out_own + sibling(out_send).astype(F32)).astype(BF)
    grad_mixed, out_own = lax.optimization_barrier((grad_mixed, out_own))
    out_came = partner(out_own[slots:])
    early, late = 2, 1
    attend = functools.partial(attend_backward, counts, place_row, packed, packed_t)
    before = attend(grad_mixed, grad_mixed_t, result_t, log_total, slots, 0, early)
    dw_early, qv_early = weight_grad(normed, *before)
    block_one = jnp.concatenate([dw_early, dwp], axis=1).reshape(owners, shard, -1)
    came_one = exchange(block_one)
    grad_mixed, out_came, block_one, scattered_one = lax.optimization_barrier(
        (grad_mixed, out_came, block_one, scattered_one)
    )
    output = hand_back(out_own, out_came)
    one_came = partner(scattered_one)
    grads = attend(grad_mixed, grad_mixed_t, result_t, log_total, slots, early, late)

    def total(came):
        return jnp.sum(came.astype(F32), axis=0).astype(BF)

    def join(value, came):
        return (value.astype(F32) + came.astype(F32)).astype(BF)

    early_total = total(came_one)
    one_came, early_total, w_qkv, grads = lax.optimization_barrier(
        (one_came, early_total, w_qkv, grads)
    )
    early_came = partner(early_total)
    one_sum = join(scattered_one, one_came)
    one_other = sibling(one_sum)
    gn1_own, gn1_send, dw_late, vec_first, qv_late = project_back(tok, normed, before, grads, w_qkv)

    def spread(vector):
        both = jnp.zeros((2, part), F32)
        return lax.dynamic_update_index_in_dim(both, vector, core, 0).reshape(width)

    def rows_of(block):
        return jnp.sum(block.reshape(block.shape[0] // 8, 8, block.shape[1]), axis=1)

    once = (core == 0).astype(F32)
    gg1, gb1 = rows_of(vec_first)
    gqb, gvb = rows_of(jnp.concatenate([qv_early, qv_late], axis=1))
    gg2, gb2, gpb = rows_of(vec_back) * once
    gf2b = jnp.sum(gf2, axis=0) * once
    gf1b = jnp.sum(gf1, axis=0).reshape(2, owners, quarter).transpose(1, 0, 2)
    gf1b = lax.dynamic_update_index_in_dim(
        jnp.zeros((owners, 2, 2, quarter), F32), gf1b, core, 1
    ).reshape(owners, ff_shard)
    late_wide = 3 * late * PAIR
    small_grads = jnp.stack(
        [gg1, gb1, spread(gqb), spread(gvb), gpb, gg2, gb2, gf2b]
    ).reshape(8, owners, shard).transpose(1, 0, 2)
    small_block = jnp.concatenate(
        [
            jnp.pad(small_grads, ((0, 0), (0, 0), (0, late_wide - shard))),
            jnp.pad(gf1b[:, None], ((0, 0), (0, VEC_ROWS - 9), (0, late_wide - ff_shard))),
        ],
        axis=1,
    ).astype(BF)
    block_two = jnp.concatenate(
        [small_block, dw_late.reshape(owners, shard, late_wide)], axis=1
    )
    gn1_sib = sibling(gn1_send)
    came_two = exchange(block_two)
    input_own, input_send = input_back(tok, gn1_own, gn1_sib, grad_middle, vec_one)
    came_two, input_send = lax.optimization_barrier((came_two, input_send))
    input_grad = hand_back(input_own, partner(input_send))

    grad_fc1, grad_fc2 = finish_ff(place_row, one_sum, one_other, width, quarter)
    early_sum = join(early_total, early_came)
    early_other = sibling(early_sum)
    late_total = total(came_two)
    late_sum = join(late_total, partner(late_total))
    late_other = sibling(late_sum)
    grad_qkv, grad_proj, small_sum = finish_attend(
        place_row, early_sum, early_other, late_sum, late_other, width
    )
    s = [small_sum[at, :shard] for at in range(8)]
    grad_f1b = small_sum[8, :ff_shard]
    return (
        output,
        input_grad,
        s[0],
        s[1],
        grad_qkv,
        s[2],
        s[3],
        grad_proj,
        s[4],
        s[5],
        s[6],
        grad_fc1,
        grad_f1b,
        grad_fc2,
        s[7],
    )


def solution(mesh):
    placed = (
        P("fsdp", "seq", None),
        P("fsdp", None),
        P("fsdp"),
        P("fsdp"),
        P("fsdp", None),
        P("fsdp"),
        P("fsdp"),
        P("fsdp", None),
        P("fsdp"),
        P("fsdp"),
        P("fsdp"),
        P("fsdp", None),
        P("fsdp"),
        P("fsdp", None),
        P("fsdp"),
        P("fsdp", "seq", None),
    )
    return jax.shard_map(
        per_device,
        mesh=mesh,
        in_specs=placed,
        out_specs=(
            P("fsdp", "seq", None),
            P("fsdp", "seq", None),
            P("fsdp"),
            P("fsdp"),
            P("fsdp", None),
            P("fsdp"),
            P("fsdp"),
            P("fsdp", None),
            P("fsdp"),
            P("fsdp"),
            P("fsdp"),
            P("fsdp", None),
            P("fsdp"),
            P("fsdp", None),
            P("fsdp"),
        ),
        check_vma=False,
    )
```

```python
import functools

import jax
import jax.numpy as jnp
from jax import lax
from jax.experimental import pallas as pl
from jax.experimental.pallas import tpu as pltpu
from jax.sharding import PartitionSpec as P

HEADS = 12
HEAD_DIM = 64
EPSILON = 1e-06
MASKED = -1e30
BF = jnp.bfloat16
F32 = jnp.float32
MIB = 1024 * 1024
PAIR = 2 * HEAD_DIM
VEC_ROWS = 16
SLOT_ORDER = (0, 2, 1, 3)


def params(mebibytes, *semantics):
    return pltpu.CompilerParams(
        dimension_semantics=semantics, vmem_limit_bytes=mebibytes * MIB
    )


def dot(left, right, left_dim=1, right_dim=0):
    return lax.dot_general(
        left, right, (((left_dim,), (right_dim,)), ((), ())), preferred_element_type=F32
    )


def cost(flops, bytes_accessed, transcendentals=0):
    return pl.CostEstimate(
        flops=int(flops), bytes_accessed=int(bytes_accessed), transcendentals=int(transcendentals)
    )


def whole(shape):
    return pl.BlockSpec(shape, lambda *_: tuple(0 for _ in shape))


def key_bias(counts_ref, place_ref, keys, slots):
    row = lax.broadcasted_iota(jnp.int32, (slots, PAIR), 0)
    place = place_ref[0]
    parts = []
    for flip in SLOT_ORDER:
        kept = counts_ref[place // 2, jnp.bitwise_xor(place, flip)]
        parts.append(jnp.where(row < kept, 0.0, MASKED).astype(F32))
    return jnp.concatenate(parts, axis=0)


def augment_keys(pair, bias, which, ones):
    lane = lax.broadcasted_iota(jnp.int32, pair.shape, 1)
    mine = (lane < HEAD_DIM) if which == 0 else (lane >= HEAD_DIM)
    start = HEAD_DIM if which == 0 else 0
    extra = jnp.where(
        lane == start, bias, jnp.where((lane > start) & (lane <= start + ones), 1.0, 0.0)
    )
    return jnp.where(mine, pair.astype(F32), extra).astype(BF)


def augment_values(pair, which, ones):
    lane = lax.broadcasted_iota(jnp.int32, pair.shape, 1)
    mine = (lane < HEAD_DIM) if which == 0 else (lane >= HEAD_DIM)
    start = HEAD_DIM if which == 0 else 0
    extra = jnp.where((lane >= start) & (lane < start + ones), 1.0, 0.0)
    return jnp.where(mine, pair.astype(F32), extra).astype(BF)


def pieces(value):
    first = value.astype(BF).astype(F32)
    rest = value - first
    second = rest.astype(BF).astype(F32)
    return first, second, rest - second


def extra_rows(rows, width):
    place = lax.broadcasted_iota(jnp.int32, (HEAD_DIM, width), 0)
    out = jnp.zeros((HEAD_DIM, width), F32)
    for at, row in enumerate(rows):
        out = jnp.where(place == at, row, out)
    return out.astype(BF)


def place_rows(head, extra, which):
    return jnp.concatenate([head, extra] if which == 0 else [extra, head], axis=0)


def attend_forward_kernel(
    slots, bq, chunk, counts_ref, place_ref, k_ref, qt_ref, vt_ref, mixed_ref, ot_ref, lse_ref,
    kaug, vaug, s_a, s_b, m_a, m_b
):
    keys = k_ref.shape[0]
    step = pl.program_id(1)
    steps = pl.num_programs(1)
    scores = (s_a, s_b)
    peaks = (m_a, m_b)
    ones_row = extra_rows([jnp.ones((1, bq), F32)], bq)

    @pl.when(step == 0)
    def _():
        bias = key_bias(counts_ref, place_ref, keys, slots)
        ones = jnp.ones((16, keys), BF)
        for which in range(2):
            kaug[which] = augment_keys(k_ref[...], bias, which, 0)
            vaug[which] = jnp.concatenate(
                [vt_ref[which * HEAD_DIM : (which + 1) * HEAD_DIM, :], ones], axis=0
            )

    def query_block(at, which):
        head = qt_ref[which * HEAD_DIM : (which + 1) * HEAD_DIM, pl.ds(at * bq, bq)]
        head = (head.astype(F32) * HEAD_DIM ** (-0.5)).astype(BF)
        return place_rows(head, ones_row, which)

    def score_chunk(query, which, at, peak):
        rows = slice(at * chunk, (at + 1) * chunk)
        s = dot(kaug[which, rows, :], query)
        scores[which][rows, :] = s
        top = jnp.max(s.reshape(chunk // 8, 8, bq), axis=0)
        return top if peak is None else jnp.maximum(peak, top)

    def weigh_chunk(which, at, peak, total):
        rows = slice(at * chunk, (at + 1) * chunk)
        p = jnp.exp(scores[which][rows, :] - peak).astype(BF)
        o = dot(vaug[which, :, rows], p)
        return o if total is None else total + o

    @pl.when(step == 0)
    def _():
        query = query_block(0, 0)
        peak = None
        for at in range(keys // chunk):
            peak = score_chunk(query, 0, at, peak)
        m_a[...] = peak

    later = jnp.minimum(step + 1, steps - 1)
    outs = []
    for which in range(2):
        other = 1 - which
        query = query_block(step if which == 0 else later, other)
        peak = jnp.max(peaks[which][...], axis=0, keepdims=True)
        next_peak, total = None, None
        for at in range(keys // chunk):
            next_peak = score_chunk(query, other, at, next_peak)
            total = weigh_chunk(which, at, peak, total)
        peaks[other][...] = next_peak
        norm = total[HEAD_DIM : HEAD_DIM + 1, :]
        outs.append(total[:HEAD_DIM, :] * (1.0 / norm))
        lse_ref[0, which : which + 1, :] = peak + jnp.log(norm)
    both = jnp.concatenate(outs, axis=0)
    ot_ref[...] = both
    mixed_ref[...] = both.T.astype(BF)


def attend_forward(counts, place, packed, packed_t, slots):
    keys, width = packed.shape
    width //= 3
    pairs = width // PAIR
    bq, chunk = 256, 256
    kernel = functools.partial(attend_forward_kernel, slots, bq, chunk)
    return pl.pallas_call(
        kernel,
        grid=(pairs, keys // bq),
        in_specs=[
            pl.BlockSpec(memory_space=pltpu.SMEM),
            pl.BlockSpec(memory_space=pltpu.SMEM),
            pl.BlockSpec((keys, PAIR), lambda p, i: (0, pairs + p)),
            pl.BlockSpec((PAIR, keys), lambda p, i: (p, 0)),
            pl.BlockSpec((PAIR, keys), lambda p, i: (2 * pairs + p, 0)),
        ],
        out_specs=[
            pl.BlockSpec((bq, PAIR), lambda p, i: (i, p)),
            pl.BlockSpec((PAIR, bq), lambda p, i: (p, i)),
            pl.BlockSpec((1, 8, bq), lambda p, i: (p, 0, i)),
        ],
        out_shape=[
            jax.ShapeDtypeStruct((keys, width), BF),
            jax.ShapeDtypeStruct((width, keys), F32),
            jax.ShapeDtypeStruct((pairs, 8, keys), F32),
        ],
        scratch_shapes=[
            pltpu.VMEM((2, keys, PAIR), BF),
            pltpu.VMEM((2, HEAD_DIM + 16, keys), BF),
            pltpu.VMEM((keys, bq), F32),
            pltpu.VMEM((keys, bq), F32),
            pltpu.VMEM((8, bq), F32),
            pltpu.VMEM((8, bq), F32),
        ],
        compiler_params=params(24, "arbitrary", "arbitrary"),
        cost_estimate=cost(
            2 * pairs * 2 * 2 * keys * keys * 256, 12 * keys * width, 2 * pairs * keys * keys
        ),
        name="attend_forward",
    )(counts, place, packed, packed_t, packed_t)


def attend_backward_kernel(
    slots, bq, chunk, counts_ref, place_ref, q_ref, k_ref, v_ref, qt_ref, kt_ref, do_ref, dot_ref, ot_ref,
    lse_ref, gq_ref, gk_ref, gv_ref, kaug, vaug, acc_k, acc_v
):
    keys = k_ref.shape[0]
    step = pl.program_id(1)
    steps = pl.num_programs(1)
    scale = HEAD_DIM ** (-0.5)

    @pl.when(step == 0)
    def _():
        bias = key_bias(counts_ref, place_ref, keys, slots)
        for which in range(2):
            kaug[which] = augment_keys(k_ref[...], bias, which, 3)
            vaug[which] = augment_values(v_ref[...], which, 3)
        acc_k[...] = jnp.zeros_like(acc_k)
        acc_v[...] = jnp.zeros_like(acc_v)

    ones_row = jnp.ones((1, bq), F32)
    queries, grads = [], []
    for which in range(2):
        rows = slice(which * HEAD_DIM, (which + 1) * HEAD_DIM)
        head = (qt_ref[rows, :].astype(F32) * scale).astype(BF)
        log_total = lse_ref[0, which : which + 1, :]
        queries.append(
            place_rows(head, extra_rows([ones_row, *pieces(-log_total)], bq), which)
        )
        grad = dot_ref[rows, :]
        delta = jnp.sum(grad.astype(F32) * ot_ref[rows, :], axis=0, keepdims=True)
        grads.append(place_rows(grad, extra_rows(list(pieces(-delta)), bq), which))

    do_pair = do_ref[...]
    q_pair = q_ref[...]
    totals = [None, None]
    units = [(at, which) for at in range(keys // chunk) for which in range(2)]

    def front(at, which):
        rows = slice(at * chunk, (at + 1) * chunk)
        return dot(kaug[which, rows, :], queries[which]), dot(vaug[which, rows, :], grads[which])

    ahead = front(*units[0])
    for unit, (at, which) in enumerate(units):
        rows = slice(at * chunk, (at + 1) * chunk)
        scores, dp = ahead
        if unit + 1 < len(units):
            ahead = front(*units[unit + 1])
        p = jnp.exp(scores)
        p_low = p.astype(BF)
        ds = (p * dp).astype(BF)
        acc_v[which, rows, :] += dot(p_low, do_pair)
        acc_k[which, rows, :] += dot(ds, q_pair)
        part = dot(kt_ref[which * HEAD_DIM : (which + 1) * HEAD_DIM, rows], ds)
        totals[which] = part if totals[which] is None else totals[which] + part
    both = jnp.concatenate(totals, axis=0) * scale
    gq_ref[...] = both.T.astype(BF)

    @pl.when(step == steps - 1)
    def _():
        lane = lax.broadcasted_iota(jnp.int32, (keys, PAIR), 1)
        gk_ref[...] = (jnp.where(lane < HEAD_DIM, acc_k[0], acc_k[1]) * scale).astype(BF)
        gv_ref[...] = jnp.where(lane < HEAD_DIM, acc_v[0], acc_v[1]).astype(BF)


def attend_backward(
    counts, place, packed, packed_t, grad, grad_t, result_t, log_total, slots, start, count
):
    keys, width = packed.shape
    width //= 3
    pairs = width // PAIR
    bq, chunk = 512, 256
    kernel = functools.partial(attend_backward_kernel, slots, bq, chunk)
    at = lambda p: p + start
    return pl.pallas_call(
        kernel,
        grid=(count, keys // bq),
        in_specs=[
            pl.BlockSpec(memory_space=pltpu.SMEM),
            pl.BlockSpec(memory_space=pltpu.SMEM),
            pl.BlockSpec((bq, PAIR), lambda p, i: (i, at(p))),
            pl.BlockSpec((keys, PAIR), lambda p, i: (0, pairs + at(p))),
            pl.BlockSpec((keys, PAIR), lambda p, i: (0, 2 * pairs + at(p))),
            pl.BlockSpec((PAIR, bq), lambda p, i: (at(p), i)),
            pl.BlockSpec((PAIR, keys), lambda p, i: (pairs + at(p), 0)),
            pl.BlockSpec((bq, PAIR), lambda p, i: (i, at(p))),
            pl.BlockSpec((PAIR, bq), lambda p, i: (at(p), i)),
            pl.BlockSpec((PAIR, bq), lambda p, i: (at(p), i)),
            pl.BlockSpec((1, 8, bq), lambda p, i: (at(p), 0, i)),
        ],
        out_specs=[
            pl.BlockSpec((bq, PAIR), lambda p, i: (i, p)),
            pl.BlockSpec((keys, PAIR), lambda p, i: (0, p)),
            pl.BlockSpec((keys, PAIR), lambda p, i: (0, p)),
        ],
        out_shape=[jax.ShapeDtypeStruct((keys, count * PAIR), BF)] * 3,
        scratch_shapes=[
            pltpu.VMEM((2, keys, PAIR), BF),
            pltpu.VMEM((2, keys, PAIR), BF),
            pltpu.VMEM((2, keys, PAIR), F32),
            pltpu.VMEM((2, keys, PAIR), F32),
        ],
        compiler_params=params(32, "arbitrary", "arbitrary"),
        cost_estimate=cost(
            2 * count * 5 * 2 * keys * keys * 256, 24 * keys * count * PAIR,
            2 * count * keys * keys,
        ),
        name="attend_backward",
    )(counts, place, packed, packed, packed, packed_t, packed_t, grad, grad_t, result_t, log_total)


def normalised(values):
    centred = values - jnp.mean(values, axis=-1, keepdims=True)
    variance = jnp.mean(centred * centred, axis=-1, keepdims=True)
    inverse = lax.rsqrt(variance + EPSILON)
    return centred * inverse, inverse


def norm_pull(grad, gain, unit, inverse):
    scaled = grad * gain
    mean = jnp.mean(scaled, axis=-1, keepdims=True)
    along = jnp.mean(scaled * unit, axis=-1, keepdims=True)
    return inverse * (scaled - mean - unit * along)


def fold(values):
    return jnp.sum(values.reshape(values.shape[0] // 8, 8, values.shape[1]), axis=0)


def feed_forward_kernel(
    chunk, core_ref, tok_ref, mo_ref, ms_ref, cot_ref, wpx_ref, g2_ref, vec_ref, f1b_ref,
    mid_ref, out_ref, send_ref, gn_ref, dw_ref, gf1_ref, gf2_ref, wpo_ref, acc1, acc2, accb, accc, wps_ref
):
    step = pl.program_id(0)
    steps = pl.num_programs(0)
    width = tok_ref.shape[1]
    half = f1b_ref.shape[1]
    part = width // 2

    @pl.when(step == 0)
    def _():
        acc1[...] = jnp.zeros_like(acc1)
        acc2[...] = jnp.zeros_like(acc2)
        accb[...] = jnp.zeros_like(accb)
        accc[...] = jnp.zeros_like(accc)
        here = pl.ds(pl.multiple_of(core_ref[0] * part, part), part)
        there = pl.ds(pl.multiple_of((1 - core_ref[0]) * part, part), part)
        wpo_ref[:, here] = g2_ref[here, :part]
        wpo_ref[:, there] = wpx_ref[here, :]
        wps_ref[:, here] = g2_ref[there, :part]
        wps_ref[:, there] = wpx_ref[there, :]

    middle = (
        tok_ref[...].astype(F32)
        + dot(mo_ref[...], wpo_ref[...])
        + dot(ms_ref[...], wps_ref[...])
        + vec_ref[0:1, :]
    )
    mid_ref[...] = middle
    unit, _ = normalised(middle)
    normed = (unit * vec_ref[1:2, :] + vec_ref[2:3, :]).astype(BF)
    normed_t = normed.T
    cot = cot_ref[...]
    out = None
    grad = None

    def weights(at):
        w1 = g2_ref[:, part + at * chunk : part + (at + 1) * chunk]
        piece, row = divmod(at * chunk, width)
        start = part + half + piece * width
        return w1, g2_ref[row : row + chunk, start : start + width]

    def front(at):
        w1, w2 = weights(at)
        hidden = dot(normed, w1) + f1b_ref[0:1, at * chunk : (at + 1) * chunk]
        return hidden, dot(cot, w2, 1, 1)

    ahead = front(0)
    for at in range(half // chunk):
        cols = slice(at * chunk, (at + 1) * chunk)
        hidden, grad_active = ahead
        if at + 1 < half // chunk:
            ahead = front(at + 1)
        w1, w2 = weights(at)
        below = 0.5 + 0.5 * lax.erf(hidden * (0.5**0.5))
        slope = below + hidden * (jnp.exp(hidden * hidden * -0.5) * 0.3989422804014327)
        active = (hidden * below).astype(BF)
        grad_hidden = (grad_active * slope).astype(BF)
        more = dot(active, w2)
        out = more if out is None else out + more
        more = dot(grad_hidden, w1, 1, 1)
        grad = more if grad is None else grad + more
        acc1[:, cols] += dot(normed_t, grad_hidden)
        acc2[cols, :] += dot(active, cot, 0, 0)
        accb[:, cols] += fold(grad_hidden.astype(F32))
    accc[...] += fold(cot.astype(F32))
    gn_ref[...] = grad.astype(BF)

    @pl.when(step < steps // 2)
    def _():
        out_ref[...] = middle + out + vec_ref[3:4, :]

    @pl.when(step >= steps // 2)
    def _():
        send_ref[...] = out.astype(BF)

    @pl.when(step == steps - 1)
    def _():
        dw_ref[:, :half] = acc1[...].astype(BF)
        for piece in range(half // width):
            dw_ref[:, half + piece * width : half + (piece + 1) * width] = acc2[
                piece * width : (piece + 1) * width, :
            ].astype(BF)
        gf1_ref[...] = accb[...]
        gf2_ref[...] = accc[...]


def feed_forward(core, tokens, mixed_own, mixed_sib, cot, wp_other, weights, vec, f1b):
    rows, width = tokens.shape
    half = f1b.shape[1]
    heads = mixed_own.shape[1]
    bt, chunk = 512, 384
    blocks = rows // bt
    kernel = functools.partial(feed_forward_kernel, chunk)
    return pl.pallas_call(
        kernel,
        grid=(blocks,),
        in_specs=[
            pl.BlockSpec(memory_space=pltpu.SMEM),
            pl.BlockSpec((bt, width), lambda i: (i, 0)),
            pl.BlockSpec((bt, heads), lambda i: (i, 0)),
            pl.BlockSpec((bt, heads), lambda i: (lax.rem(i + blocks // 2, blocks), 0)),
            pl.BlockSpec((bt, width), lambda i: (i, 0)),
            whole(wp_other.shape),
            whole(weights.shape),
            whole(vec.shape),
            whole(f1b.shape),
        ],
        out_specs=[
            pl.BlockSpec((bt, width), lambda i: (i, 0)),
            pl.BlockSpec((bt, width), lambda i: (jnp.minimum(i, blocks // 2 - 1), 0)),
            pl.BlockSpec((bt, width), lambda i: (jnp.maximum(i - blocks // 2, 0), 0)),
            pl.BlockSpec((bt, width), lambda i: (i, 0)),
            whole((width, 2 * half)),
            whole((8, half)),
            whole((8, width)),
            whole((width // 2, width)),
        ],
        out_shape=[
            jax.ShapeDtypeStruct((rows, width), F32),
            jax.ShapeDtypeStruct((rows // 2, width), F32),
            jax.ShapeDtypeStruct((rows // 2, width), BF),
            jax.ShapeDtypeStruct((rows, width), BF),
            jax.ShapeDtypeStruct((width, 2 * half), BF),
            jax.ShapeDtypeStruct((8, half), F32),
            jax.ShapeDtypeStruct((8, width), F32),
            jax.ShapeDtypeStruct((width // 2, width), BF),
        ],
        scratch_shapes=[
            pltpu.VMEM((width, half), F32),
            pltpu.VMEM((half, width), F32),
            pltpu.VMEM((8, half), F32),
            pltpu.VMEM((8, width), F32),
            pltpu.VMEM((width // 2, width), BF),
        ],
        compiler_params=params(60, "arbitrary"),
        cost_estimate=cost(
            2 * rows * width * (6 * half + width), 20 * rows * width + 8 * width * half,
            2 * rows * half,
        ),
        name="feed_forward",
    )(core, tokens, mixed_own, mixed_sib, cot, wp_other, weights, vec, f1b)


def branch_kernel(
    core_ref, mid_ref, ga_ref, gb_ref, cot_ref, mo_ref, ms_ref, wpo_ref, vec_ref,
    gm_ref, do_ref, dot_ref, dwo_ref, dws_ref, vecs_ref, acco, accs, accv, low_ref
):
    step = pl.program_id(0)
    steps = pl.num_programs(0)
    half = do_ref.shape[1]

    @pl.when(step == 0)
    def _():
        acco[...] = jnp.zeros_like(acco)
        accs[...] = jnp.zeros_like(accs)
        accv[...] = jnp.zeros_like(accv)

    unit, inverse = normalised(mid_ref[...])
    grad = ga_ref[...].astype(F32) + gb_ref[...].astype(F32)
    accv[0:8, :] += fold(grad * unit)
    accv[8:16, :] += fold(grad)
    grad_middle = cot_ref[...].astype(F32) + norm_pull(grad, vec_ref[1:2, :], unit, inverse)

    @pl.when(step < steps // 2)
    def _():
        gm_ref[...] = grad_middle

    low = grad_middle.astype(BF)
    low_ref[...] = low
    accv[16:24, :] += fold(low.astype(F32))
    do_ref[...] = dot(low, wpo_ref[...], 1, 1).astype(BF)
    dot_ref[...] = dot(wpo_ref[...], low, 1, 1).astype(BF)
    mine = low_ref[:, pl.ds(pl.multiple_of(core_ref[0] * half, half), half)]
    acco[...] += dot(mo_ref[...], mine, 0, 0)
    accs[...] += dot(ms_ref[...], mine, 0, 0)

    @pl.when(step == steps - 1)
    def _():
        dwo_ref[...] = acco[...].astype(BF)
        dws_ref[...] = accs[...].astype(BF)
        vecs_ref[...] = accv[...]


def branch(core, middle, grad_own, grad_sib, cot, mixed_own, mixed_sib, wp_own, vec):
    rows, width = middle.shape
    half = mixed_own.shape[1]
    bt = 512
    blocks = rows // bt
    swap = lambda i: (lax.rem(i + blocks // 2, blocks), 0)
    straight = lambda i: (i, 0)
    return pl.pallas_call(
        branch_kernel,
        grid=(blocks,),
        in_specs=[
            pl.BlockSpec(memory_space=pltpu.SMEM),
            pl.BlockSpec((bt, width), straight),
            pl.BlockSpec((bt, width), straight),
            pl.BlockSpec((bt, width), swap),
            pl.BlockSpec((bt, width), straight),
            pl.BlockSpec((bt, half), straight),
            pl.BlockSpec((bt, half), swap),
            whole(wp_own.shape),
            whole(vec.shape),
        ],
        out_specs=[
            pl.BlockSpec((bt, width), lambda i: (jnp.minimum(i, blocks // 2 - 1), 0)),
            pl.BlockSpec((bt, half), straight),
            pl.BlockSpec((half, bt), lambda i: (0, i)),
            whole((half, half)),
            whole((half, half)),
            whole((24, width)),
        ],
        out_shape=[
            jax.ShapeDtypeStruct((rows // 2, width), F32),
            jax.ShapeDtypeStruct((rows, half), BF),
            jax.ShapeDtypeStruct((half, rows), BF),
            jax.ShapeDtypeStruct((half, half), BF),
            jax.ShapeDtypeStruct((half, half), BF),
            jax.ShapeDtypeStruct((24, width), F32),
        ],
        scratch_shapes=[
            pltpu.VMEM((half, half), F32),
            pltpu.VMEM((half, half), F32),
            pltpu.VMEM((24, width), F32),
            pltpu.VMEM((bt, width), BF),
        ],
        compiler_params=params(40, "arbitrary"),
        cost_estimate=cost(2 * rows * width * 3 * half, 18 * rows * width),
        name="branch",
    )(core, middle, grad_own, grad_sib, cot, mixed_own, mixed_sib, wp_own, vec)


def weight_grad_kernel(normed_ref, gq_ref, gk_ref, gv_ref, dw_ref, qv_ref, accw, accqv):
    step = pl.program_id(0)
    steps = pl.num_programs(0)
    part = gq_ref.shape[1]

    @pl.when(step == 0)
    def _():
        accw[...] = jnp.zeros_like(accw)
        accqv[...] = jnp.zeros_like(accqv)

    normed_t = normed_ref[...].T
    for at, ref in enumerate((gq_ref, gk_ref, gv_ref)):
        cols = slice(at * part, (at + 1) * part)
        value = ref[...]
        accw[:, cols] += dot(normed_t, value)
        if at != 1:
            here = 0 if at == 0 else 8
            accqv[here : here + 8, :] += fold(value.astype(F32))

    @pl.when(step == steps - 1)
    def _():
        dw_ref[...] = accw[...].astype(BF)
        qv_ref[...] = accqv[...]


def weight_grad(normed, gq, gk, gv):
    rows, width = normed.shape
    part = gq.shape[1]
    bt = 512
    straight = lambda i: (i, 0)
    return pl.pallas_call(
        weight_grad_kernel,
        grid=(rows // bt,),
        in_specs=[
            pl.BlockSpec((bt, width), straight),
            pl.BlockSpec((bt, part), straight),
            pl.BlockSpec((bt, part), straight),
            pl.BlockSpec((bt, part), straight),
        ],
        out_specs=[whole((width, 3 * part)), whole((16, part))],
        out_shape=[
            jax.ShapeDtypeStruct((width, 3 * part), BF),
            jax.ShapeDtypeStruct((16, part), F32),
        ],
        scratch_shapes=[pltpu.VMEM((width, 3 * part), F32), pltpu.VMEM((16, part), F32)],
        compiler_params=params(24, "arbitrary"),
        cost_estimate=cost(2 * rows * width * 3 * part, 2 * rows * (width + 3 * part)),
        name="weight_grad",
    )(normed, gq, gk, gv)


def project_back_kernel(
    tok_ref, normed_ref, gqa_ref, gka_ref, gva_ref, gq_ref, gk_ref, gv_ref, w_ref,
    own_ref, sib_ref, dw_ref, vecs_ref, qv_ref, accw, accv, accqv
):
    step = pl.program_id(0)
    steps = pl.num_programs(0)
    early = gqa_ref.shape[1]
    part = gq_ref.shape[1]
    wide = early + part

    @pl.when(step == 0)
    def _():
        accw[...] = jnp.zeros_like(accw)
        accv[...] = jnp.zeros_like(accv)
        accqv[...] = jnp.zeros_like(accqv)

    unit, _ = normalised(tok_ref[...].astype(F32))
    normed_t = normed_ref[...].T
    grad = None
    before = (gqa_ref, gka_ref, gva_ref)
    for at, ref in enumerate((gq_ref, gk_ref, gv_ref)):
        cols = slice(at * part, (at + 1) * part)
        value = ref[...]
        more = dot(
            jnp.concatenate([before[at][...], value], axis=1),
            w_ref[:, at * wide : (at + 1) * wide], 1, 1,
        )
        grad = more if grad is None else grad + more
        accw[:, cols] += dot(normed_t, value)
        if at != 1:
            here = 0 if at == 0 else 8
            accqv[here : here + 8, :] += fold(value.astype(F32))
    accv[0:8, :] += fold(grad * unit)
    accv[8:16, :] += fold(grad)

    @pl.when(step < steps // 2)
    def _():
        own_ref[...] = grad

    @pl.when(step >= steps // 2)
    def _():
        sib_ref[...] = grad.astype(BF)

    @pl.when(step == steps - 1)
    def _():
        dw_ref[...] = accw[...].astype(BF)
        vecs_ref[...] = accv[...]
        qv_ref[...] = accqv[...]


def project_back(tokens, normed, before, grads, weight):
    rows, width = tokens.shape
    early, part = before[0].shape[1], grads[0].shape[1]
    bt = 512
    blocks = rows // bt
    straight = lambda i: (i, 0)
    return pl.pallas_call(
        project_back_kernel,
        grid=(blocks,),
        in_specs=[pl.BlockSpec((bt, width), straight)] * 2
        + [pl.BlockSpec((bt, early), straight)] * 3
        + [pl.BlockSpec((bt, part), straight)] * 3
        + [whole(weight.shape)],
        out_specs=[
            pl.BlockSpec((bt, width), lambda i: (jnp.minimum(i, blocks // 2 - 1), 0)),
            pl.BlockSpec((bt, width), lambda i: (jnp.maximum(i - blocks // 2, 0), 0)),
            whole((width, 3 * part)),
            whole((16, width)),
            whole((16, part)),
        ],
        out_shape=[
            jax.ShapeDtypeStruct((rows // 2, width), F32),
            jax.ShapeDtypeStruct((rows // 2, width), BF),
            jax.ShapeDtypeStruct((width, 3 * part), BF),
            jax.ShapeDtypeStruct((16, width), F32),
            jax.ShapeDtypeStruct((16, part), F32),
        ],
        scratch_shapes=[
            pltpu.VMEM((width, 3 * part), F32),
            pltpu.VMEM((16, width), F32),
            pltpu.VMEM((16, part), F32),
        ],
        compiler_params=params(40, "arbitrary"),
        cost_estimate=cost(2 * rows * width * (6 * part + 3 * early), 14 * rows * width),
        name="project_back",
    )(tokens, normed, *before, *grads, weight)


def input_back_kernel(tok_ref, own_ref, sib_ref, gm_ref, vec_ref, keep_ref, send_ref):
    unit, inverse = normalised(tok_ref[...].astype(F32))
    grad = own_ref[...] + sib_ref[...].astype(F32)
    total = gm_ref[...] + norm_pull(grad, vec_ref[0:1, :], unit, inverse)
    step = pl.program_id(0)
    steps = pl.num_programs(0)

    @pl.when(step < steps // 2)
    def _():
        keep_ref[...] = total

    @pl.when(step >= steps // 2)
    def _():
        send_ref[...] = total.astype(BF)


def input_back(tokens, grad_own, grad_sib, grad_middle, vec):
    rows, width = grad_own.shape
    bt = 256
    blocks = rows // bt
    straight = lambda i: (i, 0)
    return pl.pallas_call(
        input_back_kernel,
        grid=(blocks,),
        in_specs=[pl.BlockSpec((bt, width), straight)] * 4 + [whole(vec.shape)],
        out_specs=[
            pl.BlockSpec((bt, width), lambda i: (jnp.minimum(i, blocks // 2 - 1), 0)),
            pl.BlockSpec((bt, width), lambda i: (jnp.maximum(i - blocks // 2, 0), 0)),
        ],
        out_shape=[
            jax.ShapeDtypeStruct((rows // 2, width), F32),
            jax.ShapeDtypeStruct((rows // 2, width), BF),
        ],
        compiler_params=params(16, "arbitrary"),
        cost_estimate=cost(20 * rows * width, 16 * rows * width),
        name="input_back",
    )(tokens, grad_own, grad_sib, grad_middle, vec)


def finish_ff_kernel(place_ref, mine_ref, other_ref, fc1_ref, fc2_ref):
    first_core = lax.rem(place_ref[0], 2) == 0
    shard, ff = fc1_ref.shape
    half = ff // 2
    quarter = fc2_ref.shape[0] // 4
    width = fc2_ref.shape[1]
    owners = ff // (4 * quarter)
    mine = mine_ref[...].astype(F32)
    other = other_ref[...].astype(F32)
    cores = (jnp.where(first_core, mine, other), jnp.where(first_core, other, mine))
    pieces = []
    for owner in range(owners):
        for value in cores:
            for piece in range(2):
                start = (piece * owners + owner) * quarter
                pieces.append(value[:, start : start + quarter])
    fc1_ref[...] = jnp.concatenate(pieces, axis=1)
    for at, value in enumerate(cores):
        for piece in range(2):
            row = (2 * at + piece) * quarter
            start = half + piece * width
            fc2_ref[row : row + quarter, :] = value[:, start : start + width]


def finish_ff(place, mine, other, width, quarter):
    shard, wide = mine.shape
    return pl.pallas_call(
        finish_ff_kernel,
        grid=(1,),
        in_specs=[
            pl.BlockSpec(memory_space=pltpu.SMEM), whole(mine.shape), whole(other.shape)
        ],
        out_specs=[whole((shard, wide)), whole((4 * quarter, width))],
        out_shape=[
            jax.ShapeDtypeStruct((shard, wide), F32),
            jax.ShapeDtypeStruct((4 * quarter, width), F32),
        ],
        compiler_params=params(16, "arbitrary"),
        cost_estimate=cost(0, 12 * shard * wide),
        name="finish_ff",
    )(place, mine, other)


def finish_attend_kernel(place_ref, em_ref, eo_ref, lm_ref, lo_ref, qkv_ref, proj_ref, small_ref):
    first_core = lax.rem(place_ref[0], 2) == 0
    shard, width = proj_ref.shape
    part = width // 2
    late = lm_ref.shape[1] // 3
    early = part - late
    rows = lm_ref.shape[0] - shard
    lm = lm_ref[...].astype(F32)
    lo = lo_ref[...].astype(F32)
    small_ref[...] = lm[:rows] + lo[:rows]
    em = em_ref[...].astype(F32)
    eo = eo_ref[...].astype(F32)
    firsts = (jnp.where(first_core, em, eo), jnp.where(first_core, eo, em))
    lasts = (jnp.where(first_core, lm, lo)[rows:], jnp.where(first_core, lo, lm)[rows:])
    for at in range(3):
        for of in range(2):
            start = at * width + of * part
            qkv_ref[:, start : start + early] = firsts[of][:, at * early : (at + 1) * early]
            qkv_ref[:, start + early : start + part] = lasts[of][:, at * late : (at + 1) * late]
    for of in range(2):
        proj_ref[:, of * part : (of + 1) * part] = firsts[of][:, 3 * early :]


def finish_attend(place, early_mine, early_other, late_mine, late_other, width):
    shard = early_mine.shape[0]
    rows = late_mine.shape[0] - shard
    return pl.pallas_call(
        finish_attend_kernel,
        grid=(1,),
        in_specs=[pl.BlockSpec(memory_space=pltpu.SMEM)]
        + [whole(value.shape) for value in (early_mine, early_other, late_mine, late_other)],
        out_specs=[
            whole((shard, 3 * width)), whole((shard, width)), whole((rows, late_mine.shape[1]))
        ],
        out_shape=[
            jax.ShapeDtypeStruct((shard, 3 * width), F32),
            jax.ShapeDtypeStruct((shard, width), F32),
            jax.ShapeDtypeStruct((rows, late_mine.shape[1]), F32),
        ],
        compiler_params=params(16, "arbitrary"),
        cost_estimate=cost(0, 24 * shard * width),
        name="finish_attend",
    )(place, early_mine, early_other, late_mine, late_other)


def pack_kernel(place_ref, *refs):
    vectors, (qkv_ref, proj_ref, fc1_ref, fc2_ref, one_ref, two_ref) = refs[:-6], refs[-6:]
    first_core = lax.rem(place_ref[0], 2) == 0
    first_chip = place_ref[0] // 2 == 0
    shard, width = proj_ref.shape
    part = width // 2
    ff = fc1_ref.shape[1]
    owners = width // shard
    quarter = ff // owners // 4
    half = ff // 2
    one_ref[:VEC_ROWS, :] = jnp.zeros((VEC_ROWS, 3 * part), BF)
    for at, ref in enumerate(vectors):
        one_ref[at : at + 1, : ref.shape[1]] = ref[...]
    for at in range(3):
        low = qkv_ref[:, at * width : at * width + part]
        high = qkv_ref[:, at * width + part : (at + 1) * width]
        mine = jnp.where(first_core, low, high)
        mine = jnp.where(first_chip, mine[: shard // 2], mine[shard // 2 :])
        one_ref[VEC_ROWS:, at * part : (at + 1) * part] = mine
    two_ref[:, :part] = jnp.where(first_core, proj_ref[:, :part], proj_ref[:, part:])
    pieces_low, pieces_high = [], []
    for piece in range(2):
        for owner in range(owners):
            base = owner * 4 * quarter + piece * quarter
            pieces_low.append(fc1_ref[:, base : base + quarter])
            pieces_high.append(fc1_ref[:, base + 2 * quarter : base + 3 * quarter])
    two_ref[:, part : part + half] = jnp.where(
        first_core, jnp.concatenate(pieces_low, axis=1), jnp.concatenate(pieces_high, axis=1)
    )
    for piece in range(2):
        low = fc2_ref[piece * quarter : (piece + 1) * quarter, :]
        high = fc2_ref[(2 + piece) * quarter : (3 + piece) * quarter, :]
        start = part + half + piece * width
        two_ref[:, start : start + width] = jnp.where(first_core, low, high)


def pack_weights(place, vectors, qkv, proj, fc1, fc2):
    shard, width = proj.shape
    half = fc1.shape[1] // 2
    part = width // 2
    vectors = [vector.reshape(1, -1) for vector in vectors]
    values = (*vectors, qkv, proj, fc1, fc2)
    rows = VEC_ROWS + shard // 2
    return pl.pallas_call(
        pack_kernel,
        grid=(1,),
        in_specs=[pl.BlockSpec(memory_space=pltpu.SMEM)] + [whole(value.shape) for value in values],
        out_specs=[whole((rows, 3 * part)), whole((shard, 5 * part + half))],
        out_shape=[
            jax.ShapeDtypeStruct((rows, 3 * part), BF),
            jax.ShapeDtypeStruct((shard, 5 * part + half), BF),
        ],
        compiler_params=params(16, "arbitrary"),
        cost_estimate=cost(0, 5 * shard * width * 8),
        name="pack_weights",
    )(place, *values)


def project_kernel(tok_ref, w_ref, bias_ref, vec_ref, out_ref, out_t_ref, normed_ref):
    unit, _ = normalised(tok_ref[...].astype(F32))
    normed = (unit * vec_ref[0:1, :] + vec_ref[1:2, :]).astype(BF)
    normed_ref[...] = normed
    packed = dot(normed, w_ref[...]) + bias_ref[0:1, :]
    out_ref[...] = packed.astype(BF)
    out_t_ref[...] = packed.T.astype(BF)


def project(tokens, weight, bias, vec):
    rows, width = tokens.shape
    wide = weight.shape[1]
    bt = 512
    return pl.pallas_call(
        project_kernel,
        grid=(rows // bt,),
        in_specs=[
            pl.BlockSpec((bt, width), lambda i: (i, 0)),
            whole(weight.shape),
            whole(bias.shape),
            whole(vec.shape),
        ],
        out_specs=[
            pl.BlockSpec((bt, wide), lambda i: (i, 0)),
            pl.BlockSpec((wide, bt), lambda i: (0, i)),
            pl.BlockSpec((bt, width), lambda i: (i, 0)),
        ],
        out_shape=[
            jax.ShapeDtypeStruct((rows, wide), BF),
            jax.ShapeDtypeStruct((wide, rows), BF),
            jax.ShapeDtypeStruct((rows, width), BF),
        ],
        compiler_params=params(36, "arbitrary"),
        cost_estimate=cost(2 * rows * width * wide, 12 * rows * width),
        name="project",
    )(tokens, weight, bias, vec)


def exchange(value):
    return lax.all_to_all(value, "fsdp", split_axis=0, concat_axis=0, tiled=True)


def per_device(
    tokens,
    counts,
    norm1_gain,
    norm1_bias,
    qkv_weight,
    query_bias,
    value_bias,
    proj_weight,
    proj_bias,
    norm2_gain,
    norm2_bias,
    fc1_weight,
    fc1_bias,
    fc2_weight,
    fc2_bias,
    cotangent,
):
    images, slots, width = tokens.shape
    owners = lax.axis_size("fsdp")
    seq = lax.axis_size("seq")
    place = lax.axis_index("seq")
    core = lax.rem(place, 2)
    image = place // 2
    part = width // 2
    shard = width // owners
    ff = fc1_weight.shape[1]
    ff_shard = ff // owners
    quarter = ff_shard // 4
    half = ff // 2
    to_sibling = [(at, at ^ 1) for at in range(seq)]
    to_partner = [(at, at ^ 2) for at in range(seq)]

    def sibling(value):
        return lax.ppermute(value, "seq", to_sibling)

    def partner(value):
        return lax.ppermute(value, "seq", to_partner)

    def pick(value, at, axis):
        return lax.dynamic_index_in_dim(value, at, axis, keepdims=False)

    place_row = place.reshape(1).astype(jnp.int32)
    core_row = core.reshape(1).astype(jnp.int32)
    small = [
        norm1_gain, norm1_bias, query_bias, value_bias, proj_bias, norm2_gain, norm2_bias,
        fc2_bias, fc1_bias,
    ]
    one, two = pack_weights(
        place_row, small, qkv_weight, proj_weight, fc1_weight, fc2_weight
    )
    one, tokens, cotangent = lax.optimization_barrier((one, tokens, cotangent))
    mine_one = lax.all_gather(one, "fsdp", axis=0, tiled=False)
    def collect(value, theirs):
        mine = pick(value, image, 0)
        return jnp.concatenate([mine, theirs, sibling(mine), sibling(theirs)], axis=0)

    tok_came = partner(pick(tokens, 1 - image, 0))
    cot_came = partner(pick(cotangent, 1 - image, 0))
    mine_one, two, tok_came, cot_came = lax.optimization_barrier(
        (mine_one, two, tok_came, cot_came)
    )
    tok = collect(tokens, tok_came)
    cot = collect(cotangent, cot_came)
    second = lax.all_gather(two, "fsdp", axis=0, tiled=True)

    own_rows = mine_one[:, VEC_ROWS:]
    other_rows = partner(own_rows)
    w_qkv = jnp.where(
        image == 0,
        jnp.stack([own_rows, other_rows], axis=1),
        jnp.stack([other_rows, own_rows], axis=1),
    ).reshape(width, 3 * part)

    vecs = mine_one[:, :8, :shard].astype(F32).transpose(1, 0, 2).reshape(8, width)
    g1, b1, qb, vb, pb, g2, b2, f2b = vecs
    f1b = mine_one[:, 8, :ff_shard].astype(F32)
    f1b = pick(f1b.reshape(owners, 2, 2, quarter), core, 1)
    f1b = f1b.transpose(1, 0, 2).reshape(1, half)

    def mine_of(vector):
        return lax.dynamic_slice_in_dim(vector, core * part, part, 0)

    qkv_bias = jnp.concatenate([mine_of(qb), jnp.zeros((part,), F32), mine_of(vb)])
    vec_one = jnp.concatenate([jnp.stack([g1, b1]), jnp.zeros((6, width), F32)])
    packed, packed_t, normed = project(tok, w_qkv, qkv_bias.reshape(1, 3 * part), vec_one)
    packed, cot = lax.optimization_barrier((packed, cot))
    mixed, result_t, log_total = attend_forward(counts, place_row, packed, packed_t, slots)
    mixed_sib = sibling(mixed)

    wp_other = sibling(second[:, :part])
    vec_two = jnp.concatenate([jnp.stack([pb, g2, b2, f2b]), jnp.zeros((4, width), F32)])
    middle, out_own, out_send, gn_part, dw_ff, gf1, gf2, wp_own = feed_forward(
        core_row, tok, mixed, mixed_sib, cot, wp_other, second, vec_two, f1b
    )
    scattered_one = lax.psum_scatter(dw_ff, "fsdp", scatter_dimension=0, tiled=True)
    gn_sib = sibling(gn_part)
    rows_own = 2 * slots

    def hand_back(own, came):
        kept_part = own[:slots]
        came = came.astype(own.dtype)
        straight = jnp.stack([kept_part, came])
        crossed = jnp.stack([came, kept_part])
        return jnp.where(image == 0, straight, crossed)

    grad_middle, grad_mixed, grad_mixed_t, dwp_own, dwp_sib, vec_back = branch(
        core_row, middle, gn_part, gn_sib, cot, mixed, mixed_sib, wp_own, vec_two
    )
    dwp = jnp.where(
        core == 0,
        jnp.concatenate([dwp_own, dwp_sib], axis=0),
        jnp.concatenate([dwp_sib, dwp_own], axis=0),
    )
    out_own = (out_own + sibling(out_send).astype(F32)).astype(BF)
    grad_mixed, out_own = lax.optimization_barrier((grad_mixed, out_own))
    out_came = partner(out_own[slots:])
    early, late = 2, 1
    attend = functools.partial(attend_backward, counts, place_row, packed, packed_t)
    before = attend(grad_mixed, grad_mixed_t, result_t, log_total, slots, 0, early)
    dw_early, qv_early = weight_grad(normed, *before)
    block_one = jnp.concatenate([dw_early, dwp], axis=1).reshape(owners, shard, -1)
    came_one = exchange(block_one)
    grad_mixed, out_came, block_one, scattered_one = lax.optimization_barrier(
        (grad_mixed, out_came, block_one, scattered_one)
    )
    output = hand_back(out_own, out_came)
    one_came = partner(scattered_one)
    grads = attend(grad_mixed, grad_mixed_t, result_t, log_total, slots, early, late)

    def total(came):
        return jnp.sum(came.astype(F32), axis=0).astype(BF)

    def join(value, came):
        return (value.astype(F32) + came.astype(F32)).astype(BF)

    one_came, came_one, w_qkv, grads = lax.optimization_barrier(
        (one_came, came_one, w_qkv, grads)
    )
    early_total = total(came_one)
    early_came = partner(early_total)
    one_sum = join(scattered_one, one_came)
    one_other = sibling(one_sum)
    gn1_own, gn1_send, dw_late, vec_first, qv_late = project_back(tok, normed, before, grads, w_qkv)

    def spread(vector):
        both = jnp.zeros((2, part), F32)
        return lax.dynamic_update_index_in_dim(both, vector, core, 0).reshape(width)

    def rows_of(block):
        return jnp.sum(block.reshape(block.shape[0] // 8, 8, block.shape[1]), axis=1)

    once = (core == 0).astype(F32)
    gg1, gb1 = rows_of(vec_first)
    gqb, gvb = rows_of(jnp.concatenate([qv_early, qv_late], axis=1))
    gg2, gb2, gpb = rows_of(vec_back) * once
    gf2b = jnp.sum(gf2, axis=0) * once
    gf1b = jnp.sum(gf1, axis=0).reshape(2, owners, quarter).transpose(1, 0, 2)
    gf1b = lax.dynamic_update_index_in_dim(
        jnp.zeros((owners, 2, 2, quarter), F32), gf1b, core, 1
    ).reshape(owners, ff_shard)
    late_wide = 3 * late * PAIR
    small_grads = jnp.stack(
        [gg1, gb1, spread(gqb), spread(gvb), gpb, gg2, gb2, gf2b]
    ).reshape(8, owners, shard).transpose(1, 0, 2)
    small_block = jnp.concatenate(
        [
            jnp.pad(small_grads, ((0, 0), (0, 0), (0, late_wide - shard))),
            jnp.pad(gf1b[:, None], ((0, 0), (0, VEC_ROWS - 9), (0, late_wide - ff_shard))),
        ],
        axis=1,
    ).astype(BF)
    block_two = jnp.concatenate(
        [small_block, dw_late.reshape(owners, shard, late_wide)], axis=1
    )
    gn1_sib = sibling(gn1_send)
    came_two = exchange(block_two)
    input_own, input_send = input_back(tok, gn1_own, gn1_sib, grad_middle, vec_one)
    input_came = partner(input_send)
    came_two, input_own = lax.optimization_barrier((came_two, input_own))
    input_grad = hand_back(input_own, input_came)

    grad_fc1, grad_fc2 = finish_ff(place_row, one_sum, one_other, width, quarter)
    early_sum = join(early_total, early_came)
    early_other = sibling(early_sum)
    late_total = total(came_two)
    late_sum = join(late_total, partner(late_total))
    late_other = sibling(late_sum)
    grad_qkv, grad_proj, small_sum = finish_attend(
        place_row, early_sum, early_other, late_sum, late_other, width
    )
    s = [small_sum[at, :shard] for at in range(8)]
    grad_f1b = small_sum[8, :ff_shard]
    return (
        output,
        input_grad,
        s[0],
        s[1],
        grad_qkv,
        s[2],
        s[3],
        grad_proj,
        s[4],
        s[5],
        s[6],
        grad_fc1,
        grad_f1b,
        grad_fc2,
        s[7],
    )


def solution(mesh):
    placed = (
        P("fsdp", "seq", None),
        P("fsdp", None),
        P("fsdp"),
        P("fsdp"),
        P("fsdp", None),
        P("fsdp"),
        P("fsdp"),
        P("fsdp", None),
        P("fsdp"),
        P("fsdp"),
        P("fsdp"),
        P("fsdp", None),
        P("fsdp"),
        P("fsdp", None),
        P("fsdp"),
        P("fsdp", "seq", None),
    )
    return jax.shard_map(
        per_device,
        mesh=mesh,
        in_specs=placed,
        out_specs=(
            P("fsdp", "seq", None),
            P("fsdp", "seq", None),
            P("fsdp"),
            P("fsdp"),
            P("fsdp", None),
            P("fsdp"),
            P("fsdp"),
            P("fsdp", None),
            P("fsdp"),
            P("fsdp"),
            P("fsdp"),
            P("fsdp", None),
            P("fsdp"),
            P("fsdp", None),
            P("fsdp"),
        ),
        check_vma=False,
    )
```

```python
import functools

import jax
import jax.numpy as jnp
from jax import lax
from jax.experimental import pallas as pl
from jax.experimental.pallas import tpu as pltpu
from jax.sharding import PartitionSpec as P

HEADS = 12
HEAD_DIM = 64
EPSILON = 1e-06
MASKED = -1e30
BF = jnp.bfloat16
F32 = jnp.float32
MIB = 1024 * 1024
PAIR = 2 * HEAD_DIM
VEC_ROWS = 16
SLOT_ORDER = (0, 2, 1, 3)


def params(mebibytes, *semantics):
    return pltpu.CompilerParams(
        dimension_semantics=semantics, vmem_limit_bytes=mebibytes * MIB
    )


def dot(left, right, left_dim=1, right_dim=0):
    return lax.dot_general(
        left, right, (((left_dim,), (right_dim,)), ((), ())), preferred_element_type=F32
    )


def cost(flops, bytes_accessed, transcendentals=0):
    return pl.CostEstimate(
        flops=int(flops), bytes_accessed=int(bytes_accessed), transcendentals=int(transcendentals)
    )


def whole(shape):
    return pl.BlockSpec(shape, lambda *_: tuple(0 for _ in shape))


def key_bias(counts_ref, place_ref, keys, slots):
    row = lax.broadcasted_iota(jnp.int32, (slots, PAIR), 0)
    place = place_ref[0]
    parts = []
    for flip in SLOT_ORDER:
        kept = counts_ref[place // 2, jnp.bitwise_xor(place, flip)]
        parts.append(jnp.where(row < kept, 0.0, MASKED).astype(F32))
    return jnp.concatenate(parts, axis=0)


def augment_keys(pair, bias, which, ones):
    lane = lax.broadcasted_iota(jnp.int32, pair.shape, 1)
    mine = (lane < HEAD_DIM) if which == 0 else (lane >= HEAD_DIM)
    start = HEAD_DIM if which == 0 else 0
    extra = jnp.where(
        lane == start, bias, jnp.where((lane > start) & (lane <= start + ones), 1.0, 0.0)
    )
    return jnp.where(mine, pair.astype(F32), extra).astype(BF)


def augment_values(pair, which, ones):
    lane = lax.broadcasted_iota(jnp.int32, pair.shape, 1)
    mine = (lane < HEAD_DIM) if which == 0 else (lane >= HEAD_DIM)
    start = HEAD_DIM if which == 0 else 0
    extra = jnp.where((lane >= start) & (lane < start + ones), 1.0, 0.0)
    return jnp.where(mine, pair.astype(F32), extra).astype(BF)


def pieces(value):
    first = value.astype(BF).astype(F32)
    rest = value - first
    second = rest.astype(BF).astype(F32)
    return first, second, rest - second


def extra_rows(rows, width):
    place = lax.broadcasted_iota(jnp.int32, (HEAD_DIM, width), 0)
    out = jnp.zeros((HEAD_DIM, width), F32)
    for at, row in enumerate(rows):
        out = jnp.where(place == at, row, out)
    return out.astype(BF)


def place_rows(head, extra, which):
    return jnp.concatenate([head, extra] if which == 0 else [extra, head], axis=0)


def attend_forward_kernel(
    slots, bq, chunk, counts_ref, place_ref, k_ref, qt_ref, vt_ref, mixed_ref, ot_ref, lse_ref,
    kaug, vaug, s_a, s_b, m_a, m_b
):
    keys = k_ref.shape[0]
    step = pl.program_id(1)
    steps = pl.num_programs(1)
    scores = (s_a, s_b)
    peaks = (m_a, m_b)
    ones_row = extra_rows([jnp.ones((1, bq), F32)], bq)

    @pl.when(step == 0)
    def _():
        bias = key_bias(counts_ref, place_ref, keys, slots)
        ones = jnp.ones((16, keys), BF)
        for which in range(2):
            kaug[which] = augment_keys(k_ref[...], bias, which, 0)
            vaug[which] = jnp.concatenate(
                [vt_ref[which * HEAD_DIM : (which + 1) * HEAD_DIM, :], ones], axis=0
            )

    def query_block(at, which):
        head = qt_ref[which * HEAD_DIM : (which + 1) * HEAD_DIM, pl.ds(at * bq, bq)]
        head = (head.astype(F32) * HEAD_DIM ** (-0.5)).astype(BF)
        return place_rows(head, ones_row, which)

    def score_chunk(query, which, at, peak):
        rows = slice(at * chunk, (at + 1) * chunk)
        s = dot(kaug[which, rows, :], query)
        scores[which][rows, :] = s
        top = jnp.max(s.reshape(chunk // 8, 8, bq), axis=0)
        return top if peak is None else jnp.maximum(peak, top)

    def weigh_chunk(which, at, peak, total):
        rows = slice(at * chunk, (at + 1) * chunk)
        p = jnp.exp(scores[which][rows, :] - peak).astype(BF)
        o = dot(vaug[which, :, rows], p)
        return o if total is None else total + o

    @pl.when(step == 0)
    def _():
        query = query_block(0, 0)
        peak = None
        for at in range(keys // chunk):
            peak = score_chunk(query, 0, at, peak)
        m_a[...] = peak

    later = jnp.minimum(step + 1, steps - 1)
    outs = []
    for which in range(2):
        other = 1 - which
        query = query_block(step if which == 0 else later, other)
        peak = jnp.max(peaks[which][...], axis=0, keepdims=True)
        next_peak, total = None, None
        for at in range(keys // chunk):
            next_peak = score_chunk(query, other, at, next_peak)
            total = weigh_chunk(which, at, peak, total)
        peaks[other][...] = next_peak
        norm = total[HEAD_DIM : HEAD_DIM + 1, :]
        outs.append(total[:HEAD_DIM, :] * (1.0 / norm))
        lse_ref[0, which : which + 1, :] = peak + jnp.log(norm)
    both = jnp.concatenate(outs, axis=0)
    ot_ref[...] = both
    mixed_ref[...] = both.T.astype(BF)


def attend_forward(counts, place, packed, packed_t, slots):
    keys, width = packed.shape
    width //= 3
    pairs = width // PAIR
    bq, chunk = 256, 256
    kernel = functools.partial(attend_forward_kernel, slots, bq, chunk)
    return pl.pallas_call(
        kernel,
        grid=(pairs, keys // bq),
        in_specs=[
            pl.BlockSpec(memory_space=pltpu.SMEM),
            pl.BlockSpec(memory_space=pltpu.SMEM),
            pl.BlockSpec((keys, PAIR), lambda p, i: (0, pairs + p)),
            pl.BlockSpec((PAIR, keys), lambda p, i: (p, 0)),
            pl.BlockSpec((PAIR, keys), lambda p, i: (2 * pairs + p, 0)),
        ],
        out_specs=[
            pl.BlockSpec((bq, PAIR), lambda p, i: (i, p)),
            pl.BlockSpec((PAIR, bq), lambda p, i: (p, i)),
            pl.BlockSpec((1, 8, bq), lambda p, i: (p, 0, i)),
        ],
        out_shape=[
            jax.ShapeDtypeStruct((keys, width), BF),
            jax.ShapeDtypeStruct((width, keys), F32),
            jax.ShapeDtypeStruct((pairs, 8, keys), F32),
        ],
        scratch_shapes=[
            pltpu.VMEM((2, keys, PAIR), BF),
            pltpu.VMEM((2, HEAD_DIM + 16, keys), BF),
            pltpu.VMEM((keys, bq), F32),
            pltpu.VMEM((keys, bq), F32),
            pltpu.VMEM((8, bq), F32),
            pltpu.VMEM((8, bq), F32),
        ],
        compiler_params=params(60, "arbitrary", "arbitrary"),
        cost_estimate=cost(
            2 * pairs * 2 * 2 * keys * keys * 256, 12 * keys * width, 2 * pairs * keys * keys
        ),
        name="attend_forward",
    )(counts, place, packed, packed_t, packed_t)


def attend_backward_kernel(
    slots, bq, chunk, counts_ref, place_ref, q_ref, k_ref, v_ref, qt_ref, kt_ref, do_ref, dot_ref, ot_ref,
    lse_ref, gq_ref, gk_ref, gv_ref, kaug, vaug, acc_k, acc_v
):
    keys = k_ref.shape[0]
    step = pl.program_id(1)
    steps = pl.num_programs(1)
    scale = HEAD_DIM ** (-0.5)

    @pl.when(step == 0)
    def _():
        bias = key_bias(counts_ref, place_ref, keys, slots)
        for which in range(2):
            kaug[which] = augment_keys(k_ref[...], bias, which, 3)
            vaug[which] = augment_values(v_ref[...], which, 3)
        acc_k[...] = jnp.zeros_like(acc_k)
        acc_v[...] = jnp.zeros_like(acc_v)

    ones_row = jnp.ones((1, bq), F32)
    queries, grads = [], []
    for which in range(2):
        rows = slice(which * HEAD_DIM, (which + 1) * HEAD_DIM)
        head = (qt_ref[rows, :].astype(F32) * scale).astype(BF)
        log_total = lse_ref[0, which : which + 1, :]
        queries.append(
            place_rows(head, extra_rows([ones_row, *pieces(-log_total)], bq), which)
        )
        grad = dot_ref[rows, :]
        delta = jnp.sum(grad.astype(F32) * ot_ref[rows, :], axis=0, keepdims=True)
        grads.append(place_rows(grad, extra_rows(list(pieces(-delta)), bq), which))

    do_pair = do_ref[...]
    q_pair = q_ref[...]
    totals = [None, None]
    units = [(at, which) for at in range(keys // chunk) for which in range(2)]

    def front(at, which):
        rows = slice(at * chunk, (at + 1) * chunk)
        return dot(kaug[which, rows, :], queries[which]), dot(vaug[which, rows, :], grads[which])

    ahead = front(*units[0])
    for unit, (at, which) in enumerate(units):
        rows = slice(at * chunk, (at + 1) * chunk)
        scores, dp = ahead
        if unit + 1 < len(units):
            ahead = front(*units[unit + 1])
        p = jnp.exp(scores)
        p_low = p.astype(BF)
        ds = (p * dp).astype(BF)
        acc_v[which, rows, :] += dot(p_low, do_pair)
        acc_k[which, rows, :] += dot(ds, q_pair)
        part = dot(kt_ref[which * HEAD_DIM : (which + 1) * HEAD_DIM, rows], ds)
        totals[which] = part if totals[which] is None else totals[which] + part
    both = jnp.concatenate(totals, axis=0) * scale
    gq_ref[...] = both.T.astype(BF)

    @pl.when(step == steps - 1)
    def _():
        lane = lax.broadcasted_iota(jnp.int32, (keys, PAIR), 1)
        gk_ref[...] = (jnp.where(lane < HEAD_DIM, acc_k[0], acc_k[1]) * scale).astype(BF)
        gv_ref[...] = jnp.where(lane < HEAD_DIM, acc_v[0], acc_v[1]).astype(BF)


def attend_backward(
    counts, place, packed, packed_t, grad, grad_t, result_t, log_total, slots, start, count
):
    keys, width = packed.shape
    width //= 3
    pairs = width // PAIR
    bq, chunk = 512, 256
    kernel = functools.partial(attend_backward_kernel, slots, bq, chunk)
    at = lambda p: p + start
    return pl.pallas_call(
        kernel,
        grid=(count, keys // bq),
        in_specs=[
            pl.BlockSpec(memory_space=pltpu.SMEM),
            pl.BlockSpec(memory_space=pltpu.SMEM),
            pl.BlockSpec((bq, PAIR), lambda p, i: (i, at(p))),
            pl.BlockSpec((keys, PAIR), lambda p, i: (0, pairs + at(p))),
            pl.BlockSpec((keys, PAIR), lambda p, i: (0, 2 * pairs + at(p))),
            pl.BlockSpec((PAIR, bq), lambda p, i: (at(p), i)),
            pl.BlockSpec((PAIR, keys), lambda p, i: (pairs + at(p), 0)),
            pl.BlockSpec((bq, PAIR), lambda p, i: (i, at(p))),
            pl.BlockSpec((PAIR, bq), lambda p, i: (at(p), i)),
            pl.BlockSpec((PAIR, bq), lambda p, i: (at(p), i)),
            pl.BlockSpec((1, 8, bq), lambda p, i: (at(p), 0, i)),
        ],
        out_specs=[
            pl.BlockSpec((bq, PAIR), lambda p, i: (i, p)),
            pl.BlockSpec((keys, PAIR), lambda p, i: (0, p)),
            pl.BlockSpec((keys, PAIR), lambda p, i: (0, p)),
        ],
        out_shape=[jax.ShapeDtypeStruct((keys, count * PAIR), BF)] * 3,
        scratch_shapes=[
            pltpu.VMEM((2, keys, PAIR), BF),
            pltpu.VMEM((2, keys, PAIR), BF),
            pltpu.VMEM((2, keys, PAIR), F32),
            pltpu.VMEM((2, keys, PAIR), F32),
        ],
        compiler_params=params(60, "arbitrary", "arbitrary"),
        cost_estimate=cost(
            2 * count * 5 * 2 * keys * keys * 256, 24 * keys * count * PAIR,
            2 * count * keys * keys,
        ),
        name="attend_backward",
    )(counts, place, packed, packed, packed, packed_t, packed_t, grad, grad_t, result_t, log_total)


def normalised(values):
    centred = values - jnp.mean(values, axis=-1, keepdims=True)
    variance = jnp.mean(centred * centred, axis=-1, keepdims=True)
    inverse = lax.rsqrt(variance + EPSILON)
    return centred * inverse, inverse


def norm_pull(grad, gain, unit, inverse):
    scaled = grad * gain
    mean = jnp.mean(scaled, axis=-1, keepdims=True)
    along = jnp.mean(scaled * unit, axis=-1, keepdims=True)
    return inverse * (scaled - mean - unit * along)


def fold(values):
    return jnp.sum(values.reshape(values.shape[0] // 8, 8, values.shape[1]), axis=0)


def feed_forward_kernel(
    chunk, core_ref, tok_ref, mo_ref, ms_ref, cot_ref, wpx_ref, g2_ref, vec_ref, f1b_ref,
    mid_ref, out_ref, send_ref, gn_ref, dw_ref, gf1_ref, gf2_ref, wpo_ref, acc1, acc2, accb, accc, wps_ref
):
    step = pl.program_id(0)
    steps = pl.num_programs(0)
    width = tok_ref.shape[1]
    half = f1b_ref.shape[1]
    part = width // 2

    @pl.when(step == 0)
    def _():
        acc1[...] = jnp.zeros_like(acc1)
        acc2[...] = jnp.zeros_like(acc2)
        accb[...] = jnp.zeros_like(accb)
        accc[...] = jnp.zeros_like(accc)
        here = pl.ds(pl.multiple_of(core_ref[0] * part, part), part)
        there = pl.ds(pl.multiple_of((1 - core_ref[0]) * part, part), part)
        wpo_ref[:, here] = g2_ref[here, :part]
        wpo_ref[:, there] = wpx_ref[here, :]
        wps_ref[:, here] = g2_ref[there, :part]
        wps_ref[:, there] = wpx_ref[there, :]

    middle = (
        tok_ref[...].astype(F32)
        + dot(mo_ref[...], wpo_ref[...])
        + dot(ms_ref[...], wps_ref[...])
        + vec_ref[0:1, :]
    )
    mid_ref[...] = middle
    unit, _ = normalised(middle)
    normed = (unit * vec_ref[1:2, :] + vec_ref[2:3, :]).astype(BF)
    normed_t = normed.T
    cot = cot_ref[...]
    out = None
    grad = None

    def weights(at):
        w1 = g2_ref[:, part + at * chunk : part + (at + 1) * chunk]
        piece, row = divmod(at * chunk, width)
        start = part + half + piece * width
        return w1, g2_ref[row : row + chunk, start : start + width]

    def front(at):
        w1, w2 = weights(at)
        hidden = dot(normed, w1) + f1b_ref[0:1, at * chunk : (at + 1) * chunk]
        return hidden, dot(cot, w2, 1, 1)

    ahead = front(0)
    for at in range(half // chunk):
        cols = slice(at * chunk, (at + 1) * chunk)
        hidden, grad_active = ahead
        if at + 1 < half // chunk:
            ahead = front(at + 1)
        w1, w2 = weights(at)
        below = 0.5 + 0.5 * lax.erf(hidden * (0.5**0.5))
        slope = below + hidden * (jnp.exp(hidden * hidden * -0.5) * 0.3989422804014327)
        active = (hidden * below).astype(BF)
        grad_hidden = (grad_active * slope).astype(BF)
        more = dot(active, w2)
        out = more if out is None else out + more
        more = dot(grad_hidden, w1, 1, 1)
        grad = more if grad is None else grad + more
        acc1[:, cols] += dot(normed_t, grad_hidden)
        acc2[cols, :] += dot(active, cot, 0, 0)
        accb[:, cols] += fold(grad_hidden.astype(F32))
    accc[...] += fold(cot.astype(F32))
    gn_ref[...] = grad.astype(BF)

    @pl.when(step < steps // 2)
    def _():
        out_ref[...] = middle + out + vec_ref[3:4, :]

    @pl.when(step >= steps // 2)
    def _():
        send_ref[...] = out.astype(BF)

    @pl.when(step == steps - 1)
    def _():
        dw_ref[:, :half] = acc1[...].astype(BF)
        for piece in range(half // width):
            dw_ref[:, half + piece * width : half + (piece + 1) * width] = acc2[
                piece * width : (piece + 1) * width, :
            ].astype(BF)
        gf1_ref[...] = accb[...]
        gf2_ref[...] = accc[...]


def feed_forward(core, tokens, mixed_own, mixed_sib, cot, wp_other, weights, vec, f1b):
    rows, width = tokens.shape
    half = f1b.shape[1]
    heads = mixed_own.shape[1]
    bt, chunk = 512, 384
    blocks = rows // bt
    kernel = functools.partial(feed_forward_kernel, chunk)
    return pl.pallas_call(
        kernel,
        grid=(blocks,),
        in_specs=[
            pl.BlockSpec(memory_space=pltpu.SMEM),
            pl.BlockSpec((bt, width), lambda i: (i, 0)),
            pl.BlockSpec((bt, heads), lambda i: (i, 0)),
            pl.BlockSpec((bt, heads), lambda i: (lax.rem(i + blocks // 2, blocks), 0)),
            pl.BlockSpec((bt, width), lambda i: (i, 0)),
            whole(wp_other.shape),
            whole(weights.shape),
            whole(vec.shape),
            whole(f1b.shape),
        ],
        out_specs=[
            pl.BlockSpec((bt, width), lambda i: (i, 0)),
            pl.BlockSpec((bt, width), lambda i: (jnp.minimum(i, blocks // 2 - 1), 0)),
            pl.BlockSpec((bt, width), lambda i: (jnp.maximum(i - blocks // 2, 0), 0)),
            pl.BlockSpec((bt, width), lambda i: (i, 0)),
            whole((width, 2 * half)),
            whole((8, half)),
            whole((8, width)),
            whole((width // 2, width)),
        ],
        out_shape=[
            jax.ShapeDtypeStruct((rows, width), F32),
            jax.ShapeDtypeStruct((rows // 2, width), F32),
            jax.ShapeDtypeStruct((rows // 2, width), BF),
            jax.ShapeDtypeStruct((rows, width), BF),
            jax.ShapeDtypeStruct((width, 2 * half), BF),
            jax.ShapeDtypeStruct((8, half), F32),
            jax.ShapeDtypeStruct((8, width), F32),
            jax.ShapeDtypeStruct((width // 2, width), BF),
        ],
        scratch_shapes=[
            pltpu.VMEM((width, half), F32),
            pltpu.VMEM((half, width), F32),
            pltpu.VMEM((8, half), F32),
            pltpu.VMEM((8, width), F32),
            pltpu.VMEM((width // 2, width), BF),
        ],
        compiler_params=params(60, "arbitrary"),
        cost_estimate=cost(
            2 * rows * width * (6 * half + width), 20 * rows * width + 8 * width * half,
            2 * rows * half,
        ),
        name="feed_forward",
    )(core, tokens, mixed_own, mixed_sib, cot, wp_other, weights, vec, f1b)


def branch_kernel(
    core_ref, mid_ref, ga_ref, gb_ref, cot_ref, mo_ref, ms_ref, wpo_ref, vec_ref,
    gm_ref, do_ref, dot_ref, dwo_ref, dws_ref, vecs_ref, acco, accs, accv, low_ref
):
    step = pl.program_id(0)
    steps = pl.num_programs(0)
    half = do_ref.shape[1]

    @pl.when(step == 0)
    def _():
        acco[...] = jnp.zeros_like(acco)
        accs[...] = jnp.zeros_like(accs)
        accv[...] = jnp.zeros_like(accv)

    unit, inverse = normalised(mid_ref[...])
    grad = ga_ref[...].astype(F32) + gb_ref[...].astype(F32)
    accv[0:8, :] += fold(grad * unit)
    accv[8:16, :] += fold(grad)
    grad_middle = cot_ref[...].astype(F32) + norm_pull(grad, vec_ref[1:2, :], unit, inverse)

    @pl.when(step < steps // 2)
    def _():
        gm_ref[...] = grad_middle

    low = grad_middle.astype(BF)
    low_ref[...] = low
    accv[16:24, :] += fold(low.astype(F32))
    do_ref[...] = dot(low, wpo_ref[...], 1, 1).astype(BF)
    dot_ref[...] = dot(wpo_ref[...], low, 1, 1).astype(BF)
    mine = low_ref[:, pl.ds(pl.multiple_of(core_ref[0] * half, half), half)]
    acco[...] += dot(mo_ref[...], mine, 0, 0)
    accs[...] += dot(ms_ref[...], mine, 0, 0)

    @pl.when(step == steps - 1)
    def _():
        dwo_ref[...] = acco[...].astype(BF)
        dws_ref[...] = accs[...].astype(BF)
        vecs_ref[...] = accv[...]


def branch(core, middle, grad_own, grad_sib, cot, mixed_own, mixed_sib, wp_own, vec):
    rows, width = middle.shape
    half = mixed_own.shape[1]
    bt = 512
    blocks = rows // bt
    swap = lambda i: (lax.rem(i + blocks // 2, blocks), 0)
    straight = lambda i: (i, 0)
    return pl.pallas_call(
        branch_kernel,
        grid=(blocks,),
        in_specs=[
            pl.BlockSpec(memory_space=pltpu.SMEM),
            pl.BlockSpec((bt, width), straight),
            pl.BlockSpec((bt, width), straight),
            pl.BlockSpec((bt, width), swap),
            pl.BlockSpec((bt, width), straight),
            pl.BlockSpec((bt, half), straight),
            pl.BlockSpec((bt, half), swap),
            whole(wp_own.shape),
            whole(vec.shape),
        ],
        out_specs=[
            pl.BlockSpec((bt, width), lambda i: (jnp.minimum(i, blocks // 2 - 1), 0)),
            pl.BlockSpec((bt, half), straight),
            pl.BlockSpec((half, bt), lambda i: (0, i)),
            whole((half, half)),
            whole((half, half)),
            whole((24, width)),
        ],
        out_shape=[
            jax.ShapeDtypeStruct((rows // 2, width), F32),
            jax.ShapeDtypeStruct((rows, half), BF),
            jax.ShapeDtypeStruct((half, rows), BF),
            jax.ShapeDtypeStruct((half, half), BF),
            jax.ShapeDtypeStruct((half, half), BF),
            jax.ShapeDtypeStruct((24, width), F32),
        ],
        scratch_shapes=[
            pltpu.VMEM((half, half), F32),
            pltpu.VMEM((half, half), F32),
            pltpu.VMEM((24, width), F32),
            pltpu.VMEM((bt, width), BF),
        ],
        compiler_params=params(60, "arbitrary"),
        cost_estimate=cost(2 * rows * width * 3 * half, 18 * rows * width),
        name="branch",
    )(core, middle, grad_own, grad_sib, cot, mixed_own, mixed_sib, wp_own, vec)


def weight_grad_kernel(normed_ref, gq_ref, gk_ref, gv_ref, dw_ref, qv_ref, accw, accqv):
    step = pl.program_id(0)
    steps = pl.num_programs(0)
    part = gq_ref.shape[1]

    @pl.when(step == 0)
    def _():
        accw[...] = jnp.zeros_like(accw)
        accqv[...] = jnp.zeros_like(accqv)

    normed_t = normed_ref[...].T
    for at, ref in enumerate((gq_ref, gk_ref, gv_ref)):
        cols = slice(at * part, (at + 1) * part)
        value = ref[...]
        accw[:, cols] += dot(normed_t, value)
        if at != 1:
            here = 0 if at == 0 else 8
            accqv[here : here + 8, :] += fold(value.astype(F32))

    @pl.when(step == steps - 1)
    def _():
        dw_ref[...] = accw[...].astype(BF)
        qv_ref[...] = accqv[...]


def weight_grad(normed, gq, gk, gv):
    rows, width = normed.shape
    part = gq.shape[1]
    bt = 512
    straight = lambda i: (i, 0)
    return pl.pallas_call(
        weight_grad_kernel,
        grid=(rows // bt,),
        in_specs=[
            pl.BlockSpec((bt, width), straight),
            pl.BlockSpec((bt, part), straight),
            pl.BlockSpec((bt, part), straight),
            pl.BlockSpec((bt, part), straight),
        ],
        out_specs=[whole((width, 3 * part)), whole((16, part))],
        out_shape=[
            jax.ShapeDtypeStruct((width, 3 * part), BF),
            jax.ShapeDtypeStruct((16, part), F32),
        ],
        scratch_shapes=[pltpu.VMEM((width, 3 * part), F32), pltpu.VMEM((16, part), F32)],
        compiler_params=params(60, "arbitrary"),
        cost_estimate=cost(2 * rows * width * 3 * part, 2 * rows * (width + 3 * part)),
        name="weight_grad",
    )(normed, gq, gk, gv)


def project_back_kernel(
    tok_ref, normed_ref, gqa_ref, gka_ref, gva_ref, gq_ref, gk_ref, gv_ref, w_ref,
    own_ref, sib_ref, dw_ref, vecs_ref, qv_ref, accw, accv, accqv
):
    step = pl.program_id(0)
    steps = pl.num_programs(0)
    early = gqa_ref.shape[1]
    part = gq_ref.shape[1]
    wide = early + part

    @pl.when(step == 0)
    def _():
        accw[...] = jnp.zeros_like(accw)
        accv[...] = jnp.zeros_like(accv)
        accqv[...] = jnp.zeros_like(accqv)

    unit, _ = normalised(tok_ref[...].astype(F32))
    normed_t = normed_ref[...].T
    grad = None
    before = (gqa_ref, gka_ref, gva_ref)
    for at, ref in enumerate((gq_ref, gk_ref, gv_ref)):
        cols = slice(at * part, (at + 1) * part)
        value = ref[...]
        more = dot(
            jnp.concatenate([before[at][...], value], axis=1),
            w_ref[:, at * wide : (at + 1) * wide], 1, 1,
        )
        grad = more if grad is None else grad + more
        accw[:, cols] += dot(normed_t, value)
        if at != 1:
            here = 0 if at == 0 else 8
            accqv[here : here + 8, :] += fold(value.astype(F32))
    accv[0:8, :] += fold(grad * unit)
    accv[8:16, :] += fold(grad)

    @pl.when(step < steps // 2)
    def _():
        own_ref[...] = grad

    @pl.when(step >= steps // 2)
    def _():
        sib_ref[...] = grad.astype(BF)

    @pl.when(step == steps - 1)
    def _():
        dw_ref[...] = accw[...].astype(BF)
        vecs_ref[...] = accv[...]
        qv_ref[...] = accqv[...]


def project_back(tokens, normed, before, grads, weight):
    rows, width = tokens.shape
    early, part = before[0].shape[1], grads[0].shape[1]
    bt = 512
    blocks = rows // bt
    straight = lambda i: (i, 0)
    return pl.pallas_call(
        project_back_kernel,
        grid=(blocks,),
        in_specs=[pl.BlockSpec((bt, width), straight)] * 2
        + [pl.BlockSpec((bt, early), straight)] * 3
        + [pl.BlockSpec((bt, part), straight)] * 3
        + [whole(weight.shape)],
        out_specs=[
            pl.BlockSpec((bt, width), lambda i: (jnp.minimum(i, blocks // 2 - 1), 0)),
            pl.BlockSpec((bt, width), lambda i: (jnp.maximum(i - blocks // 2, 0), 0)),
            whole((width, 3 * part)),
            whole((16, width)),
            whole((16, part)),
        ],
        out_shape=[
            jax.ShapeDtypeStruct((rows // 2, width), F32),
            jax.ShapeDtypeStruct((rows // 2, width), BF),
            jax.ShapeDtypeStruct((width, 3 * part), BF),
            jax.ShapeDtypeStruct((16, width), F32),
            jax.ShapeDtypeStruct((16, part), F32),
        ],
        scratch_shapes=[
            pltpu.VMEM((width, 3 * part), F32),
            pltpu.VMEM((16, width), F32),
            pltpu.VMEM((16, part), F32),
        ],
        compiler_params=params(60, "arbitrary"),
        cost_estimate=cost(2 * rows * width * (6 * part + 3 * early), 14 * rows * width),
        name="project_back",
    )(tokens, normed, *before, *grads, weight)


def input_back_kernel(tok_ref, own_ref, sib_ref, gm_ref, vec_ref, keep_ref, send_ref):
    unit, inverse = normalised(tok_ref[...].astype(F32))
    grad = own_ref[...] + sib_ref[...].astype(F32)
    total = gm_ref[...] + norm_pull(grad, vec_ref[0:1, :], unit, inverse)
    step = pl.program_id(0)
    steps = pl.num_programs(0)

    @pl.when(step < steps // 2)
    def _():
        keep_ref[...] = total

    @pl.when(step >= steps // 2)
    def _():
        send_ref[...] = total.astype(BF)


def input_back(tokens, grad_own, grad_sib, grad_middle, vec):
    rows, width = grad_own.shape
    bt = 256
    blocks = rows // bt
    straight = lambda i: (i, 0)
    return pl.pallas_call(
        input_back_kernel,
        grid=(blocks,),
        in_specs=[pl.BlockSpec((bt, width), straight)] * 4 + [whole(vec.shape)],
        out_specs=[
            pl.BlockSpec((bt, width), lambda i: (jnp.minimum(i, blocks // 2 - 1), 0)),
            pl.BlockSpec((bt, width), lambda i: (jnp.maximum(i - blocks // 2, 0), 0)),
        ],
        out_shape=[
            jax.ShapeDtypeStruct((rows // 2, width), F32),
            jax.ShapeDtypeStruct((rows // 2, width), BF),
        ],
        compiler_params=params(60, "arbitrary"),
        cost_estimate=cost(20 * rows * width, 16 * rows * width),
        name="input_back",
    )(tokens, grad_own, grad_sib, grad_middle, vec)


def finish_ff_kernel(place_ref, mine_ref, other_ref, fc1_ref, fc2_ref):
    first_core = lax.rem(place_ref[0], 2) == 0
    shard, ff = fc1_ref.shape
    half = ff // 2
    quarter = fc2_ref.shape[0] // 4
    width = fc2_ref.shape[1]
    owners = ff // (4 * quarter)
    mine = mine_ref[...].astype(F32)
    other = other_ref[...].astype(F32)
    cores = (jnp.where(first_core, mine, other), jnp.where(first_core, other, mine))
    pieces = []
    for owner in range(owners):
        for value in cores:
            for piece in range(2):
                start = (piece * owners + owner) * quarter
                pieces.append(value[:, start : start + quarter])
    fc1_ref[...] = jnp.concatenate(pieces, axis=1)
    for at, value in enumerate(cores):
        for piece in range(2):
            row = (2 * at + piece) * quarter
            start = half + piece * width
            fc2_ref[row : row + quarter, :] = value[:, start : start + width]


def finish_ff(place, mine, other, width, quarter):
    shard, wide = mine.shape
    return pl.pallas_call(
        finish_ff_kernel,
        grid=(1,),
        in_specs=[
            pl.BlockSpec(memory_space=pltpu.SMEM), whole(mine.shape), whole(other.shape)
        ],
        out_specs=[whole((shard, wide)), whole((4 * quarter, width))],
        out_shape=[
            jax.ShapeDtypeStruct((shard, wide), F32),
            jax.ShapeDtypeStruct((4 * quarter, width), F32),
        ],
        compiler_params=params(60, "arbitrary"),
        cost_estimate=cost(0, 12 * shard * wide),
        name="finish_ff",
    )(place, mine, other)


def finish_attend_kernel(place_ref, em_ref, eo_ref, lm_ref, lo_ref, qkv_ref, proj_ref, small_ref):
    first_core = lax.rem(place_ref[0], 2) == 0
    shard, width = proj_ref.shape
    part = width // 2
    late = lm_ref.shape[1] // 3
    early = part - late
    rows = lm_ref.shape[0] - shard
    lm = lm_ref[...].astype(F32)
    lo = lo_ref[...].astype(F32)
    small_ref[...] = lm[:rows] + lo[:rows]
    em = em_ref[...].astype(F32)
    eo = eo_ref[...].astype(F32)
    firsts = (jnp.where(first_core, em, eo), jnp.where(first_core, eo, em))
    lasts = (jnp.where(first_core, lm, lo)[rows:], jnp.where(first_core, lo, lm)[rows:])
    for at in range(3):
        for of in range(2):
            start = at * width + of * part
            qkv_ref[:, start : start + early] = firsts[of][:, at * early : (at + 1) * early]
            qkv_ref[:, start + early : start + part] = lasts[of][:, at * late : (at + 1) * late]
    for of in range(2):
        proj_ref[:, of * part : (of + 1) * part] = firsts[of][:, 3 * early :]


def finish_attend(place, early_mine, early_other, late_mine, late_other, width):
    shard = early_mine.shape[0]
    rows = late_mine.shape[0] - shard
    return pl.pallas_call(
        finish_attend_kernel,
        grid=(1,),
        in_specs=[pl.BlockSpec(memory_space=pltpu.SMEM)]
        + [whole(value.shape) for value in (early_mine, early_other, late_mine, late_other)],
        out_specs=[
            whole((shard, 3 * width)), whole((shard, width)), whole((rows, late_mine.shape[1]))
        ],
        out_shape=[
            jax.ShapeDtypeStruct((shard, 3 * width), F32),
            jax.ShapeDtypeStruct((shard, width), F32),
            jax.ShapeDtypeStruct((rows, late_mine.shape[1]), F32),
        ],
        compiler_params=params(60, "arbitrary"),
        cost_estimate=cost(0, 24 * shard * width),
        name="finish_attend",
    )(place, early_mine, early_other, late_mine, late_other)


def pack_kernel(place_ref, *refs):
    vectors, (qkv_ref, proj_ref, fc1_ref, fc2_ref, one_ref, two_ref) = refs[:-6], refs[-6:]
    first_core = lax.rem(place_ref[0], 2) == 0
    first_chip = place_ref[0] // 2 == 0
    shard, width = proj_ref.shape
    part = width // 2
    ff = fc1_ref.shape[1]
    owners = width // shard
    quarter = ff // owners // 4
    half = ff // 2
    one_ref[:VEC_ROWS, :] = jnp.zeros((VEC_ROWS, 3 * part), BF)
    for at, ref in enumerate(vectors):
        one_ref[at : at + 1, : ref.shape[1]] = ref[...]
    for at in range(3):
        low = qkv_ref[:, at * width : at * width + part]
        high = qkv_ref[:, at * width + part : (at + 1) * width]
        mine = jnp.where(first_core, low, high)
        mine = jnp.where(first_chip, mine[: shard // 2], mine[shard // 2 :])
        one_ref[VEC_ROWS:, at * part : (at + 1) * part] = mine
    two_ref[:, :part] = jnp.where(first_core, proj_ref[:, :part], proj_ref[:, part:])
    pieces_low, pieces_high = [], []
    for piece in range(2):
        for owner in range(owners):
            base = owner * 4 * quarter + piece * quarter
            pieces_low.append(fc1_ref[:, base : base + quarter])
            pieces_high.append(fc1_ref[:, base + 2 * quarter : base + 3 * quarter])
    two_ref[:, part : part + half] = jnp.where(
        first_core, jnp.concatenate(pieces_low, axis=1), jnp.concatenate(pieces_high, axis=1)
    )
    for piece in range(2):
        low = fc2_ref[piece * quarter : (piece + 1) * quarter, :]
        high = fc2_ref[(2 + piece) * quarter : (3 + piece) * quarter, :]
        start = part + half + piece * width
        two_ref[:, start : start + width] = jnp.where(first_core, low, high)


def pack_weights(place, vectors, qkv, proj, fc1, fc2):
    shard, width = proj.shape
    half = fc1.shape[1] // 2
    part = width // 2
    vectors = [vector.reshape(1, -1) for vector in vectors]
    values = (*vectors, qkv, proj, fc1, fc2)
    rows = VEC_ROWS + shard // 2
    return pl.pallas_call(
        pack_kernel,
        grid=(1,),
        in_specs=[pl.BlockSpec(memory_space=pltpu.SMEM)] + [whole(value.shape) for value in values],
        out_specs=[whole((rows, 3 * part)), whole((shard, 5 * part + half))],
        out_shape=[
            jax.ShapeDtypeStruct((rows, 3 * part), BF),
            jax.ShapeDtypeStruct((shard, 5 * part + half), BF),
        ],
        compiler_params=params(60, "arbitrary"),
        cost_estimate=cost(0, 5 * shard * width * 8),
        name="pack_weights",
    )(place, *values)


def project_kernel(tok_ref, w_ref, bias_ref, vec_ref, out_ref, out_t_ref, normed_ref):
    unit, _ = normalised(tok_ref[...].astype(F32))
    normed = (unit * vec_ref[0:1, :] + vec_ref[1:2, :]).astype(BF)
    normed_ref[...] = normed
    packed = dot(normed, w_ref[...]) + bias_ref[0:1, :]
    out_ref[...] = packed.astype(BF)
    out_t_ref[...] = packed.T.astype(BF)


def project(tokens, weight, bias, vec):
    rows, width = tokens.shape
    wide = weight.shape[1]
    bt = 512
    return pl.pallas_call(
        project_kernel,
        grid=(rows // bt,),
        in_specs=[
            pl.BlockSpec((bt, width), lambda i: (i, 0)),
            whole(weight.shape),
            whole(bias.shape),
            whole(vec.shape),
        ],
        out_specs=[
            pl.BlockSpec((bt, wide), lambda i: (i, 0)),
            pl.BlockSpec((wide, bt), lambda i: (0, i)),
            pl.BlockSpec((bt, width), lambda i: (i, 0)),
        ],
        out_shape=[
            jax.ShapeDtypeStruct((rows, wide), BF),
            jax.ShapeDtypeStruct((wide, rows), BF),
            jax.ShapeDtypeStruct((rows, width), BF),
        ],
        compiler_params=params(60, "arbitrary"),
        cost_estimate=cost(2 * rows * width * wide, 12 * rows * width),
        name="project",
    )(tokens, weight, bias, vec)


def exchange(value):
    return lax.all_to_all(value, "fsdp", split_axis=0, concat_axis=0, tiled=True)


def per_device(
    tokens,
    counts,
    norm1_gain,
    norm1_bias,
    qkv_weight,
    query_bias,
    value_bias,
    proj_weight,
    proj_bias,
    norm2_gain,
    norm2_bias,
    fc1_weight,
    fc1_bias,
    fc2_weight,
    fc2_bias,
    cotangent,
):
    images, slots, width = tokens.shape
    owners = lax.axis_size("fsdp")
    seq = lax.axis_size("seq")
    place = lax.axis_index("seq")
    core = lax.rem(place, 2)
    image = place // 2
    part = width // 2
    shard = width // owners
    ff = fc1_weight.shape[1]
    ff_shard = ff // owners
    quarter = ff_shard // 4
    half = ff // 2
    to_sibling = [(at, at ^ 1) for at in range(seq)]
    to_partner = [(at, at ^ 2) for at in range(seq)]

    def sibling(value):
        return lax.ppermute(value, "seq", to_sibling)

    def partner(value):
        return lax.ppermute(value, "seq", to_partner)

    def pick(value, at, axis):
        return lax.dynamic_index_in_dim(value, at, axis, keepdims=False)

    place_row = place.reshape(1).astype(jnp.int32)
    core_row = core.reshape(1).astype(jnp.int32)
    small = [
        norm1_gain, norm1_bias, query_bias, value_bias, proj_bias, norm2_gain, norm2_bias,
        fc2_bias, fc1_bias,
    ]
    one, two = pack_weights(
        place_row, small, qkv_weight, proj_weight, fc1_weight, fc2_weight
    )
    one, tokens, cotangent = lax.optimization_barrier((one, tokens, cotangent))
    mine_one = lax.all_gather(one, "fsdp", axis=0, tiled=False)
    def collect(value, theirs):
        mine = pick(value, image, 0)
        return jnp.concatenate([mine, theirs, sibling(mine), sibling(theirs)], axis=0)

    tok_came = partner(pick(tokens, 1 - image, 0))
    cot_came = partner(pick(cotangent, 1 - image, 0))
    mine_one, two, tok_came, cot_came = lax.optimization_barrier(
        (mine_one, two, tok_came, cot_came)
    )
    tok = collect(tokens, tok_came)
    cot = collect(cotangent, cot_came)
    second = lax.all_gather(two, "fsdp", axis=0, tiled=True)

    own_rows = mine_one[:, VEC_ROWS:]
    other_rows = partner(own_rows)
    w_qkv = jnp.where(
        image == 0,
        jnp.stack([own_rows, other_rows], axis=1),
        jnp.stack([other_rows, own_rows], axis=1),
    ).reshape(width, 3 * part)

    vecs = mine_one[:, :8, :shard].astype(F32).transpose(1, 0, 2).reshape(8, width)
    g1, b1, qb, vb, pb, g2, b2, f2b = vecs
    f1b = mine_one[:, 8, :ff_shard].astype(F32)
    f1b = pick(f1b.reshape(owners, 2, 2, quarter), core, 1)
    f1b = f1b.transpose(1, 0, 2).reshape(1, half)

    def mine_of(vector):
        return lax.dynamic_slice_in_dim(vector, core * part, part, 0)

    qkv_bias = jnp.concatenate([mine_of(qb), jnp.zeros((part,), F32), mine_of(vb)])
    vec_one = jnp.concatenate([jnp.stack([g1, b1]), jnp.zeros((6, width), F32)])
    packed, packed_t, normed = project(tok, w_qkv, qkv_bias.reshape(1, 3 * part), vec_one)
    packed, cot = lax.optimization_barrier((packed, cot))
    mixed, result_t, log_total = attend_forward(counts, place_row, packed, packed_t, slots)
    mixed_sib = sibling(mixed)

    wp_other = sibling(second[:, :part])
    vec_two = jnp.concatenate([jnp.stack([pb, g2, b2, f2b]), jnp.zeros((4, width), F32)])
    middle, out_own, out_send, gn_part, dw_ff, gf1, gf2, wp_own = feed_forward(
        core_row, tok, mixed, mixed_sib, cot, wp_other, second, vec_two, f1b
    )
    scattered_one = lax.psum_scatter(dw_ff, "fsdp", scatter_dimension=0, tiled=True)
    gn_sib = sibling(gn_part)
    rows_own = 2 * slots

    def hand_back(own, came):
        kept_part = own[:slots]
        came = came.astype(own.dtype)
        straight = jnp.stack([kept_part, came])
        crossed = jnp.stack([came, kept_part])
        return jnp.where(image == 0, straight, crossed)

    grad_middle, grad_mixed, grad_mixed_t, dwp_own, dwp_sib, vec_back = branch(
        core_row, middle, gn_part, gn_sib, cot, mixed, mixed_sib, wp_own, vec_two
    )
    dwp = jnp.where(
        core == 0,
        jnp.concatenate([dwp_own, dwp_sib], axis=0),
        jnp.concatenate([dwp_sib, dwp_own], axis=0),
    )
    grad_mixed, out_send, out_own = lax.optimization_barrier((grad_mixed, out_send, out_own))
    out_sib = sibling(out_send)
    early, late = 2, 1
    attend = functools.partial(attend_backward, counts, place_row, packed, packed_t)
    before = attend(grad_mixed, grad_mixed_t, result_t, log_total, slots, 0, early)
    before, out_sib = lax.optimization_barrier((before, out_sib))
    dw_early, qv_early = weight_grad(normed, *before)
    out_own = (out_own + out_sib.astype(F32)).astype(BF)
    block_one = jnp.concatenate([dw_early, dwp], axis=1).reshape(owners, shard, -1)
    grad_mixed, out_own, block_one = lax.optimization_barrier((grad_mixed, out_own, block_one))
    came_one = exchange(block_one)
    out_came = partner(out_own[slots:])
    grads = attend(grad_mixed, grad_mixed_t, result_t, log_total, slots, early, late)

    def total(came):
        return jnp.sum(came.astype(F32), axis=0).astype(BF)

    def join(value, came):
        return (value.astype(F32) + came.astype(F32)).astype(BF)

    scattered_one, came_one, out_came, grads = lax.optimization_barrier(
        (scattered_one, came_one, out_came, grads)
    )
    output = hand_back(out_own, out_came)
    one_came = partner(scattered_one)
    early_total = total(came_one)
    early_came = partner(early_total)
    one_sum = join(scattered_one, one_came)
    gn1_own, gn1_send, dw_late, vec_first, qv_late = project_back(tok, normed, before, grads, w_qkv)

    def spread(vector):
        both = jnp.zeros((2, part), F32)
        return lax.dynamic_update_index_in_dim(both, vector, core, 0).reshape(width)

    def rows_of(block):
        return jnp.sum(block.reshape(block.shape[0] // 8, 8, block.shape[1]), axis=1)

    once = (core == 0).astype(F32)
    gg1, gb1 = rows_of(vec_first)
    gqb, gvb = rows_of(jnp.concatenate([qv_early, qv_late], axis=1))
    gg2, gb2, gpb = rows_of(vec_back) * once
    gf2b = jnp.sum(gf2, axis=0) * once
    gf1b = jnp.sum(gf1, axis=0).reshape(2, owners, quarter).transpose(1, 0, 2)
    gf1b = lax.dynamic_update_index_in_dim(
        jnp.zeros((owners, 2, 2, quarter), F32), gf1b, core, 1
    ).reshape(owners, ff_shard)
    late_wide = 3 * late * PAIR
    small_grads = jnp.stack(
        [gg1, gb1, spread(gqb), spread(gvb), gpb, gg2, gb2, gf2b]
    ).reshape(8, owners, shard).transpose(1, 0, 2)
    small_block = jnp.concatenate(
        [
            jnp.pad(small_grads, ((0, 0), (0, 0), (0, late_wide - shard))),
            jnp.pad(gf1b[:, None], ((0, 0), (0, VEC_ROWS - 9), (0, late_wide - ff_shard))),
        ],
        axis=1,
    ).astype(BF)
    block_two = jnp.concatenate(
        [small_block, dw_late.reshape(owners, shard, late_wide)], axis=1
    )
    gn1_sib = sibling(gn1_send)
    came_two = exchange(block_two)
    input_own, input_send = input_back(tok, gn1_own, gn1_sib, grad_middle, vec_one)
    input_came = partner(input_send)
    came_two, input_own, one_sum = lax.optimization_barrier((came_two, input_own, one_sum))
    one_other = sibling(one_sum)
    input_grad = hand_back(input_own, input_came)

    grad_fc1, grad_fc2 = finish_ff(place_row, one_sum, one_other, width, quarter)
    early_sum = join(early_total, early_came)
    early_other = sibling(early_sum)
    late_total = total(came_two)
    late_sum = join(late_total, partner(late_total))
    late_other = sibling(late_sum)
    grad_qkv, grad_proj, small_sum = finish_attend(
        place_row, early_sum, early_other, late_sum, late_other, width
    )
    s = [small_sum[at, :shard] for at in range(8)]
    grad_f1b = small_sum[8, :ff_shard]
    return (
        output,
        input_grad,
        s[0],
        s[1],
        grad_qkv,
        s[2],
        s[3],
        grad_proj,
        s[4],
        s[5],
        s[6],
        grad_fc1,
        grad_f1b,
        grad_fc2,
        s[7],
    )


def solution(mesh):
    placed = (
        P("fsdp", "seq", None),
        P("fsdp", None),
        P("fsdp"),
        P("fsdp"),
        P("fsdp", None),
        P("fsdp"),
        P("fsdp"),
        P("fsdp", None),
        P("fsdp"),
        P("fsdp"),
        P("fsdp"),
        P("fsdp", None),
        P("fsdp"),
        P("fsdp", None),
        P("fsdp"),
        P("fsdp", "seq", None),
    )
    return jax.shard_map(
        per_device,
        mesh=mesh,
        in_specs=placed,
        out_specs=(
            P("fsdp", "seq", None),
            P("fsdp", "seq", None),
            P("fsdp"),
            P("fsdp"),
            P("fsdp", None),
            P("fsdp"),
            P("fsdp"),
            P("fsdp", None),
            P("fsdp"),
            P("fsdp"),
            P("fsdp"),
            P("fsdp", None),
            P("fsdp"),
            P("fsdp", None),
            P("fsdp"),
        ),
        check_vma=False,
    )
```

```python
import functools

import jax
import jax.numpy as jnp
from jax import lax
from jax.experimental import pallas as pl
from jax.experimental.pallas import tpu as pltpu
from jax.sharding import PartitionSpec as P

HEADS = 12
HEAD_DIM = 64
EPSILON = 1e-06
MASKED = -1e30
BF = jnp.bfloat16
F32 = jnp.float32
MIB = 1024 * 1024
PAIR = 2 * HEAD_DIM
VEC_ROWS = 16
SLOT_ORDER = (0, 2, 1, 3)


def params(mebibytes, *semantics):
    return pltpu.CompilerParams(
        dimension_semantics=semantics, vmem_limit_bytes=mebibytes * MIB
    )


def dot(left, right, left_dim=1, right_dim=0):
    return lax.dot_general(
        left, right, (((left_dim,), (right_dim,)), ((), ())), preferred_element_type=F32
    )


def cost(flops, bytes_accessed, transcendentals=0):
    return pl.CostEstimate(
        flops=int(flops), bytes_accessed=int(bytes_accessed), transcendentals=int(transcendentals)
    )


def whole(shape):
    return pl.BlockSpec(shape, lambda *_: tuple(0 for _ in shape))


def key_bias(counts_ref, place_ref, keys, slots):
    row = lax.broadcasted_iota(jnp.int32, (slots, PAIR), 0)
    place = place_ref[0]
    parts = []
    for flip in SLOT_ORDER:
        kept = counts_ref[place // 2, jnp.bitwise_xor(place, flip)]
        parts.append(jnp.where(row < kept, 0.0, MASKED).astype(F32))
    return jnp.concatenate(parts, axis=0)


def augment_keys(pair, bias, which, ones):
    lane = lax.broadcasted_iota(jnp.int32, pair.shape, 1)
    mine = (lane < HEAD_DIM) if which == 0 else (lane >= HEAD_DIM)
    start = HEAD_DIM if which == 0 else 0
    extra = jnp.where(
        lane == start, bias, jnp.where((lane > start) & (lane <= start + ones), 1.0, 0.0)
    )
    return jnp.where(mine, pair.astype(F32), extra).astype(BF)


def augment_values(pair, which, ones):
    lane = lax.broadcasted_iota(jnp.int32, pair.shape, 1)
    mine = (lane < HEAD_DIM) if which == 0 else (lane >= HEAD_DIM)
    start = HEAD_DIM if which == 0 else 0
    extra = jnp.where((lane >= start) & (lane < start + ones), 1.0, 0.0)
    return jnp.where(mine, pair.astype(F32), extra).astype(BF)


def pieces(value):
    first = value.astype(BF).astype(F32)
    rest = value - first
    second = rest.astype(BF).astype(F32)
    return first, second, rest - second


def extra_rows(rows, width):
    place = lax.broadcasted_iota(jnp.int32, (HEAD_DIM, width), 0)
    out = jnp.zeros((HEAD_DIM, width), F32)
    for at, row in enumerate(rows):
        out = jnp.where(place == at, row, out)
    return out.astype(BF)


def place_rows(head, extra, which):
    return jnp.concatenate([head, extra] if which == 0 else [extra, head], axis=0)


def attend_forward_kernel(
    slots, bq, chunk, counts_ref, place_ref, k_ref, qt_ref, vt_ref, mixed_ref, ot_ref, lse_ref,
    kaug, vaug, s_a, s_b, m_a, m_b
):
    keys = k_ref.shape[0]
    step = pl.program_id(1)
    steps = pl.num_programs(1)
    scores = (s_a, s_b)
    peaks = (m_a, m_b)
    ones_row = extra_rows([jnp.ones((1, bq), F32)], bq)

    @pl.when(step == 0)
    def _():
        bias = key_bias(counts_ref, place_ref, keys, slots)
        ones = jnp.ones((16, keys), BF)
        for which in range(2):
            kaug[which] = augment_keys(k_ref[...], bias, which, 0)
            vaug[which] = jnp.concatenate(
                [vt_ref[which * HEAD_DIM : (which + 1) * HEAD_DIM, :], ones], axis=0
            )

    def query_block(at, which):
        head = qt_ref[which * HEAD_DIM : (which + 1) * HEAD_DIM, pl.ds(at * bq, bq)]
        head = (head.astype(F32) * HEAD_DIM ** (-0.5)).astype(BF)
        return place_rows(head, ones_row, which)

    def score_chunk(query, which, at, peak):
        rows = slice(at * chunk, (at + 1) * chunk)
        s = dot(kaug[which, rows, :], query)
        scores[which][rows, :] = s
        top = jnp.max(s.reshape(chunk // 8, 8, bq), axis=0)
        return top if peak is None else jnp.maximum(peak, top)

    def raise_chunk(which, at, peak):
        rows = slice(at * chunk, (at + 1) * chunk)
        return jnp.exp(scores[which][rows, :] - peak).astype(BF)

    def weigh_chunk(which, at, p, total):
        o = dot(vaug[which, :, at * chunk : (at + 1) * chunk], p)
        return o if total is None else total + o

    @pl.when(step == 0)
    def _():
        query = query_block(0, 0)
        peak = None
        for at in range(keys // chunk):
            peak = score_chunk(query, 0, at, peak)
        m_a[...] = peak

    later = jnp.minimum(step + 1, steps - 1)
    outs = []
    for which in range(2):
        other = 1 - which
        query = query_block(step if which == 0 else later, other)
        peak = jnp.max(peaks[which][...], axis=0, keepdims=True)
        next_peak, total, behind = None, None, None
        for at in range(keys // chunk):
            next_peak = score_chunk(query, other, at, next_peak)
            if behind is not None:
                total = weigh_chunk(which, at - 1, behind, total)
            behind = raise_chunk(which, at, peak)
        total = weigh_chunk(which, keys // chunk - 1, behind, total)
        peaks[other][...] = next_peak
        norm = total[HEAD_DIM : HEAD_DIM + 1, :]
        outs.append(total[:HEAD_DIM, :] * (1.0 / norm))
        lse_ref[0, which : which + 1, :] = peak + jnp.log(norm)
    both = jnp.concatenate(outs, axis=0)
    ot_ref[...] = both
    mixed_ref[...] = both.T.astype(BF)


def attend_forward(counts, place, packed, packed_t, slots):
    keys, width = packed.shape
    width //= 3
    pairs = width // PAIR
    bq, chunk = 256, 256
    kernel = functools.partial(attend_forward_kernel, slots, bq, chunk)
    return pl.pallas_call(
        kernel,
        grid=(pairs, keys // bq),
        in_specs=[
            pl.BlockSpec(memory_space=pltpu.SMEM),
            pl.BlockSpec(memory_space=pltpu.SMEM),
            pl.BlockSpec((keys, PAIR), lambda p, i: (0, pairs + p)),
            pl.BlockSpec((PAIR, keys), lambda p, i: (p, 0)),
            pl.BlockSpec((PAIR, keys), lambda p, i: (2 * pairs + p, 0)),
        ],
        out_specs=[
            pl.BlockSpec((bq, PAIR), lambda p, i: (i, p)),
            pl.BlockSpec((PAIR, bq), lambda p, i: (p, i)),
            pl.BlockSpec((1, 8, bq), lambda p, i: (p, 0, i)),
        ],
        out_shape=[
            jax.ShapeDtypeStruct((keys, width), BF),
            jax.ShapeDtypeStruct((width, keys), F32),
            jax.ShapeDtypeStruct((pairs, 8, keys), F32),
        ],
        scratch_shapes=[
            pltpu.VMEM((2, keys, PAIR), BF),
            pltpu.VMEM((2, HEAD_DIM + 16, keys), BF),
            pltpu.VMEM((keys, bq), F32),
            pltpu.VMEM((keys, bq), F32),
            pltpu.VMEM((8, bq), F32),
            pltpu.VMEM((8, bq), F32),
        ],
        compiler_params=params(60, "arbitrary", "arbitrary"),
        cost_estimate=cost(
            2 * pairs * 2 * 2 * keys * keys * 256, 12 * keys * width, 2 * pairs * keys * keys
        ),
        name="attend_forward",
    )(counts, place, packed, packed_t, packed_t)


def attend_backward_kernel(
    slots, bq, chunk, counts_ref, place_ref, q_ref, k_ref, v_ref, qt_ref, kt_ref, do_ref, dot_ref, ot_ref,
    lse_ref, gq_ref, gk_ref, gv_ref, kaug, vaug, acc_k, acc_v
):
    keys = k_ref.shape[0]
    step = pl.program_id(1)
    steps = pl.num_programs(1)
    scale = HEAD_DIM ** (-0.5)

    @pl.when(step == 0)
    def _():
        bias = key_bias(counts_ref, place_ref, keys, slots)
        for which in range(2):
            kaug[which] = augment_keys(k_ref[...], bias, which, 3)
            vaug[which] = augment_values(v_ref[...], which, 3)
        acc_k[...] = jnp.zeros_like(acc_k)
        acc_v[...] = jnp.zeros_like(acc_v)

    ones_row = jnp.ones((1, bq), F32)
    queries, grads = [], []
    for which in range(2):
        rows = slice(which * HEAD_DIM, (which + 1) * HEAD_DIM)
        head = (qt_ref[rows, :].astype(F32) * scale).astype(BF)
        log_total = lse_ref[0, which : which + 1, :]
        queries.append(
            place_rows(head, extra_rows([ones_row, *pieces(-log_total)], bq), which)
        )
        grad = dot_ref[rows, :]
        delta = jnp.sum(grad.astype(F32) * ot_ref[rows, :], axis=0, keepdims=True)
        grads.append(place_rows(grad, extra_rows(list(pieces(-delta)), bq), which))

    do_pair = do_ref[...]
    q_pair = q_ref[...]
    totals = [None, None]
    units = [(at, which) for at in range(keys // chunk) for which in range(2)]

    def front(at, which):
        rows = slice(at * chunk, (at + 1) * chunk)
        return dot(kaug[which, rows, :], queries[which]), dot(vaug[which, rows, :], grads[which])

    ahead = front(*units[0])
    behind = None
    for unit in range(len(units) + 1):
        now = ahead
        if unit + 1 < len(units):
            ahead = front(*units[unit + 1])
        if behind is not None:
            at, which = units[unit - 1]
            rows = slice(at * chunk, (at + 1) * chunk)
            p_low, ds = behind
            acc_v[which, rows, :] += dot(p_low, do_pair)
            acc_k[which, rows, :] += dot(ds, q_pair)
            part = dot(kt_ref[which * HEAD_DIM : (which + 1) * HEAD_DIM, rows], ds)
            totals[which] = part if totals[which] is None else totals[which] + part
        if unit < len(units):
            p = jnp.exp(now[0])
            behind = p.astype(BF), (p * now[1]).astype(BF)
    both = jnp.concatenate(totals, axis=0) * scale
    gq_ref[...] = both.T.astype(BF)

    @pl.when(step == steps - 1)
    def _():
        lane = lax.broadcasted_iota(jnp.int32, (keys, PAIR), 1)
        gk_ref[...] = (jnp.where(lane < HEAD_DIM, acc_k[0], acc_k[1]) * scale).astype(BF)
        gv_ref[...] = jnp.where(lane < HEAD_DIM, acc_v[0], acc_v[1]).astype(BF)


def attend_backward(
    counts, place, packed, packed_t, grad, grad_t, result_t, log_total, slots, start, count
):
    keys, width = packed.shape
    width //= 3
    pairs = width // PAIR
    bq, chunk = 512, 256
    kernel = functools.partial(attend_backward_kernel, slots, bq, chunk)
    at = lambda p: p + start
    return pl.pallas_call(
        kernel,
        grid=(count, keys // bq),
        in_specs=[
            pl.BlockSpec(memory_space=pltpu.SMEM),
            pl.BlockSpec(memory_space=pltpu.SMEM),
            pl.BlockSpec((bq, PAIR), lambda p, i: (i, at(p))),
            pl.BlockSpec((keys, PAIR), lambda p, i: (0, pairs + at(p))),
            pl.BlockSpec((keys, PAIR), lambda p, i: (0, 2 * pairs + at(p))),
            pl.BlockSpec((PAIR, bq), lambda p, i: (at(p), i)),
            pl.BlockSpec((PAIR, keys), lambda p, i: (pairs + at(p), 0)),
            pl.BlockSpec((bq, PAIR), lambda p, i: (i, at(p))),
            pl.BlockSpec((PAIR, bq), lambda p, i: (at(p), i)),
            pl.BlockSpec((PAIR, bq), lambda p, i: (at(p), i)),
            pl.BlockSpec((1, 8, bq), lambda p, i: (at(p), 0, i)),
        ],
        out_specs=[
            pl.BlockSpec((bq, PAIR), lambda p, i: (i, p)),
            pl.BlockSpec((keys, PAIR), lambda p, i: (0, p)),
            pl.BlockSpec((keys, PAIR), lambda p, i: (0, p)),
        ],
        out_shape=[jax.ShapeDtypeStruct((keys, count * PAIR), BF)] * 3,
        scratch_shapes=[
            pltpu.VMEM((2, keys, PAIR), BF),
            pltpu.VMEM((2, keys, PAIR), BF),
            pltpu.VMEM((2, keys, PAIR), F32),
            pltpu.VMEM((2, keys, PAIR), F32),
        ],
        compiler_params=params(60, "arbitrary", "arbitrary"),
        cost_estimate=cost(
            2 * count * 5 * 2 * keys * keys * 256, 24 * keys * count * PAIR,
            2 * count * keys * keys,
        ),
        name="attend_backward",
    )(counts, place, packed, packed, packed, packed_t, packed_t, grad, grad_t, result_t, log_total)


def normalised(values):
    centred = values - jnp.mean(values, axis=-1, keepdims=True)
    variance = jnp.mean(centred * centred, axis=-1, keepdims=True)
    inverse = lax.rsqrt(variance + EPSILON)
    return centred * inverse, inverse


def norm_pull(grad, gain, unit, inverse):
    scaled = grad * gain
    mean = jnp.mean(scaled, axis=-1, keepdims=True)
    along = jnp.mean(scaled * unit, axis=-1, keepdims=True)
    return inverse * (scaled - mean - unit * along)


def fold(values):
    return jnp.sum(values.reshape(values.shape[0] // 8, 8, values.shape[1]), axis=0)


def feed_forward_kernel(
    chunk, core_ref, tok_ref, mo_ref, ms_ref, cot_ref, wpx_ref, g2_ref, vec_ref, f1b_ref,
    mid_ref, out_ref, send_ref, gn_ref, dw_ref, gf1_ref, gf2_ref, wpo_ref, acc1, acc2, accb, accc, wps_ref
):
    step = pl.program_id(0)
    steps = pl.num_programs(0)
    width = tok_ref.shape[1]
    half = f1b_ref.shape[1]
    part = width // 2

    @pl.when(step == 0)
    def _():
        acc1[...] = jnp.zeros_like(acc1)
        acc2[...] = jnp.zeros_like(acc2)
        accb[...] = jnp.zeros_like(accb)
        accc[...] = jnp.zeros_like(accc)
        here = pl.ds(pl.multiple_of(core_ref[0] * part, part), part)
        there = pl.ds(pl.multiple_of((1 - core_ref[0]) * part, part), part)
        wpo_ref[:, here] = g2_ref[here, :part]
        wpo_ref[:, there] = wpx_ref[here, :]
        wps_ref[:, here] = g2_ref[there, :part]
        wps_ref[:, there] = wpx_ref[there, :]

    middle = (
        tok_ref[...].astype(F32)
        + dot(mo_ref[...], wpo_ref[...])
        + dot(ms_ref[...], wps_ref[...])
        + vec_ref[0:1, :]
    )
    mid_ref[...] = middle
    unit, _ = normalised(middle)
    normed = (unit * vec_ref[1:2, :] + vec_ref[2:3, :]).astype(BF)
    normed_t = normed.T
    cot = cot_ref[...]
    out = None
    grad = None

    def weights(at):
        w1 = g2_ref[:, part + at * chunk : part + (at + 1) * chunk]
        piece, row = divmod(at * chunk, width)
        start = part + half + piece * width
        return w1, g2_ref[row : row + chunk, start : start + width]

    def front(at):
        w1, w2 = weights(at)
        hidden = dot(normed, w1) + f1b_ref[0:1, at * chunk : (at + 1) * chunk]
        return hidden, dot(cot, w2, 1, 1)

    def middle_part(hidden, grad_active):
        below = 0.5 + 0.5 * lax.erf(hidden * (0.5**0.5))
        slope = below + hidden * (jnp.exp(hidden * hidden * -0.5) * 0.3989422804014327)
        return (hidden * below).astype(BF), (grad_active * slope).astype(BF)

    chunks = half // chunk
    ahead = front(0)
    behind = None
    for at in range(chunks + 1):
        now = ahead
        if at + 1 < chunks:
            ahead = front(at + 1)
        if behind is not None:
            active, grad_hidden = behind
            cols = slice((at - 1) * chunk, at * chunk)
            w1, w2 = weights(at - 1)
            more = dot(active, w2)
            out = more if out is None else out + more
            more = dot(grad_hidden, w1, 1, 1)
            grad = more if grad is None else grad + more
            acc1[:, cols] += dot(normed_t, grad_hidden)
            acc2[cols, :] += dot(active, cot, 0, 0)
            accb[:, cols] += fold(grad_hidden.astype(F32))
        if at < chunks:
            behind = middle_part(*now)
    accc[...] += fold(cot.astype(F32))
    gn_ref[...] = grad.astype(BF)

    @pl.when(step < steps // 2)
    def _():
        out_ref[...] = middle + out + vec_ref[3:4, :]

    @pl.when(step >= steps // 2)
    def _():
        send_ref[...] = out.astype(BF)

    @pl.when(step == steps - 1)
    def _():
        dw_ref[:, :half] = acc1[...].astype(BF)
        for piece in range(half // width):
            dw_ref[:, half + piece * width : half + (piece + 1) * width] = acc2[
                piece * width : (piece + 1) * width, :
            ].astype(BF)
        gf1_ref[...] = accb[...]
        gf2_ref[...] = accc[...]


def feed_forward(core, tokens, mixed_own, mixed_sib, cot, wp_other, weights, vec, f1b):
    rows, width = tokens.shape
    half = f1b.shape[1]
    heads = mixed_own.shape[1]
    bt, chunk = 512, 384
    blocks = rows // bt
    kernel = functools.partial(feed_forward_kernel, chunk)
    return pl.pallas_call(
        kernel,
        grid=(blocks,),
        in_specs=[
            pl.BlockSpec(memory_space=pltpu.SMEM),
            pl.BlockSpec((bt, width), lambda i: (i, 0)),
            pl.BlockSpec((bt, heads), lambda i: (i, 0)),
            pl.BlockSpec((bt, heads), lambda i: (lax.rem(i + blocks // 2, blocks), 0)),
            pl.BlockSpec((bt, width), lambda i: (i, 0)),
            whole(wp_other.shape),
            whole(weights.shape),
            whole(vec.shape),
            whole(f1b.shape),
        ],
        out_specs=[
            pl.BlockSpec((bt, width), lambda i: (i, 0)),
            pl.BlockSpec((bt, width), lambda i: (jnp.minimum(i, blocks // 2 - 1), 0)),
            pl.BlockSpec((bt, width), lambda i: (jnp.maximum(i - blocks // 2, 0), 0)),
            pl.BlockSpec((bt, width), lambda i: (i, 0)),
            whole((width, 2 * half)),
            whole((8, half)),
            whole((8, width)),
            whole((width // 2, width)),
        ],
        out_shape=[
            jax.ShapeDtypeStruct((rows, width), F32),
            jax.ShapeDtypeStruct((rows // 2, width), F32),
            jax.ShapeDtypeStruct((rows // 2, width), BF),
            jax.ShapeDtypeStruct((rows, width), BF),
            jax.ShapeDtypeStruct((width, 2 * half), BF),
            jax.ShapeDtypeStruct((8, half), F32),
            jax.ShapeDtypeStruct((8, width), F32),
            jax.ShapeDtypeStruct((width // 2, width), BF),
        ],
        scratch_shapes=[
            pltpu.VMEM((width, half), F32),
            pltpu.VMEM((half, width), F32),
            pltpu.VMEM((8, half), F32),
            pltpu.VMEM((8, width), F32),
            pltpu.VMEM((width // 2, width), BF),
        ],
        compiler_params=params(60, "arbitrary"),
        cost_estimate=cost(
            2 * rows * width * (6 * half + width), 20 * rows * width + 8 * width * half,
            2 * rows * half,
        ),
        name="feed_forward",
    )(core, tokens, mixed_own, mixed_sib, cot, wp_other, weights, vec, f1b)


def branch_kernel(
    core_ref, mid_ref, ga_ref, gb_ref, cot_ref, mo_ref, ms_ref, wpo_ref, vec_ref,
    gm_ref, do_ref, dot_ref, dwo_ref, dws_ref, vecs_ref, acco, accs, accv, low_ref
):
    step = pl.program_id(0)
    steps = pl.num_programs(0)
    half = do_ref.shape[1]

    @pl.when(step == 0)
    def _():
        acco[...] = jnp.zeros_like(acco)
        accs[...] = jnp.zeros_like(accs)
        accv[...] = jnp.zeros_like(accv)

    unit, inverse = normalised(mid_ref[...])
    grad = ga_ref[...].astype(F32) + gb_ref[...].astype(F32)
    accv[0:8, :] += fold(grad * unit)
    accv[8:16, :] += fold(grad)
    grad_middle = cot_ref[...].astype(F32) + norm_pull(grad, vec_ref[1:2, :], unit, inverse)

    @pl.when(step < steps // 2)
    def _():
        gm_ref[...] = grad_middle

    low = grad_middle.astype(BF)
    low_ref[...] = low
    accv[16:24, :] += fold(low.astype(F32))
    do_ref[...] = dot(low, wpo_ref[...], 1, 1).astype(BF)
    dot_ref[...] = dot(wpo_ref[...], low, 1, 1).astype(BF)
    mine = low_ref[:, pl.ds(pl.multiple_of(core_ref[0] * half, half), half)]
    acco[...] += dot(mo_ref[...], mine, 0, 0)
    accs[...] += dot(ms_ref[...], mine, 0, 0)

    @pl.when(step == steps - 1)
    def _():
        dwo_ref[...] = acco[...].astype(BF)
        dws_ref[...] = accs[...].astype(BF)
        vecs_ref[...] = accv[...]


def branch(core, middle, grad_own, grad_sib, cot, mixed_own, mixed_sib, wp_own, vec):
    rows, width = middle.shape
    half = mixed_own.shape[1]
    bt = 512
    blocks = rows // bt
    swap = lambda i: (lax.rem(i + blocks // 2, blocks), 0)
    straight = lambda i: (i, 0)
    return pl.pallas_call(
        branch_kernel,
        grid=(blocks,),
        in_specs=[
            pl.BlockSpec(memory_space=pltpu.SMEM),
            pl.BlockSpec((bt, width), straight),
            pl.BlockSpec((bt, width), straight),
            pl.BlockSpec((bt, width), swap),
            pl.BlockSpec((bt, width), straight),
            pl.BlockSpec((bt, half), straight),
            pl.BlockSpec((bt, half), swap),
            whole(wp_own.shape),
            whole(vec.shape),
        ],
        out_specs=[
            pl.BlockSpec((bt, width), lambda i: (jnp.minimum(i, blocks // 2 - 1), 0)),
            pl.BlockSpec((bt, half), straight),
            pl.BlockSpec((half, bt), lambda i: (0, i)),
            whole((half, half)),
            whole((half, half)),
            whole((24, width)),
        ],
        out_shape=[
            jax.ShapeDtypeStruct((rows // 2, width), F32),
            jax.ShapeDtypeStruct((rows, half), BF),
            jax.ShapeDtypeStruct((half, rows), BF),
            jax.ShapeDtypeStruct((half, half), BF),
            jax.ShapeDtypeStruct((half, half), BF),
            jax.ShapeDtypeStruct((24, width), F32),
        ],
        scratch_shapes=[
            pltpu.VMEM((half, half), F32),
            pltpu.VMEM((half, half), F32),
            pltpu.VMEM((24, width), F32),
            pltpu.VMEM((bt, width), BF),
        ],
        compiler_params=params(60, "arbitrary"),
        cost_estimate=cost(2 * rows * width * 3 * half, 18 * rows * width),
        name="branch",
    )(core, middle, grad_own, grad_sib, cot, mixed_own, mixed_sib, wp_own, vec)


def weight_grad_kernel(normed_ref, gq_ref, gk_ref, gv_ref, dw_ref, qv_ref, accw, accqv):
    step = pl.program_id(0)
    steps = pl.num_programs(0)
    part = gq_ref.shape[1]

    @pl.when(step == 0)
    def _():
        accw[...] = jnp.zeros_like(accw)
        accqv[...] = jnp.zeros_like(accqv)

    normed_t = normed_ref[...].T
    for at, ref in enumerate((gq_ref, gk_ref, gv_ref)):
        cols = slice(at * part, (at + 1) * part)
        value = ref[...]
        accw[:, cols] += dot(normed_t, value)
        if at != 1:
            here = 0 if at == 0 else 8
            accqv[here : here + 8, :] += fold(value.astype(F32))

    @pl.when(step == steps - 1)
    def _():
        dw_ref[...] = accw[...].astype(BF)
        qv_ref[...] = accqv[...]


def weight_grad(normed, gq, gk, gv):
    rows, width = normed.shape
    part = gq.shape[1]
    bt = 512
    straight = lambda i: (i, 0)
    return pl.pallas_call(
        weight_grad_kernel,
        grid=(rows // bt,),
        in_specs=[
            pl.BlockSpec((bt, width), straight),
            pl.BlockSpec((bt, part), straight),
            pl.BlockSpec((bt, part), straight),
            pl.BlockSpec((bt, part), straight),
        ],
        out_specs=[whole((width, 3 * part)), whole((16, part))],
        out_shape=[
            jax.ShapeDtypeStruct((width, 3 * part), BF),
            jax.ShapeDtypeStruct((16, part), F32),
        ],
        scratch_shapes=[pltpu.VMEM((width, 3 * part), F32), pltpu.VMEM((16, part), F32)],
        compiler_params=params(60, "arbitrary"),
        cost_estimate=cost(2 * rows * width * 3 * part, 2 * rows * (width + 3 * part)),
        name="weight_grad",
    )(normed, gq, gk, gv)


def project_back_kernel(
    tok_ref, normed_ref, gqa_ref, gka_ref, gva_ref, gq_ref, gk_ref, gv_ref, w_ref,
    own_ref, sib_ref, dw_ref, vecs_ref, qv_ref, accw, accv, accqv
):
    step = pl.program_id(0)
    steps = pl.num_programs(0)
    early = gqa_ref.shape[1]
    part = gq_ref.shape[1]
    wide = early + part

    @pl.when(step == 0)
    def _():
        accw[...] = jnp.zeros_like(accw)
        accv[...] = jnp.zeros_like(accv)
        accqv[...] = jnp.zeros_like(accqv)

    unit, _ = normalised(tok_ref[...].astype(F32))
    normed_t = normed_ref[...].T
    grad = None
    before = (gqa_ref, gka_ref, gva_ref)
    for at, ref in enumerate((gq_ref, gk_ref, gv_ref)):
        cols = slice(at * part, (at + 1) * part)
        value = ref[...]
        more = dot(
            jnp.concatenate([before[at][...], value], axis=1),
            w_ref[:, at * wide : (at + 1) * wide], 1, 1,
        )
        grad = more if grad is None else grad + more
        accw[:, cols] += dot(normed_t, value)
        if at != 1:
            here = 0 if at == 0 else 8
            accqv[here : here + 8, :] += fold(value.astype(F32))
    accv[0:8, :] += fold(grad * unit)
    accv[8:16, :] += fold(grad)

    @pl.when(step < steps // 2)
    def _():
        own_ref[...] = grad

    @pl.when(step >= steps // 2)
    def _():
        sib_ref[...] = grad.astype(BF)

    @pl.when(step == steps - 1)
    def _():
        dw_ref[...] = accw[...].astype(BF)
        vecs_ref[...] = accv[...]
        qv_ref[...] = accqv[...]


def project_back(tokens, normed, before, grads, weight):
    rows, width = tokens.shape
    early, part = before[0].shape[1], grads[0].shape[1]
    bt = 512
    blocks = rows // bt
    straight = lambda i: (i, 0)
    return pl.pallas_call(
        project_back_kernel,
        grid=(blocks,),
        in_specs=[pl.BlockSpec((bt, width), straight)] * 2
        + [pl.BlockSpec((bt, early), straight)] * 3
        + [pl.BlockSpec((bt, part), straight)] * 3
        + [whole(weight.shape)],
        out_specs=[
            pl.BlockSpec((bt, width), lambda i: (jnp.minimum(i, blocks // 2 - 1), 0)),
            pl.BlockSpec((bt, width), lambda i: (jnp.maximum(i - blocks // 2, 0), 0)),
            whole((width, 3 * part)),
            whole((16, width)),
            whole((16, part)),
        ],
        out_shape=[
            jax.ShapeDtypeStruct((rows // 2, width), F32),
            jax.ShapeDtypeStruct((rows // 2, width), BF),
            jax.ShapeDtypeStruct((width, 3 * part), BF),
            jax.ShapeDtypeStruct((16, width), F32),
            jax.ShapeDtypeStruct((16, part), F32),
        ],
        scratch_shapes=[
            pltpu.VMEM((width, 3 * part), F32),
            pltpu.VMEM((16, width), F32),
            pltpu.VMEM((16, part), F32),
        ],
        compiler_params=params(60, "arbitrary"),
        cost_estimate=cost(2 * rows * width * (6 * part + 3 * early), 14 * rows * width),
        name="project_back",
    )(tokens, normed, *before, *grads, weight)


def input_back_kernel(tok_ref, own_ref, sib_ref, gm_ref, vec_ref, keep_ref, send_ref):
    unit, inverse = normalised(tok_ref[...].astype(F32))
    grad = own_ref[...] + sib_ref[...].astype(F32)
    total = gm_ref[...] + norm_pull(grad, vec_ref[0:1, :], unit, inverse)
    step = pl.program_id(0)
    steps = pl.num_programs(0)

    @pl.when(step < steps // 2)
    def _():
        keep_ref[...] = total

    @pl.when(step >= steps // 2)
    def _():
        send_ref[...] = total.astype(BF)


def input_back(tokens, grad_own, grad_sib, grad_middle, vec):
    rows, width = grad_own.shape
    bt = 256
    blocks = rows // bt
    straight = lambda i: (i, 0)
    return pl.pallas_call(
        input_back_kernel,
        grid=(blocks,),
        in_specs=[pl.BlockSpec((bt, width), straight)] * 4 + [whole(vec.shape)],
        out_specs=[
            pl.BlockSpec((bt, width), lambda i: (jnp.minimum(i, blocks // 2 - 1), 0)),
            pl.BlockSpec((bt, width), lambda i: (jnp.maximum(i - blocks // 2, 0), 0)),
        ],
        out_shape=[
            jax.ShapeDtypeStruct((rows // 2, width), F32),
            jax.ShapeDtypeStruct((rows // 2, width), BF),
        ],
        compiler_params=params(60, "arbitrary"),
        cost_estimate=cost(20 * rows * width, 16 * rows * width),
        name="input_back",
    )(tokens, grad_own, grad_sib, grad_middle, vec)


def finish_ff_kernel(place_ref, mine_ref, other_ref, fc1_ref, fc2_ref):
    first_core = lax.rem(place_ref[0], 2) == 0
    shard, ff = fc1_ref.shape
    half = ff // 2
    quarter = fc2_ref.shape[0] // 4
    width = fc2_ref.shape[1]
    owners = ff // (4 * quarter)
    mine = mine_ref[...].astype(F32)
    other = other_ref[...].astype(F32)
    cores = (jnp.where(first_core, mine, other), jnp.where(first_core, other, mine))
    pieces = []
    for owner in range(owners):
        for value in cores:
            for piece in range(2):
                start = (piece * owners + owner) * quarter
                pieces.append(value[:, start : start + quarter])
    fc1_ref[...] = jnp.concatenate(pieces, axis=1)
    for at, value in enumerate(cores):
        for piece in range(2):
            row = (2 * at + piece) * quarter
            start = half + piece * width
            fc2_ref[row : row + quarter, :] = value[:, start : start + width]


def finish_ff(place, mine, other, width, quarter):
    shard, wide = mine.shape
    return pl.pallas_call(
        finish_ff_kernel,
        grid=(1,),
        in_specs=[
            pl.BlockSpec(memory_space=pltpu.SMEM), whole(mine.shape), whole(other.shape)
        ],
        out_specs=[whole((shard, wide)), whole((4 * quarter, width))],
        out_shape=[
            jax.ShapeDtypeStruct((shard, wide), F32),
            jax.ShapeDtypeStruct((4 * quarter, width), F32),
        ],
        compiler_params=params(60, "arbitrary"),
        cost_estimate=cost(0, 12 * shard * wide),
        name="finish_ff",
    )(place, mine, other)


def finish_attend_kernel(
    place_ref, em_ref, eo_ref, la_ref, lb_ref, lc_ref, ld_ref, qkv_ref, proj_ref, small_ref
):
    first_core = lax.rem(place_ref[0], 2) == 0
    shard, width = proj_ref.shape
    part = width // 2
    late = la_ref.shape[1] // 3
    early = part - late
    rows = la_ref.shape[0] - shard
    lm = la_ref[...].astype(F32) + lb_ref[...].astype(F32)
    lo = lc_ref[...].astype(F32) + ld_ref[...].astype(F32)
    small_ref[...] = lm[:rows] + lo[:rows]
    em = em_ref[...].astype(F32)
    eo = eo_ref[...].astype(F32)
    firsts = (jnp.where(first_core, em, eo), jnp.where(first_core, eo, em))
    lasts = (jnp.where(first_core, lm, lo)[rows:], jnp.where(first_core, lo, lm)[rows:])
    for at in range(3):
        for of in range(2):
            start = at * width + of * part
            qkv_ref[:, start : start + early] = firsts[of][:, at * early : (at + 1) * early]
            qkv_ref[:, start + early : start + part] = lasts[of][:, at * late : (at + 1) * late]
    for of in range(2):
        proj_ref[:, of * part : (of + 1) * part] = firsts[of][:, 3 * early :]


def finish_attend(place, early_mine, early_other, late_mine, late_b, late_c, late_d, width):
    shard = early_mine.shape[0]
    rows = late_mine.shape[0] - shard
    return pl.pallas_call(
        finish_attend_kernel,
        grid=(1,),
        in_specs=[pl.BlockSpec(memory_space=pltpu.SMEM)]
        + [whole(value.shape) for value in (early_mine, early_other)]
        + [whole(late_mine.shape)] * 4,
        out_specs=[
            whole((shard, 3 * width)), whole((shard, width)), whole((rows, late_mine.shape[1]))
        ],
        out_shape=[
            jax.ShapeDtypeStruct((shard, 3 * width), F32),
            jax.ShapeDtypeStruct((shard, width), F32),
            jax.ShapeDtypeStruct((rows, late_mine.shape[1]), F32),
        ],
        compiler_params=params(60, "arbitrary"),
        cost_estimate=cost(0, 24 * shard * width),
        name="finish_attend",
    )(place, early_mine, early_other, late_mine, late_b, late_c, late_d)


def pack_kernel(place_ref, *refs):
    vectors, (qkv_ref, proj_ref, fc1_ref, fc2_ref, one_ref, two_ref) = refs[:-6], refs[-6:]
    first_core = lax.rem(place_ref[0], 2) == 0
    first_chip = place_ref[0] // 2 == 0
    shard, width = proj_ref.shape
    part = width // 2
    ff = fc1_ref.shape[1]
    owners = width // shard
    quarter = ff // owners // 4
    half = ff // 2
    one_ref[:VEC_ROWS, :] = jnp.zeros((VEC_ROWS, 3 * part), BF)
    for at, ref in enumerate(vectors):
        one_ref[at : at + 1, : ref.shape[1]] = ref[...]
    for at in range(3):
        low = qkv_ref[:, at * width : at * width + part]
        high = qkv_ref[:, at * width + part : (at + 1) * width]
        mine = jnp.where(first_core, low, high)
        mine = jnp.where(first_chip, mine[: shard // 2], mine[shard // 2 :])
        one_ref[VEC_ROWS:, at * part : (at + 1) * part] = mine
    two_ref[:, :part] = jnp.where(first_core, proj_ref[:, :part], proj_ref[:, part:])
    pieces_low, pieces_high = [], []
    for piece in range(2):
        for owner in range(owners):
            base = owner * 4 * quarter + piece * quarter
            pieces_low.append(fc1_ref[:, base : base + quarter])
            pieces_high.append(fc1_ref[:, base + 2 * quarter : base + 3 * quarter])
    two_ref[:, part : part + half] = jnp.where(
        first_core, jnp.concatenate(pieces_low, axis=1), jnp.concatenate(pieces_high, axis=1)
    )
    for piece in range(2):
        low = fc2_ref[piece * quarter : (piece + 1) * quarter, :]
        high = fc2_ref[(2 + piece) * quarter : (3 + piece) * quarter, :]
        start = part + half + piece * width
        two_ref[:, start : start + width] = jnp.where(first_core, low, high)


def pack_weights(place, vectors, qkv, proj, fc1, fc2):
    shard, width = proj.shape
    half = fc1.shape[1] // 2
    part = width // 2
    vectors = [vector.reshape(1, -1) for vector in vectors]
    values = (*vectors, qkv, proj, fc1, fc2)
    rows = VEC_ROWS + shard // 2
    return pl.pallas_call(
        pack_kernel,
        grid=(1,),
        in_specs=[pl.BlockSpec(memory_space=pltpu.SMEM)] + [whole(value.shape) for value in values],
        out_specs=[whole((rows, 3 * part)), whole((shard, 5 * part + half))],
        out_shape=[
            jax.ShapeDtypeStruct((rows, 3 * part), BF),
            jax.ShapeDtypeStruct((shard, 5 * part + half), BF),
        ],
        compiler_params=params(60, "arbitrary"),
        cost_estimate=cost(0, 5 * shard * width * 8),
        name="pack_weights",
    )(place, *values)


def project_kernel(tok_ref, w_ref, bias_ref, vec_ref, out_ref, out_t_ref, normed_ref):
    unit, _ = normalised(tok_ref[...].astype(F32))
    normed = (unit * vec_ref[0:1, :] + vec_ref[1:2, :]).astype(BF)
    normed_ref[...] = normed
    packed = dot(normed, w_ref[...]) + bias_ref[0:1, :]
    out_ref[...] = packed.astype(BF)
    out_t_ref[...] = packed.T.astype(BF)


def project(tokens, weight, bias, vec):
    rows, width = tokens.shape
    wide = weight.shape[1]
    bt = 512
    return pl.pallas_call(
        project_kernel,
        grid=(rows // bt,),
        in_specs=[
            pl.BlockSpec((bt, width), lambda i: (i, 0)),
            whole(weight.shape),
            whole(bias.shape),
            whole(vec.shape),
        ],
        out_specs=[
            pl.BlockSpec((bt, wide), lambda i: (i, 0)),
            pl.BlockSpec((wide, bt), lambda i: (0, i)),
            pl.BlockSpec((bt, width), lambda i: (i, 0)),
        ],
        out_shape=[
            jax.ShapeDtypeStruct((rows, wide), BF),
            jax.ShapeDtypeStruct((wide, rows), BF),
            jax.ShapeDtypeStruct((rows, width), BF),
        ],
        compiler_params=params(60, "arbitrary"),
        cost_estimate=cost(2 * rows * width * wide, 12 * rows * width),
        name="project",
    )(tokens, weight, bias, vec)


def exchange(value):
    return lax.all_to_all(value, "fsdp", split_axis=0, concat_axis=0, tiled=True)


def per_device(
    tokens,
    counts,
    norm1_gain,
    norm1_bias,
    qkv_weight,
    query_bias,
    value_bias,
    proj_weight,
    proj_bias,
    norm2_gain,
    norm2_bias,
    fc1_weight,
    fc1_bias,
    fc2_weight,
    fc2_bias,
    cotangent,
):
    images, slots, width = tokens.shape
    owners = lax.axis_size("fsdp")
    seq = lax.axis_size("seq")
    place = lax.axis_index("seq")
    core = lax.rem(place, 2)
    image = place // 2
    part = width // 2
    shard = width // owners
    ff = fc1_weight.shape[1]
    ff_shard = ff // owners
    quarter = ff_shard // 4
    half = ff // 2
    to_sibling = [(at, at ^ 1) for at in range(seq)]
    to_partner = [(at, at ^ 2) for at in range(seq)]

    def sibling(value):
        return lax.ppermute(value, "seq", to_sibling)

    def partner(value):
        return lax.ppermute(value, "seq", to_partner)

    def pick(value, at, axis):
        return lax.dynamic_index_in_dim(value, at, axis, keepdims=False)

    place_row = place.reshape(1).astype(jnp.int32)
    core_row = core.reshape(1).astype(jnp.int32)
    small = [
        norm1_gain, norm1_bias, query_bias, value_bias, proj_bias, norm2_gain, norm2_bias,
        fc2_bias, fc1_bias,
    ]
    one, two = pack_weights(
        place_row, small, qkv_weight, proj_weight, fc1_weight, fc2_weight
    )
    one, tokens, cotangent = lax.optimization_barrier((one, tokens, cotangent))
    mine_one = lax.all_gather(one, "fsdp", axis=0, tiled=False)
    def collect(value, theirs):
        mine = pick(value, image, 0)
        return jnp.concatenate([mine, theirs, sibling(mine), sibling(theirs)], axis=0)

    tok_came = partner(pick(tokens, 1 - image, 0))
    cot_came = partner(pick(cotangent, 1 - image, 0))
    mine_one, two, tok_came, cot_came = lax.optimization_barrier(
        (mine_one, two, tok_came, cot_came)
    )
    tok = collect(tokens, tok_came)
    cot = collect(cotangent, cot_came)
    second = lax.all_gather(two, "fsdp", axis=0, tiled=True)

    own_rows = mine_one[:, VEC_ROWS:]
    other_rows = partner(own_rows)
    w_qkv = jnp.where(
        image == 0,
        jnp.stack([own_rows, other_rows], axis=1),
        jnp.stack([other_rows, own_rows], axis=1),
    ).reshape(width, 3 * part)

    vecs = mine_one[:, :8, :shard].astype(F32).transpose(1, 0, 2).reshape(8, width)
    g1, b1, qb, vb, pb, g2, b2, f2b = vecs
    f1b = mine_one[:, 8, :ff_shard].astype(F32)
    f1b = pick(f1b.reshape(owners, 2, 2, quarter), core, 1)
    f1b = f1b.transpose(1, 0, 2).reshape(1, half)

    def mine_of(vector):
        return lax.dynamic_slice_in_dim(vector, core * part, part, 0)

    qkv_bias = jnp.concatenate([mine_of(qb), jnp.zeros((part,), F32), mine_of(vb)])
    vec_one = jnp.concatenate([jnp.stack([g1, b1]), jnp.zeros((6, width), F32)])
    packed, packed_t, normed = project(tok, w_qkv, qkv_bias.reshape(1, 3 * part), vec_one)
    packed, cot = lax.optimization_barrier((packed, cot))
    mixed, result_t, log_total = attend_forward(counts, place_row, packed, packed_t, slots)
    mixed_sib = sibling(mixed)

    wp_other = sibling(second[:, :part])
    vec_two = jnp.concatenate([jnp.stack([pb, g2, b2, f2b]), jnp.zeros((4, width), F32)])
    middle, out_own, out_send, gn_part, dw_ff, gf1, gf2, wp_own = feed_forward(
        core_row, tok, mixed, mixed_sib, cot, wp_other, second, vec_two, f1b
    )
    scattered_one = lax.psum_scatter(dw_ff, "fsdp", scatter_dimension=0, tiled=True)
    gn_sib = sibling(gn_part)
    rows_own = 2 * slots

    def hand_back(own, came):
        kept_part = own[:slots]
        came = came.astype(own.dtype)
        straight = jnp.stack([kept_part, came])
        crossed = jnp.stack([came, kept_part])
        return jnp.where(image == 0, straight, crossed)

    grad_middle, grad_mixed, grad_mixed_t, dwp_own, dwp_sib, vec_back = branch(
        core_row, middle, gn_part, gn_sib, cot, mixed, mixed_sib, wp_own, vec_two
    )
    dwp = jnp.where(
        core == 0,
        jnp.concatenate([dwp_own, dwp_sib], axis=0),
        jnp.concatenate([dwp_sib, dwp_own], axis=0),
    )
    grad_mixed, out_send, out_own = lax.optimization_barrier((grad_mixed, out_send, out_own))
    out_sib = sibling(out_send)
    early, late = 2, 1
    attend = functools.partial(attend_backward, counts, place_row, packed, packed_t)
    before = attend(grad_mixed, grad_mixed_t, result_t, log_total, slots, 0, early)
    before, out_sib = lax.optimization_barrier((before, out_sib))
    dw_early, qv_early = weight_grad(normed, *before)
    out_own = (out_own + out_sib.astype(F32)).astype(BF)
    block_one = jnp.concatenate([dw_early, dwp], axis=1).reshape(owners, shard, -1)
    grad_mixed, out_own, block_one = lax.optimization_barrier((grad_mixed, out_own, block_one))
    came_one = exchange(block_one)
    out_came = partner(out_own[slots:])
    grads = attend(grad_mixed, grad_mixed_t, result_t, log_total, slots, early, late)

    def total(came):
        return jnp.sum(came.astype(F32), axis=0).astype(BF)

    def join(value, came):
        return (value.astype(F32) + came.astype(F32)).astype(BF)

    scattered_one, out_came, grads = lax.optimization_barrier((scattered_one, out_came, grads))
    output = hand_back(out_own, out_came)
    one_came = partner(scattered_one)
    one_sum = join(scattered_one, one_came)
    gn1_own, gn1_send, dw_late, vec_first, qv_late = project_back(tok, normed, before, grads, w_qkv)

    def spread(vector):
        both = jnp.zeros((2, part), F32)
        return lax.dynamic_update_index_in_dim(both, vector, core, 0).reshape(width)

    def rows_of(block):
        return jnp.sum(block.reshape(block.shape[0] // 8, 8, block.shape[1]), axis=1)

    once = (core == 0).astype(F32)
    gg1, gb1 = rows_of(vec_first)
    gqb, gvb = rows_of(jnp.concatenate([qv_early, qv_late], axis=1))
    gg2, gb2, gpb = rows_of(vec_back) * once
    gf2b = jnp.sum(gf2, axis=0) * once
    gf1b = jnp.sum(gf1, axis=0).reshape(2, owners, quarter).transpose(1, 0, 2)
    gf1b = lax.dynamic_update_index_in_dim(
        jnp.zeros((owners, 2, 2, quarter), F32), gf1b, core, 1
    ).reshape(owners, ff_shard)
    late_wide = 3 * late * PAIR
    small_grads = jnp.stack(
        [gg1, gb1, spread(gqb), spread(gvb), gpb, gg2, gb2, gf2b]
    ).reshape(8, owners, shard).transpose(1, 0, 2)
    small_block = jnp.concatenate(
        [
            jnp.pad(small_grads, ((0, 0), (0, 0), (0, late_wide - shard))),
            jnp.pad(gf1b[:, None], ((0, 0), (0, VEC_ROWS - 9), (0, late_wide - ff_shard))),
        ],
        axis=1,
    ).astype(BF)
    block_two = jnp.concatenate(
        [small_block, dw_late.reshape(owners, shard, late_wide)], axis=1
    )
    gn1_sib = sibling(gn1_send)
    block_two, came_one = lax.optimization_barrier((block_two, came_one))
    early_total = total(came_one)
    early_came = partner(early_total)
    came_two = exchange(block_two)
    input_own, input_send = input_back(tok, gn1_own, gn1_sib, grad_middle, vec_one)
    input_came = partner(input_send)
    came_two, input_own, one_sum, output = lax.optimization_barrier(
        (came_two, input_own, one_sum, output)
    )
    one_other = sibling(one_sum)
    grad_fc1, grad_fc2 = finish_ff(place_row, one_sum, one_other, width, quarter)
    input_grad = hand_back(input_own, input_came)

    early_sum = join(early_total, early_came)
    early_other = sibling(early_sum)
    late_total = total(came_two)
    late_came = [
        lax.ppermute(late_total, "seq", [(at, at ^ flip) for at in range(seq)])
        for flip in (2, 1, 3)
    ]
    late_came, grad_fc1, grad_fc2 = lax.optimization_barrier((late_came, grad_fc1, grad_fc2))
    grad_qkv, grad_proj, small_sum = finish_attend(
        place_row, early_sum, early_other, late_total, *late_came, width
    )
    s = [small_sum[at, :shard] for at in range(8)]
    grad_f1b = small_sum[8, :ff_shard]
    return (
        output,
        input_grad,
        s[0],
        s[1],
        grad_qkv,
        s[2],
        s[3],
        grad_proj,
        s[4],
        s[5],
        s[6],
        grad_fc1,
        grad_f1b,
        grad_fc2,
        s[7],
    )


def solution(mesh):
    placed = (
        P("fsdp", "seq", None),
        P("fsdp", None),
        P("fsdp"),
        P("fsdp"),
        P("fsdp", None),
        P("fsdp"),
        P("fsdp"),
        P("fsdp", None),
        P("fsdp"),
        P("fsdp"),
        P("fsdp"),
        P("fsdp", None),
        P("fsdp"),
        P("fsdp", None),
        P("fsdp"),
        P("fsdp", "seq", None),
    )
    return jax.shard_map(
        per_device,
        mesh=mesh,
        in_specs=placed,
        out_specs=(
            P("fsdp", "seq", None),
            P("fsdp", "seq", None),
            P("fsdp"),
            P("fsdp"),
            P("fsdp", None),
            P("fsdp"),
            P("fsdp"),
            P("fsdp", None),
            P("fsdp"),
            P("fsdp"),
            P("fsdp"),
            P("fsdp", None),
            P("fsdp"),
            P("fsdp", None),
            P("fsdp"),
        ),
        check_vma=False,
    )
```

```python
import functools

import jax
import jax.numpy as jnp
from jax import lax
from jax.experimental import pallas as pl
from jax.experimental.pallas import tpu as pltpu
from jax.sharding import PartitionSpec as P

HEADS = 12
HEAD_DIM = 64
EPSILON = 1e-06
MASKED = -1e30
BF = jnp.bfloat16
F32 = jnp.float32
MIB = 1024 * 1024
PAIR = 2 * HEAD_DIM
VEC_ROWS = 16
SLOT_ORDER = (0, 2, 1, 3)


def params(mebibytes, *semantics):
    return pltpu.CompilerParams(
        dimension_semantics=semantics, vmem_limit_bytes=mebibytes * MIB
    )


def dot(left, right, left_dim=1, right_dim=0):
    return lax.dot_general(
        left, right, (((left_dim,), (right_dim,)), ((), ())), preferred_element_type=F32
    )


def cost(flops, bytes_accessed, transcendentals=0):
    return pl.CostEstimate(
        flops=int(flops), bytes_accessed=int(bytes_accessed), transcendentals=int(transcendentals)
    )


def whole(shape):
    return pl.BlockSpec(shape, lambda *_: tuple(0 for _ in shape))


def key_bias(counts_ref, place_ref, keys, slots):
    row = lax.broadcasted_iota(jnp.int32, (slots, PAIR), 0)
    place = place_ref[0]
    parts = []
    for flip in SLOT_ORDER:
        kept = counts_ref[place // 2, jnp.bitwise_xor(place, flip)]
        parts.append(jnp.where(row < kept, 0.0, MASKED).astype(F32))
    return jnp.concatenate(parts, axis=0)


def augment_keys(pair, bias, which, ones):
    lane = lax.broadcasted_iota(jnp.int32, pair.shape, 1)
    mine = (lane < HEAD_DIM) if which == 0 else (lane >= HEAD_DIM)
    start = HEAD_DIM if which == 0 else 0
    extra = jnp.where(
        lane == start, bias, jnp.where((lane > start) & (lane <= start + ones), 1.0, 0.0)
    )
    return jnp.where(mine, pair.astype(F32), extra).astype(BF)


def augment_values(pair, which, ones):
    lane = lax.broadcasted_iota(jnp.int32, pair.shape, 1)
    mine = (lane < HEAD_DIM) if which == 0 else (lane >= HEAD_DIM)
    start = HEAD_DIM if which == 0 else 0
    extra = jnp.where((lane >= start) & (lane < start + ones), 1.0, 0.0)
    return jnp.where(mine, pair.astype(F32), extra).astype(BF)


def pieces(value):
    first = value.astype(BF).astype(F32)
    rest = value - first
    second = rest.astype(BF).astype(F32)
    return first, second, rest - second


def extra_rows(rows, width):
    place = lax.broadcasted_iota(jnp.int32, (HEAD_DIM, width), 0)
    out = jnp.zeros((HEAD_DIM, width), F32)
    for at, row in enumerate(rows):
        out = jnp.where(place == at, row, out)
    return out.astype(BF)


def place_rows(head, extra, which):
    return jnp.concatenate([head, extra] if which == 0 else [extra, head], axis=0)


def attend_forward_kernel(
    slots, bq, chunk, counts_ref, place_ref, k_ref, qt_ref, vt_ref, mixed_ref, ot_ref, lse_ref,
    kaug, vaug, s_a, s_b, m_a, m_b
):
    keys = k_ref.shape[0]
    step = pl.program_id(1)
    steps = pl.num_programs(1)
    scores = (s_a, s_b)
    peaks = (m_a, m_b)
    ones_row = extra_rows([jnp.ones((1, bq), F32)], bq)

    @pl.when(step == 0)
    def _():
        bias = key_bias(counts_ref, place_ref, keys, slots)
        ones = jnp.ones((16, keys), BF)
        for which in range(2):
            kaug[which] = augment_keys(k_ref[...], bias, which, 0)
            vaug[which] = jnp.concatenate(
                [vt_ref[which * HEAD_DIM : (which + 1) * HEAD_DIM, :], ones], axis=0
            )

    def query_block(at, which):
        head = qt_ref[which * HEAD_DIM : (which + 1) * HEAD_DIM, pl.ds(at * bq, bq)]
        head = (head.astype(F32) * HEAD_DIM ** (-0.5)).astype(BF)
        return place_rows(head, ones_row, which)

    def score_chunk(query, which, at, peak):
        rows = slice(at * chunk, (at + 1) * chunk)
        s = dot(kaug[which, rows, :], query)
        scores[which][rows, :] = s
        top = jnp.max(s.reshape(chunk // 8, 8, bq), axis=0)
        return top if peak is None else jnp.maximum(peak, top)

    def raise_chunk(which, at, peak):
        rows = slice(at * chunk, (at + 1) * chunk)
        return jnp.exp(scores[which][rows, :] - peak).astype(BF)

    def weigh_chunk(which, at, p, total):
        o = dot(vaug[which, :, at * chunk : (at + 1) * chunk], p)
        return o if total is None else total + o

    @pl.when(step == 0)
    def _():
        query = query_block(0, 0)
        peak = None
        for at in range(keys // chunk):
            peak = score_chunk(query, 0, at, peak)
        m_a[...] = peak

    later = jnp.minimum(step + 1, steps - 1)
    outs = []
    for which in range(2):
        other = 1 - which
        query = query_block(step if which == 0 else later, other)
        peak = jnp.max(peaks[which][...], axis=0, keepdims=True)
        next_peak, total, behind = None, None, None
        for at in range(keys // chunk):
            next_peak = score_chunk(query, other, at, next_peak)
            if behind is not None:
                total = weigh_chunk(which, at - 1, behind, total)
            behind = raise_chunk(which, at, peak)
        total = weigh_chunk(which, keys // chunk - 1, behind, total)
        peaks[other][...] = next_peak
        norm = total[HEAD_DIM : HEAD_DIM + 1, :]
        outs.append(total[:HEAD_DIM, :] * (1.0 / norm))
        lse_ref[0, which : which + 1, :] = peak + jnp.log(norm)
    both = jnp.concatenate(outs, axis=0)
    ot_ref[...] = both
    mixed_ref[...] = both.T.astype(BF)


def attend_forward(counts, place, packed, packed_t, slots):
    keys, width = packed.shape
    width //= 3
    pairs = width // PAIR
    bq, chunk = 256, 256
    kernel = functools.partial(attend_forward_kernel, slots, bq, chunk)
    return pl.pallas_call(
        kernel,
        grid=(pairs, keys // bq),
        in_specs=[
            pl.BlockSpec(memory_space=pltpu.SMEM),
            pl.BlockSpec(memory_space=pltpu.SMEM),
            pl.BlockSpec((keys, PAIR), lambda p, i: (0, pairs + p)),
            pl.BlockSpec((PAIR, keys), lambda p, i: (p, 0)),
            pl.BlockSpec((PAIR, keys), lambda p, i: (2 * pairs + p, 0)),
        ],
        out_specs=[
            pl.BlockSpec((bq, PAIR), lambda p, i: (i, p)),
            pl.BlockSpec((PAIR, bq), lambda p, i: (p, i)),
            pl.BlockSpec((1, 8, bq), lambda p, i: (p, 0, i)),
        ],
        out_shape=[
            jax.ShapeDtypeStruct((keys, width), BF),
            jax.ShapeDtypeStruct((width, keys), F32),
            jax.ShapeDtypeStruct((pairs, 8, keys), F32),
        ],
        scratch_shapes=[
            pltpu.VMEM((2, keys, PAIR), BF),
            pltpu.VMEM((2, HEAD_DIM + 16, keys), BF),
            pltpu.VMEM((keys, bq), F32),
            pltpu.VMEM((keys, bq), F32),
            pltpu.VMEM((8, bq), F32),
            pltpu.VMEM((8, bq), F32),
        ],
        compiler_params=params(60, "arbitrary", "arbitrary"),
        cost_estimate=cost(
            2 * pairs * 2 * 2 * keys * keys * 256, 12 * keys * width, 2 * pairs * keys * keys
        ),
        name="attend_forward",
    )(counts, place, packed, packed_t, packed_t)


def attend_backward_kernel(
    slots, bq, chunk, counts_ref, place_ref, q_ref, k_ref, v_ref, qt_ref, kt_ref, do_ref, dot_ref, ot_ref,
    lse_ref, gq_ref, gk_ref, gv_ref, kaug, vaug, acc_k, acc_v
):
    keys = k_ref.shape[0]
    step = pl.program_id(1)
    steps = pl.num_programs(1)
    scale = HEAD_DIM ** (-0.5)

    @pl.when(step == 0)
    def _():
        bias = key_bias(counts_ref, place_ref, keys, slots)
        for which in range(2):
            kaug[which] = augment_keys(k_ref[...], bias, which, 3)
            vaug[which] = augment_values(v_ref[...], which, 3)
        acc_k[...] = jnp.zeros_like(acc_k)
        acc_v[...] = jnp.zeros_like(acc_v)

    ones_row = jnp.ones((1, bq), F32)
    queries, grads = [], []
    for which in range(2):
        rows = slice(which * HEAD_DIM, (which + 1) * HEAD_DIM)
        head = (qt_ref[rows, :].astype(F32) * scale).astype(BF)
        log_total = lse_ref[0, which : which + 1, :]
        queries.append(
            place_rows(head, extra_rows([ones_row, *pieces(-log_total)], bq), which)
        )
        grad = dot_ref[rows, :]
        delta = jnp.sum(grad.astype(F32) * ot_ref[rows, :], axis=0, keepdims=True)
        grads.append(place_rows(grad, extra_rows(list(pieces(-delta)), bq), which))

    do_pair = do_ref[...]
    q_pair = q_ref[...]
    totals = [None, None]
    units = [(at, which) for at in range(keys // chunk) for which in range(2)]

    def front(at, which):
        rows = slice(at * chunk, (at + 1) * chunk)
        return dot(kaug[which, rows, :], queries[which]), dot(vaug[which, rows, :], grads[which])

    ahead = front(*units[0])
    behind = None
    for unit in range(len(units) + 1):
        now = ahead
        if unit + 1 < len(units):
            ahead = front(*units[unit + 1])
        if behind is not None:
            at, which = units[unit - 1]
            rows = slice(at * chunk, (at + 1) * chunk)
            p_low, ds = behind
            acc_v[which, rows, :] += dot(p_low, do_pair)
            acc_k[which, rows, :] += dot(ds, q_pair)
            part = dot(kt_ref[which * HEAD_DIM : (which + 1) * HEAD_DIM, rows], ds)
            totals[which] = part if totals[which] is None else totals[which] + part
        if unit < len(units):
            p = jnp.exp(now[0])
            behind = p.astype(BF), (p * now[1]).astype(BF)
    both = jnp.concatenate(totals, axis=0) * scale
    gq_ref[...] = both.T.astype(BF)

    @pl.when(step == steps - 1)
    def _():
        lane = lax.broadcasted_iota(jnp.int32, (keys, PAIR), 1)
        gk_ref[...] = (jnp.where(lane < HEAD_DIM, acc_k[0], acc_k[1]) * scale).astype(BF)
        gv_ref[...] = jnp.where(lane < HEAD_DIM, acc_v[0], acc_v[1]).astype(BF)


def attend_backward(
    counts, place, packed, packed_t, grad, grad_t, result_t, log_total, slots, start, count
):
    keys, width = packed.shape
    width //= 3
    pairs = width // PAIR
    bq, chunk = 512, 256
    kernel = functools.partial(attend_backward_kernel, slots, bq, chunk)
    at = lambda p: p + start
    return pl.pallas_call(
        kernel,
        grid=(count, keys // bq),
        in_specs=[
            pl.BlockSpec(memory_space=pltpu.SMEM),
            pl.BlockSpec(memory_space=pltpu.SMEM),
            pl.BlockSpec((bq, PAIR), lambda p, i: (i, at(p))),
            pl.BlockSpec((keys, PAIR), lambda p, i: (0, pairs + at(p))),
            pl.BlockSpec((keys, PAIR), lambda p, i: (0, 2 * pairs + at(p))),
            pl.BlockSpec((PAIR, bq), lambda p, i: (at(p), i)),
            pl.BlockSpec((PAIR, keys), lambda p, i: (pairs + at(p), 0)),
            pl.BlockSpec((bq, PAIR), lambda p, i: (i, at(p))),
            pl.BlockSpec((PAIR, bq), lambda p, i: (at(p), i)),
            pl.BlockSpec((PAIR, bq), lambda p, i: (at(p), i)),
            pl.BlockSpec((1, 8, bq), lambda p, i: (at(p), 0, i)),
        ],
        out_specs=[
            pl.BlockSpec((bq, PAIR), lambda p, i: (i, p)),
            pl.BlockSpec((keys, PAIR), lambda p, i: (0, p)),
            pl.BlockSpec((keys, PAIR), lambda p, i: (0, p)),
        ],
        out_shape=[jax.ShapeDtypeStruct((keys, count * PAIR), BF)] * 3,
        scratch_shapes=[
            pltpu.VMEM((2, keys, PAIR), BF),
            pltpu.VMEM((2, keys, PAIR), BF),
            pltpu.VMEM((2, keys, PAIR), F32),
            pltpu.VMEM((2, keys, PAIR), F32),
        ],
        compiler_params=params(60, "arbitrary", "arbitrary"),
        cost_estimate=cost(
            2 * count * 5 * 2 * keys * keys * 256, 24 * keys * count * PAIR,
            2 * count * keys * keys,
        ),
        name="attend_backward",
    )(counts, place, packed, packed, packed, packed_t, packed_t, grad, grad_t, result_t, log_total)


def normalised(values):
    centred = values - jnp.mean(values, axis=-1, keepdims=True)
    variance = jnp.mean(centred * centred, axis=-1, keepdims=True)
    inverse = lax.rsqrt(variance + EPSILON)
    return centred * inverse, inverse


def norm_pull(grad, gain, unit, inverse):
    scaled = grad * gain
    mean = jnp.mean(scaled, axis=-1, keepdims=True)
    along = jnp.mean(scaled * unit, axis=-1, keepdims=True)
    return inverse * (scaled - mean - unit * along)


def fold(values):
    return jnp.sum(values.reshape(values.shape[0] // 8, 8, values.shape[1]), axis=0)


def feed_forward_kernel(
    chunk, core_ref, tok_ref, mo_ref, ms_ref, cot_ref, wpx_ref, g2_ref, vec_ref, f1b_ref,
    mid_ref, out_ref, send_ref, gn_ref, dw_ref, gf1_ref, gf2_ref, wpo_ref, acc1, acc2, accb, accc, wps_ref,
    w1t_ref, w2t_ref
):
    step = pl.program_id(0)
    steps = pl.num_programs(0)
    width = tok_ref.shape[1]
    half = f1b_ref.shape[1]
    part = width // 2

    def weights(at):
        w1 = g2_ref[:, part + at * chunk : part + (at + 1) * chunk]
        piece, row = divmod(at * chunk, width)
        start = part + half + piece * width
        return w1, g2_ref[row : row + chunk, start : start + width]

    @pl.when(step == 0)
    def _():
        acc1[...] = jnp.zeros_like(acc1)
        acc2[...] = jnp.zeros_like(acc2)
        accb[...] = jnp.zeros_like(accb)
        accc[...] = jnp.zeros_like(accc)
        here = pl.ds(pl.multiple_of(core_ref[0] * part, part), part)
        there = pl.ds(pl.multiple_of((1 - core_ref[0]) * part, part), part)
        wpo_ref[:, here] = g2_ref[here, :part]
        wpo_ref[:, there] = wpx_ref[here, :]
        wps_ref[:, here] = g2_ref[there, :part]
        wps_ref[:, there] = wpx_ref[there, :]
        for at in range(half // chunk):
            cols = slice(at * chunk, (at + 1) * chunk)
            w1, w2 = weights(at)
            w1t_ref[cols, :] = w1.T
            w2t_ref[:, cols] = w2.T

    middle = (
        tok_ref[...].astype(F32)
        + dot(mo_ref[...], wpo_ref[...])
        + dot(ms_ref[...], wps_ref[...])
        + vec_ref[0:1, :]
    )
    mid_ref[...] = middle
    unit, _ = normalised(middle)
    normed = (unit * vec_ref[1:2, :] + vec_ref[2:3, :]).astype(BF)
    normed_t = normed.T
    cot = cot_ref[...]
    out = None
    grad = None

    def front(at):
        w1, _ = weights(at)
        hidden = dot(normed, w1) + f1b_ref[0:1, at * chunk : (at + 1) * chunk]
        return hidden, dot(cot, w2t_ref[:, at * chunk : (at + 1) * chunk])

    def middle_part(hidden, grad_active):
        below = 0.5 + 0.5 * lax.erf(hidden * (0.5**0.5))
        slope = below + hidden * (jnp.exp(hidden * hidden * -0.5) * 0.3989422804014327)
        return (hidden * below).astype(BF), (grad_active * slope).astype(BF)

    chunks = half // chunk
    ahead = front(0)
    behind = None
    for at in range(chunks + 1):
        now = ahead
        if at + 1 < chunks:
            ahead = front(at + 1)
        if behind is not None:
            active, grad_hidden = behind
            cols = slice((at - 1) * chunk, at * chunk)
            _, w2 = weights(at - 1)
            more = dot(active, w2)
            out = more if out is None else out + more
            more = dot(grad_hidden, w1t_ref[cols, :])
            grad = more if grad is None else grad + more
            acc1[:, cols] += dot(normed_t, grad_hidden)
            acc2[cols, :] += dot(active, cot, 0, 0)
            accb[:, cols] += fold(grad_hidden.astype(F32))
        if at < chunks:
            behind = middle_part(*now)
    accc[...] += fold(cot.astype(F32))
    gn_ref[...] = grad.astype(BF)

    @pl.when(step < steps // 2)
    def _():
        out_ref[...] = middle + out + vec_ref[3:4, :]

    @pl.when(step >= steps // 2)
    def _():
        send_ref[...] = out.astype(BF)

    @pl.when(step == steps - 1)
    def _():
        dw_ref[:, :half] = acc1[...].astype(BF)
        for piece in range(half // width):
            dw_ref[:, half + piece * width : half + (piece + 1) * width] = acc2[
                piece * width : (piece + 1) * width, :
            ].astype(BF)
        gf1_ref[...] = accb[...]
        gf2_ref[...] = accc[...]


def feed_forward(core, tokens, mixed_own, mixed_sib, cot, wp_other, weights, vec, f1b):
    rows, width = tokens.shape
    half = f1b.shape[1]
    heads = mixed_own.shape[1]
    bt, chunk = 512, 384
    blocks = rows // bt
    kernel = functools.partial(feed_forward_kernel, chunk)
    return pl.pallas_call(
        kernel,
        grid=(blocks,),
        in_specs=[
            pl.BlockSpec(memory_space=pltpu.SMEM),
            pl.BlockSpec((bt, width), lambda i: (i, 0)),
            pl.BlockSpec((bt, heads), lambda i: (i, 0)),
            pl.BlockSpec((bt, heads), lambda i: (lax.rem(i + blocks // 2, blocks), 0)),
            pl.BlockSpec((bt, width), lambda i: (i, 0)),
            whole(wp_other.shape),
            whole(weights.shape),
            whole(vec.shape),
            whole(f1b.shape),
        ],
        out_specs=[
            pl.BlockSpec((bt, width), lambda i: (i, 0)),
            pl.BlockSpec((bt, width), lambda i: (jnp.minimum(i, blocks // 2 - 1), 0)),
            pl.BlockSpec((bt, width), lambda i: (jnp.maximum(i - blocks // 2, 0), 0)),
            pl.BlockSpec((bt, width), lambda i: (i, 0)),
            whole((width, 2 * half)),
            whole((8, half)),
            whole((8, width)),
            whole((width // 2, width)),
        ],
        out_shape=[
            jax.ShapeDtypeStruct((rows, width), F32),
            jax.ShapeDtypeStruct((rows // 2, width), F32),
            jax.ShapeDtypeStruct((rows // 2, width), BF),
            jax.ShapeDtypeStruct((rows, width), BF),
            jax.ShapeDtypeStruct((width, 2 * half), BF),
            jax.ShapeDtypeStruct((8, half), F32),
            jax.ShapeDtypeStruct((8, width), F32),
            jax.ShapeDtypeStruct((width // 2, width), BF),
        ],
        scratch_shapes=[
            pltpu.VMEM((width, half), F32),
            pltpu.VMEM((half, width), F32),
            pltpu.VMEM((8, half), F32),
            pltpu.VMEM((8, width), F32),
            pltpu.VMEM((width // 2, width), BF),
            pltpu.VMEM((half, width), BF),
            pltpu.VMEM((width, half), BF),
        ],
        compiler_params=params(60, "arbitrary"),
        cost_estimate=cost(
            2 * rows * width * (6 * half + width), 20 * rows * width + 8 * width * half,
            2 * rows * half,
        ),
        name="feed_forward",
    )(core, tokens, mixed_own, mixed_sib, cot, wp_other, weights, vec, f1b)


def branch_kernel(
    core_ref, mid_ref, ga_ref, gb_ref, cot_ref, mo_ref, ms_ref, wpo_ref, vec_ref,
    gm_ref, do_ref, dot_ref, dwo_ref, dws_ref, vecs_ref, acco, accs, accv, low_ref, wpt_ref
):
    step = pl.program_id(0)
    steps = pl.num_programs(0)
    half = do_ref.shape[1]

    @pl.when(step == 0)
    def _():
        acco[...] = jnp.zeros_like(acco)
        accs[...] = jnp.zeros_like(accs)
        wpt_ref[...] = wpo_ref[...].T
        accv[...] = jnp.zeros_like(accv)

    unit, inverse = normalised(mid_ref[...])
    grad = ga_ref[...].astype(F32) + gb_ref[...].astype(F32)
    accv[0:8, :] += fold(grad * unit)
    accv[8:16, :] += fold(grad)
    grad_middle = cot_ref[...].astype(F32) + norm_pull(grad, vec_ref[1:2, :], unit, inverse)

    @pl.when(step < steps // 2)
    def _():
        gm_ref[...] = grad_middle

    low = grad_middle.astype(BF)
    low_ref[...] = low
    accv[16:24, :] += fold(low.astype(F32))
    back = dot(low, wpt_ref[...])
    do_ref[...] = back.astype(BF)
    dot_ref[...] = back.T.astype(BF)
    mine = low_ref[:, pl.ds(pl.multiple_of(core_ref[0] * half, half), half)]
    acco[...] += dot(mo_ref[...].astype(BF), mine)
    accs[...] += dot(ms_ref[...], mine, 0, 0)

    @pl.when(step == steps - 1)
    def _():
        dwo_ref[...] = acco[...].astype(BF)
        dws_ref[...] = accs[...].astype(BF)
        vecs_ref[...] = accv[...]


def branch(core, middle, grad_own, grad_sib, cot, result_t, mixed_sib, wp_own, vec):
    rows, width = middle.shape
    half = mixed_sib.shape[1]
    bt = 512
    blocks = rows // bt
    swap = lambda i: (lax.rem(i + blocks // 2, blocks), 0)
    straight = lambda i: (i, 0)
    return pl.pallas_call(
        branch_kernel,
        grid=(blocks,),
        in_specs=[
            pl.BlockSpec(memory_space=pltpu.SMEM),
            pl.BlockSpec((bt, width), straight),
            pl.BlockSpec((bt, width), straight),
            pl.BlockSpec((bt, width), swap),
            pl.BlockSpec((bt, width), straight),
            pl.BlockSpec((half, bt), lambda i: (0, i)),
            pl.BlockSpec((bt, half), swap),
            whole(wp_own.shape),
            whole(vec.shape),
        ],
        out_specs=[
            pl.BlockSpec((bt, width), lambda i: (jnp.minimum(i, blocks // 2 - 1), 0)),
            pl.BlockSpec((bt, half), straight),
            pl.BlockSpec((half, bt), lambda i: (0, i)),
            whole((half, half)),
            whole((half, half)),
            whole((24, width)),
        ],
        out_shape=[
            jax.ShapeDtypeStruct((rows // 2, width), F32),
            jax.ShapeDtypeStruct((rows, half), BF),
            jax.ShapeDtypeStruct((half, rows), BF),
            jax.ShapeDtypeStruct((half, half), BF),
            jax.ShapeDtypeStruct((half, half), BF),
            jax.ShapeDtypeStruct((24, width), F32),
        ],
        scratch_shapes=[
            pltpu.VMEM((half, half), F32),
            pltpu.VMEM((half, half), F32),
            pltpu.VMEM((24, width), F32),
            pltpu.VMEM((bt, width), BF),
            pltpu.VMEM((width, half), BF),
        ],
        compiler_params=params(60, "arbitrary"),
        cost_estimate=cost(2 * rows * width * 3 * half, 18 * rows * width),
        name="branch",
    )(core, middle, grad_own, grad_sib, cot, result_t, mixed_sib, wp_own, vec)


def weight_grad_kernel(normed_ref, gq_ref, gk_ref, gv_ref, dw_ref, qv_ref, accw, accqv):
    step = pl.program_id(0)
    steps = pl.num_programs(0)
    part = gq_ref.shape[1]

    @pl.when(step == 0)
    def _():
        accw[...] = jnp.zeros_like(accw)
        accqv[...] = jnp.zeros_like(accqv)

    normed_t = normed_ref[...].T
    for at, ref in enumerate((gq_ref, gk_ref, gv_ref)):
        cols = slice(at * part, (at + 1) * part)
        value = ref[...]
        accw[:, cols] += dot(normed_t, value)
        if at != 1:
            here = 0 if at == 0 else 8
            accqv[here : here + 8, :] += fold(value.astype(F32))

    @pl.when(step == steps - 1)
    def _():
        dw_ref[...] = accw[...].astype(BF)
        qv_ref[...] = accqv[...]


def weight_grad(normed, gq, gk, gv):
    rows, width = normed.shape
    part = gq.shape[1]
    bt = 512
    straight = lambda i: (i, 0)
    return pl.pallas_call(
        weight_grad_kernel,
        grid=(rows // bt,),
        in_specs=[
            pl.BlockSpec((bt, width), straight),
            pl.BlockSpec((bt, part), straight),
            pl.BlockSpec((bt, part), straight),
            pl.BlockSpec((bt, part), straight),
        ],
        out_specs=[whole((width, 3 * part)), whole((16, part))],
        out_shape=[
            jax.ShapeDtypeStruct((width, 3 * part), BF),
            jax.ShapeDtypeStruct((16, part), F32),
        ],
        scratch_shapes=[pltpu.VMEM((width, 3 * part), F32), pltpu.VMEM((16, part), F32)],
        compiler_params=params(60, "arbitrary"),
        cost_estimate=cost(2 * rows * width * 3 * part, 2 * rows * (width + 3 * part)),
        name="weight_grad",
    )(normed, gq, gk, gv)


def project_back_kernel(
    tok_ref, normed_ref, gqa_ref, gka_ref, gva_ref, gq_ref, gk_ref, gv_ref, w_ref,
    own_ref, sib_ref, dw_ref, vecs_ref, qv_ref, accw, accv, accqv, wt_ref
):
    step = pl.program_id(0)
    steps = pl.num_programs(0)
    early = gqa_ref.shape[1]
    part = gq_ref.shape[1]
    wide = early + part

    @pl.when(step == 0)
    def _():
        accw[...] = jnp.zeros_like(accw)
        accv[...] = jnp.zeros_like(accv)
        accqv[...] = jnp.zeros_like(accqv)
        wt_ref[...] = w_ref[...].T

    unit, _ = normalised(tok_ref[...].astype(F32))
    normed_t = normed_ref[...].T
    grad = None
    before = (gqa_ref, gka_ref, gva_ref)
    for at, ref in enumerate((gq_ref, gk_ref, gv_ref)):
        cols = slice(at * part, (at + 1) * part)
        value = ref[...]
        more = dot(
            jnp.concatenate([before[at][...], value], axis=1),
            wt_ref[at * wide : (at + 1) * wide, :],
        )
        grad = more if grad is None else grad + more
        accw[:, cols] += dot(normed_t, value)
        if at != 1:
            here = 0 if at == 0 else 8
            accqv[here : here + 8, :] += fold(value.astype(F32))
    accv[0:8, :] += fold(grad * unit)
    accv[8:16, :] += fold(grad)

    @pl.when(step < steps // 2)
    def _():
        own_ref[...] = grad

    @pl.when(step >= steps // 2)
    def _():
        sib_ref[...] = grad.astype(BF)

    @pl.when(step == steps - 1)
    def _():
        dw_ref[...] = accw[...].astype(BF)
        vecs_ref[...] = accv[...]
        qv_ref[...] = accqv[...]


def project_back(tokens, normed, before, grads, weight):
    rows, width = tokens.shape
    early, part = before[0].shape[1], grads[0].shape[1]
    bt = 512
    blocks = rows // bt
    straight = lambda i: (i, 0)
    return pl.pallas_call(
        project_back_kernel,
        grid=(blocks,),
        in_specs=[pl.BlockSpec((bt, width), straight)] * 2
        + [pl.BlockSpec((bt, early), straight)] * 3
        + [pl.BlockSpec((bt, part), straight)] * 3
        + [whole(weight.shape)],
        out_specs=[
            pl.BlockSpec((bt, width), lambda i: (jnp.minimum(i, blocks // 2 - 1), 0)),
            pl.BlockSpec((bt, width), lambda i: (jnp.maximum(i - blocks // 2, 0), 0)),
            whole((width, 3 * part)),
            whole((16, width)),
            whole((16, part)),
        ],
        out_shape=[
            jax.ShapeDtypeStruct((rows // 2, width), F32),
            jax.ShapeDtypeStruct((rows // 2, width), BF),
            jax.ShapeDtypeStruct((width, 3 * part), BF),
            jax.ShapeDtypeStruct((16, width), F32),
            jax.ShapeDtypeStruct((16, part), F32),
        ],
        scratch_shapes=[
            pltpu.VMEM((width, 3 * part), F32),
            pltpu.VMEM((16, width), F32),
            pltpu.VMEM((16, part), F32),
            pltpu.VMEM((3 * (early + part), width), BF),
        ],
        compiler_params=params(60, "arbitrary"),
        cost_estimate=cost(2 * rows * width * (6 * part + 3 * early), 14 * rows * width),
        name="project_back",
    )(tokens, normed, *before, *grads, weight)


def input_back_kernel(tok_ref, own_ref, sib_ref, gm_ref, vec_ref, keep_ref, send_ref):
    unit, inverse = normalised(tok_ref[...].astype(F32))
    grad = own_ref[...] + sib_ref[...].astype(F32)
    total = gm_ref[...] + norm_pull(grad, vec_ref[0:1, :], unit, inverse)
    step = pl.program_id(0)
    steps = pl.num_programs(0)

    @pl.when(step < steps // 2)
    def _():
        keep_ref[...] = total

    @pl.when(step >= steps // 2)
    def _():
        send_ref[...] = total.astype(BF)


def input_back(tokens, grad_own, grad_sib, grad_middle, vec):
    rows, width = grad_own.shape
    bt = 256
    blocks = rows // bt
    straight = lambda i: (i, 0)
    return pl.pallas_call(
        input_back_kernel,
        grid=(blocks,),
        in_specs=[pl.BlockSpec((bt, width), straight)] * 4 + [whole(vec.shape)],
        out_specs=[
            pl.BlockSpec((bt, width), lambda i: (jnp.minimum(i, blocks // 2 - 1), 0)),
            pl.BlockSpec((bt, width), lambda i: (jnp.maximum(i - blocks // 2, 0), 0)),
        ],
        out_shape=[
            jax.ShapeDtypeStruct((rows // 2, width), F32),
            jax.ShapeDtypeStruct((rows // 2, width), BF),
        ],
        compiler_params=params(60, "arbitrary"),
        cost_estimate=cost(20 * rows * width, 16 * rows * width),
        name="input_back",
    )(tokens, grad_own, grad_sib, grad_middle, vec)


def finish_ff_kernel(place_ref, mine_ref, other_ref, fc1_ref, fc2_ref):
    first_core = lax.rem(place_ref[0], 2) == 0
    shard, ff = fc1_ref.shape
    half = ff // 2
    quarter = fc2_ref.shape[0] // 4
    width = fc2_ref.shape[1]
    owners = ff // (4 * quarter)
    mine = mine_ref[...].astype(F32)
    other = other_ref[...].astype(F32)
    cores = (jnp.where(first_core, mine, other), jnp.where(first_core, other, mine))
    pieces = []
    for owner in range(owners):
        for value in cores:
            for piece in range(2):
                start = (piece * owners + owner) * quarter
                pieces.append(value[:, start : start + quarter])
    fc1_ref[...] = jnp.concatenate(pieces, axis=1)
    for at, value in enumerate(cores):
        for piece in range(2):
            row = (2 * at + piece) * quarter
            start = half + piece * width
            fc2_ref[row : row + quarter, :] = value[:, start : start + width]


def finish_ff(place, mine, other, width, quarter):
    shard, wide = mine.shape
    return pl.pallas_call(
        finish_ff_kernel,
        grid=(1,),
        in_specs=[
            pl.BlockSpec(memory_space=pltpu.SMEM), whole(mine.shape), whole(other.shape)
        ],
        out_specs=[whole((shard, wide)), whole((4 * quarter, width))],
        out_shape=[
            jax.ShapeDtypeStruct((shard, wide), F32),
            jax.ShapeDtypeStruct((4 * quarter, width), F32),
        ],
        compiler_params=params(60, "arbitrary"),
        cost_estimate=cost(0, 12 * shard * wide),
        name="finish_ff",
    )(place, mine, other)


def finish_attend_kernel(
    place_ref, em_ref, eo_ref, la_ref, lb_ref, lc_ref, ld_ref, qkv_ref, proj_ref, small_ref
):
    first_core = lax.rem(place_ref[0], 2) == 0
    shard, width = proj_ref.shape
    part = width // 2
    late = la_ref.shape[1] // 3
    early = part - late
    rows = la_ref.shape[0] - shard
    lm = la_ref[...].astype(F32) + lb_ref[...].astype(F32)
    lo = lc_ref[...].astype(F32) + ld_ref[...].astype(F32)
    small_ref[...] = lm[:rows] + lo[:rows]
    em = em_ref[...].astype(F32)
    eo = eo_ref[...].astype(F32)
    firsts = (jnp.where(first_core, em, eo), jnp.where(first_core, eo, em))
    lasts = (jnp.where(first_core, lm, lo)[rows:], jnp.where(first_core, lo, lm)[rows:])
    for at in range(3):
        for of in range(2):
            start = at * width + of * part
            qkv_ref[:, start : start + early] = firsts[of][:, at * early : (at + 1) * early]
            qkv_ref[:, start + early : start + part] = lasts[of][:, at * late : (at + 1) * late]
    for of in range(2):
        proj_ref[:, of * part : (of + 1) * part] = firsts[of][:, 3 * early :]


def finish_attend(place, early_mine, early_other, late_mine, late_b, late_c, late_d, width):
    shard = early_mine.shape[0]
    rows = late_mine.shape[0] - shard
    return pl.pallas_call(
        finish_attend_kernel,
        grid=(1,),
        in_specs=[pl.BlockSpec(memory_space=pltpu.SMEM)]
        + [whole(value.shape) for value in (early_mine, early_other)]
        + [whole(late_mine.shape)] * 4,
        out_specs=[
            whole((shard, 3 * width)), whole((shard, width)), whole((rows, late_mine.shape[1]))
        ],
        out_shape=[
            jax.ShapeDtypeStruct((shard, 3 * width), F32),
            jax.ShapeDtypeStruct((shard, width), F32),
            jax.ShapeDtypeStruct((rows, late_mine.shape[1]), F32),
        ],
        compiler_params=params(60, "arbitrary"),
        cost_estimate=cost(0, 24 * shard * width),
        name="finish_attend",
    )(place, early_mine, early_other, late_mine, late_b, late_c, late_d)


def pack_kernel(place_ref, *refs):
    vectors, (qkv_ref, proj_ref, fc1_ref, fc2_ref, one_ref, two_ref) = refs[:-6], refs[-6:]
    first_core = lax.rem(place_ref[0], 2) == 0
    first_chip = place_ref[0] // 2 == 0
    shard, width = proj_ref.shape
    part = width // 2
    ff = fc1_ref.shape[1]
    owners = width // shard
    quarter = ff // owners // 4
    half = ff // 2
    one_ref[:VEC_ROWS, :] = jnp.zeros((VEC_ROWS, 3 * part), BF)
    for at, ref in enumerate(vectors):
        one_ref[at : at + 1, : ref.shape[1]] = ref[...]
    for at in range(3):
        low = qkv_ref[:, at * width : at * width + part]
        high = qkv_ref[:, at * width + part : (at + 1) * width]
        mine = jnp.where(first_core, low, high)
        mine = jnp.where(first_chip, mine[: shard // 2], mine[shard // 2 :])
        one_ref[VEC_ROWS:, at * part : (at + 1) * part] = mine
    two_ref[:, :part] = jnp.where(first_core, proj_ref[:, :part], proj_ref[:, part:])
    pieces_low, pieces_high = [], []
    for piece in range(2):
        for owner in range(owners):
            base = owner * 4 * quarter + piece * quarter
            pieces_low.append(fc1_ref[:, base : base + quarter])
            pieces_high.append(fc1_ref[:, base + 2 * quarter : base + 3 * quarter])
    two_ref[:, part : part + half] = jnp.where(
        first_core, jnp.concatenate(pieces_low, axis=1), jnp.concatenate(pieces_high, axis=1)
    )
    for piece in range(2):
        low = fc2_ref[piece * quarter : (piece + 1) * quarter, :]
        high = fc2_ref[(2 + piece) * quarter : (3 + piece) * quarter, :]
        start = part + half + piece * width
        two_ref[:, start : start + width] = jnp.where(first_core, low, high)


def pack_weights(place, vectors, qkv, proj, fc1, fc2):
    shard, width = proj.shape
    half = fc1.shape[1] // 2
    part = width // 2
    vectors = [vector.reshape(1, -1) for vector in vectors]
    values = (*vectors, qkv, proj, fc1, fc2)
    rows = VEC_ROWS + shard // 2
    return pl.pallas_call(
        pack_kernel,
        grid=(1,),
        in_specs=[pl.BlockSpec(memory_space=pltpu.SMEM)] + [whole(value.shape) for value in values],
        out_specs=[whole((rows, 3 * part)), whole((shard, 5 * part + half))],
        out_shape=[
            jax.ShapeDtypeStruct((rows, 3 * part), BF),
            jax.ShapeDtypeStruct((shard, 5 * part + half), BF),
        ],
        compiler_params=params(60, "arbitrary"),
        cost_estimate=cost(0, 5 * shard * width * 8),
        name="pack_weights",
    )(place, *values)


def project_kernel(tok_ref, w_ref, bias_ref, vec_ref, out_ref, out_t_ref, normed_ref):
    unit, _ = normalised(tok_ref[...].astype(F32))
    normed = (unit * vec_ref[0:1, :] + vec_ref[1:2, :]).astype(BF)
    normed_ref[...] = normed
    packed = dot(normed, w_ref[...]) + bias_ref[0:1, :]
    out_ref[...] = packed.astype(BF)
    out_t_ref[...] = packed.T.astype(BF)


def project(tokens, weight, bias, vec):
    rows, width = tokens.shape
    wide = weight.shape[1]
    bt = 512
    return pl.pallas_call(
        project_kernel,
        grid=(rows // bt,),
        in_specs=[
            pl.BlockSpec((bt, width), lambda i: (i, 0)),
            whole(weight.shape),
            whole(bias.shape),
            whole(vec.shape),
        ],
        out_specs=[
            pl.BlockSpec((bt, wide), lambda i: (i, 0)),
            pl.BlockSpec((wide, bt), lambda i: (0, i)),
            pl.BlockSpec((bt, width), lambda i: (i, 0)),
        ],
        out_shape=[
            jax.ShapeDtypeStruct((rows, wide), BF),
            jax.ShapeDtypeStruct((wide, rows), BF),
            jax.ShapeDtypeStruct((rows, width), BF),
        ],
        compiler_params=params(60, "arbitrary"),
        cost_estimate=cost(2 * rows * width * wide, 12 * rows * width),
        name="project",
    )(tokens, weight, bias, vec)


def exchange(value):
    return lax.all_to_all(value, "fsdp", split_axis=0, concat_axis=0, tiled=True)


def per_device(
    tokens,
    counts,
    norm1_gain,
    norm1_bias,
    qkv_weight,
    query_bias,
    value_bias,
    proj_weight,
    proj_bias,
    norm2_gain,
    norm2_bias,
    fc1_weight,
    fc1_bias,
    fc2_weight,
    fc2_bias,
    cotangent,
):
    images, slots, width = tokens.shape
    owners = lax.axis_size("fsdp")
    seq = lax.axis_size("seq")
    place = lax.axis_index("seq")
    core = lax.rem(place, 2)
    image = place // 2
    part = width // 2
    shard = width // owners
    ff = fc1_weight.shape[1]
    ff_shard = ff // owners
    quarter = ff_shard // 4
    half = ff // 2
    to_sibling = [(at, at ^ 1) for at in range(seq)]
    to_partner = [(at, at ^ 2) for at in range(seq)]

    def sibling(value):
        return lax.ppermute(value, "seq", to_sibling)

    def partner(value):
        return lax.ppermute(value, "seq", to_partner)

    def pick(value, at, axis):
        return lax.dynamic_index_in_dim(value, at, axis, keepdims=False)

    place_row = place.reshape(1).astype(jnp.int32)
    core_row = core.reshape(1).astype(jnp.int32)
    small = [
        norm1_gain, norm1_bias, query_bias, value_bias, proj_bias, norm2_gain, norm2_bias,
        fc2_bias, fc1_bias,
    ]
    one, two = pack_weights(
        place_row, small, qkv_weight, proj_weight, fc1_weight, fc2_weight
    )
    one, tokens, cotangent = lax.optimization_barrier((one, tokens, cotangent))
    mine_one = lax.all_gather(one, "fsdp", axis=0, tiled=False)
    def collect(value, theirs):
        mine = pick(value, image, 0)
        return jnp.concatenate([mine, theirs, sibling(mine), sibling(theirs)], axis=0)

    tok_came = partner(pick(tokens, 1 - image, 0))
    cot_came = partner(pick(cotangent, 1 - image, 0))
    mine_one, two, tok_came, cot_came = lax.optimization_barrier(
        (mine_one, two, tok_came, cot_came)
    )
    tok = collect(tokens, tok_came)
    cot = collect(cotangent, cot_came)
    second = lax.all_gather(two, "fsdp", axis=0, tiled=True)

    own_rows = mine_one[:, VEC_ROWS:]
    other_rows = partner(own_rows)
    w_qkv = jnp.where(
        image == 0,
        jnp.stack([own_rows, other_rows], axis=1),
        jnp.stack([other_rows, own_rows], axis=1),
    ).reshape(width, 3 * part)

    vecs = mine_one[:, :8, :shard].astype(F32).transpose(1, 0, 2).reshape(8, width)
    g1, b1, qb, vb, pb, g2, b2, f2b = vecs
    f1b = mine_one[:, 8, :ff_shard].astype(F32)
    f1b = pick(f1b.reshape(owners, 2, 2, quarter), core, 1)
    f1b = f1b.transpose(1, 0, 2).reshape(1, half)

    def mine_of(vector):
        return lax.dynamic_slice_in_dim(vector, core * part, part, 0)

    qkv_bias = jnp.concatenate([mine_of(qb), jnp.zeros((part,), F32), mine_of(vb)])
    vec_one = jnp.concatenate([jnp.stack([g1, b1]), jnp.zeros((6, width), F32)])
    packed, packed_t, normed = project(tok, w_qkv, qkv_bias.reshape(1, 3 * part), vec_one)
    packed, cot = lax.optimization_barrier((packed, cot))
    mixed, result_t, log_total = attend_forward(counts, place_row, packed, packed_t, slots)
    mixed_sib = sibling(mixed)

    wp_other = sibling(second[:, :part])
    vec_two = jnp.concatenate([jnp.stack([pb, g2, b2, f2b]), jnp.zeros((4, width), F32)])
    middle, out_own, out_send, gn_part, dw_ff, gf1, gf2, wp_own = feed_forward(
        core_row, tok, mixed, mixed_sib, cot, wp_other, second, vec_two, f1b
    )
    scattered_one = lax.psum_scatter(dw_ff, "fsdp", scatter_dimension=0, tiled=True)
    gn_sib = sibling(gn_part)
    rows_own = 2 * slots

    def hand_back(own, came):
        kept_part = own[:slots]
        came = came.astype(own.dtype)
        straight = jnp.stack([kept_part, came])
        crossed = jnp.stack([came, kept_part])
        return jnp.where(image == 0, straight, crossed)

    grad_middle, grad_mixed, grad_mixed_t, dwp_own, dwp_sib, vec_back = branch(
        core_row, middle, gn_part, gn_sib, cot, result_t, mixed_sib, wp_own, vec_two
    )
    dwp = jnp.where(
        core == 0,
        jnp.concatenate([dwp_own, dwp_sib], axis=0),
        jnp.concatenate([dwp_sib, dwp_own], axis=0),
    )
    grad_mixed, out_send, out_own = lax.optimization_barrier((grad_mixed, out_send, out_own))
    out_sib = sibling(out_send)
    early, late = 2, 1
    attend = functools.partial(attend_backward, counts, place_row, packed, packed_t)
    before = attend(grad_mixed, grad_mixed_t, result_t, log_total, slots, 0, early)
    before, out_sib = lax.optimization_barrier((before, out_sib))
    dw_early, qv_early = weight_grad(normed, *before)
    out_own = (out_own + out_sib.astype(F32)).astype(BF)
    block_one = jnp.concatenate([dw_early, dwp], axis=1).reshape(owners, shard, -1)
    grad_mixed, out_own, block_one = lax.optimization_barrier((grad_mixed, out_own, block_one))
    came_one = exchange(block_one)
    out_came = partner(out_own[slots:])
    grads = attend(grad_mixed, grad_mixed_t, result_t, log_total, slots, early, late)

    def total(came):
        return jnp.sum(came.astype(F32), axis=0).astype(BF)

    def join(value, came):
        return (value.astype(F32) + came.astype(F32)).astype(BF)

    scattered_one, out_came, grads = lax.optimization_barrier((scattered_one, out_came, grads))
    output = hand_back(out_own, out_came)
    one_came = partner(scattered_one)
    one_sum = join(scattered_one, one_came)
    gn1_own, gn1_send, dw_late, vec_first, qv_late = project_back(tok, normed, before, grads, w_qkv)

    def spread(vector):
        both = jnp.zeros((2, part), F32)
        return lax.dynamic_update_index_in_dim(both, vector, core, 0).reshape(width)

    def rows_of(block):
        return jnp.sum(block.reshape(block.shape[0] // 8, 8, block.shape[1]), axis=1)

    once = (core == 0).astype(F32)
    gg1, gb1 = rows_of(vec_first)
    gqb, gvb = rows_of(jnp.concatenate([qv_early, qv_late], axis=1))
    gg2, gb2, gpb = rows_of(vec_back) * once
    gf2b = jnp.sum(gf2, axis=0) * once
    gf1b = jnp.sum(gf1, axis=0).reshape(2, owners, quarter).transpose(1, 0, 2)
    gf1b = lax.dynamic_update_index_in_dim(
        jnp.zeros((owners, 2, 2, quarter), F32), gf1b, core, 1
    ).reshape(owners, ff_shard)
    late_wide = 3 * late * PAIR
    small_grads = jnp.stack(
        [gg1, gb1, spread(gqb), spread(gvb), gpb, gg2, gb2, gf2b]
    ).reshape(8, owners, shard).transpose(1, 0, 2)
    small_block = jnp.concatenate(
        [
            jnp.pad(small_grads, ((0, 0), (0, 0), (0, late_wide - shard))),
            jnp.pad(gf1b[:, None], ((0, 0), (0, VEC_ROWS - 9), (0, late_wide - ff_shard))),
        ],
        axis=1,
    ).astype(BF)
    block_two = jnp.concatenate(
        [small_block, dw_late.reshape(owners, shard, late_wide)], axis=1
    )
    gn1_sib = sibling(gn1_send)
    block_two, came_one = lax.optimization_barrier((block_two, came_one))
    came_two = exchange(block_two)
    input_own, input_send = input_back(tok, gn1_own, gn1_sib, grad_middle, vec_one)
    input_came = partner(input_send)
    early_total = total(came_one)
    early_came = partner(early_total)
    one_came, input_own, output = lax.optimization_barrier((one_came, input_own, output))
    one_sum = join(scattered_one, one_came)
    came_two, one_sum = lax.optimization_barrier((came_two, one_sum))
    one_other = sibling(one_sum)
    grad_fc1, grad_fc2 = finish_ff(place_row, one_sum, one_other, width, quarter)

    early_sum = join(early_total, early_came)
    early_other = sibling(early_sum)
    late_total, input_came = lax.optimization_barrier((total(came_two), input_came))
    input_grad = hand_back(input_own, input_came)
    late_came = [
        lax.ppermute(late_total, "seq", [(at, at ^ flip) for at in range(seq)])
        for flip in (2, 1, 3)
    ]
    late_came, grad_fc1, grad_fc2 = lax.optimization_barrier((late_came, grad_fc1, grad_fc2))
    grad_qkv, grad_proj, small_sum = finish_attend(
        place_row, early_sum, early_other, late_total, *late_came, width
    )
    s = [small_sum[at, :shard] for at in range(8)]
    grad_f1b = small_sum[8, :ff_shard]
    return (
        output,
        input_grad,
        s[0],
        s[1],
        grad_qkv,
        s[2],
        s[3],
        grad_proj,
        s[4],
        s[5],
        s[6],
        grad_fc1,
        grad_f1b,
        grad_fc2,
        s[7],
    )


def solution(mesh):
    placed = (
        P("fsdp", "seq", None),
        P("fsdp", None),
        P("fsdp"),
        P("fsdp"),
        P("fsdp", None),
        P("fsdp"),
        P("fsdp"),
        P("fsdp", None),
        P("fsdp"),
        P("fsdp"),
        P("fsdp"),
        P("fsdp", None),
        P("fsdp"),
        P("fsdp", None),
        P("fsdp"),
        P("fsdp", "seq", None),
    )
    return jax.shard_map(
        per_device,
        mesh=mesh,
        in_specs=placed,
        out_specs=(
            P("fsdp", "seq", None),
            P("fsdp", "seq", None),
            P("fsdp"),
            P("fsdp"),
            P("fsdp", None),
            P("fsdp"),
            P("fsdp"),
            P("fsdp", None),
            P("fsdp"),
            P("fsdp"),
            P("fsdp"),
            P("fsdp", None),
            P("fsdp"),
            P("fsdp", None),
            P("fsdp"),
        ),
        check_vma=False,
    )
```

```python
import functools

import jax
import jax.numpy as jnp
from jax import lax
from jax.experimental import pallas as pl
from jax.experimental.pallas import tpu as pltpu
from jax.sharding import PartitionSpec as P

HEADS = 12
HEAD_DIM = 64
EPSILON = 1e-06
MASKED = -1e30
BF = jnp.bfloat16
F32 = jnp.float32
MIB = 1024 * 1024
PAIR = 2 * HEAD_DIM
VEC_ROWS = 16
SLOT_ORDER = (0, 2, 1, 3)
ERF_TERMS = tuple(
    0.5 * term for term in (0.254829592, -0.284496736, 1.421413741, -1.453152027, 1.061405429)
)


def params(mebibytes, *semantics):
    return pltpu.CompilerParams(
        dimension_semantics=semantics, vmem_limit_bytes=mebibytes * MIB
    )


def dot(left, right, left_dim=1, right_dim=0):
    return lax.dot_general(
        left, right, (((left_dim,), (right_dim,)), ((), ())), preferred_element_type=F32
    )


def cost(flops, bytes_accessed, transcendentals=0):
    return pl.CostEstimate(
        flops=int(flops), bytes_accessed=int(bytes_accessed), transcendentals=int(transcendentals)
    )


def whole(shape):
    return pl.BlockSpec(shape, lambda *_: tuple(0 for _ in shape))


def key_bias(counts_ref, place_ref, keys, slots):
    row = lax.broadcasted_iota(jnp.int32, (slots, PAIR), 0)
    place = place_ref[0]
    parts = []
    for flip in SLOT_ORDER:
        kept = counts_ref[place // 2, jnp.bitwise_xor(place, flip)]
        parts.append(jnp.where(row < kept, 0.0, MASKED).astype(F32))
    return jnp.concatenate(parts, axis=0)


def augment_keys(pair, bias, which, ones):
    lane = lax.broadcasted_iota(jnp.int32, pair.shape, 1)
    mine = (lane < HEAD_DIM) if which == 0 else (lane >= HEAD_DIM)
    start = HEAD_DIM if which == 0 else 0
    extra = jnp.where(
        lane == start, bias, jnp.where((lane > start) & (lane <= start + ones), 1.0, 0.0)
    )
    return jnp.where(mine, pair.astype(F32), extra).astype(BF)


def augment_values(pair, which, ones):
    lane = lax.broadcasted_iota(jnp.int32, pair.shape, 1)
    mine = (lane < HEAD_DIM) if which == 0 else (lane >= HEAD_DIM)
    start = HEAD_DIM if which == 0 else 0
    extra = jnp.where((lane >= start) & (lane < start + ones), 1.0, 0.0)
    return jnp.where(mine, pair.astype(F32), extra).astype(BF)


def pieces(value):
    first = value.astype(BF).astype(F32)
    rest = value - first
    second = rest.astype(BF).astype(F32)
    return first, second, rest - second


def extra_rows(rows, width):
    place = lax.broadcasted_iota(jnp.int32, (HEAD_DIM, width), 0)
    out = jnp.zeros((HEAD_DIM, width), F32)
    for at, row in enumerate(rows):
        out = jnp.where(place == at, row, out)
    return out.astype(BF)


def place_rows(head, extra, which):
    return jnp.concatenate([head, extra] if which == 0 else [extra, head], axis=0)


def attend_forward_kernel(
    slots, bq, chunk, counts_ref, place_ref, k_ref, qt_ref, vt_ref, mixed_ref, ot_ref, lse_ref,
    kaug, vaug, s_a, s_b, m_a, m_b
):
    keys = k_ref.shape[0]
    step = pl.program_id(1)
    steps = pl.num_programs(1)
    scores = (s_a, s_b)
    peaks = (m_a, m_b)
    ones_row = extra_rows([jnp.ones((1, bq), F32)], bq)

    @pl.when(step == 0)
    def _():
        bias = key_bias(counts_ref, place_ref, keys, slots)
        ones = jnp.ones((16, keys), BF)
        for which in range(2):
            kaug[which] = augment_keys(k_ref[...], bias, which, 0)
            vaug[which] = jnp.concatenate(
                [vt_ref[which * HEAD_DIM : (which + 1) * HEAD_DIM, :], ones], axis=0
            )

    def query_block(at, which):
        head = qt_ref[which * HEAD_DIM : (which + 1) * HEAD_DIM, pl.ds(at * bq, bq)]
        head = (head.astype(F32) * HEAD_DIM ** (-0.5)).astype(BF)
        return place_rows(head, ones_row, which)

    def score_chunk(query, which, at, peak):
        rows = slice(at * chunk, (at + 1) * chunk)
        s = dot(kaug[which, rows, :], query)
        scores[which][rows, :] = s
        top = jnp.max(s.reshape(chunk // 8, 8, bq), axis=0)
        return top if peak is None else jnp.maximum(peak, top)

    def raise_chunk(which, at, peak):
        rows = slice(at * chunk, (at + 1) * chunk)
        return jnp.exp(scores[which][rows, :] - peak).astype(BF)

    def weigh_chunk(which, at, p, total):
        o = dot(vaug[which, :, at * chunk : (at + 1) * chunk], p)
        return o if total is None else total + o

    @pl.when(step == 0)
    def _():
        query = query_block(0, 0)
        peak = None
        for at in range(keys // chunk):
            peak = score_chunk(query, 0, at, peak)
        m_a[...] = peak

    later = jnp.minimum(step + 1, steps - 1)
    outs = []
    for which in range(2):
        other = 1 - which
        query = query_block(step if which == 0 else later, other)
        peak = jnp.max(peaks[which][...], axis=0, keepdims=True)
        next_peak, total, behind = None, None, None
        for at in range(keys // chunk):
            next_peak = score_chunk(query, other, at, next_peak)
            if behind is not None:
                total = weigh_chunk(which, at - 1, behind, total)
            behind = raise_chunk(which, at, peak)
        total = weigh_chunk(which, keys // chunk - 1, behind, total)
        peaks[other][...] = next_peak
        norm = total[HEAD_DIM : HEAD_DIM + 1, :]
        outs.append(total[:HEAD_DIM, :] * (1.0 / norm))
        lse_ref[0, which : which + 1, :] = peak + jnp.log(norm)
    both = jnp.concatenate(outs, axis=0)
    ot_ref[...] = both
    mixed_ref[...] = both.T.astype(BF)


def attend_forward(counts, place, packed, packed_t, slots):
    keys, width = packed.shape
    width //= 3
    pairs = width // PAIR
    bq, chunk = 256, 256
    kernel = functools.partial(attend_forward_kernel, slots, bq, chunk)
    return pl.pallas_call(
        kernel,
        grid=(pairs, keys // bq),
        in_specs=[
            pl.BlockSpec(memory_space=pltpu.SMEM),
            pl.BlockSpec(memory_space=pltpu.SMEM),
            pl.BlockSpec((keys, PAIR), lambda p, i: (0, pairs + p)),
            pl.BlockSpec((PAIR, keys), lambda p, i: (p, 0)),
            pl.BlockSpec((PAIR, keys), lambda p, i: (2 * pairs + p, 0)),
        ],
        out_specs=[
            pl.BlockSpec((bq, PAIR), lambda p, i: (i, p)),
            pl.BlockSpec((PAIR, bq), lambda p, i: (p, i)),
            pl.BlockSpec((1, 8, bq), lambda p, i: (p, 0, i)),
        ],
        out_shape=[
            jax.ShapeDtypeStruct((keys, width), BF),
            jax.ShapeDtypeStruct((width, keys), F32),
            jax.ShapeDtypeStruct((pairs, 8, keys), F32),
        ],
        scratch_shapes=[
            pltpu.VMEM((2, keys, PAIR), BF),
            pltpu.VMEM((2, HEAD_DIM + 16, keys), BF),
            pltpu.VMEM((keys, bq), F32),
            pltpu.VMEM((keys, bq), F32),
            pltpu.VMEM((8, bq), F32),
            pltpu.VMEM((8, bq), F32),
        ],
        compiler_params=params(60, "arbitrary", "arbitrary"),
        cost_estimate=cost(
            2 * pairs * 2 * 2 * keys * keys * 256, 12 * keys * width, 2 * pairs * keys * keys
        ),
        name="attend_forward",
    )(counts, place, packed, packed_t, packed_t)


def attend_backward_kernel(
    slots, bq, chunk, counts_ref, place_ref, q_ref, k_ref, v_ref, qt_ref, kt_ref, do_ref, dot_ref, ot_ref,
    lse_ref, gq_ref, gk_ref, gv_ref, kaug, vaug, acc_k, acc_v
):
    keys = k_ref.shape[0]
    step = pl.program_id(1)
    steps = pl.num_programs(1)
    scale = HEAD_DIM ** (-0.5)

    @pl.when(step == 0)
    def _():
        bias = key_bias(counts_ref, place_ref, keys, slots)
        for which in range(2):
            kaug[which] = augment_keys(k_ref[...], bias, which, 3)
            vaug[which] = augment_values(v_ref[...], which, 3)
        acc_k[...] = jnp.zeros_like(acc_k)
        acc_v[...] = jnp.zeros_like(acc_v)

    ones_row = jnp.ones((1, bq), F32)
    queries, grads = [], []
    for which in range(2):
        rows = slice(which * HEAD_DIM, (which + 1) * HEAD_DIM)
        head = (qt_ref[rows, :].astype(F32) * scale).astype(BF)
        log_total = lse_ref[0, which : which + 1, :]
        queries.append(
            place_rows(head, extra_rows([ones_row, *pieces(-log_total)], bq), which)
        )
        grad = dot_ref[rows, :]
        delta = jnp.sum(grad.astype(F32) * ot_ref[rows, :], axis=0, keepdims=True)
        grads.append(place_rows(grad, extra_rows(list(pieces(-delta)), bq), which))

    do_pair = do_ref[...]
    q_pair = q_ref[...]
    totals = [None, None]
    units = [(at, which) for at in range(keys // chunk) for which in range(2)]

    def front(at, which):
        rows = slice(at * chunk, (at + 1) * chunk)
        return dot(kaug[which, rows, :], queries[which]), dot(vaug[which, rows, :], grads[which])

    ahead = front(*units[0])
    behind = None
    for unit in range(len(units) + 1):
        now = ahead
        if unit + 1 < len(units):
            ahead = front(*units[unit + 1])
        if behind is not None:
            at, which = units[unit - 1]
            rows = slice(at * chunk, (at + 1) * chunk)
            p_low, ds = behind
            acc_v[which, rows, :] += dot(p_low, do_pair)
            acc_k[which, rows, :] += dot(ds, q_pair)
            part = dot(kt_ref[which * HEAD_DIM : (which + 1) * HEAD_DIM, rows], ds)
            totals[which] = part if totals[which] is None else totals[which] + part
        if unit < len(units):
            p = jnp.exp(now[0])
            behind = p.astype(BF), (p * now[1]).astype(BF)
    both = jnp.concatenate(totals, axis=0) * scale
    gq_ref[...] = both.T.astype(BF)

    @pl.when(step == steps - 1)
    def _():
        lane = lax.broadcasted_iota(jnp.int32, (keys, PAIR), 1)
        gk_ref[...] = (jnp.where(lane < HEAD_DIM, acc_k[0], acc_k[1]) * scale).astype(BF)
        gv_ref[...] = jnp.where(lane < HEAD_DIM, acc_v[0], acc_v[1]).astype(BF)


def attend_backward(
    counts, place, packed, packed_t, grad, grad_t, result_t, log_total, slots, start, count
):
    keys, width = packed.shape
    width //= 3
    pairs = width // PAIR
    bq, chunk = 512, 256
    kernel = functools.partial(attend_backward_kernel, slots, bq, chunk)
    at = lambda p: p + start
    return pl.pallas_call(
        kernel,
        grid=(count, keys // bq),
        in_specs=[
            pl.BlockSpec(memory_space=pltpu.SMEM),
            pl.BlockSpec(memory_space=pltpu.SMEM),
            pl.BlockSpec((bq, PAIR), lambda p, i: (i, at(p))),
            pl.BlockSpec((keys, PAIR), lambda p, i: (0, pairs + at(p))),
            pl.BlockSpec((keys, PAIR), lambda p, i: (0, 2 * pairs + at(p))),
            pl.BlockSpec((PAIR, bq), lambda p, i: (at(p), i)),
            pl.BlockSpec((PAIR, keys), lambda p, i: (pairs + at(p), 0)),
            pl.BlockSpec((bq, PAIR), lambda p, i: (i, at(p))),
            pl.BlockSpec((PAIR, bq), lambda p, i: (at(p), i)),
            pl.BlockSpec((PAIR, bq), lambda p, i: (at(p), i)),
            pl.BlockSpec((1, 8, bq), lambda p, i: (at(p), 0, i)),
        ],
        out_specs=[
            pl.BlockSpec((bq, PAIR), lambda p, i: (i, p)),
            pl.BlockSpec((keys, PAIR), lambda p, i: (0, p)),
            pl.BlockSpec((keys, PAIR), lambda p, i: (0, p)),
        ],
        out_shape=[jax.ShapeDtypeStruct((keys, count * PAIR), BF)] * 3,
        scratch_shapes=[
            pltpu.VMEM((2, keys, PAIR), BF),
            pltpu.VMEM((2, keys, PAIR), BF),
            pltpu.VMEM((2, keys, PAIR), F32),
            pltpu.VMEM((2, keys, PAIR), F32),
        ],
        compiler_params=params(60, "arbitrary", "arbitrary"),
        cost_estimate=cost(
            2 * count * 5 * 2 * keys * keys * 256, 24 * keys * count * PAIR,
            2 * count * keys * keys,
        ),
        name="attend_backward",
    )(counts, place, packed, packed, packed, packed_t, packed_t, grad, grad_t, result_t, log_total)


def normalised(values):
    centred = values - jnp.mean(values, axis=-1, keepdims=True)
    variance = jnp.mean(centred * centred, axis=-1, keepdims=True)
    inverse = lax.rsqrt(variance + EPSILON)
    return centred * inverse, inverse


def norm_pull(grad, gain, unit, inverse):
    scaled = grad * gain
    mean = jnp.mean(scaled, axis=-1, keepdims=True)
    along = jnp.mean(scaled * unit, axis=-1, keepdims=True)
    return inverse * (scaled - mean - unit * along)


def fold(values):
    return jnp.sum(values.reshape(values.shape[0] // 8, 8, values.shape[1]), axis=0)


def feed_forward_kernel(
    chunk, core_ref, tok_ref, mo_ref, ms_ref, cot_ref, wpx_ref, g2_ref, vec_ref, f1b_ref,
    mid_ref, out_ref, send_ref, gn_ref, dw_ref, gf1_ref, gf2_ref, wpo_ref, acc1, acc2, accb, accc, wps_ref,
    w1t_ref, w2t_ref
):
    step = pl.program_id(0)
    steps = pl.num_programs(0)
    width = tok_ref.shape[1]
    half = f1b_ref.shape[1]
    part = width // 2

    def weights(at):
        w1 = g2_ref[:, part + at * chunk : part + (at + 1) * chunk]
        piece, row = divmod(at * chunk, width)
        start = part + half + piece * width
        return w1, g2_ref[row : row + chunk, start : start + width]

    @pl.when(step == 0)
    def _():
        acc1[...] = jnp.zeros_like(acc1)
        acc2[...] = jnp.zeros_like(acc2)
        accb[...] = jnp.zeros_like(accb)
        accc[...] = jnp.zeros_like(accc)
        here = pl.ds(pl.multiple_of(core_ref[0] * part, part), part)
        there = pl.ds(pl.multiple_of((1 - core_ref[0]) * part, part), part)
        wpo_ref[:, here] = g2_ref[here, :part]
        wpo_ref[:, there] = wpx_ref[here, :]
        wps_ref[:, here] = g2_ref[there, :part]
        wps_ref[:, there] = wpx_ref[there, :]
        for at in range(half // chunk):
            cols = slice(at * chunk, (at + 1) * chunk)
            w1, w2 = weights(at)
            w1t_ref[cols, :] = w1.T
            w2t_ref[:, cols] = w2.T

    middle = (
        tok_ref[...].astype(F32)
        + dot(mo_ref[...], wpo_ref[...])
        + dot(ms_ref[...], wps_ref[...])
        + vec_ref[0:1, :]
    )
    mid_ref[...] = middle
    unit, _ = normalised(middle)
    normed = (unit * vec_ref[1:2, :] + vec_ref[2:3, :]).astype(BF)
    normed_t = normed.T
    cot = cot_ref[...]
    out = None
    grad = None

    def front(at):
        w1, _ = weights(at)
        hidden = dot(normed, w1) + f1b_ref[0:1, at * chunk : (at + 1) * chunk]
        return hidden, dot(cot, w2t_ref[:, at * chunk : (at + 1) * chunk])

    def middle_part(hidden, grad_active):
        bell = jnp.exp(hidden * hidden * -0.5)
        inverse = pl.reciprocal(1.0 + jnp.abs(hidden) * (0.3275911 * 0.5**0.5), approx=False)
        tail = ERF_TERMS[4]
        for term in ERF_TERMS[3::-1]:
            tail = tail * inverse + term
        tail = tail * inverse * bell
        below = jnp.where(hidden >= 0.0, 1.0 - tail, tail)
        slope = below + hidden * (bell * 0.3989422804014327)
        return (hidden * below).astype(BF), (grad_active * slope).astype(BF)

    chunks = half // chunk
    ahead = front(0)
    behind = None
    for at in range(chunks + 1):
        now = ahead
        if at + 1 < chunks:
            ahead = front(at + 1)
        if behind is not None:
            active, grad_hidden = behind
            cols = slice((at - 1) * chunk, at * chunk)
            _, w2 = weights(at - 1)
            more = dot(active, w2)
            out = more if out is None else out + more
            more = dot(grad_hidden, w1t_ref[cols, :])
            grad = more if grad is None else grad + more
            acc1[:, cols] += dot(normed_t, grad_hidden)
            acc2[cols, :] += dot(active, cot, 0, 0)
            accb[:, cols] += fold(grad_hidden.astype(F32))
        if at < chunks:
            behind = middle_part(*now)
    accc[...] += fold(cot.astype(F32))
    gn_ref[...] = grad.astype(BF)

    @pl.when(step < steps // 2)
    def _():
        out_ref[...] = middle + out + vec_ref[3:4, :]

    @pl.when(step >= steps // 2)
    def _():
        send_ref[...] = out.astype(BF)

    @pl.when(step == steps - 1)
    def _():
        dw_ref[:, :half] = acc1[...].astype(BF)
        for piece in range(half // width):
            dw_ref[:, half + piece * width : half + (piece + 1) * width] = acc2[
                piece * width : (piece + 1) * width, :
            ].astype(BF)
        gf1_ref[...] = accb[...]
        gf2_ref[...] = accc[...]


def feed_forward(core, tokens, mixed_own, mixed_sib, cot, wp_other, weights, vec, f1b):
    rows, width = tokens.shape
    half = f1b.shape[1]
    heads = mixed_own.shape[1]
    bt, chunk = 512, 768
    blocks = rows // bt
    kernel = functools.partial(feed_forward_kernel, chunk)
    return pl.pallas_call(
        kernel,
        grid=(blocks,),
        in_specs=[
            pl.BlockSpec(memory_space=pltpu.SMEM),
            pl.BlockSpec((bt, width), lambda i: (i, 0)),
            pl.BlockSpec((bt, heads), lambda i: (i, 0)),
            pl.BlockSpec((bt, heads), lambda i: (lax.rem(i + blocks // 2, blocks), 0)),
            pl.BlockSpec((bt, width), lambda i: (i, 0)),
            whole(wp_other.shape),
            whole(weights.shape),
            whole(vec.shape),
            whole(f1b.shape),
        ],
        out_specs=[
            pl.BlockSpec((bt, width), lambda i: (i, 0)),
            pl.BlockSpec((bt, width), lambda i: (jnp.minimum(i, blocks // 2 - 1), 0)),
            pl.BlockSpec((bt, width), lambda i: (jnp.maximum(i - blocks // 2, 0), 0)),
            pl.BlockSpec((bt, width), lambda i: (i, 0)),
            whole((width, 2 * half)),
            whole((8, half)),
            whole((8, width)),
            whole((width // 2, width)),
        ],
        out_shape=[
            jax.ShapeDtypeStruct((rows, width), F32),
            jax.ShapeDtypeStruct((rows // 2, width), F32),
            jax.ShapeDtypeStruct((rows // 2, width), BF),
            jax.ShapeDtypeStruct((rows, width), BF),
            jax.ShapeDtypeStruct((width, 2 * half), BF),
            jax.ShapeDtypeStruct((8, half), F32),
            jax.ShapeDtypeStruct((8, width), F32),
            jax.ShapeDtypeStruct((width // 2, width), BF),
        ],
        scratch_shapes=[
            pltpu.VMEM((width, half), F32),
            pltpu.VMEM((half, width), F32),
            pltpu.VMEM((8, half), F32),
            pltpu.VMEM((8, width), F32),
            pltpu.VMEM((width // 2, width), BF),
            pltpu.VMEM((half, width), BF),
            pltpu.VMEM((width, half), BF),
        ],
        compiler_params=params(60, "arbitrary"),
        cost_estimate=cost(
            2 * rows * width * (6 * half + width), 20 * rows * width + 8 * width * half,
            2 * rows * half,
        ),
        name="feed_forward",
    )(core, tokens, mixed_own, mixed_sib, cot, wp_other, weights, vec, f1b)


def branch_kernel(
    core_ref, mid_ref, ga_ref, gb_ref, cot_ref, mo_ref, ms_ref, wpo_ref, vec_ref,
    gm_ref, do_ref, dot_ref, dwo_ref, dws_ref, vecs_ref, acco, accs, accv, low_ref, wpt_ref
):
    step = pl.program_id(0)
    steps = pl.num_programs(0)
    half = do_ref.shape[1]

    @pl.when(step == 0)
    def _():
        acco[...] = jnp.zeros_like(acco)
        accs[...] = jnp.zeros_like(accs)
        wpt_ref[...] = wpo_ref[...].T
        accv[...] = jnp.zeros_like(accv)

    unit, inverse = normalised(mid_ref[...])
    grad = ga_ref[...].astype(F32) + gb_ref[...].astype(F32)
    accv[0:8, :] += fold(grad * unit)
    accv[8:16, :] += fold(grad)
    grad_middle = cot_ref[...].astype(F32) + norm_pull(grad, vec_ref[1:2, :], unit, inverse)

    @pl.when(step < steps // 2)
    def _():
        gm_ref[...] = grad_middle

    low = grad_middle.astype(BF)
    low_ref[...] = low
    accv[16:24, :] += fold(low.astype(F32))
    back = dot(low, wpt_ref[...])
    do_ref[...] = back.astype(BF)
    dot_ref[...] = back.T.astype(BF)
    mine = low_ref[:, pl.ds(pl.multiple_of(core_ref[0] * half, half), half)]
    acco[...] += dot(mo_ref[...].astype(BF), mine)
    accs[...] += dot(ms_ref[...], mine, 0, 0)

    @pl.when(step == steps - 1)
    def _():
        dwo_ref[...] = acco[...].astype(BF)
        dws_ref[...] = accs[...].astype(BF)
        vecs_ref[...] = accv[...]


def branch(core, middle, grad_own, grad_sib, cot, result_t, mixed_sib, wp_own, vec):
    rows, width = middle.shape
    half = mixed_sib.shape[1]
    bt = 512
    blocks = rows // bt
    swap = lambda i: (lax.rem(i + blocks // 2, blocks), 0)
    straight = lambda i: (i, 0)
    return pl.pallas_call(
        branch_kernel,
        grid=(blocks,),
        in_specs=[
            pl.BlockSpec(memory_space=pltpu.SMEM),
            pl.BlockSpec((bt, width), straight),
            pl.BlockSpec((bt, width), straight),
            pl.BlockSpec((bt, width), swap),
            pl.BlockSpec((bt, width), straight),
            pl.BlockSpec((half, bt), lambda i: (0, i)),
            pl.BlockSpec((bt, half), swap),
            whole(wp_own.shape),
            whole(vec.shape),
        ],
        out_specs=[
            pl.BlockSpec((bt, width), lambda i: (jnp.minimum(i, blocks // 2 - 1), 0)),
            pl.BlockSpec((bt, half), straight),
            pl.BlockSpec((half, bt), lambda i: (0, i)),
            whole((half, half)),
            whole((half, half)),
            whole((24, width)),
        ],
        out_shape=[
            jax.ShapeDtypeStruct((rows // 2, width), F32),
            jax.ShapeDtypeStruct((rows, half), BF),
            jax.ShapeDtypeStruct((half, rows), BF),
            jax.ShapeDtypeStruct((half, half), BF),
            jax.ShapeDtypeStruct((half, half), BF),
            jax.ShapeDtypeStruct((24, width), F32),
        ],
        scratch_shapes=[
            pltpu.VMEM((half, half), F32),
            pltpu.VMEM((half, half), F32),
            pltpu.VMEM((24, width), F32),
            pltpu.VMEM((bt, width), BF),
            pltpu.VMEM((width, half), BF),
        ],
        compiler_params=params(60, "arbitrary"),
        cost_estimate=cost(2 * rows * width * 3 * half, 18 * rows * width),
        name="branch",
    )(core, middle, grad_own, grad_sib, cot, result_t, mixed_sib, wp_own, vec)


def weight_grad_kernel(
    core_ref, normed_ref, gq_ref, gk_ref, gv_ref, dwo_ref, dws_ref, dw_ref, qv_ref, accw, accqv
):
    step = pl.program_id(0)
    steps = pl.num_programs(0)
    part = gq_ref.shape[1]

    @pl.when(step == 0)
    def _():
        accw[...] = jnp.zeros_like(accw)
        accqv[...] = jnp.zeros_like(accqv)

    normed_t = normed_ref[...].T
    for at, ref in enumerate((gq_ref, gk_ref, gv_ref)):
        cols = slice(at * part, (at + 1) * part)
        value = ref[...]
        accw[:, cols] += dot(normed_t, value)
        if at != 1:
            here = 0 if at == 0 else 8
            accqv[here : here + 8, :] += fold(value.astype(F32))

    @pl.when(step == steps - 1)
    def _():
        dw_ref[:, : 3 * part] = accw[...].astype(BF)
        rows = dwo_ref.shape[0]
        first_core = core_ref[0] == 0
        dwo, dws = dwo_ref[...], dws_ref[...]
        dw_ref[:rows, 3 * part :] = jnp.where(first_core, dwo, dws)
        dw_ref[rows:, 3 * part :] = jnp.where(first_core, dws, dwo)
        qv_ref[...] = accqv[...]


def weight_grad(core, normed, gq, gk, gv, dw_own, dw_sib):
    rows, width = normed.shape
    part = gq.shape[1]
    bt = 512
    wide = 3 * part + dw_own.shape[1]
    straight = lambda i: (i, 0)
    return pl.pallas_call(
        weight_grad_kernel,
        grid=(rows // bt,),
        in_specs=[
            pl.BlockSpec(memory_space=pltpu.SMEM),
            pl.BlockSpec((bt, width), straight),
            pl.BlockSpec((bt, part), straight),
            pl.BlockSpec((bt, part), straight),
            pl.BlockSpec((bt, part), straight),
            whole(dw_own.shape),
            whole(dw_sib.shape),
        ],
        out_specs=[whole((width, wide)), whole((16, part))],
        out_shape=[
            jax.ShapeDtypeStruct((width, wide), BF),
            jax.ShapeDtypeStruct((16, part), F32),
        ],
        scratch_shapes=[pltpu.VMEM((width, 3 * part), F32), pltpu.VMEM((16, part), F32)],
        compiler_params=params(60, "arbitrary"),
        cost_estimate=cost(2 * rows * width * 3 * part, 2 * rows * (width + 3 * part)),
        name="weight_grad",
    )(core, normed, gq, gk, gv, dw_own, dw_sib)


def project_back_kernel(
    tok_ref, normed_ref, gqa_ref, gka_ref, gva_ref, gq_ref, gk_ref, gv_ref, w_ref,
    own_ref, sib_ref, dw_ref, vecs_ref, qv_ref, accw, accv, accqv, wt_ref
):
    step = pl.program_id(0)
    steps = pl.num_programs(0)
    early = gqa_ref.shape[1]
    part = gq_ref.shape[1]
    wide = early + part

    @pl.when(step == 0)
    def _():
        accw[...] = jnp.zeros_like(accw)
        accv[...] = jnp.zeros_like(accv)
        accqv[...] = jnp.zeros_like(accqv)
        wt_ref[...] = w_ref[...].T

    unit, _ = normalised(tok_ref[...].astype(F32))
    normed_t = normed_ref[...].T
    grad = None
    before = (gqa_ref, gka_ref, gva_ref)
    for at, ref in enumerate((gq_ref, gk_ref, gv_ref)):
        cols = slice(at * part, (at + 1) * part)
        value = ref[...]
        more = dot(
            jnp.concatenate([before[at][...], value], axis=1),
            wt_ref[at * wide : (at + 1) * wide, :],
        )
        grad = more if grad is None else grad + more
        accw[:, cols] += dot(normed_t, value)
        if at != 1:
            here = 0 if at == 0 else 8
            accqv[here : here + 8, :] += fold(value.astype(F32))
    accv[0:8, :] += fold(grad * unit)
    accv[8:16, :] += fold(grad)

    @pl.when(step < steps // 2)
    def _():
        own_ref[...] = grad

    @pl.when(step >= steps // 2)
    def _():
        sib_ref[...] = grad.astype(BF)

    @pl.when(step == steps - 1)
    def _():
        dw_ref[...] = accw[...].astype(BF)
        vecs_ref[...] = accv[...]
        qv_ref[...] = accqv[...]


def project_back(tokens, normed, before, grads, weight):
    rows, width = tokens.shape
    early, part = before[0].shape[1], grads[0].shape[1]
    bt = 512
    blocks = rows // bt
    straight = lambda i: (i, 0)
    return pl.pallas_call(
        project_back_kernel,
        grid=(blocks,),
        in_specs=[pl.BlockSpec((bt, width), straight)] * 2
        + [pl.BlockSpec((bt, early), straight)] * 3
        + [pl.BlockSpec((bt, part), straight)] * 3
        + [whole(weight.shape)],
        out_specs=[
            pl.BlockSpec((bt, width), lambda i: (jnp.minimum(i, blocks // 2 - 1), 0)),
            pl.BlockSpec((bt, width), lambda i: (jnp.maximum(i - blocks // 2, 0), 0)),
            whole((width, 3 * part)),
            whole((16, width)),
            whole((16, part)),
        ],
        out_shape=[
            jax.ShapeDtypeStruct((rows // 2, width), F32),
            jax.ShapeDtypeStruct((rows // 2, width), BF),
            jax.ShapeDtypeStruct((width, 3 * part), BF),
            jax.ShapeDtypeStruct((16, width), F32),
            jax.ShapeDtypeStruct((16, part), F32),
        ],
        scratch_shapes=[
            pltpu.VMEM((width, 3 * part), F32),
            pltpu.VMEM((16, width), F32),
            pltpu.VMEM((16, part), F32),
            pltpu.VMEM((3 * (early + part), width), BF),
        ],
        compiler_params=params(60, "arbitrary"),
        cost_estimate=cost(2 * rows * width * (6 * part + 3 * early), 14 * rows * width),
        name="project_back",
    )(tokens, normed, *before, *grads, weight)


def input_back_kernel(tok_ref, own_ref, sib_ref, gm_ref, vec_ref, keep_ref, send_ref):
    unit, inverse = normalised(tok_ref[...].astype(F32))
    grad = own_ref[...] + sib_ref[...].astype(F32)
    total = gm_ref[...] + norm_pull(grad, vec_ref[0:1, :], unit, inverse)
    step = pl.program_id(0)
    steps = pl.num_programs(0)

    @pl.when(step < steps // 2)
    def _():
        keep_ref[...] = total

    @pl.when(step >= steps // 2)
    def _():
        send_ref[...] = total.astype(BF)


def input_back(tokens, grad_own, grad_sib, grad_middle, vec):
    rows, width = grad_own.shape
    bt = 256
    blocks = rows // bt
    straight = lambda i: (i, 0)
    return pl.pallas_call(
        input_back_kernel,
        grid=(blocks,),
        in_specs=[pl.BlockSpec((bt, width), straight)] * 4 + [whole(vec.shape)],
        out_specs=[
            pl.BlockSpec((bt, width), lambda i: (jnp.minimum(i, blocks // 2 - 1), 0)),
            pl.BlockSpec((bt, width), lambda i: (jnp.maximum(i - blocks // 2, 0), 0)),
        ],
        out_shape=[
            jax.ShapeDtypeStruct((rows // 2, width), F32),
            jax.ShapeDtypeStruct((rows // 2, width), BF),
        ],
        compiler_params=params(60, "arbitrary"),
        cost_estimate=cost(20 * rows * width, 16 * rows * width),
        name="input_back",
    )(tokens, grad_own, grad_sib, grad_middle, vec)


def finish_ff_kernel(place_ref, mine_ref, other_ref, fc1_ref, fc2_ref):
    first_core = lax.rem(place_ref[0], 2) == 0
    shard, ff = fc1_ref.shape
    half = ff // 2
    quarter = fc2_ref.shape[0] // 4
    width = fc2_ref.shape[1]
    owners = ff // (4 * quarter)
    mine = mine_ref[...].astype(F32)
    other = other_ref[...].astype(F32)
    cores = (jnp.where(first_core, mine, other), jnp.where(first_core, other, mine))
    pieces = []
    for owner in range(owners):
        for value in cores:
            for piece in range(2):
                start = (piece * owners + owner) * quarter
                pieces.append(value[:, start : start + quarter])
    fc1_ref[...] = jnp.concatenate(pieces, axis=1)
    for at, value in enumerate(cores):
        for piece in range(2):
            row = (2 * at + piece) * quarter
            start = half + piece * width
            fc2_ref[row : row + quarter, :] = value[:, start : start + width]


def finish_ff(place, mine, other, width, quarter):
    shard, wide = mine.shape
    return pl.pallas_call(
        finish_ff_kernel,
        grid=(1,),
        in_specs=[
            pl.BlockSpec(memory_space=pltpu.SMEM), whole(mine.shape), whole(other.shape)
        ],
        out_specs=[whole((shard, wide)), whole((4 * quarter, width))],
        out_shape=[
            jax.ShapeDtypeStruct((shard, wide), F32),
            jax.ShapeDtypeStruct((4 * quarter, width), F32),
        ],
        compiler_params=params(60, "arbitrary"),
        cost_estimate=cost(0, 12 * shard * wide),
        name="finish_ff",
    )(place, mine, other)


def finish_attend_kernel(
    place_ref, em_ref, eo_ref, la_ref, lb_ref, lc_ref, ld_ref, qkv_ref, proj_ref, small_ref
):
    first_core = lax.rem(place_ref[0], 2) == 0
    shard, width = proj_ref.shape
    part = width // 2
    late = la_ref.shape[1] // 3
    early = part - late
    rows = la_ref.shape[0] - shard
    lm = la_ref[...].astype(F32) + lb_ref[...].astype(F32)
    lo = lc_ref[...].astype(F32) + ld_ref[...].astype(F32)
    small_ref[...] = lm[:rows] + lo[:rows]
    em = em_ref[...].astype(F32)
    eo = eo_ref[...].astype(F32)
    firsts = (jnp.where(first_core, em, eo), jnp.where(first_core, eo, em))
    lasts = (jnp.where(first_core, lm, lo)[rows:], jnp.where(first_core, lo, lm)[rows:])
    for at in range(3):
        for of in range(2):
            start = at * width + of * part
            qkv_ref[:, start : start + early] = firsts[of][:, at * early : (at + 1) * early]
            qkv_ref[:, start + early : start + part] = lasts[of][:, at * late : (at + 1) * late]
    for of in range(2):
        proj_ref[:, of * part : (of + 1) * part] = firsts[of][:, 3 * early :]


def finish_attend(place, early_mine, early_other, late_mine, late_b, late_c, late_d, width):
    shard = early_mine.shape[0]
    rows = late_mine.shape[0] - shard
    return pl.pallas_call(
        finish_attend_kernel,
        grid=(1,),
        in_specs=[pl.BlockSpec(memory_space=pltpu.SMEM)]
        + [whole(value.shape) for value in (early_mine, early_other)]
        + [whole(late_mine.shape)] * 4,
        out_specs=[
            whole((shard, 3 * width)), whole((shard, width)), whole((rows, late_mine.shape[1]))
        ],
        out_shape=[
            jax.ShapeDtypeStruct((shard, 3 * width), F32),
            jax.ShapeDtypeStruct((shard, width), F32),
            jax.ShapeDtypeStruct((rows, late_mine.shape[1]), F32),
        ],
        compiler_params=params(60, "arbitrary"),
        cost_estimate=cost(0, 24 * shard * width),
        name="finish_attend",
    )(place, early_mine, early_other, late_mine, late_b, late_c, late_d)


def pack_kernel(place_ref, *refs):
    vectors, (qkv_ref, proj_ref, fc1_ref, fc2_ref, one_ref, two_ref) = refs[:-6], refs[-6:]
    first_core = lax.rem(place_ref[0], 2) == 0
    first_chip = place_ref[0] // 2 == 0
    shard, width = proj_ref.shape
    part = width // 2
    ff = fc1_ref.shape[1]
    owners = width // shard
    quarter = ff // owners // 4
    half = ff // 2
    one_ref[:VEC_ROWS, :] = jnp.zeros((VEC_ROWS, 3 * part), BF)
    for at, ref in enumerate(vectors):
        one_ref[at : at + 1, : ref.shape[1]] = ref[...]
    for at in range(3):
        low = qkv_ref[:, at * width : at * width + part]
        high = qkv_ref[:, at * width + part : (at + 1) * width]
        mine = jnp.where(first_core, low, high)
        mine = jnp.where(first_chip, mine[: shard // 2], mine[shard // 2 :])
        one_ref[VEC_ROWS:, at * part : (at + 1) * part] = mine
    two_ref[:, :part] = jnp.where(first_core, proj_ref[:, :part], proj_ref[:, part:])
    pieces_low, pieces_high = [], []
    for piece in range(2):
        for owner in range(owners):
            base = owner * 4 * quarter + piece * quarter
            pieces_low.append(fc1_ref[:, base : base + quarter])
            pieces_high.append(fc1_ref[:, base + 2 * quarter : base + 3 * quarter])
    two_ref[:, part : part + half] = jnp.where(
        first_core, jnp.concatenate(pieces_low, axis=1), jnp.concatenate(pieces_high, axis=1)
    )
    for piece in range(2):
        low = fc2_ref[piece * quarter : (piece + 1) * quarter, :]
        high = fc2_ref[(2 + piece) * quarter : (3 + piece) * quarter, :]
        start = part + half + piece * width
        two_ref[:, start : start + width] = jnp.where(first_core, low, high)


def pack_weights(place, vectors, qkv, proj, fc1, fc2):
    shard, width = proj.shape
    half = fc1.shape[1] // 2
    part = width // 2
    vectors = [vector.reshape(1, -1) for vector in vectors]
    values = (*vectors, qkv, proj, fc1, fc2)
    rows = VEC_ROWS + shard // 2
    return pl.pallas_call(
        pack_kernel,
        grid=(1,),
        in_specs=[pl.BlockSpec(memory_space=pltpu.SMEM)] + [whole(value.shape) for value in values],
        out_specs=[whole((rows, 3 * part)), whole((shard, 5 * part + half))],
        out_shape=[
            jax.ShapeDtypeStruct((rows, 3 * part), BF),
            jax.ShapeDtypeStruct((shard, 5 * part + half), BF),
        ],
        compiler_params=params(60, "arbitrary"),
        cost_estimate=cost(0, 5 * shard * width * 8),
        name="pack_weights",
    )(place, *values)


def project_kernel(tok_ref, w_ref, bias_ref, vec_ref, out_ref, out_t_ref, normed_ref):
    unit, _ = normalised(tok_ref[...].astype(F32))
    normed = (unit * vec_ref[0:1, :] + vec_ref[1:2, :]).astype(BF)
    normed_ref[...] = normed
    packed = dot(normed, w_ref[...]) + bias_ref[0:1, :]
    out_ref[...] = packed.astype(BF)
    out_t_ref[...] = packed.T.astype(BF)


def project(tokens, weight, bias, vec):
    rows, width = tokens.shape
    wide = weight.shape[1]
    bt = 512
    return pl.pallas_call(
        project_kernel,
        grid=(rows // bt,),
        in_specs=[
            pl.BlockSpec((bt, width), lambda i: (i, 0)),
            whole(weight.shape),
            whole(bias.shape),
            whole(vec.shape),
        ],
        out_specs=[
            pl.BlockSpec((bt, wide), lambda i: (i, 0)),
            pl.BlockSpec((wide, bt), lambda i: (0, i)),
            pl.BlockSpec((bt, width), lambda i: (i, 0)),
        ],
        out_shape=[
            jax.ShapeDtypeStruct((rows, wide), BF),
            jax.ShapeDtypeStruct((wide, rows), BF),
            jax.ShapeDtypeStruct((rows, width), BF),
        ],
        compiler_params=params(60, "arbitrary"),
        cost_estimate=cost(2 * rows * width * wide, 12 * rows * width),
        name="project",
    )(tokens, weight, bias, vec)


def exchange(value):
    return lax.all_to_all(value, "fsdp", split_axis=0, concat_axis=0, tiled=True)


def per_device(
    tokens,
    counts,
    norm1_gain,
    norm1_bias,
    qkv_weight,
    query_bias,
    value_bias,
    proj_weight,
    proj_bias,
    norm2_gain,
    norm2_bias,
    fc1_weight,
    fc1_bias,
    fc2_weight,
    fc2_bias,
    cotangent,
):
    images, slots, width = tokens.shape
    owners = lax.axis_size("fsdp")
    seq = lax.axis_size("seq")
    place = lax.axis_index("seq")
    core = lax.rem(place, 2)
    image = place // 2
    part = width // 2
    shard = width // owners
    ff = fc1_weight.shape[1]
    ff_shard = ff // owners
    quarter = ff_shard // 4
    half = ff // 2
    to_sibling = [(at, at ^ 1) for at in range(seq)]
    to_partner = [(at, at ^ 2) for at in range(seq)]

    def sibling(value):
        return lax.ppermute(value, "seq", to_sibling)

    def partner(value):
        return lax.ppermute(value, "seq", to_partner)

    def pick(value, at, axis):
        return lax.dynamic_index_in_dim(value, at, axis, keepdims=False)

    place_row = place.reshape(1).astype(jnp.int32)
    core_row = core.reshape(1).astype(jnp.int32)
    small = [
        norm1_gain, norm1_bias, query_bias, value_bias, proj_bias, norm2_gain, norm2_bias,
        fc2_bias, fc1_bias,
    ]
    one, two = pack_weights(
        place_row, small, qkv_weight, proj_weight, fc1_weight, fc2_weight
    )
    one, tokens, cotangent = lax.optimization_barrier((one, tokens, cotangent))
    mine_one = lax.all_gather(one, "fsdp", axis=0, tiled=False)
    def collect(value, theirs):
        mine = pick(value, image, 0)
        return jnp.concatenate([mine, theirs, sibling(mine), sibling(theirs)], axis=0)

    tok_came = partner(pick(tokens, 1 - image, 0))
    cot_came = partner(pick(cotangent, 1 - image, 0))
    mine_one, two, tok_came, cot_came = lax.optimization_barrier(
        (mine_one, two, tok_came, cot_came)
    )
    tok = collect(tokens, tok_came)
    cot = collect(cotangent, cot_came)
    second = lax.all_gather(two, "fsdp", axis=0, tiled=True)

    own_rows = mine_one[:, VEC_ROWS:]
    other_rows = partner(own_rows)
    w_qkv = jnp.where(
        image == 0,
        jnp.stack([own_rows, other_rows], axis=1),
        jnp.stack([other_rows, own_rows], axis=1),
    ).reshape(width, 3 * part)

    vecs = mine_one[:, :8, :shard].astype(F32).transpose(1, 0, 2).reshape(8, width)
    g1, b1, qb, vb, pb, g2, b2, f2b = vecs
    f1b = mine_one[:, 8, :ff_shard].astype(F32)
    f1b = pick(f1b.reshape(owners, 2, 2, quarter), core, 1)
    f1b = f1b.transpose(1, 0, 2).reshape(1, half)

    def mine_of(vector):
        return lax.dynamic_slice_in_dim(vector, core * part, part, 0)

    qkv_bias = jnp.concatenate([mine_of(qb), jnp.zeros((part,), F32), mine_of(vb)])
    vec_one = jnp.concatenate([jnp.stack([g1, b1]), jnp.zeros((6, width), F32)])
    packed, packed_t, normed = project(tok, w_qkv, qkv_bias.reshape(1, 3 * part), vec_one)
    packed, cot = lax.optimization_barrier((packed, cot))
    mixed, result_t, log_total = attend_forward(counts, place_row, packed, packed_t, slots)
    mixed_sib = sibling(mixed)

    wp_other = sibling(second[:, :part])
    vec_two = jnp.concatenate([jnp.stack([pb, g2, b2, f2b]), jnp.zeros((4, width), F32)])
    middle, out_own, out_send, gn_part, dw_ff, gf1, gf2, wp_own = feed_forward(
        core_row, tok, mixed, mixed_sib, cot, wp_other, second, vec_two, f1b
    )
    scattered_one = lax.psum_scatter(dw_ff, "fsdp", scatter_dimension=0, tiled=True)
    gn_sib = sibling(gn_part)
    rows_own = 2 * slots

    def hand_back(own, came):
        kept_part = own[:slots]
        came = came.astype(own.dtype)
        straight = jnp.stack([kept_part, came])
        crossed = jnp.stack([came, kept_part])
        return jnp.where(image == 0, straight, crossed)

    grad_middle, grad_mixed, grad_mixed_t, dwp_own, dwp_sib, vec_back = branch(
        core_row, middle, gn_part, gn_sib, cot, result_t, mixed_sib, wp_own, vec_two
    )
    grad_mixed, out_send, out_own = lax.optimization_barrier((grad_mixed, out_send, out_own))
    out_sib = sibling(out_send)
    early, late = 2, 1
    attend = functools.partial(attend_backward, counts, place_row, packed, packed_t)
    before = attend(grad_mixed, grad_mixed_t, result_t, log_total, slots, 0, early)
    before, out_sib = lax.optimization_barrier((before, out_sib))
    block_one, qv_early = weight_grad(core_row, normed, *before, dwp_own, dwp_sib)
    out_own = (out_own + out_sib.astype(F32)).astype(BF)
    block_one = block_one.reshape(owners, shard, -1)
    grad_mixed, out_own, block_one = lax.optimization_barrier((grad_mixed, out_own, block_one))
    came_one = exchange(block_one)
    out_came = partner(out_own[slots:])
    grads = attend(grad_mixed, grad_mixed_t, result_t, log_total, slots, early, late)

    def total(came):
        return jnp.sum(came.astype(F32), axis=0).astype(BF)

    def join(value, came):
        return (value.astype(F32) + came.astype(F32)).astype(BF)

    scattered_one, out_came, grads = lax.optimization_barrier((scattered_one, out_came, grads))
    output = hand_back(out_own, out_came)
    one_came = partner(scattered_one)
    gn1_own, gn1_send, dw_late, vec_first, qv_late = project_back(tok, normed, before, grads, w_qkv)

    def spread(vector):
        both = jnp.zeros((2, part), F32)
        return lax.dynamic_update_index_in_dim(both, vector, core, 0).reshape(width)

    def rows_of(block):
        return jnp.sum(block.reshape(block.shape[0] // 8, 8, block.shape[1]), axis=1)

    once = (core == 0).astype(F32)
    gg1, gb1 = rows_of(vec_first)
    gqb, gvb = rows_of(jnp.concatenate([qv_early, qv_late], axis=1))
    gg2, gb2, gpb = rows_of(vec_back) * once
    gf2b = jnp.sum(gf2, axis=0) * once
    gf1b = jnp.sum(gf1, axis=0).reshape(2, owners, quarter).transpose(1, 0, 2)
    gf1b = lax.dynamic_update_index_in_dim(
        jnp.zeros((owners, 2, 2, quarter), F32), gf1b, core, 1
    ).reshape(owners, ff_shard)
    late_wide = 3 * late * PAIR
    small_grads = jnp.stack(
        [gg1, gb1, spread(gqb), spread(gvb), gpb, gg2, gb2, gf2b]
    ).reshape(8, owners, shard).transpose(1, 0, 2)
    small_block = jnp.concatenate(
        [
            jnp.pad(small_grads, ((0, 0), (0, 0), (0, late_wide - shard))),
            jnp.pad(gf1b[:, None], ((0, 0), (0, VEC_ROWS - 9), (0, late_wide - ff_shard))),
        ],
        axis=1,
    ).astype(BF)
    block_two = jnp.concatenate(
        [small_block, dw_late.reshape(owners, shard, late_wide)], axis=1
    )
    gn1_sib = sibling(gn1_send)
    block_two, came_one = lax.optimization_barrier((block_two, came_one))
    came_two = exchange(block_two)
    input_own, input_send = input_back(tok, gn1_own, gn1_sib, grad_middle, vec_one)
    input_came = partner(input_send)
    early_total = total(came_one)
    early_came = partner(early_total)
    one_came, input_own = lax.optimization_barrier((one_came, input_own))
    one_sum = join(scattered_one, one_came)
    came_two, one_sum = lax.optimization_barrier((came_two, one_sum))
    one_other = sibling(one_sum)
    grad_fc1, grad_fc2 = finish_ff(place_row, one_sum, one_other, width, quarter)

    early_sum = join(early_total, early_came)
    early_other = sibling(early_sum)
    late_total, input_came, output = lax.optimization_barrier(
        (total(came_two), input_came, output)
    )
    input_grad = hand_back(input_own, input_came)
    late_came = [
        lax.ppermute(late_total, "seq", [(at, at ^ flip) for at in range(seq)])
        for flip in (2, 1, 3)
    ]
    late_came, grad_fc1, grad_fc2 = lax.optimization_barrier((late_came, grad_fc1, grad_fc2))
    grad_qkv, grad_proj, small_sum = finish_attend(
        place_row, early_sum, early_other, late_total, *late_came, width
    )
    s = [small_sum[at, :shard] for at in range(8)]
    grad_f1b = small_sum[8, :ff_shard]
    return (
        output,
        input_grad,
        s[0],
        s[1],
        grad_qkv,
        s[2],
        s[3],
        grad_proj,
        s[4],
        s[5],
        s[6],
        grad_fc1,
        grad_f1b,
        grad_fc2,
        s[7],
    )


def solution(mesh):
    placed = (
        P("fsdp", "seq", None),
        P("fsdp", None),
        P("fsdp"),
        P("fsdp"),
        P("fsdp", None),
        P("fsdp"),
        P("fsdp"),
        P("fsdp", None),
        P("fsdp"),
        P("fsdp"),
        P("fsdp"),
        P("fsdp", None),
        P("fsdp"),
        P("fsdp", None),
        P("fsdp"),
        P("fsdp", "seq", None),
    )
    return jax.shard_map(
        per_device,
        mesh=mesh,
        in_specs=placed,
        out_specs=(
            P("fsdp", "seq", None),
            P("fsdp", "seq", None),
            P("fsdp"),
            P("fsdp"),
            P("fsdp", None),
            P("fsdp"),
            P("fsdp"),
            P("fsdp", None),
            P("fsdp"),
            P("fsdp"),
            P("fsdp"),
            P("fsdp", None),
            P("fsdp"),
            P("fsdp", None),
            P("fsdp"),
        ),
        check_vma=False,
    )
```

```python
import functools

import jax
import jax.numpy as jnp
from jax import lax
from jax.experimental import pallas as pl
from jax.experimental.pallas import tpu as pltpu
from jax.sharding import PartitionSpec as P

HEADS = 12
HEAD_DIM = 64
EPSILON = 1e-06
MASKED = -1e30
BF = jnp.bfloat16
F32 = jnp.float32
MIB = 1024 * 1024
PAIR = 2 * HEAD_DIM
VEC_ROWS = 16
SLOT_ORDER = (0, 2, 1, 3)
ERF_TERMS = tuple(
    0.5 * term for term in (0.254829592, -0.284496736, 1.421413741, -1.453152027, 1.061405429)
)


def params(mebibytes, *semantics):
    return pltpu.CompilerParams(
        dimension_semantics=semantics, vmem_limit_bytes=mebibytes * MIB
    )


def dot(left, right, left_dim=1, right_dim=0):
    return lax.dot_general(
        left, right, (((left_dim,), (right_dim,)), ((), ())), preferred_element_type=F32
    )


def cost(flops, bytes_accessed, transcendentals=0):
    return pl.CostEstimate(
        flops=int(flops), bytes_accessed=int(bytes_accessed), transcendentals=int(transcendentals)
    )


def whole(shape):
    return pl.BlockSpec(shape, lambda *_: tuple(0 for _ in shape))


def key_bias(counts_ref, place_ref, keys, slots):
    row = lax.broadcasted_iota(jnp.int32, (slots, PAIR), 0)
    place = place_ref[0]
    parts = []
    for flip in SLOT_ORDER:
        kept = counts_ref[place // 2, jnp.bitwise_xor(place, flip)]
        parts.append(jnp.where(row < kept, 0.0, MASKED).astype(F32))
    return jnp.concatenate(parts, axis=0)


def augment_keys(pair, bias, which, ones):
    lane = lax.broadcasted_iota(jnp.int32, pair.shape, 1)
    mine = (lane < HEAD_DIM) if which == 0 else (lane >= HEAD_DIM)
    start = HEAD_DIM if which == 0 else 0
    extra = jnp.where(
        lane == start, bias, jnp.where((lane > start) & (lane <= start + ones), 1.0, 0.0)
    )
    return jnp.where(mine, pair.astype(F32), extra).astype(BF)


def augment_values(pair, which, ones):
    lane = lax.broadcasted_iota(jnp.int32, pair.shape, 1)
    mine = (lane < HEAD_DIM) if which == 0 else (lane >= HEAD_DIM)
    start = HEAD_DIM if which == 0 else 0
    extra = jnp.where((lane >= start) & (lane < start + ones), 1.0, 0.0)
    return jnp.where(mine, pair.astype(F32), extra).astype(BF)


def pieces(value):
    first = value.astype(BF).astype(F32)
    rest = value - first
    second = rest.astype(BF).astype(F32)
    return first, second, rest - second


def extra_rows(rows, width):
    place = lax.broadcasted_iota(jnp.int32, (HEAD_DIM, width), 0)
    out = jnp.zeros((HEAD_DIM, width), F32)
    for at, row in enumerate(rows):
        out = jnp.where(place == at, row, out)
    return out.astype(BF)


def place_rows(head, extra, which):
    return jnp.concatenate([head, extra] if which == 0 else [extra, head], axis=0)


def attend_forward_kernel(
    slots, bq, chunk, counts_ref, place_ref, k_ref, qt_ref, vt_ref, mixed_ref, ot_ref, lse_ref,
    kaug, vaug, s_a, s_b, m_a, m_b
):
    keys = k_ref.shape[0]
    step = pl.program_id(1)
    steps = pl.num_programs(1)
    scores = (s_a, s_b)
    peaks = (m_a, m_b)
    ones_row = extra_rows([jnp.ones((1, bq), F32)], bq)

    @pl.when(step == 0)
    def _():
        bias = key_bias(counts_ref, place_ref, keys, slots)
        ones = jnp.ones((16, keys), BF)
        for which in range(2):
            kaug[which] = augment_keys(k_ref[...], bias, which, 0)
            vaug[which] = jnp.concatenate(
                [vt_ref[which * HEAD_DIM : (which + 1) * HEAD_DIM, :], ones], axis=0
            )

    def query_block(at, which):
        head = qt_ref[which * HEAD_DIM : (which + 1) * HEAD_DIM, pl.ds(at * bq, bq)]
        head = (head.astype(F32) * HEAD_DIM ** (-0.5)).astype(BF)
        return place_rows(head, ones_row, which)

    def score_chunk(query, which, at, peak):
        rows = slice(at * chunk, (at + 1) * chunk)
        s = dot(kaug[which, rows, :], query)
        scores[which][rows, :] = s
        top = jnp.max(s.reshape(chunk // 8, 8, bq), axis=0)
        return top if peak is None else jnp.maximum(peak, top)

    def raise_chunk(which, at, peak):
        rows = slice(at * chunk, (at + 1) * chunk)
        return jnp.exp(scores[which][rows, :] - peak).astype(BF)

    def weigh_chunk(which, at, p, total):
        o = dot(vaug[which, :, at * chunk : (at + 1) * chunk], p)
        return o if total is None else total + o

    @pl.when(step == 0)
    def _():
        query = query_block(0, 0)
        peak = None
        for at in range(keys // chunk):
            peak = score_chunk(query, 0, at, peak)
        m_a[...] = peak

    later = jnp.minimum(step + 1, steps - 1)
    outs = []
    for which in range(2):
        other = 1 - which
        query = query_block(step if which == 0 else later, other)
        peak = jnp.max(peaks[which][...], axis=0, keepdims=True)
        next_peak, total, behind = None, None, None
        for at in range(keys // chunk):
            next_peak = score_chunk(query, other, at, next_peak)
            if behind is not None:
                total = weigh_chunk(which, at - 1, behind, total)
            behind = raise_chunk(which, at, peak)
        total = weigh_chunk(which, keys // chunk - 1, behind, total)
        peaks[other][...] = next_peak
        norm = total[HEAD_DIM : HEAD_DIM + 1, :]
        outs.append(total[:HEAD_DIM, :] * (1.0 / norm))
        lse_ref[0, which : which + 1, :] = peak + jnp.log(norm)
    both = jnp.concatenate(outs, axis=0)
    ot_ref[...] = both
    mixed_ref[...] = both.T.astype(BF)


def attend_forward(counts, place, packed, packed_t, slots):
    keys, width = packed.shape
    width //= 3
    pairs = width // PAIR
    bq, chunk = 256, 256
    kernel = functools.partial(attend_forward_kernel, slots, bq, chunk)
    return pl.pallas_call(
        kernel,
        grid=(pairs, keys // bq),
        in_specs=[
            pl.BlockSpec(memory_space=pltpu.SMEM),
            pl.BlockSpec(memory_space=pltpu.SMEM),
            pl.BlockSpec((keys, PAIR), lambda p, i: (0, pairs + p)),
            pl.BlockSpec((PAIR, keys), lambda p, i: (p, 0)),
            pl.BlockSpec((PAIR, keys), lambda p, i: (2 * pairs + p, 0)),
        ],
        out_specs=[
            pl.BlockSpec((bq, PAIR), lambda p, i: (i, p)),
            pl.BlockSpec((PAIR, bq), lambda p, i: (p, i)),
            pl.BlockSpec((1, 8, bq), lambda p, i: (p, 0, i)),
        ],
        out_shape=[
            jax.ShapeDtypeStruct((keys, width), BF),
            jax.ShapeDtypeStruct((width, keys), F32),
            jax.ShapeDtypeStruct((pairs, 8, keys), F32),
        ],
        scratch_shapes=[
            pltpu.VMEM((2, keys, PAIR), BF),
            pltpu.VMEM((2, HEAD_DIM + 16, keys), BF),
            pltpu.VMEM((keys, bq), F32),
            pltpu.VMEM((keys, bq), F32),
            pltpu.VMEM((8, bq), F32),
            pltpu.VMEM((8, bq), F32),
        ],
        compiler_params=params(60, "arbitrary", "arbitrary"),
        cost_estimate=cost(
            2 * pairs * 2 * 2 * keys * keys * 256, 12 * keys * width, 2 * pairs * keys * keys
        ),
        name="attend_forward",
    )(counts, place, packed, packed_t, packed_t)


def attend_backward_kernel(
    slots, bq, chunk, counts_ref, place_ref, q_ref, k_ref, v_ref, qt_ref, kt_ref, do_ref, dot_ref, ot_ref,
    lse_ref, gq_ref, gk_ref, gv_ref, kaug, vaug, acc_k, acc_v
):
    keys = k_ref.shape[0]
    step = pl.program_id(1)
    steps = pl.num_programs(1)
    scale = HEAD_DIM ** (-0.5)

    @pl.when(step == 0)
    def _():
        bias = key_bias(counts_ref, place_ref, keys, slots)
        for which in range(2):
            kaug[which] = augment_keys(k_ref[...], bias, which, 3)
            vaug[which] = augment_values(v_ref[...], which, 3)
        acc_k[...] = jnp.zeros_like(acc_k)
        acc_v[...] = jnp.zeros_like(acc_v)

    ones_row = jnp.ones((1, bq), F32)
    queries, grads = [], []
    for which in range(2):
        rows = slice(which * HEAD_DIM, (which + 1) * HEAD_DIM)
        head = (qt_ref[rows, :].astype(F32) * scale).astype(BF)
        log_total = lse_ref[0, which : which + 1, :]
        queries.append(
            place_rows(head, extra_rows([ones_row, *pieces(-log_total)], bq), which)
        )
        grad = dot_ref[rows, :]
        delta = jnp.sum(grad.astype(F32) * ot_ref[rows, :], axis=0, keepdims=True)
        grads.append(place_rows(grad, extra_rows(list(pieces(-delta)), bq), which))

    do_pair = do_ref[...]
    q_pair = q_ref[...]
    totals = [None, None]
    units = [(at, which) for at in range(keys // chunk) for which in range(2)]

    def front(at, which):
        rows = slice(at * chunk, (at + 1) * chunk)
        return dot(kaug[which, rows, :], queries[which]), dot(vaug[which, rows, :], grads[which])

    ahead = front(*units[0])
    behind = None
    for unit in range(len(units) + 1):
        now = ahead
        if unit + 1 < len(units):
            ahead = front(*units[unit + 1])
        if behind is not None:
            at, which = units[unit - 1]
            rows = slice(at * chunk, (at + 1) * chunk)
            p_low, ds = behind
            acc_v[which, rows, :] += dot(p_low, do_pair)
            acc_k[which, rows, :] += dot(ds, q_pair)
            part = dot(kt_ref[which * HEAD_DIM : (which + 1) * HEAD_DIM, rows], ds)
            totals[which] = part if totals[which] is None else totals[which] + part
        if unit < len(units):
            p = jnp.exp(now[0])
            behind = p.astype(BF), (p * now[1]).astype(BF)
    both = jnp.concatenate(totals, axis=0) * scale
    gq_ref[...] = both.T.astype(BF)

    @pl.when(step == steps - 1)
    def _():
        lane = lax.broadcasted_iota(jnp.int32, (keys, PAIR), 1)
        gk_ref[...] = (jnp.where(lane < HEAD_DIM, acc_k[0], acc_k[1]) * scale).astype(BF)
        gv_ref[...] = jnp.where(lane < HEAD_DIM, acc_v[0], acc_v[1]).astype(BF)


def attend_backward(
    counts, place, packed, packed_t, grad, grad_t, result_t, log_total, slots, start, count
):
    keys, width = packed.shape
    width //= 3
    pairs = width // PAIR
    bq, chunk = 512, 256
    kernel = functools.partial(attend_backward_kernel, slots, bq, chunk)
    at = lambda p: p + start
    return pl.pallas_call(
        kernel,
        grid=(count, keys // bq),
        in_specs=[
            pl.BlockSpec(memory_space=pltpu.SMEM),
            pl.BlockSpec(memory_space=pltpu.SMEM),
            pl.BlockSpec((bq, PAIR), lambda p, i: (i, at(p))),
            pl.BlockSpec((keys, PAIR), lambda p, i: (0, pairs + at(p))),
            pl.BlockSpec((keys, PAIR), lambda p, i: (0, 2 * pairs + at(p))),
            pl.BlockSpec((PAIR, bq), lambda p, i: (at(p), i)),
            pl.BlockSpec((PAIR, keys), lambda p, i: (pairs + at(p), 0)),
            pl.BlockSpec((bq, PAIR), lambda p, i: (i, at(p))),
            pl.BlockSpec((PAIR, bq), lambda p, i: (at(p), i)),
            pl.BlockSpec((PAIR, bq), lambda p, i: (at(p), i)),
            pl.BlockSpec((1, 8, bq), lambda p, i: (at(p), 0, i)),
        ],
        out_specs=[
            pl.BlockSpec((bq, PAIR), lambda p, i: (i, p)),
            pl.BlockSpec((keys, PAIR), lambda p, i: (0, p)),
            pl.BlockSpec((keys, PAIR), lambda p, i: (0, p)),
        ],
        out_shape=[jax.ShapeDtypeStruct((keys, count * PAIR), BF)] * 3,
        scratch_shapes=[
            pltpu.VMEM((2, keys, PAIR), BF),
            pltpu.VMEM((2, keys, PAIR), BF),
            pltpu.VMEM((2, keys, PAIR), F32),
            pltpu.VMEM((2, keys, PAIR), F32),
        ],
        compiler_params=params(60, "arbitrary", "arbitrary"),
        cost_estimate=cost(
            2 * count * 5 * 2 * keys * keys * 256, 24 * keys * count * PAIR,
            2 * count * keys * keys,
        ),
        name="attend_backward",
    )(counts, place, packed, packed, packed, packed_t, packed_t, grad, grad_t, result_t, log_total)


def normalised(values):
    centred = values - jnp.mean(values, axis=-1, keepdims=True)
    variance = jnp.mean(centred * centred, axis=-1, keepdims=True)
    inverse = lax.rsqrt(variance + EPSILON)
    return centred * inverse, inverse


def norm_pull(grad, gain, unit, inverse):
    scaled = grad * gain
    mean = jnp.mean(scaled, axis=-1, keepdims=True)
    along = jnp.mean(scaled * unit, axis=-1, keepdims=True)
    return inverse * (scaled - mean - unit * along)


def fold(values):
    return jnp.sum(values.reshape(values.shape[0] // 8, 8, values.shape[1]), axis=0)


def feed_forward_kernel(
    chunk, core_ref, tok_ref, mo_ref, ms_ref, cot_ref, wpx_ref, g2_ref, vec_ref, f1b_ref,
    mid_ref, out_ref, send_ref, gn_ref, dw_ref, gf1_ref, gf2_ref, wpo_ref, acc1, acc2, accb, accc, wps_ref,
    w1t_ref, w2t_ref
):
    step = pl.program_id(0)
    steps = pl.num_programs(0)
    width = tok_ref.shape[1]
    half = f1b_ref.shape[1]
    part = width // 2

    def weights(at):
        w1 = g2_ref[:, part + at * chunk : part + (at + 1) * chunk]
        piece, row = divmod(at * chunk, width)
        start = part + half + piece * width
        return w1, g2_ref[row : row + chunk, start : start + width]

    @pl.when(step == 0)
    def _():
        acc1[...] = jnp.zeros_like(acc1)
        acc2[...] = jnp.zeros_like(acc2)
        accb[...] = jnp.zeros_like(accb)
        accc[...] = jnp.zeros_like(accc)
        here = pl.ds(pl.multiple_of(core_ref[0] * part, part), part)
        there = pl.ds(pl.multiple_of((1 - core_ref[0]) * part, part), part)
        wpo_ref[:, here] = g2_ref[here, :part]
        wpo_ref[:, there] = wpx_ref[here, :]
        wps_ref[:, here] = g2_ref[there, :part]
        wps_ref[:, there] = wpx_ref[there, :]
        for at in range(half // chunk):
            cols = slice(at * chunk, (at + 1) * chunk)
            w1, w2 = weights(at)
            w1t_ref[cols, :] = w1.T
            w2t_ref[:, cols] = w2.T

    middle = (
        tok_ref[...].astype(F32)
        + dot(mo_ref[...], wpo_ref[...])
        + dot(ms_ref[...], wps_ref[...])
        + vec_ref[0:1, :]
    )
    mid_ref[...] = middle
    unit, _ = normalised(middle)
    normed = (unit * vec_ref[1:2, :] + vec_ref[2:3, :]).astype(BF)
    normed_t = normed.T
    cot = cot_ref[...]
    out = None
    grad = None

    def front(at):
        w1, _ = weights(at)
        hidden = dot(normed, w1) + f1b_ref[0:1, at * chunk : (at + 1) * chunk]
        return hidden, dot(cot, w2t_ref[:, at * chunk : (at + 1) * chunk])

    def middle_part(hidden, grad_active):
        bell = jnp.exp(hidden * hidden * -0.5)
        inverse = pl.reciprocal(1.0 + jnp.abs(hidden) * (0.3275911 * 0.5**0.5), approx=False)
        tail = ERF_TERMS[4]
        for term in ERF_TERMS[3::-1]:
            tail = tail * inverse + term
        tail = tail * inverse * bell
        below = jnp.where(hidden >= 0.0, 1.0 - tail, tail)
        slope = below + hidden * (bell * 0.3989422804014327)
        return (hidden * below).astype(BF), (grad_active * slope).astype(BF)

    chunks = half // chunk
    ahead = front(0)
    behind = None
    for at in range(chunks + 1):
        now = ahead
        if at + 1 < chunks:
            ahead = front(at + 1)
        if behind is not None:
            active, grad_hidden = behind
            cols = slice((at - 1) * chunk, at * chunk)
            _, w2 = weights(at - 1)
            more = dot(active, w2)
            out = more if out is None else out + more
            more = dot(grad_hidden, w1t_ref[cols, :])
            grad = more if grad is None else grad + more
            acc1[:, cols] += dot(normed_t, grad_hidden)
            acc2[cols, :] += dot(active, cot, 0, 0)
            accb[:, cols] += fold(grad_hidden.astype(F32))
        if at < chunks:
            behind = middle_part(*now)
    accc[...] += fold(cot.astype(F32))
    gn_ref[...] = grad.astype(BF)

    @pl.when(step < steps // 2)
    def _():
        out_ref[...] = middle + out + vec_ref[3:4, :]

    @pl.when(step >= steps // 2)
    def _():
        send_ref[...] = out.astype(BF)

    @pl.when(step == steps - 1)
    def _():
        dw_ref[:, :half] = acc1[...].astype(BF)
        for piece in range(half // width):
            dw_ref[:, half + piece * width : half + (piece + 1) * width] = acc2[
                piece * width : (piece + 1) * width, :
            ].astype(BF)
        gf1_ref[...] = accb[...]
        gf2_ref[...] = accc[...]


def feed_forward(core, tokens, mixed_own, mixed_sib, cot, wp_other, weights, vec, f1b):
    rows, width = tokens.shape
    half = f1b.shape[1]
    heads = mixed_own.shape[1]
    bt, chunk = 512, 768
    blocks = rows // bt
    kernel = functools.partial(feed_forward_kernel, chunk)
    return pl.pallas_call(
        kernel,
        grid=(blocks,),
        in_specs=[
            pl.BlockSpec(memory_space=pltpu.SMEM),
            pl.BlockSpec((bt, width), lambda i: (i, 0)),
            pl.BlockSpec((bt, heads), lambda i: (i, 0)),
            pl.BlockSpec((bt, heads), lambda i: (lax.rem(i + blocks // 2, blocks), 0)),
            pl.BlockSpec((bt, width), lambda i: (i, 0)),
            whole(wp_other.shape),
            whole(weights.shape),
            whole(vec.shape),
            whole(f1b.shape),
        ],
        out_specs=[
            pl.BlockSpec((bt, width), lambda i: (i, 0)),
            pl.BlockSpec((bt, width), lambda i: (jnp.minimum(i, blocks // 2 - 1), 0)),
            pl.BlockSpec((bt, width), lambda i: (jnp.maximum(i - blocks // 2, 0), 0)),
            pl.BlockSpec((bt, width), lambda i: (i, 0)),
            whole((width, 2 * half)),
            whole((8, half)),
            whole((8, width)),
            whole((width // 2, width)),
        ],
        out_shape=[
            jax.ShapeDtypeStruct((rows, width), F32),
            jax.ShapeDtypeStruct((rows // 2, width), F32),
            jax.ShapeDtypeStruct((rows // 2, width), BF),
            jax.ShapeDtypeStruct((rows, width), BF),
            jax.ShapeDtypeStruct((width, 2 * half), BF),
            jax.ShapeDtypeStruct((8, half), F32),
            jax.ShapeDtypeStruct((8, width), F32),
            jax.ShapeDtypeStruct((width // 2, width), BF),
        ],
        scratch_shapes=[
            pltpu.VMEM((width, half), F32),
            pltpu.VMEM((half, width), F32),
            pltpu.VMEM((8, half), F32),
            pltpu.VMEM((8, width), F32),
            pltpu.VMEM((width // 2, width), BF),
            pltpu.VMEM((half, width), BF),
            pltpu.VMEM((width, half), BF),
        ],
        compiler_params=params(60, "arbitrary"),
        cost_estimate=cost(
            2 * rows * width * (6 * half + width), 20 * rows * width + 8 * width * half,
            2 * rows * half,
        ),
        name="feed_forward",
    )(core, tokens, mixed_own, mixed_sib, cot, wp_other, weights, vec, f1b)


def branch_kernel(
    core_ref, mid_ref, ga_ref, gb_ref, cot_ref, mo_ref, ms_ref, wpo_ref, vec_ref,
    gm_ref, do_ref, dot_ref, dwo_ref, dws_ref, vecs_ref, acco, accs, accv, low_ref, wpt_ref
):
    step = pl.program_id(0)
    steps = pl.num_programs(0)
    half = do_ref.shape[1]

    @pl.when(step == 0)
    def _():
        acco[...] = jnp.zeros_like(acco)
        accs[...] = jnp.zeros_like(accs)
        wpt_ref[...] = wpo_ref[...].T
        accv[...] = jnp.zeros_like(accv)

    unit, inverse = normalised(mid_ref[...])
    grad = ga_ref[...].astype(F32) + gb_ref[...].astype(F32)
    accv[0:8, :] += fold(grad * unit)
    accv[8:16, :] += fold(grad)
    grad_middle = cot_ref[...].astype(F32) + norm_pull(grad, vec_ref[1:2, :], unit, inverse)

    @pl.when(step < steps // 2)
    def _():
        gm_ref[...] = grad_middle

    low = grad_middle.astype(BF)
    low_ref[...] = low
    accv[16:24, :] += fold(low.astype(F32))
    back = dot(low, wpt_ref[...])
    do_ref[...] = back.astype(BF)
    dot_ref[...] = back.T.astype(BF)
    mine = low_ref[:, pl.ds(pl.multiple_of(core_ref[0] * half, half), half)]
    acco[...] += dot(mo_ref[...].astype(BF), mine)
    accs[...] += dot(ms_ref[...], mine, 0, 0)

    @pl.when(step == steps - 1)
    def _():
        dwo_ref[...] = acco[...].astype(BF)
        dws_ref[...] = accs[...].astype(BF)
        vecs_ref[...] = accv[...]


def branch(core, middle, grad_own, grad_sib, cot, result_t, mixed_sib, wp_own, vec):
    rows, width = middle.shape
    half = mixed_sib.shape[1]
    bt = 512
    blocks = rows // bt
    swap = lambda i: (lax.rem(i + blocks // 2, blocks), 0)
    straight = lambda i: (i, 0)
    return pl.pallas_call(
        branch_kernel,
        grid=(blocks,),
        in_specs=[
            pl.BlockSpec(memory_space=pltpu.SMEM),
            pl.BlockSpec((bt, width), straight),
            pl.BlockSpec((bt, width), straight),
            pl.BlockSpec((bt, width), swap),
            pl.BlockSpec((bt, width), straight),
            pl.BlockSpec((half, bt), lambda i: (0, i)),
            pl.BlockSpec((bt, half), swap),
            whole(wp_own.shape),
            whole(vec.shape),
        ],
        out_specs=[
            pl.BlockSpec((bt, width), lambda i: (jnp.minimum(i, blocks // 2 - 1), 0)),
            pl.BlockSpec((bt, half), straight),
            pl.BlockSpec((half, bt), lambda i: (0, i)),
            whole((half, half)),
            whole((half, half)),
            whole((24, width)),
        ],
        out_shape=[
            jax.ShapeDtypeStruct((rows // 2, width), F32),
            jax.ShapeDtypeStruct((rows, half), BF),
            jax.ShapeDtypeStruct((half, rows), BF),
            jax.ShapeDtypeStruct((half, half), BF),
            jax.ShapeDtypeStruct((half, half), BF),
            jax.ShapeDtypeStruct((24, width), F32),
        ],
        scratch_shapes=[
            pltpu.VMEM((half, half), F32),
            pltpu.VMEM((half, half), F32),
            pltpu.VMEM((24, width), F32),
            pltpu.VMEM((bt, width), BF),
            pltpu.VMEM((width, half), BF),
        ],
        compiler_params=params(60, "arbitrary"),
        cost_estimate=cost(2 * rows * width * 3 * half, 18 * rows * width),
        name="branch",
    )(core, middle, grad_own, grad_sib, cot, result_t, mixed_sib, wp_own, vec)


def weight_grad_kernel(
    core_ref, normed_ref, gq_ref, gk_ref, gv_ref, dwo_ref, dws_ref, dw_ref, qv_ref, accw, accqv
):
    step = pl.program_id(0)
    steps = pl.num_programs(0)
    part = gq_ref.shape[1]

    @pl.when(step == 0)
    def _():
        accw[...] = jnp.zeros_like(accw)
        accqv[...] = jnp.zeros_like(accqv)

    normed_t = normed_ref[...].T
    for at, ref in enumerate((gq_ref, gk_ref, gv_ref)):
        cols = slice(at * part, (at + 1) * part)
        value = ref[...]
        accw[:, cols] += dot(normed_t, value)
        if at != 1:
            here = 0 if at == 0 else 8
            accqv[here : here + 8, :] += fold(value.astype(F32))

    @pl.when(step == steps - 1)
    def _():
        dw_ref[:, : 3 * part] = accw[...].astype(BF)
        rows = dwo_ref.shape[0]
        first_core = core_ref[0] == 0
        dwo, dws = dwo_ref[...], dws_ref[...]
        dw_ref[:rows, 3 * part :] = jnp.where(first_core, dwo, dws)
        dw_ref[rows:, 3 * part :] = jnp.where(first_core, dws, dwo)
        qv_ref[...] = accqv[...]


def weight_grad(core, normed, gq, gk, gv, dw_own, dw_sib):
    rows, width = normed.shape
    part = gq.shape[1]
    bt = 512
    wide = 3 * part + dw_own.shape[1]
    straight = lambda i: (i, 0)
    return pl.pallas_call(
        weight_grad_kernel,
        grid=(rows // bt,),
        in_specs=[
            pl.BlockSpec(memory_space=pltpu.SMEM),
            pl.BlockSpec((bt, width), straight),
            pl.BlockSpec((bt, part), straight),
            pl.BlockSpec((bt, part), straight),
            pl.BlockSpec((bt, part), straight),
            whole(dw_own.shape),
            whole(dw_sib.shape),
        ],
        out_specs=[whole((width, wide)), whole((16, part))],
        out_shape=[
            jax.ShapeDtypeStruct((width, wide), BF),
            jax.ShapeDtypeStruct((16, part), F32),
        ],
        scratch_shapes=[pltpu.VMEM((width, 3 * part), F32), pltpu.VMEM((16, part), F32)],
        compiler_params=params(60, "arbitrary"),
        cost_estimate=cost(2 * rows * width * 3 * part, 2 * rows * (width + 3 * part)),
        name="weight_grad",
    )(core, normed, gq, gk, gv, dw_own, dw_sib)


def project_back_kernel(
    tok_ref, normed_ref, gqa_ref, gka_ref, gva_ref, gq_ref, gk_ref, gv_ref, w_ref,
    own_ref, sib_ref, dw_ref, vecs_ref, qv_ref, accw, accv, accqv, wt_ref
):
    step = pl.program_id(0)
    steps = pl.num_programs(0)
    early = gqa_ref.shape[1]
    part = gq_ref.shape[1]
    wide = early + part

    @pl.when(step == 0)
    def _():
        accw[...] = jnp.zeros_like(accw)
        accv[...] = jnp.zeros_like(accv)
        accqv[...] = jnp.zeros_like(accqv)
        wt_ref[...] = w_ref[...].T

    unit, _ = normalised(tok_ref[...].astype(F32))
    normed_t = normed_ref[...].T
    grad = None
    before = (gqa_ref, gka_ref, gva_ref)
    for at, ref in enumerate((gq_ref, gk_ref, gv_ref)):
        cols = slice(at * part, (at + 1) * part)
        value = ref[...]
        more = dot(
            jnp.concatenate([before[at][...], value], axis=1),
            wt_ref[at * wide : (at + 1) * wide, :],
        )
        grad = more if grad is None else grad + more
        accw[:, cols] += dot(normed_t, value)
        if at != 1:
            here = 0 if at == 0 else 8
            accqv[here : here + 8, :] += fold(value.astype(F32))
    accv[0:8, :] += fold(grad * unit)
    accv[8:16, :] += fold(grad)

    @pl.when(step < steps // 2)
    def _():
        own_ref[...] = grad

    @pl.when(step >= steps // 2)
    def _():
        sib_ref[...] = grad.astype(BF)

    @pl.when(step == steps - 1)
    def _():
        dw_ref[...] = accw[...].astype(BF)
        vecs_ref[...] = accv[...]
        qv_ref[...] = accqv[...]


def project_back(tokens, normed, before, grads, weight):
    rows, width = tokens.shape
    early, part = before[0].shape[1], grads[0].shape[1]
    bt = 512
    blocks = rows // bt
    straight = lambda i: (i, 0)
    return pl.pallas_call(
        project_back_kernel,
        grid=(blocks,),
        in_specs=[pl.BlockSpec((bt, width), straight)] * 2
        + [pl.BlockSpec((bt, early), straight)] * 3
        + [pl.BlockSpec((bt, part), straight)] * 3
        + [whole(weight.shape)],
        out_specs=[
            pl.BlockSpec((bt, width), lambda i: (jnp.minimum(i, blocks // 2 - 1), 0)),
            pl.BlockSpec((bt, width), lambda i: (jnp.maximum(i - blocks // 2, 0), 0)),
            whole((width, 3 * part)),
            whole((16, width)),
            whole((16, part)),
        ],
        out_shape=[
            jax.ShapeDtypeStruct((rows // 2, width), F32),
            jax.ShapeDtypeStruct((rows // 2, width), BF),
            jax.ShapeDtypeStruct((width, 3 * part), BF),
            jax.ShapeDtypeStruct((16, width), F32),
            jax.ShapeDtypeStruct((16, part), F32),
        ],
        scratch_shapes=[
            pltpu.VMEM((width, 3 * part), F32),
            pltpu.VMEM((16, width), F32),
            pltpu.VMEM((16, part), F32),
            pltpu.VMEM((3 * (early + part), width), BF),
        ],
        compiler_params=params(60, "arbitrary"),
        cost_estimate=cost(2 * rows * width * (6 * part + 3 * early), 14 * rows * width),
        name="project_back",
    )(tokens, normed, *before, *grads, weight)


def input_back_kernel(tok_ref, own_ref, sib_ref, gm_ref, vec_ref, *out_refs):
    unit, inverse = normalised(tok_ref[...].astype(F32))
    grad = own_ref[...] + sib_ref[...].astype(F32)
    total = gm_ref[...] + norm_pull(grad, vec_ref[0:1, :], unit, inverse)
    step = pl.program_id(0)
    for at, ref in enumerate(out_refs):

        @pl.when(step == at)
        def _():
            ref[...] = total.astype(ref.dtype)


def input_back(tokens, grad_own, grad_sib, grad_middle, vec, part, dtype):
    rows, width = grad_own.shape
    bt = rows // 4
    here = lambda i: (2 * part + i, 0)
    return pl.pallas_call(
        input_back_kernel,
        grid=(2,),
        in_specs=[pl.BlockSpec((bt, width), here)] * 4 + [whole(vec.shape)],
        out_specs=[whole((bt, width))] * 2,
        out_shape=[jax.ShapeDtypeStruct((bt, width), dtype)] * 2,
        compiler_params=params(60, "arbitrary"),
        cost_estimate=cost(10 * rows * width, 8 * rows * width),
        name="input_back",
    )(tokens, grad_own, grad_sib, grad_middle, vec)


def finish_ff_kernel(place_ref, mine_ref, other_ref, fc1_ref, fc2_ref):
    first_core = lax.rem(place_ref[0], 2) == 0
    shard, ff = fc1_ref.shape
    half = ff // 2
    quarter = fc2_ref.shape[0] // 4
    width = fc2_ref.shape[1]
    owners = ff // (4 * quarter)
    mine = mine_ref[...].astype(F32)
    other = other_ref[...].astype(F32)
    cores = (jnp.where(first_core, mine, other), jnp.where(first_core, other, mine))
    pieces = []
    for owner in range(owners):
        for value in cores:
            for piece in range(2):
                start = (piece * owners + owner) * quarter
                pieces.append(value[:, start : start + quarter])
    fc1_ref[...] = jnp.concatenate(pieces, axis=1)
    for at, value in enumerate(cores):
        for piece in range(2):
            row = (2 * at + piece) * quarter
            start = half + piece * width
            fc2_ref[row : row + quarter, :] = value[:, start : start + width]


def finish_ff(place, mine, other, width, quarter):
    shard, wide = mine.shape
    return pl.pallas_call(
        finish_ff_kernel,
        grid=(1,),
        in_specs=[
            pl.BlockSpec(memory_space=pltpu.SMEM), whole(mine.shape), whole(other.shape)
        ],
        out_specs=[whole((shard, wide)), whole((4 * quarter, width))],
        out_shape=[
            jax.ShapeDtypeStruct((shard, wide), F32),
            jax.ShapeDtypeStruct((4 * quarter, width), F32),
        ],
        compiler_params=params(60, "arbitrary"),
        cost_estimate=cost(0, 12 * shard * wide),
        name="finish_ff",
    )(place, mine, other)


def finish_attend_kernel(
    place_ref, em_ref, eo_ref, la_ref, lb_ref, lc_ref, ld_ref, qkv_ref, proj_ref, small_ref
):
    first_core = lax.rem(place_ref[0], 2) == 0
    shard, width = proj_ref.shape
    part = width // 2
    late = la_ref.shape[1] // 3
    early = part - late
    rows = la_ref.shape[0] - shard
    lm = la_ref[...].astype(F32) + lb_ref[...].astype(F32)
    lo = lc_ref[...].astype(F32) + ld_ref[...].astype(F32)
    small_ref[...] = lm[:rows] + lo[:rows]
    em = em_ref[...].astype(F32)
    eo = eo_ref[...].astype(F32)
    firsts = (jnp.where(first_core, em, eo), jnp.where(first_core, eo, em))
    lasts = (jnp.where(first_core, lm, lo)[rows:], jnp.where(first_core, lo, lm)[rows:])
    for at in range(3):
        for of in range(2):
            start = at * width + of * part
            qkv_ref[:, start : start + early] = firsts[of][:, at * early : (at + 1) * early]
            qkv_ref[:, start + early : start + part] = lasts[of][:, at * late : (at + 1) * late]
    for of in range(2):
        proj_ref[:, of * part : (of + 1) * part] = firsts[of][:, 3 * early :]


def finish_attend(place, early_mine, early_other, late_mine, late_b, late_c, late_d, width):
    shard = early_mine.shape[0]
    rows = late_mine.shape[0] - shard
    return pl.pallas_call(
        finish_attend_kernel,
        grid=(1,),
        in_specs=[pl.BlockSpec(memory_space=pltpu.SMEM)]
        + [whole(value.shape) for value in (early_mine, early_other)]
        + [whole(late_mine.shape)] * 4,
        out_specs=[
            whole((shard, 3 * width)), whole((shard, width)), whole((rows, late_mine.shape[1]))
        ],
        out_shape=[
            jax.ShapeDtypeStruct((shard, 3 * width), F32),
            jax.ShapeDtypeStruct((shard, width), F32),
            jax.ShapeDtypeStruct((rows, late_mine.shape[1]), F32),
        ],
        compiler_params=params(60, "arbitrary"),
        cost_estimate=cost(0, 24 * shard * width),
        name="finish_attend",
    )(place, early_mine, early_other, late_mine, late_b, late_c, late_d)


def pack_kernel(place_ref, *refs):
    vectors, (qkv_ref, proj_ref, fc1_ref, fc2_ref, one_ref, two_ref) = refs[:-6], refs[-6:]
    first_core = lax.rem(place_ref[0], 2) == 0
    first_chip = place_ref[0] // 2 == 0
    shard, width = proj_ref.shape
    part = width // 2
    ff = fc1_ref.shape[1]
    owners = width // shard
    quarter = ff // owners // 4
    half = ff // 2
    one_ref[:VEC_ROWS, :] = jnp.zeros((VEC_ROWS, 3 * part), BF)
    for at, ref in enumerate(vectors):
        one_ref[at : at + 1, : ref.shape[1]] = ref[...]
    for at in range(3):
        low = qkv_ref[:, at * width : at * width + part]
        high = qkv_ref[:, at * width + part : (at + 1) * width]
        mine = jnp.where(first_core, low, high)
        mine = jnp.where(first_chip, mine[: shard // 2], mine[shard // 2 :])
        one_ref[VEC_ROWS:, at * part : (at + 1) * part] = mine
    two_ref[:, :part] = jnp.where(first_core, proj_ref[:, :part], proj_ref[:, part:])
    pieces_low, pieces_high = [], []
    for piece in range(2):
        for owner in range(owners):
            base = owner * 4 * quarter + piece * quarter
            pieces_low.append(fc1_ref[:, base : base + quarter])
            pieces_high.append(fc1_ref[:, base + 2 * quarter : base + 3 * quarter])
    two_ref[:, part : part + half] = jnp.where(
        first_core, jnp.concatenate(pieces_low, axis=1), jnp.concatenate(pieces_high, axis=1)
    )
    for piece in range(2):
        low = fc2_ref[piece * quarter : (piece + 1) * quarter, :]
        high = fc2_ref[(2 + piece) * quarter : (3 + piece) * quarter, :]
        start = part + half + piece * width
        two_ref[:, start : start + width] = jnp.where(first_core, low, high)


def pack_weights(place, vectors, qkv, proj, fc1, fc2):
    shard, width = proj.shape
    half = fc1.shape[1] // 2
    part = width // 2
    vectors = [vector.reshape(1, -1) for vector in vectors]
    values = (*vectors, qkv, proj, fc1, fc2)
    rows = VEC_ROWS + shard // 2
    return pl.pallas_call(
        pack_kernel,
        grid=(1,),
        in_specs=[pl.BlockSpec(memory_space=pltpu.SMEM)] + [whole(value.shape) for value in values],
        out_specs=[whole((rows, 3 * part)), whole((shard, 5 * part + half))],
        out_shape=[
            jax.ShapeDtypeStruct((rows, 3 * part), BF),
            jax.ShapeDtypeStruct((shard, 5 * part + half), BF),
        ],
        compiler_params=params(60, "arbitrary"),
        cost_estimate=cost(0, 5 * shard * width * 8),
        name="pack_weights",
    )(place, *values)


def project_kernel(tok_ref, w_ref, bias_ref, vec_ref, out_ref, out_t_ref, normed_ref):
    unit, _ = normalised(tok_ref[...].astype(F32))
    normed = (unit * vec_ref[0:1, :] + vec_ref[1:2, :]).astype(BF)
    normed_ref[...] = normed
    packed = dot(normed, w_ref[...]) + bias_ref[0:1, :]
    out_ref[...] = packed.astype(BF)
    out_t_ref[...] = packed.T.astype(BF)


def project(tokens, weight, bias, vec):
    rows, width = tokens.shape
    wide = weight.shape[1]
    bt = 512
    return pl.pallas_call(
        project_kernel,
        grid=(rows // bt,),
        in_specs=[
            pl.BlockSpec((bt, width), lambda i: (i, 0)),
            whole(weight.shape),
            whole(bias.shape),
            whole(vec.shape),
        ],
        out_specs=[
            pl.BlockSpec((bt, wide), lambda i: (i, 0)),
            pl.BlockSpec((wide, bt), lambda i: (0, i)),
            pl.BlockSpec((bt, width), lambda i: (i, 0)),
        ],
        out_shape=[
            jax.ShapeDtypeStruct((rows, wide), BF),
            jax.ShapeDtypeStruct((wide, rows), BF),
            jax.ShapeDtypeStruct((rows, width), BF),
        ],
        compiler_params=params(60, "arbitrary"),
        cost_estimate=cost(2 * rows * width * wide, 12 * rows * width),
        name="project",
    )(tokens, weight, bias, vec)


def exchange(value):
    return lax.all_to_all(value, "fsdp", split_axis=0, concat_axis=0, tiled=True)


def per_device(
    tokens,
    counts,
    norm1_gain,
    norm1_bias,
    qkv_weight,
    query_bias,
    value_bias,
    proj_weight,
    proj_bias,
    norm2_gain,
    norm2_bias,
    fc1_weight,
    fc1_bias,
    fc2_weight,
    fc2_bias,
    cotangent,
):
    images, slots, width = tokens.shape
    owners = lax.axis_size("fsdp")
    seq = lax.axis_size("seq")
    place = lax.axis_index("seq")
    core = lax.rem(place, 2)
    image = place // 2
    part = width // 2
    shard = width // owners
    ff = fc1_weight.shape[1]
    ff_shard = ff // owners
    quarter = ff_shard // 4
    half = ff // 2
    to_sibling = [(at, at ^ 1) for at in range(seq)]
    to_partner = [(at, at ^ 2) for at in range(seq)]

    def sibling(value):
        return lax.ppermute(value, "seq", to_sibling)

    def partner(value):
        return lax.ppermute(value, "seq", to_partner)

    def pick(value, at, axis):
        return lax.dynamic_index_in_dim(value, at, axis, keepdims=False)

    place_row = place.reshape(1).astype(jnp.int32)
    core_row = core.reshape(1).astype(jnp.int32)
    small = [
        norm1_gain, norm1_bias, query_bias, value_bias, proj_bias, norm2_gain, norm2_bias,
        fc2_bias, fc1_bias,
    ]
    one, two = pack_weights(
        place_row, small, qkv_weight, proj_weight, fc1_weight, fc2_weight
    )
    one, tokens, cotangent = lax.optimization_barrier((one, tokens, cotangent))
    mine_one = lax.all_gather(one, "fsdp", axis=0, tiled=False)
    def collect(value, theirs):
        mine = pick(value, image, 0)
        return jnp.concatenate([mine, theirs, sibling(mine), sibling(theirs)], axis=0)

    tok_came = partner(pick(tokens, 1 - image, 0))
    cot_came = partner(pick(cotangent, 1 - image, 0))
    mine_one, two, tok_came, cot_came = lax.optimization_barrier(
        (mine_one, two, tok_came, cot_came)
    )
    tok = collect(tokens, tok_came)
    cot = collect(cotangent, cot_came)
    second = lax.all_gather(two, "fsdp", axis=0, tiled=True)

    own_rows = mine_one[:, VEC_ROWS:]
    other_rows = partner(own_rows)
    w_qkv = jnp.where(
        image == 0,
        jnp.stack([own_rows, other_rows], axis=1),
        jnp.stack([other_rows, own_rows], axis=1),
    ).reshape(width, 3 * part)

    vecs = mine_one[:, :8, :shard].astype(F32).transpose(1, 0, 2).reshape(8, width)
    g1, b1, qb, vb, pb, g2, b2, f2b = vecs
    f1b = mine_one[:, 8, :ff_shard].astype(F32)
    f1b = pick(f1b.reshape(owners, 2, 2, quarter), core, 1)
    f1b = f1b.transpose(1, 0, 2).reshape(1, half)

    def mine_of(vector):
        return lax.dynamic_slice_in_dim(vector, core * part, part, 0)

    qkv_bias = jnp.concatenate([mine_of(qb), jnp.zeros((part,), F32), mine_of(vb)])
    vec_one = jnp.concatenate([jnp.stack([g1, b1]), jnp.zeros((6, width), F32)])
    packed, packed_t, normed = project(tok, w_qkv, qkv_bias.reshape(1, 3 * part), vec_one)
    packed, cot = lax.optimization_barrier((packed, cot))
    mixed, result_t, log_total = attend_forward(counts, place_row, packed, packed_t, slots)
    mixed_sib = sibling(mixed)

    wp_other = sibling(second[:, :part])
    vec_two = jnp.concatenate([jnp.stack([pb, g2, b2, f2b]), jnp.zeros((4, width), F32)])
    middle, out_own, out_send, gn_part, dw_ff, gf1, gf2, wp_own = feed_forward(
        core_row, tok, mixed, mixed_sib, cot, wp_other, second, vec_two, f1b
    )
    scattered_one = lax.psum_scatter(dw_ff, "fsdp", scatter_dimension=0, tiled=True)
    gn_sib = sibling(gn_part)
    rows_own = 2 * slots

    def hand_back(own, came):
        kept_part = own[:slots]
        came = came.astype(own.dtype)
        straight = jnp.stack([kept_part, came])
        crossed = jnp.stack([came, kept_part])
        return jnp.where(image == 0, straight, crossed)

    grad_middle, grad_mixed, grad_mixed_t, dwp_own, dwp_sib, vec_back = branch(
        core_row, middle, gn_part, gn_sib, cot, result_t, mixed_sib, wp_own, vec_two
    )
    grad_mixed, out_send, out_own = lax.optimization_barrier((grad_mixed, out_send, out_own))
    out_sib = sibling(out_send)
    early, late = 2, 1
    attend = functools.partial(attend_backward, counts, place_row, packed, packed_t)
    before = attend(grad_mixed, grad_mixed_t, result_t, log_total, slots, 0, early)
    before, out_sib = lax.optimization_barrier((before, out_sib))
    block_one, qv_early = weight_grad(core_row, normed, *before, dwp_own, dwp_sib)
    out_own = (out_own + out_sib.astype(F32)).astype(BF)
    block_one = block_one.reshape(owners, shard, -1)
    grad_mixed, out_own, block_one = lax.optimization_barrier((grad_mixed, out_own, block_one))
    came_one = exchange(block_one)
    out_came = partner(out_own[slots:])
    grads = attend(grad_mixed, grad_mixed_t, result_t, log_total, slots, early, late)

    def total(came):
        return jnp.sum(came.astype(F32), axis=0).astype(BF)

    def join(value, came):
        return (value.astype(F32) + came.astype(F32)).astype(BF)

    scattered_one, out_came, grads = lax.optimization_barrier((scattered_one, out_came, grads))
    output = hand_back(out_own, out_came)
    one_came = partner(scattered_one)
    gn1_own, gn1_send, dw_late, vec_first, qv_late = project_back(tok, normed, before, grads, w_qkv)

    def spread(vector):
        both = jnp.zeros((2, part), F32)
        return lax.dynamic_update_index_in_dim(both, vector, core, 0).reshape(width)

    def rows_of(block):
        return jnp.sum(block.reshape(block.shape[0] // 8, 8, block.shape[1]), axis=1)

    once = (core == 0).astype(F32)
    gg1, gb1 = rows_of(vec_first)
    gqb, gvb = rows_of(jnp.concatenate([qv_early, qv_late], axis=1))
    gg2, gb2, gpb = rows_of(vec_back) * once
    gf2b = jnp.sum(gf2, axis=0) * once
    gf1b = jnp.sum(gf1, axis=0).reshape(2, owners, quarter).transpose(1, 0, 2)
    gf1b = lax.dynamic_update_index_in_dim(
        jnp.zeros((owners, 2, 2, quarter), F32), gf1b, core, 1
    ).reshape(owners, ff_shard)
    late_wide = 3 * late * PAIR
    small_grads = jnp.stack(
        [gg1, gb1, spread(gqb), spread(gvb), gpb, gg2, gb2, gf2b]
    ).reshape(8, owners, shard).transpose(1, 0, 2)
    small_block = jnp.concatenate(
        [
            jnp.pad(small_grads, ((0, 0), (0, 0), (0, late_wide - shard))),
            jnp.pad(gf1b[:, None], ((0, 0), (0, VEC_ROWS - 9), (0, late_wide - ff_shard))),
        ],
        axis=1,
    ).astype(BF)
    block_two = jnp.concatenate(
        [small_block, dw_late.reshape(owners, shard, late_wide)], axis=1
    )
    gn1_sib = sibling(gn1_send)
    block_two, came_one = lax.optimization_barrier((block_two, came_one))
    came_two = exchange(block_two)
    pull = functools.partial(input_back, tok, gn1_own, gn1_sib, grad_middle, vec_one)
    input_send = pull(1, BF)
    came_a, came_b = partner(input_send[0]), partner(input_send[1])
    early_total = total(came_one)
    early_came = partner(early_total)
    one_came, input_send, gn1_own = lax.optimization_barrier((one_came, input_send, gn1_own))
    input_own = input_back(tok, gn1_own, gn1_sib, grad_middle, vec_one, 0, F32)
    one_sum = join(scattered_one, one_came)
    came_two, one_sum = lax.optimization_barrier((came_two, one_sum))
    one_other = sibling(one_sum)
    grad_fc1, grad_fc2 = finish_ff(place_row, one_sum, one_other, width, quarter)

    early_sum = join(early_total, early_came)
    early_other = sibling(early_sum)
    late_total, came_a, input_own, output = lax.optimization_barrier(
        (total(came_two), came_a, input_own, output)
    )
    late_came = [
        lax.ppermute(late_total, "seq", [(at, at ^ flip) for at in range(seq)])
        for flip in (2, 1, 3)
    ]
    kept = jnp.stack(input_own)
    late_came, grad_fc1, grad_fc2, came_b, kept = lax.optimization_barrier(
        (late_came, grad_fc1, grad_fc2, came_b, kept)
    )
    came = jnp.stack([came_a, came_b]).astype(F32)
    input_grad = jnp.where(image == 0, jnp.stack([kept, came]), jnp.stack([came, kept]))
    input_grad = input_grad.reshape(images, slots, width)
    grad_qkv, grad_proj, small_sum = finish_attend(
        place_row, early_sum, early_other, late_total, *late_came, width
    )
    s = [small_sum[at, :shard] for at in range(8)]
    grad_f1b = small_sum[8, :ff_shard]
    return (
        output,
        input_grad,
        s[0],
        s[1],
        grad_qkv,
        s[2],
        s[3],
        grad_proj,
        s[4],
        s[5],
        s[6],
        grad_fc1,
        grad_f1b,
        grad_fc2,
        s[7],
    )


def solution(mesh):
    placed = (
        P("fsdp", "seq", None),
        P("fsdp", None),
        P("fsdp"),
        P("fsdp"),
        P("fsdp", None),
        P("fsdp"),
        P("fsdp"),
        P("fsdp", None),
        P("fsdp"),
        P("fsdp"),
        P("fsdp"),
        P("fsdp", None),
        P("fsdp"),
        P("fsdp", None),
        P("fsdp"),
        P("fsdp", "seq", None),
    )
    return jax.shard_map(
        per_device,
        mesh=mesh,
        in_specs=placed,
        out_specs=(
            P("fsdp", "seq", None),
            P("fsdp", "seq", None),
            P("fsdp"),
            P("fsdp"),
            P("fsdp", None),
            P("fsdp"),
            P("fsdp"),
            P("fsdp", None),
            P("fsdp"),
            P("fsdp"),
            P("fsdp"),
            P("fsdp", None),
            P("fsdp"),
            P("fsdp", None),
            P("fsdp"),
        ),
        check_vma=False,
    )
```
